32 devices in a mesh: fsdp: 4 (over y, core), ctx: 8 (over z, x).
Axes of the slice: x: 2, y: 2, z: 4, core: 2. Of those that a mesh axis runs over, the one named last changes fastest.
Arguments:
- tokens: bfloat16 [8, 1024, 2048], P('fsdp', 'ctx'), may hold values from -6 to 6
- lengths: int32 [8], P('fsdp'), may hold values from 1024 to 1024, as said below
- cotangent: bfloat16 [8, 1024, 2048], P('fsdp', 'ctx'), may hold values from -6 to 6
- norm_gain: bfloat16 [2048], P('fsdp'), may hold values from 0.5 to 1.5
- norm_shift: bfloat16 [2048], P('fsdp'), may hold values from -1.75 to 1.75
- query_weight: bfloat16 [2048, 2048], P('fsdp'), may hold values from -0.125 to 0.125
- query_bias: bfloat16 [2048], P('fsdp'), may hold values from -3 to 3
- keyval_weight: bfloat16 [2048, 256], P('fsdp'), may hold values from -0.125 to 0.125
- value_bias: bfloat16 [128], P('fsdp'), may hold values from -0.3125 to 0.3125
- mixer_weight: bfloat16 [2048, 2048], P('fsdp'), may hold values from -0.5 to 0.5
- mixer_bias: bfloat16 [2048], P('fsdp'), may hold values from -1.75 to 1.75
- ffnorm_gain: bfloat16 [2048], P('fsdp'), may hold values from 0.5 to 1.5
- ffnorm_shift: bfloat16 [2048], P('fsdp'), may hold values from -1.75 to 1.75
- up_weight: bfloat16 [2048, 8192], P('fsdp'), may hold values from -0.125 to 0.125
- up_bias: bfloat16 [8192], P('fsdp'), may hold values from -3 to 3
- down_weight: bfloat16 [8192, 2048], P('fsdp'), may hold values from -0.0625 to 0.0625
- down_bias: bfloat16 [2048], P('fsdp'), may hold values from -1.75 to 1.75
Outputs:
- layer_out: bfloat16 [8, 1024, 2048], P('fsdp', 'ctx')
- tokens_grad: bfloat16 [8, 1024, 2048], P('fsdp', 'ctx')
- gain_grad: float32 [2048], P(('fsdp', 'ctx'))
- shift_grad: float32 [2048], P(('fsdp', 'ctx'))
- query_grad: float32 [2048, 2048], P(('fsdp', 'ctx'))
- qbias_grad: float32 [2048], P(('fsdp', 'ctx'))
- keyval_grad: float32 [2048, 256], P(('fsdp', 'ctx'))
- vbias_grad: float32 [128], P(('fsdp', 'ctx'))
- mixer_grad: float32 [2048, 2048], P(('fsdp', 'ctx'))
- mbias_grad: float32 [2048], P(('fsdp', 'ctx'))
- ffgain_grad: float32 [2048], P(('fsdp', 'ctx'))
- ffshift_grad: float32 [2048], P(('fsdp', 'ctx'))
- up_grad: float32 [2048, 8192], P(('fsdp', 'ctx'))
- ubias_grad: float32 [8192], P(('fsdp', 'ctx'))
- down_grad: float32 [8192, 2048], P(('fsdp', 'ctx'))
- dbias_grad: float32 [2048], P(('fsdp', 'ctx'))
The draws below stay inside these ranges and needn't reach their ends.
Inputs may be any that keep to these rules, and one draw needn't show every extreme that they name: Slot s holds one sequence in its first lengths[s] positions and padding after it; of the 2 slots of each index of fsdp, one is full.
All inputs are finite; a program needn't handle non-finite values.
Results may differ from the reference program's by a relative error of at most 0.015.
Values may be sent and summed in bfloat16 or wider, within the bound.
A program may use at most 384 MiB of HBM per device.

```python
import jax
import jax.numpy as jnp
from jax import lax

D = 2048
HEADS = 16
HEAD_DIM = 128
FF = 8192
SLOTS_DEV = 2
MIN_LEN = 1024
SLOT = 1024
SLOTS = 8


def draw_lengths(key, part):
    key = jax.random.fold_in(key, 7)
    first_key, second_key = jax.random.split(key)
    shortest = min(MIN_LEN, SLOT)
    drawn = jax.random.randint(first_key, (SLOTS,), shortest, SLOT + 1)
    chosen = jax.random.randint(second_key, (SLOTS // SLOTS_DEV, 1), 0, SLOTS_DEV)
    full_slot = (jnp.arange(SLOTS_DEV)[None, :] == chosen).reshape(SLOTS)
    return jnp.where(full_slot, SLOT, drawn).astype(jnp.int32)


def steps_of(stream_key, dims, shards, low, top_value):
    def one(position, shards_of):
        heights = jax.random.uniform(jax.random.fold_in(jax.random.fold_in(stream_key, 6), position), (shards_of,), jnp.float32, low / len(shards), top_value / len(shards))
        return jnp.repeat(jnp.exp(heights), dims[position] // shards_of).reshape((-1,) + (1,) * (len(dims) - position - 1))

    level = one(*shards[0])
    for cut in shards[1:]:
        level = level * one(*cut)
    return level


def gaussian(stream_key, extent, deviation, limit, pieces=(), held_as=jnp.bfloat16):
    values = deviation * jax.random.normal(stream_key, extent, jnp.float32)
    if pieces:
        values = values * steps_of(stream_key, extent, pieces, -0.22, 0.18)
    return jnp.clip(values, -limit, limit).astype(held_as)


def setup_inputs(seed: int = 0) -> dict:
    splits = jax.random.split(jax.random.key(seed), 18)
    return {
        "tokens": gaussian(splits[0], (SLOTS, SLOT, D), 1.0, 6.0, ((0, 4), (1, 8))),
        "lengths": draw_lengths(jax.random.fold_in(splits[17], 71), 0),
        "cotangent": gaussian(splits[2], (SLOTS, SLOT, D), 1.0, 6.0, ((0, 4), (1, 8))),
        "norm_gain": jnp.clip(1.0 + 0.1 * jax.random.normal(splits[3], (D,), jnp.float32), 0.5, 1.5).astype(jnp.bfloat16),
        "norm_shift": gaussian(splits[4], (D,), 0.3, 1.75, ((0, 4),)),
        "query_weight": gaussian(splits[5], (D, D), D ** -0.5, 0.125, ((0, 4),)),
        "query_bias": gaussian(splits[6], (D,), 0.5, 3.0, ((0, 4),)),
        "keyval_weight": gaussian(splits[7], (D, 2 * HEAD_DIM), D ** -0.5, 0.125, ((0, 4),)),
        "value_bias": gaussian(splits[8], (HEAD_DIM,), 0.05, 0.3125, ((0, 4),)),
        "mixer_weight": gaussian(splits[9], (D, D), (max(1, D * 64 // SLOT)) ** -0.5, 0.5, ((0, 4),)),
        "mixer_bias": gaussian(splits[10], (D,), 0.3, 1.75, ((0, 4),)),
        "ffnorm_gain": jnp.clip(1.0 + 0.1 * jax.random.normal(splits[11], (D,), jnp.float32), 0.5, 1.5).astype(jnp.bfloat16),
        "ffnorm_shift": gaussian(splits[12], (D,), 0.3, 1.75, ((0, 4),)),
        "up_weight": gaussian(splits[13], (D, FF), D ** -0.5, 0.125, ((0, 4),)),
        "up_bias": gaussian(splits[14], (FF,), 0.5, 3.0, ((0, 4),)),
        "down_weight": gaussian(splits[15], (FF, D), FF ** -0.5, 0.0625, ((0, 4),)),
        "down_bias": gaussian(splits[16], (D,), 0.3, 1.75, ((0, 4),)),
    }


@jax.custom_vjp
def low(v):
    return lax.optimization_barrier(v.astype(jnp.bfloat16)).astype(jnp.float32)

@jax.custom_vjp
def low_back(v):
    return v

def low_keep(v):
    return (low(v), None)

def low_pass(kept, grad):
    return (grad,)

def back_keep(v):
    return (v, None)

def back_low(kept, grad):
    return (low(grad),)
low.defvjp(low_keep, low_pass)
low_back.defvjp(back_keep, back_low)
EPSILON = 1e-05
NEG_LARGE = -1e+30

def matmul(left_side, right_side):
    return jnp.dot(left_side, right_side, precision=lax.Precision.HIGHEST, preferred_element_type=jnp.float32)

def normalize(values, gain, shift):
    center = values - lax.optimization_barrier(jnp.mean(values, axis=-1, keepdims=True))
    spread = lax.optimization_barrier(jnp.mean(center * center, axis=-1, keepdims=True))
    return center * lax.rsqrt(spread + EPSILON) * gain + shift

def attend_block(block_queries, block_pos, key_rows, value_rows, length):
    scores = low_back(matmul(block_queries, key_rows.T) * HEAD_DIM ** (-0.5))
    key_pos = jnp.arange(SLOT, dtype=jnp.int32)
    allowed = (key_pos[None, :] <= block_pos[:, None]) & (key_pos[None, :] < length)
    scores = jnp.where(allowed, scores, NEG_LARGE)
    row_top = lax.optimization_barrier(jnp.max(scores, axis=1, keepdims=True))
    exp_terms = jnp.where(allowed, jnp.exp(scores - row_top), 0.0)
    attn_probs = exp_terms / lax.optimization_barrier(jnp.sum(exp_terms, axis=1, keepdims=True))
    return matmul(low(attn_probs), value_rows)

def slot_forward(params, slot_tokens, length):
    norm_gain, norm_shift, query_weight, query_bias, keyval_weight, value_bias, mixer_weight, mixer_bias, ffnorm_gain, ffnorm_shift, up_weight, up_bias, down_weight, down_bias = params
    first = low(normalize(slot_tokens, norm_gain, norm_shift))
    queries = low(low_back(matmul(first, query_weight) + query_bias))
    pair_bias = jnp.concatenate([jnp.zeros((HEAD_DIM,), jnp.float32), value_bias])
    keyvals = low(low_back(matmul(first, keyval_weight) + pair_bias))
    key_rows = keyvals[:, :HEAD_DIM]
    value_rows = keyvals[:, HEAD_DIM:]
    query_block = min(512, SLOT)
    block_count = SLOT // query_block
    query_blocks = queries.reshape(block_count, query_block * HEADS, HEAD_DIM)
    block_pos = jnp.repeat(jnp.arange(SLOT, dtype=jnp.int32), HEADS).reshape(block_count, query_block * HEADS)

    def one_block(block_args):
        return attend_block(block_args[0], block_args[1], key_rows, value_rows, length)
    mixed = lax.map(jax.checkpoint(one_block), (query_blocks, block_pos))
    mixed = low(low_back(mixed.reshape(SLOT, D)))
    residual = slot_tokens + low_back(matmul(mixed, mixer_weight) + mixer_bias)
    second = low(normalize(residual, ffnorm_gain, ffnorm_shift))
    upper = low_back(matmul(second, up_weight) + up_bias)
    active = low(jax.nn.gelu(upper, approximate=True))
    return residual + low_back(matmul(active, down_weight) + down_bias)

def reference(tokens, lengths, cotangent, norm_gain, norm_shift, query_weight, query_bias, keyval_weight, value_bias, mixer_weight, mixer_bias, ffnorm_gain, ffnorm_shift, up_weight, up_bias, down_weight, down_bias):
    params = tuple((param.astype(jnp.float32) for param in (norm_gain, norm_shift, query_weight, query_bias, keyval_weight, value_bias, mixer_weight, mixer_bias, ffnorm_gain, ffnorm_shift, up_weight, up_bias, down_weight, down_bias)))

    def one_slot(totals, scan_item):
        slot_tokens, slot_cot, length = scan_item
        layer_out, pull_back = jax.vjp(lambda param_set, values: slot_forward(param_set, values, length), params, slot_tokens.astype(jnp.float32))
        valid_rows = (jnp.arange(SLOT, dtype=jnp.int32) < length).astype(jnp.float32)[:, None]
        param_grads, input_grad = pull_back(slot_cot.astype(jnp.float32) * valid_rows)
        totals = jax.tree.map(lambda left_side, right_side: left_side + right_side, totals, param_grads)
        return (totals, (layer_out.astype(jnp.bfloat16), input_grad.astype(jnp.bfloat16)))
    zero_grads = jax.tree.map(jnp.zeros_like, params)
    totals, (layer_out, tokens_grad) = lax.scan(one_slot, zero_grads, (tokens, cotangent, lengths))
    return (layer_out, tokens_grad, totals[0], totals[1], totals[2], totals[3], totals[4], totals[5], totals[6], totals[7], totals[8], totals[9], totals[10], totals[11], totals[12], totals[13])
```

```python
import functools

import jax
import jax.numpy as jnp
from jax import lax
from jax.experimental import pallas as pl
from jax.experimental.pallas import tpu as pltpu
from jax.sharding import Mesh, PartitionSpec as P

EPSILON = 1e-05
NEG_LARGE = -1e30
MIN_LEN = 1024
BF = jnp.bfloat16
F32 = jnp.float32
GELU_K = 0.7978845608028654
GELU_C = 0.044715


def dot(left_side, right_side, dims=((1,), (0,))):
    return lax.dot_general(left_side, right_side, (dims, ((), ())), preferred_element_type=F32)


def swap(values, axis):
    return lax.ppermute(values, axis, [(0, 1), (1, 0)])


def pick(values, index, axis):
    return lax.dynamic_index_in_dim(values, index, axis, keepdims=False)


def stack_heads(block, head_dim):
    heads = block.shape[0] // head_dim
    return jnp.concatenate([block[h * head_dim : (h + 1) * head_dim] for h in range(heads)], axis=1)


def unstack_heads(stacked, seg):
    heads = stacked.shape[1] // seg
    return jnp.concatenate([stacked[:, h * seg : (h + 1) * seg] for h in range(heads)], axis=0)


def masked_scores(scal_ref, queries, keys, step, seg, heads, with_length, first_block):
    scores = dot(keys, queries) * (keys.shape[1] ** (-0.5))
    pair = keys.shape[0]
    if not (with_length or first_block):
        return scores
    key_pos = lax.broadcasted_iota(jnp.int32, (pair, seg), 0)
    allowed = None
    if first_block:
        query_pos = lax.broadcasted_iota(jnp.int32, (pair, seg), 1) + scal_ref[1] * seg
        allowed = key_pos <= query_pos
    if with_length:
        length = scal_ref[2 + pl.program_id(0)]
        inside = key_pos + (scal_ref[0] - step) * pair < length
        allowed = inside if allowed is None else allowed & inside
    bias = jnp.where(allowed, 0.0, NEG_LARGE).astype(F32)
    return scores + jnp.concatenate([bias] * heads, axis=1)


def attn_fwd_kernel(scal_ref, q_ref, kv_ref, out_ref, lse_ref, *, with_length):
    head_dim = kv_ref.shape[-1] // 2
    seg = q_ref.shape[1]
    heads = q_ref.shape[0] // head_dim
    queries = stack_heads(q_ref[...], head_dim)

    def block(step, state, first_block):
        top, total, accum = state
        keys = kv_ref[0, step, :, :head_dim]
        values = kv_ref[0, step, :, head_dim:]
        scores = masked_scores(scal_ref, queries, keys, step, seg, heads, with_length, first_block)
        new_top = jnp.maximum(top, jnp.max(scores, axis=0, keepdims=True))
        terms = jnp.exp(scores - new_top)
        fade = jnp.exp(top - new_top)
        total = total * fade + jnp.sum(terms, axis=0, keepdims=True)
        accum = accum * fade + dot(values, terms.astype(BF), ((0,), (0,)))
        return new_top, total, accum

    lanes = heads * seg
    state = (
        jnp.full((1, lanes), NEG_LARGE, F32),
        jnp.zeros((1, lanes), F32),
        jnp.zeros((head_dim, lanes), F32),
    )
    state = block(0, state, True)
    top, total, accum = lax.fori_loop(1, scal_ref[0] + 1, lambda t, s: block(t, s, False), state)
    out_ref[...] = unstack_heads(accum / total, seg).astype(BF)
    lse_ref[0, 0] = top + jnp.log(total)


def attn_bwd_kernel(scal_ref, q_ref, kv_ref, out_ref, dout_ref, lse_ref, dq_ref, dkv_ref, *, with_length):
    head_dim = kv_ref.shape[-1] // 2
    seg = q_ref.shape[1]
    heads = q_ref.shape[0] // head_dim
    scale = head_dim ** (-0.5)
    queries = stack_heads(q_ref[...], head_dim)
    d_mixed = stack_heads(dout_ref[...], head_dim)
    mixed = stack_heads(out_ref[...], head_dim)
    delta = jnp.sum(mixed.astype(F32) * d_mixed.astype(F32), axis=0, keepdims=True)
    lse = lse_ref[0, 0]

    @pl.when(pl.program_id(1) == 0)
    def clear():
        dkv_ref[...] = jnp.zeros_like(dkv_ref)

    def block(step, accum, first_block):
        keys = kv_ref[0, step, :, :head_dim]
        values = kv_ref[0, step, :, head_dim:]
        scores = masked_scores(scal_ref, queries, keys, step, seg, heads, with_length, first_block)
        probs = jnp.exp(scores - lse)
        d_probs = dot(values, d_mixed)
        d_scores = (probs * (d_probs - delta)).astype(BF)
        dkv_ref[0, step, :, :head_dim] += dot(d_scores, queries, ((1,), (1,))) * scale
        dkv_ref[0, step, :, head_dim:] += dot(probs.astype(BF), d_mixed, ((1,), (1,)))
        return accum + dot(keys, d_scores, ((0,), (0,)))

    accum = block(0, jnp.zeros((head_dim, heads * seg), F32), True)
    accum = lax.fori_loop(1, scal_ref[0] + 1, lambda t, s: block(t, s, False), accum)
    dq_ref[...] = (unstack_heads(accum, seg) * scale).astype(BF)


def attn_specs(slots, steps, pair, seg, rows, groups, head_dim):
    lanes = rows // groups // head_dim * seg
    scal = pl.BlockSpec(memory_space=pltpu.SMEM)
    feat = pl.BlockSpec((rows // groups, seg), lambda s, g: (g, s))
    kv = pl.BlockSpec((1, steps, pair, 2 * head_dim), lambda s, g: (s, 0, 0, 0))
    lse = pl.BlockSpec((1, 1, 1, lanes), lambda s, g: (s, g, 0, 0))
    return scal, feat, kv, lse, lanes


def attn_forward(scal, q_t, kv, groups, with_length):
    slots, steps, pair, width = kv.shape
    rows, cols = q_t.shape
    seg = cols // slots
    scal_s, feat, kv_s, lse_s, lanes = attn_specs(slots, steps, pair, seg, rows, groups, width // 2)
    return pl.pallas_call(
        functools.partial(attn_fwd_kernel, with_length=with_length),
        grid=(slots, groups),
        in_specs=[scal_s, feat, kv_s],
        out_specs=[feat, lse_s],
        out_shape=[
            jax.ShapeDtypeStruct((rows, cols), BF),
            jax.ShapeDtypeStruct((slots, groups, 1, lanes), F32),
        ],
        compiler_params=pltpu.CompilerParams(vmem_limit_bytes=40 << 20),
        cost_estimate=pl.CostEstimate(
            flops=4 * rows * cols * steps * pair, bytes_accessed=6 << 20, transcendentals=0
        ),
    )(scal, q_t, kv)


def attn_backward(scal, q_t, kv, out_t, dout_t, lse, groups, with_length):
    slots, steps, pair, width = kv.shape
    rows, cols = q_t.shape
    seg = cols // slots
    scal_s, feat, kv_s, lse_s, lanes = attn_specs(slots, steps, pair, seg, rows, groups, width // 2)
    return pl.pallas_call(
        functools.partial(attn_bwd_kernel, with_length=with_length),
        grid=(slots, groups),
        in_specs=[scal_s, feat, kv_s, feat, feat, lse_s],
        out_specs=[feat, kv_s],
        out_shape=[
            jax.ShapeDtypeStruct((rows, cols), BF),
            jax.ShapeDtypeStruct(kv.shape, F32),
        ],
        compiler_params=pltpu.CompilerParams(vmem_limit_bytes=48 << 20),
        cost_estimate=pl.CostEstimate(
            flops=10 * rows * cols * steps * pair, bytes_accessed=9 << 20, transcendentals=0
        ),
    )(scal, q_t, kv, out_t, dout_t, lse)


def norm_stats(values):
    center = values - jnp.mean(values, axis=-1, keepdims=True)
    spread = jnp.mean(center * center, axis=-1, keepdims=True)
    rstd = lax.rsqrt(spread + EPSILON)
    return center * rstd, rstd


def norm_backward(d_values, unit, rstd, gain):
    scaled = d_values * gain
    return rstd * (
        scaled
        - jnp.mean(scaled, axis=-1, keepdims=True)
        - unit * jnp.mean(scaled * unit, axis=-1, keepdims=True)
    )


def gather_rows(shard, x, place):
    rows = shard.shape[0]
    half = rows // 2
    mine = lax.dynamic_slice_in_dim(shard, x * half, half, 0)
    direct = swap(mine, "y")
    other = swap(direct, "x")
    sib = swap(shard, "c")
    sib_direct = swap(direct, "c")
    sib_other = swap(other, "c")
    full = jnp.zeros((4 * rows,) + shard.shape[1:], shard.dtype)
    far = place ^ 2
    pieces = (
        (shard, place * rows),
        (sib, (place ^ 1) * rows),
        (direct, far * rows + x * half),
        (other, far * rows + (1 - x) * half),
        (sib_direct, (far ^ 1) * rows + x * half),
        (sib_other, (far ^ 1) * rows + (1 - x) * half),
    )
    for piece, start in pieces:
        full = lax.dynamic_update_slice_in_dim(full, piece, start, 0)
    return full


def gather_plane(block):
    half = block.shape[0] // 2
    from_x = swap(block, "x")
    from_y = swap(block, "y")
    diag = jnp.concatenate([swap(from_y[:half], "x"), swap(from_x[half:], "y")], axis=0)
    return [
        jnp.concatenate([part, swap(part, "c")], axis=0) for part in (block, from_x, from_y, diag)
    ]


def scatter_plane(parts):
    rows = parts[0].shape[0] // 2
    half = rows // 2
    own, to_x, to_y, diag = [
        part[:rows].astype(F32) + swap(part[rows:].astype(BF), "c").astype(F32) for part in parts
    ]
    via_x = swap(diag[:half].astype(BF), "x").astype(F32)
    via_y = swap(diag[half:].astype(BF), "y").astype(F32)
    to_y = jnp.concatenate([to_y[:half] + via_x, to_y[half:]], axis=0)
    to_x = jnp.concatenate([to_x[:half], to_x[half:] + via_y], axis=0)
    return own + swap(to_x.astype(BF), "x").astype(F32) + swap(to_y.astype(BF), "y").astype(F32)


def scatter_line(parts, z, length):
    def block(index):
        return pick(parts, jnp.clip(index, 0, length - 1), 0).astype(F32)

    from_left = from_right = None
    for step in range(1, length):
        up = block(length - step + z)
        down = block(z - length + step)
        if from_left is not None:
            up, down = up + from_left, down + from_right
        from_left = lax.ppermute(up.astype(BF), "z", [(i, i + 1) for i in range(step)]).astype(F32)
        from_right = lax.ppermute(
            down.astype(BF), "z", [(i, i - 1) for i in range(length - step, length)]
        ).astype(F32)
    return block(z) + from_left + from_right


def scatter_all(left_side, right_side, vectors, place_yczx, sizes):
    y, c, z, x = place_yczx
    length, width = sizes
    tokens = left_side.shape[0]
    block = width // (8 * length)
    left_parts = left_side.reshape(tokens, 2, 2, width // 4)
    left_mine = pick(left_parts, c, 2).reshape(tokens, width // 2)
    left_sib = swap(pick(left_parts, 1 - c, 2), "c").reshape(tokens, width // 2)
    right_sib = swap(right_side, "c")
    partial = dot(
        jnp.concatenate([left_mine, left_sib], axis=0),
        jnp.concatenate([right_side, right_sib], axis=0),
        ((0,), (0,)),
    )
    extra = jnp.pad(jnp.stack(vectors, axis=1), ((0, 0), (0, 128 - len(vectors))))
    extra = extra.reshape(2, 2, width // 4, 128)
    extra = pick(extra, c, 1) + swap(pick(extra, 1 - c, 1).astype(BF), "c").astype(F32)
    partial = jnp.concatenate([partial, extra.reshape(width // 2, 128)], axis=1)
    cols = partial.shape[1]
    partial = partial.reshape(2, length, 2, block, cols)
    cut = (cols // 256) * 128
    side_a, side_b = partial[..., :cut], partial[..., cut:]
    side_a = pick(side_a, y, 0) + swap(pick(side_a, 1 - y, 0).astype(BF), "y").astype(F32)
    side_b = pick(side_b, x, 2) + swap(pick(side_b, 1 - x, 2).astype(BF), "x").astype(F32)
    side_a = pick(side_a, x, 1) + swap(pick(side_a, 1 - x, 1).astype(BF), "x").astype(F32)
    side_b = pick(side_b, y, 0) + swap(pick(side_b, 1 - y, 0).astype(BF), "y").astype(F32)
    return scatter_line(jnp.concatenate([side_a, side_b], axis=-1), z, length)


def body(
    tokens,
    lengths,
    cotangent,
    norm_gain,
    norm_shift,
    query_weight,
    query_bias,
    keyval_weight,
    value_bias,
    mixer_weight,
    mixer_bias,
    ffnorm_gain,
    ffnorm_shift,
    up_weight,
    up_bias,
    down_weight,
    down_bias,
):
    y, c, z, x = [lax.axis_index(name) for name in ("y", "c", "z", "x")]
    length = lax.axis_size("z")
    place = y * 2 + c
    slots, seg, width = tokens.shape
    rows = slots * seg
    head_dim = value_bias.shape[0] * 4
    hidden = up_weight.shape[1]
    hidden_block = hidden // (8 * length)
    hidden_mine = hidden // 8
    with_length = 2 * length * seg > MIN_LEN
    scal = jnp.concatenate([jnp.stack([z, x]).astype(jnp.int32), lengths])

    quarter = width // 4
    small = jnp.stack(
        [
            norm_gain,
            norm_shift,
            query_bias,
            mixer_bias,
            ffnorm_gain,
            ffnorm_shift,
            down_bias,
            jnp.pad(value_bias, (0, quarter - value_bias.shape[0])),
        ]
    )
    pair = jnp.stack([small, swap(small, "c")])
    pair = jnp.where(c == 0, pair, pair[::-1])
    quad = jnp.stack([pair, swap(pair, "y")])
    quad = jnp.where(y == 0, quad, quad[::-1]).reshape(4, 8, quarter)
    smalls = quad.transpose(1, 0, 2).reshape(8, width).astype(F32)
    gain, shift, q_bias, m_bias, ffgain, ffshift, d_bias = [smalls[i][None, :] for i in range(7)]
    v_bias = quad[:, 7, : value_bias.shape[0]].reshape(1, head_dim).astype(F32)

    full_keyval = gather_rows(keyval_weight, x, place)
    full_query = gather_rows(query_weight, x, place)
    full_mixer = gather_rows(mixer_weight, x, place)

    down_mine = pick(down_weight.reshape(length, 2, hidden_block, width), x, 1).reshape(
        hidden_mine, width
    )
    up_bias_mine = pick(up_bias.reshape(length, 2, hidden_block), x, 1).reshape(1, hidden_mine)
    up_parts = pick(up_weight.reshape(quarter, 4, length, 2, hidden_block), x, 3).reshape(
        quarter, 4, hidden_mine
    )
    up_mine = jnp.zeros((width, hidden_mine), BF)
    for flip in range(4):
        piece = pick(up_parts, place ^ flip, 1)
        if flip:
            piece = lax.ppermute(piece, ("y", "c"), [(i, i ^ flip) for i in range(4)])
        up_mine = lax.dynamic_update_slice_in_dim(up_mine, piece, (place ^ flip) * quarter, 0)

    inputs = tokens.reshape(rows, width).astype(F32)
    unit1, rstd1 = norm_stats(inputs)
    first = (unit1 * gain + shift).astype(BF)
    kv_bias = jnp.concatenate([jnp.zeros_like(v_bias), v_bias], axis=1)
    keyvals = (dot(first, full_keyval) + kv_bias).astype(BF).reshape(slots, seg, 2 * head_dim)
    blocks = []
    current = keyvals
    for step in range(length):
        if step:
            current = lax.ppermute(current, "z", [(i, i + 1) for i in range(length - 1)])
        both = jnp.stack([current, swap(current, "x")], axis=1)
        both = jnp.where(x == 0, both, both[:, ::-1])
        blocks.append(both.reshape(slots, 2 * seg, 2 * head_dim))
    kv_all = jnp.stack(blocks, axis=1)
    q_t = (dot(full_query, first, ((0,), (1,))) + q_bias.reshape(width, 1)).astype(BF)
    mixed_t, lse = attn_forward(scal, q_t, kv_all, 4, with_length)
    residual = inputs + dot(mixed_t, full_mixer, ((0,), (0,))) + m_bias
    unit2, rstd2 = norm_stats(residual)
    second = (unit2 * ffgain + ffshift).astype(BF)

    token_pos = (z * 2 + x) * seg + jnp.arange(seg, dtype=jnp.int32)
    valid = (token_pos[None, :] < lengths[:, None]).astype(F32).reshape(rows, 1)
    d_out = cotangent.reshape(rows, width).astype(F32) * valid
    d_down = d_out.astype(BF)

    down_all = gather_plane(d_down)
    second_all = gather_plane(second)
    out_parts, dsecond_parts, actives, d_uppers = [], [], [], []
    for chip in range(4):
        d_active = dot(down_all[chip], down_mine, ((1,), (1,)))
        upper = dot(second_all[chip], up_mine) + up_bias_mine.astype(F32)
        inner = jnp.tanh(GELU_K * (upper + GELU_C * upper * upper * upper))
        active = (0.5 * upper * (1.0 + inner)).astype(BF)
        slope = 0.5 * (1.0 + inner) + 0.5 * upper * (1.0 - inner * inner) * GELU_K * (
            1.0 + 3.0 * GELU_C * upper * upper
        )
        d_upper = (d_active * slope).astype(BF)
        actives.append(active)
        d_uppers.append(d_upper)
        dsecond_parts.append(dot(d_upper, up_mine, ((1,), (1,))))
        out_parts.append(dot(active, down_mine))
    d_second = scatter_plane(dsecond_parts)
    output = residual + scatter_plane(out_parts) + d_bias
    layer_out = output.astype(BF).reshape(tokens.shape)
    active_cat = jnp.concatenate(actives, axis=0)
    d_upper_cat = jnp.concatenate(d_uppers, axis=0)
    down_cat = jnp.concatenate(down_all, axis=0)
    second_cat = jnp.concatenate(second_all, axis=0)
    down_part = dot(active_cat, down_cat, ((0,), (0,)))
    down_grad = scatter_line(down_part.reshape(length, hidden_block, width), z, length)
    ubias_part = jnp.sum(d_upper_cat.astype(F32), axis=0).reshape(length, hidden_block)
    ubias_grad = scatter_line(ubias_part, z, length)
    up_part = dot(second_cat, d_upper_cat, ((0,), (0,)))
    out_rows = width // (8 * length)
    up_part = up_part.reshape(4, length, 2, out_rows, hidden_mine).transpose(1, 0, 2, 3, 4)
    up_sum = scatter_line(up_part, z, length).astype(BF)
    up_sum = up_sum.reshape(2, 2, 2, out_rows, hidden_mine)
    up_rows = lax.all_to_all(
        up_sum.reshape(8, out_rows, hidden_mine), ("y", "c", "x"), 0, 0, tiled=True
    )
    up_grad = (
        up_rows.reshape(4, 2, out_rows, length, hidden_block)
        .transpose(2, 0, 3, 1, 4)
        .reshape(out_rows, hidden)
        .astype(F32)
    )

    d_residual = d_out + norm_backward(d_second, unit2, rstd2, ffgain)
    d_mix = d_residual.astype(BF)
    d_mixed_t = dot(full_mixer, d_mix, ((1,), (1,))).astype(BF)
    where = (y, c, z, x)
    sizes = (length, width)
    mixer_all = scatter_all(
        mixed_t.T,
        d_mix,
        (
            jnp.sum(d_mix.astype(F32), axis=0),
            jnp.sum(d_second * unit2, axis=0),
            jnp.sum(d_second, axis=0),
            jnp.sum(d_out, axis=0),
        ),
        where,
        sizes,
    )

    dq_t, dkv = attn_backward(scal, q_t, kv_all, mixed_t, d_mixed_t, lse, 4, with_length)
    dkv = dkv.reshape(slots, length, 2, seg, 2 * head_dim)
    running = None
    for step in range(length - 1, -1, -1):
        term = dkv[:, step]
        term = pick(term, x, 1) + swap(pick(term, 1 - x, 1).astype(BF), "x").astype(F32)
        if running is not None:
            term = term + lax.ppermute(
                running.astype(BF), "z", [(i, i - 1) for i in range(1, length)]
            ).astype(F32)
        running = term
    d_keyvals = running.reshape(rows, 2 * head_dim).astype(BF)
    d_first = dot(dq_t, full_query, ((0,), (1,))) + dot(d_keyvals, full_keyval, ((1,), (1,)))
    tokens_grad = (d_residual + norm_backward(d_first, unit1, rstd1, gain)).astype(BF)
    d_queries = dq_t.T
    devices = 8 * length
    vbias = jnp.sum(d_keyvals[:, head_dim:].astype(F32), axis=0)
    vbias = jnp.pad(
        vbias.reshape(devices, head_dim // devices),
        ((0, 0), (0, out_rows - head_dim // devices)),
    ).reshape(width)
    query_all = scatter_all(
        first,
        jnp.concatenate([d_queries, d_keyvals], axis=1),
        (
            jnp.sum(d_first * unit1, axis=0),
            jnp.sum(d_first, axis=0),
            jnp.sum(d_queries.astype(F32), axis=0),
            vbias,
        ),
        where,
        sizes,
    )
    kv_end = width + 2 * head_dim
    return (
        layer_out,
        tokens_grad.reshape(tokens.shape),
        query_all[:, kv_end],
        query_all[:, kv_end + 1],
        query_all[:, :width],
        query_all[:, kv_end + 2],
        query_all[:, width:kv_end],
        query_all[: head_dim // devices, kv_end + 3],
        mixer_all[:, :width],
        mixer_all[:, width],
        mixer_all[:, width + 1],
        mixer_all[:, width + 2],
        up_grad,
        ubias_grad,
        down_grad,
        mixer_all[:, width + 3],
    )


def solution(mesh):
    ctx = mesh.shape["ctx"]
    fine = Mesh(mesh.devices.reshape(2, 2, ctx // 2, 2), ("y", "c", "z", "x"))
    fsdp, both, every = ("y", "c"), ("z", "x"), ("y", "c", "z", "x")
    return jax.shard_map(
        body,
        mesh=fine,
        in_specs=(
            P(fsdp, both, None),
            P(fsdp),
            P(fsdp, both, None),
            P(fsdp),
            P(fsdp),
            P(fsdp, None),
            P(fsdp),
            P(fsdp, None),
            P(fsdp),
            P(fsdp, None),
            P(fsdp),
            P(fsdp),
            P(fsdp),
            P(fsdp, None),
            P(fsdp),
            P(fsdp, None),
            P(fsdp),
        ),
        out_specs=(
            P(fsdp, both, None),
            P(fsdp, both, None),
            P(every),
            P(every),
            P(every, None),
            P(every),
            P(every, None),
            P(every),
            P(every, None),
            P(every),
            P(every),
            P(every),
            P(every, None),
            P(every),
            P(every, None),
            P(every),
        ),
        check_vma=False,
    )
```

```python
import functools

import jax
import jax.numpy as jnp
from jax import lax
from jax.experimental import pallas as pl
from jax.experimental.pallas import tpu as pltpu
from jax.sharding import Mesh, PartitionSpec as P

EPSILON = 1e-05
NEG_LARGE = -1e30
MIN_LEN = 1024
BF = jnp.bfloat16
F32 = jnp.float32
GELU_K = 0.7978845608028654
GELU_C = 0.044715


def dot(left_side, right_side, dims=((1,), (0,))):
    return lax.dot_general(left_side, right_side, (dims, ((), ())), preferred_element_type=F32)


def swap(values, axis):
    return lax.ppermute(values, axis, [(0, 1), (1, 0)])


def pick(values, index, axis):
    return lax.dynamic_index_in_dim(values, index, axis, keepdims=False)


def stack_heads(block, head_dim):
    heads = block.shape[0] // head_dim
    return jnp.concatenate([block[h * head_dim : (h + 1) * head_dim] for h in range(heads)], axis=1)


def unstack_heads(stacked, seg):
    heads = stacked.shape[1] // seg
    return jnp.concatenate([stacked[:, h * seg : (h + 1) * seg] for h in range(heads)], axis=0)


def masked_scores(scal_ref, queries, keys, step, seg, heads, with_length, first_block):
    scores = dot(keys, queries) * (keys.shape[1] ** (-0.5))
    pair = keys.shape[0]
    if not (with_length or first_block):
        return scores
    key_pos = lax.broadcasted_iota(jnp.int32, (pair, seg), 0)
    allowed = None
    if first_block:
        query_pos = lax.broadcasted_iota(jnp.int32, (pair, seg), 1) + scal_ref[1] * seg
        allowed = key_pos <= query_pos
    if with_length:
        length = scal_ref[2 + pl.program_id(0)]
        inside = key_pos + (scal_ref[0] - step) * pair < length
        allowed = inside if allowed is None else allowed & inside
    bias = jnp.where(allowed, 0.0, NEG_LARGE).astype(F32)
    return scores + jnp.concatenate([bias] * heads, axis=1)


def attn_fwd_kernel(scal_ref, q_ref, kv_ref, out_ref, lse_ref, *, with_length):
    head_dim = kv_ref.shape[-1] // 2
    seg = q_ref.shape[1]
    heads = q_ref.shape[0] // head_dim
    queries = stack_heads(q_ref[...], head_dim)

    def block(step, state, first_block):
        top, total, accum = state
        keys = kv_ref[0, step, :, :head_dim]
        values = kv_ref[0, step, :, head_dim:]
        scores = masked_scores(scal_ref, queries, keys, step, seg, heads, with_length, first_block)
        new_top = jnp.maximum(top, jnp.max(scores, axis=0, keepdims=True))
        terms = jnp.exp(scores - new_top)
        fade = jnp.exp(top - new_top)
        total = total * fade + jnp.sum(terms, axis=0, keepdims=True)
        accum = accum * fade + dot(values, terms.astype(BF), ((0,), (0,)))
        return new_top, total, accum

    lanes = heads * seg
    state = (
        jnp.full((1, lanes), NEG_LARGE, F32),
        jnp.zeros((1, lanes), F32),
        jnp.zeros((head_dim, lanes), F32),
    )
    state = block(0, state, True)
    top, total, accum = lax.fori_loop(1, scal_ref[0] + 1, lambda t, s: block(t, s, False), state)
    out_ref[...] = unstack_heads(accum / total, seg).astype(BF)
    lse_ref[0, 0] = top + jnp.log(total)


def attn_bwd_kernel(scal_ref, q_ref, kv_ref, out_ref, dout_ref, lse_ref, dq_ref, dkv_ref, *, with_length):
    head_dim = kv_ref.shape[-1] // 2
    seg = q_ref.shape[1]
    heads = q_ref.shape[0] // head_dim
    scale = head_dim ** (-0.5)
    queries = stack_heads(q_ref[...], head_dim)
    d_mixed = stack_heads(dout_ref[...], head_dim)
    mixed = stack_heads(out_ref[...], head_dim)
    delta = jnp.sum(mixed.astype(F32) * d_mixed.astype(F32), axis=0, keepdims=True)
    lse = lse_ref[0, 0]

    @pl.when(pl.program_id(1) == 0)
    def clear():
        dkv_ref[...] = jnp.zeros_like(dkv_ref)

    def block(step, accum, first_block):
        keys = kv_ref[0, step, :, :head_dim]
        values = kv_ref[0, step, :, head_dim:]
        scores = masked_scores(scal_ref, queries, keys, step, seg, heads, with_length, first_block)
        probs = jnp.exp(scores - lse)
        d_probs = dot(values, d_mixed)
        d_scores = (probs * (d_probs - delta)).astype(BF)
        dkv_ref[0, step, :, :head_dim] += dot(d_scores, queries, ((1,), (1,))) * scale
        dkv_ref[0, step, :, head_dim:] += dot(probs.astype(BF), d_mixed, ((1,), (1,)))
        return accum + dot(keys, d_scores, ((0,), (0,)))

    accum = block(0, jnp.zeros((head_dim, heads * seg), F32), True)
    accum = lax.fori_loop(1, scal_ref[0] + 1, lambda t, s: block(t, s, False), accum)
    dq_ref[...] = (unstack_heads(accum, seg) * scale).astype(BF)


def attn_specs(slots, steps, pair, seg, rows, groups, head_dim):
    lanes = rows // groups // head_dim * seg
    scal = pl.BlockSpec(memory_space=pltpu.SMEM)
    feat = pl.BlockSpec((rows // groups, seg), lambda s, g: (g, s))
    kv = pl.BlockSpec((1, steps, pair, 2 * head_dim), lambda s, g: (s, 0, 0, 0))
    lse = pl.BlockSpec((1, 1, 1, lanes), lambda s, g: (s, g, 0, 0))
    return scal, feat, kv, lse, lanes


def attn_forward(scal, q_t, kv, groups, with_length):
    slots, steps, pair, width = kv.shape
    rows, cols = q_t.shape
    seg = cols // slots
    scal_s, feat, kv_s, lse_s, lanes = attn_specs(slots, steps, pair, seg, rows, groups, width // 2)
    return pl.pallas_call(
        functools.partial(attn_fwd_kernel, with_length=with_length),
        grid=(slots, groups),
        in_specs=[scal_s, feat, kv_s],
        out_specs=[feat, lse_s],
        out_shape=[
            jax.ShapeDtypeStruct((rows, cols), BF),
            jax.ShapeDtypeStruct((slots, groups, 1, lanes), F32),
        ],
        compiler_params=pltpu.CompilerParams(vmem_limit_bytes=40 << 20),
        cost_estimate=pl.CostEstimate(
            flops=4 * rows * cols * steps * pair, bytes_accessed=6 << 20, transcendentals=0
        ),
    )(scal, q_t, kv)


def attn_backward(scal, q_t, kv, out_t, dout_t, lse, groups, with_length):
    slots, steps, pair, width = kv.shape
    rows, cols = q_t.shape
    seg = cols // slots
    scal_s, feat, kv_s, lse_s, lanes = attn_specs(slots, steps, pair, seg, rows, groups, width // 2)
    return pl.pallas_call(
        functools.partial(attn_bwd_kernel, with_length=with_length),
        grid=(slots, groups),
        in_specs=[scal_s, feat, kv_s, feat, feat, lse_s],
        out_specs=[feat, kv_s],
        out_shape=[
            jax.ShapeDtypeStruct((rows, cols), BF),
            jax.ShapeDtypeStruct(kv.shape, F32),
        ],
        compiler_params=pltpu.CompilerParams(vmem_limit_bytes=48 << 20),
        cost_estimate=pl.CostEstimate(
            flops=10 * rows * cols * steps * pair, bytes_accessed=9 << 20, transcendentals=0
        ),
    )(scal, q_t, kv, out_t, dout_t, lse)


def norm_stats(values):
    center = values - jnp.mean(values, axis=-1, keepdims=True)
    spread = jnp.mean(center * center, axis=-1, keepdims=True)
    rstd = lax.rsqrt(spread + EPSILON)
    return center * rstd, rstd


def norm_backward(d_values, unit, rstd, gain):
    scaled = d_values * gain
    return rstd * (
        scaled
        - jnp.mean(scaled, axis=-1, keepdims=True)
        - unit * jnp.mean(scaled * unit, axis=-1, keepdims=True)
    )


def gather_rows(shard, x, place):
    rows = shard.shape[0]
    half = rows // 2
    mine = lax.dynamic_slice_in_dim(shard, x * half, half, 0)
    direct = swap(mine, "y")
    other = swap(direct, "x")
    sib = swap(shard, "c")
    sib_direct = swap(direct, "c")
    sib_other = swap(other, "c")
    full = jnp.zeros((4 * rows,) + shard.shape[1:], shard.dtype)
    far = place ^ 2
    pieces = (
        (shard, place * rows),
        (sib, (place ^ 1) * rows),
        (direct, far * rows + x * half),
        (other, far * rows + (1 - x) * half),
        (sib_direct, (far ^ 1) * rows + x * half),
        (sib_other, (far ^ 1) * rows + (1 - x) * half),
    )
    for piece, start in pieces:
        full = lax.dynamic_update_slice_in_dim(full, piece, start, 0)
    return full


def gather_plane(block):
    half = block.shape[0] // 2
    from_x = swap(block, "x")
    from_y = swap(block, "y")
    diag = jnp.concatenate([swap(from_y[:half], "x"), swap(from_x[half:], "y")], axis=0)
    return [
        jnp.concatenate([part, swap(part, "c")], axis=0) for part in (block, from_x, from_y, diag)
    ]


def scatter_plane(parts):
    rows = parts[0].shape[0] // 2
    half = rows // 2
    own, to_x, to_y, diag = [
        part[:rows].astype(F32) + swap(part[rows:].astype(BF), "c").astype(F32) for part in parts
    ]
    via_x = swap(diag[:half].astype(BF), "x").astype(F32)
    via_y = swap(diag[half:].astype(BF), "y").astype(F32)
    to_y = jnp.concatenate([to_y[:half] + via_x, to_y[half:]], axis=0)
    to_x = jnp.concatenate([to_x[:half], to_x[half:] + via_y], axis=0)
    return own + swap(to_x.astype(BF), "x").astype(F32) + swap(to_y.astype(BF), "y").astype(F32)


def scatter_line(parts, z, length):
    def block(index):
        return pick(parts, jnp.clip(index, 0, length - 1), 0).astype(F32)

    from_left = from_right = None
    for step in range(1, length):
        up = block(length - step + z)
        down = block(z - length + step)
        if from_left is not None:
            up, down = up + from_left, down + from_right
        from_left = lax.ppermute(up.astype(BF), "z", [(i, i + 1) for i in range(step)]).astype(F32)
        from_right = lax.ppermute(
            down.astype(BF), "z", [(i, i - 1) for i in range(length - step, length)]
        ).astype(F32)
    return block(z) + from_left + from_right


def scatter_all(left_side, right_side, vectors, place_yczx, sizes):
    y, c, z, x = place_yczx
    length, width = sizes
    tokens = left_side.shape[0]
    block = width // (8 * length)
    left_parts = left_side.reshape(tokens, 2, 2, width // 4)
    left_mine = pick(left_parts, c, 2).reshape(tokens, width // 2)
    left_sib = swap(pick(left_parts, 1 - c, 2), "c").reshape(tokens, width // 2)
    right_sib = swap(right_side, "c")
    partial = dot(
        jnp.concatenate([left_mine, left_sib], axis=0),
        jnp.concatenate([right_side, right_sib], axis=0),
        ((0,), (0,)),
    )
    extra = jnp.pad(jnp.stack(vectors, axis=1), ((0, 0), (0, 128 - len(vectors))))
    extra = extra.reshape(2, 2, width // 4, 128)
    extra = pick(extra, c, 1) + swap(pick(extra, 1 - c, 1).astype(BF), "c").astype(F32)
    partial = jnp.concatenate([partial, extra.reshape(width // 2, 128)], axis=1)
    cols = partial.shape[1]
    partial = partial.reshape(2, length, 2, block, cols)
    cut = (cols // 256) * 128
    side_a, side_b = partial[..., :cut], partial[..., cut:]
    side_a = pick(side_a, y, 0) + swap(pick(side_a, 1 - y, 0).astype(BF), "y").astype(F32)
    side_b = pick(side_b, x, 2) + swap(pick(side_b, 1 - x, 2).astype(BF), "x").astype(F32)
    side_a = pick(side_a, x, 1) + swap(pick(side_a, 1 - x, 1).astype(BF), "x").astype(F32)
    side_b = pick(side_b, y, 0) + swap(pick(side_b, 1 - y, 0).astype(BF), "y").astype(F32)
    return scatter_line(jnp.concatenate([side_a, side_b], axis=-1), z, length)


MESH = pl.DeviceIdType.MESH


def remote(src, dst, send_sems, recv_sems, index, device):
    return pltpu.make_async_remote_copy(
        src_ref=src,
        dst_ref=dst,
        send_sem=send_sems.at[index],
        recv_sem=recv_sems.at[index],
        device_id=device,
        device_id_type=MESH,
    )


def greet(devices):
    barrier = pltpu.get_barrier_semaphore()
    for device in devices:
        pl.semaphore_signal(barrier, inc=1, device_id=device, device_id_type=MESH)
    pl.semaphore_wait(barrier, len(devices))


def tiles(count, size):
    def over(fn):
        @pl.loop(0, count)
        def step(index):
            fn(pl.ds(pl.multiple_of(index * size, size), size), index)

    return over


def gelu_pair(upper):
    inner = jnp.tanh(upper * (GELU_K + (GELU_K * GELU_C) * (upper * upper)))
    half = 0.5 + 0.5 * inner
    slope = half + (0.5 * upper) * (1.0 - inner * inner) * (
        GELU_K + (3.0 * GELU_K * GELU_C) * (upper * upper)
    )
    return upper * half, slope


def ffn_kernel(
    second_ref,
    down_all_ref,
    up_ref,
    ubias_ref,
    down_ref,
    dsecond_ref,
    out_parts_ref,
    down_part_ref,
    up_part_ref,
    ubias_part_ref,
    tokens_v,
    cots_v,
    up_v,
    down_v,
    active_v,
    dupper_v,
    sib_out,
    sib_in,
    chip_out,
    chip_in,
    acc_v,
    stage_v,
    load_sem,
    stage_sem,
    gs_send,
    gs_recv,
    rs_send,
    rs_recv,
    *,
    length,
):
    rows, width = second_ref.shape
    hidden = up_ref.shape[1]
    half = rows // 2
    chunk = 2 * rows
    y, c, x = [lax.axis_index(name) for name in ("y", "c", "x")]
    sib, to_x, to_y = {"c": 1 - c}, {"x": 1 - x}, {"y": 1 - y}
    diag = {"x": 1 - x, "y": 1 - y}
    chips = (None, to_x, to_y, diag)

    loads = [
        pltpu.make_async_copy(second_ref, tokens_v.at[0, pl.ds(0, rows)], load_sem.at[0]),
        pltpu.make_async_copy(down_ref, down_v, load_sem.at[1]),
        pltpu.make_async_copy(down_all_ref, cots_v, load_sem.at[2]),
        pltpu.make_async_copy(up_ref, up_v, load_sem.at[3]),
    ]
    for load in loads:
        load.start()
    greet((sib, to_x, to_y, diag))
    loads[0].wait()

    same, other = pl.ds(0, rows), pl.ds(rows, rows)
    top, bottom = pl.ds(0, half), pl.ds(half, half)

    def gather(index, chip, span_src, chip_dst, span_dst, device):
        return remote(
            tokens_v.at[chip, span_src], tokens_v.at[chip_dst, span_dst], gs_send, gs_recv, index, device
        )

    send_x = gather(0, 0, same, 1, same, to_x)
    send_y = gather(1, 0, same, 2, same, to_y)
    share = [gather(2 + k, k, same, k, other, sib) for k in range(4)]
    diag_x = gather(6, 2, top, 3, top, to_x)
    diag_y = gather(7, 1, bottom, 3, bottom, to_y)
    send_x.start()
    send_y.start()
    share[0].start()

    loads[1].wait()
    loads[2].wait()

    @tiles(4 * chunk // 512, 512)
    def grad_active(span, index):
        @tiles(hidden // 512, 512)
        def columns(cols, _):
            dupper_v[span, cols] = dot(cots_v[span, :], down_v[cols, :], ((1,), (1,))).astype(BF)

    loads[3].wait()

    def chip_work(k):
        @tiles(hidden // 256, 256)
        def columns(cols, _):
            block = pl.ds(k * chunk, chunk)
            upper = dot(tokens_v[k], up_v[:, cols]) + ubias_ref[:, cols]
            active, slope = gelu_pair(upper)
            active_v[block, cols] = active.astype(BF)
            d_upper = (dupper_v[block, cols].astype(F32) * slope).astype(BF)
            dupper_v[block, cols] = d_upper
            part = jnp.sum(d_upper.astype(F32), axis=0, keepdims=True)
            if k == 0:
                ubias_part_ref[:, cols] = part
            else:
                ubias_part_ref[:, cols] += part

        @tiles(width // 512, 512)
        def to_sibling(cols, _):
            sib_out[k, :, cols] = dot(
                dupper_v[pl.ds(k * chunk + rows, rows), :], up_v[cols, :], ((1,), (1,))
            ).astype(BF)

        pair = remote(sib_out.at[k], sib_in.at[k], rs_send, rs_recv, k, sib)
        pair.start()

        @tiles(width // 512, 512)
        def keep(cols, _):
            acc_v[:, cols] = dot(dupper_v[pl.ds(k * chunk, rows), :], up_v[cols, :], ((1,), (1,)))

        pair.wait_recv()
        if k == 0:
            dsecond_ref[...] = acc_v[...] + sib_in[0].astype(F32)
            return [pair]
        chip_out[k - 1] = (acc_v[...] + sib_in[k].astype(F32)).astype(BF)
        far = remote(chip_out.at[k - 1], chip_in.at[k - 1], rs_send, rs_recv, 3 + k, chips[k])
        far.start()
        return [pair, far]

    share[0].wait_recv()
    sent = chip_work(0)
    send_x.wait_recv()
    share[1].start()
    diag_y.start()
    send_y.wait_recv()
    share[2].start()
    diag_x.start()
    share[1].wait_recv()
    sent += chip_work(1)
    share[2].wait_recv()
    sent += chip_work(2)
    diag_x.wait_recv()
    diag_y.wait_recv()
    share[3].start()
    share[3].wait_recv()
    sent += chip_work(3)

    def staged(slot, value, target):
        stage_v[slot] = value.astype(BF)
        copy = pltpu.make_async_copy(stage_v.at[slot], target, stage_sem.at[slot])
        copy.start()
        return copy

    @pl.loop(0, 4)
    def outputs(k):
        block = pl.ds(pl.multiple_of(k * chunk, chunk), chunk)
        copies = []
        for j in range(width // 512):
            cols = pl.ds(j * 512, 512)
            copies.append(
                staged(j, dot(active_v[block, :], down_v[:, cols]), out_parts_ref.at[k, :, cols])
            )
        for copy in copies:
            copy.wait()

    @pl.loop(0, hidden // 512)
    def downs(r):
        block = pl.ds(pl.multiple_of(r * 512, 512), 512)
        copies = []
        for j in range(width // 512):
            cols = pl.ds(j * 512, 512)
            copies.append(
                staged(
                    j,
                    dot(active_v[:, block], cots_v[:, cols], ((0,), (0,))),
                    down_part_ref.at[block, cols],
                )
            )
        for copy in copies:
            copy.wait()

    quarter = width // 4
    piece = quarter // length

    @pl.loop(0, hidden // 512)
    def ups(r):
        cols = pl.ds(pl.multiple_of(r * 512, 512), 512)
        copies = []
        for f in range(4):
            value = None
            for k in range(4):
                term = dot(
                    tokens_v[k, :, f * quarter : (f + 1) * quarter],
                    dupper_v[k * chunk : (k + 1) * chunk, cols],
                    ((0,), (0,)),
                )
                value = term if value is None else value + term
            stage_v[f] = value.astype(BF)
            for level in range(length):
                copy = pltpu.make_async_copy(
                    stage_v.at[f, pl.ds(level * piece, piece)],
                    up_part_ref.at[level, f, :, cols],
                    stage_sem.at[4 + f * length + level],
                )
                copy.start()
                copies.append(copy)
        for copy in copies:
            copy.wait()

    for k in range(3):
        remote(chip_out.at[k], chip_in.at[k], rs_send, rs_recv, 4 + k, chips[k + 1]).wait_recv()
    dsecond_ref[...] += (
        chip_in[0].astype(F32) + chip_in[1].astype(F32) + chip_in[2].astype(F32)
    )
    for copy in [send_x, send_y, diag_x, diag_y] + share + sent:
        copy.wait_send()


def ffn(second, down_all, up_mine, ubias, down_mine, length):
    rows, width = second.shape
    hidden = up_mine.shape[1]
    hbm = pl.BlockSpec(memory_space=pltpu.HBM)
    vmem = pl.BlockSpec(memory_space=pltpu.VMEM)
    sems = pltpu.SemaphoreType.DMA
    return pl.pallas_call(
        functools.partial(ffn_kernel, length=length),
        in_specs=[hbm, hbm, hbm, vmem, hbm],
        out_specs=[vmem, hbm, hbm, hbm, vmem],
        out_shape=[
            jax.ShapeDtypeStruct((rows, width), F32),
            jax.ShapeDtypeStruct((4, 2 * rows, width), BF),
            jax.ShapeDtypeStruct((hidden, width), BF),
            jax.ShapeDtypeStruct((length, 4, width // 4 // length, hidden), BF),
            jax.ShapeDtypeStruct((1, hidden), F32),
        ],
        scratch_shapes=[
            pltpu.VMEM((4, 2 * rows, width), BF),
            pltpu.VMEM((8 * rows, width), BF),
            pltpu.VMEM((width, hidden), BF),
            pltpu.VMEM((hidden, width), BF),
            pltpu.VMEM((8 * rows, hidden), BF),
            pltpu.VMEM((8 * rows, hidden), BF),
            pltpu.VMEM((4, rows, width), BF),
            pltpu.VMEM((4, rows, width), BF),
            pltpu.VMEM((3, rows, width), BF),
            pltpu.VMEM((3, rows, width), BF),
            pltpu.VMEM((rows, width), F32),
            pltpu.VMEM((4, 512, 512), BF),
            sems((4,)),
            sems((4 + 4 * length,)),
            sems((8,)),
            sems((8,)),
            sems((7,)),
            sems((7,)),
        ],
        compiler_params=pltpu.CompilerParams(
            collective_id=1, has_side_effects=True, vmem_limit_bytes=60 << 20
        ),
        cost_estimate=pl.CostEstimate(
            flops=12 * 8 * rows * width * hidden, bytes_accessed=40 << 20, transcendentals=0
        ),
    )(second, down_all, up_mine, ubias, down_mine)


def body(
    tokens,
    lengths,
    cotangent,
    norm_gain,
    norm_shift,
    query_weight,
    query_bias,
    keyval_weight,
    value_bias,
    mixer_weight,
    mixer_bias,
    ffnorm_gain,
    ffnorm_shift,
    up_weight,
    up_bias,
    down_weight,
    down_bias,
):
    y, c, z, x = [lax.axis_index(name) for name in ("y", "c", "z", "x")]
    length = lax.axis_size("z")
    place = y * 2 + c
    slots, seg, width = tokens.shape
    rows = slots * seg
    head_dim = value_bias.shape[0] * 4
    hidden = up_weight.shape[1]
    hidden_block = hidden // (8 * length)
    hidden_mine = hidden // 8
    with_length = 2 * length * seg > MIN_LEN
    scal = jnp.concatenate([jnp.stack([z, x]).astype(jnp.int32), lengths])

    quarter = width // 4
    small = jnp.stack(
        [
            norm_gain,
            norm_shift,
            query_bias,
            mixer_bias,
            ffnorm_gain,
            ffnorm_shift,
            down_bias,
            jnp.pad(value_bias, (0, quarter - value_bias.shape[0])),
        ]
    )
    pair = jnp.stack([small, swap(small, "c")])
    pair = jnp.where(c == 0, pair, pair[::-1])
    quad = jnp.stack([pair, swap(pair, "y")])
    quad = jnp.where(y == 0, quad, quad[::-1]).reshape(4, 8, quarter)
    smalls = quad.transpose(1, 0, 2).reshape(8, width).astype(F32)
    gain, shift, q_bias, m_bias, ffgain, ffshift, d_bias = [smalls[i][None, :] for i in range(7)]
    v_bias = quad[:, 7, : value_bias.shape[0]].reshape(1, head_dim).astype(F32)

    full_keyval = gather_rows(keyval_weight, x, place)
    full_query = gather_rows(query_weight, x, place)
    full_mixer = gather_rows(mixer_weight, x, place)

    down_mine = pick(down_weight.reshape(length, 2, hidden_block, width), x, 1).reshape(
        hidden_mine, width
    )
    up_bias_mine = pick(up_bias.reshape(length, 2, hidden_block), x, 1).reshape(1, hidden_mine)
    up_parts = pick(up_weight.reshape(quarter, 4, length, 2, hidden_block), x, 3).reshape(
        quarter, 4, hidden_mine
    )
    up_mine = jnp.zeros((width, hidden_mine), BF)
    for flip in range(4):
        piece = pick(up_parts, place ^ flip, 1)
        if flip:
            piece = lax.ppermute(piece, ("y", "c"), [(i, i ^ flip) for i in range(4)])
        up_mine = lax.dynamic_update_slice_in_dim(up_mine, piece, (place ^ flip) * quarter, 0)

    inputs = tokens.reshape(rows, width).astype(F32)
    unit1, rstd1 = norm_stats(inputs)
    first = (unit1 * gain + shift).astype(BF)
    kv_bias = jnp.concatenate([jnp.zeros_like(v_bias), v_bias], axis=1)
    keyvals = (dot(first, full_keyval) + kv_bias).astype(BF).reshape(slots, seg, 2 * head_dim)
    blocks = []
    current = keyvals
    for step in range(length):
        if step:
            current = lax.ppermute(current, "z", [(i, i + 1) for i in range(length - 1)])
        both = jnp.stack([current, swap(current, "x")], axis=1)
        both = jnp.where(x == 0, both, both[:, ::-1])
        blocks.append(both.reshape(slots, 2 * seg, 2 * head_dim))
    kv_all = jnp.stack(blocks, axis=1)
    q_t = (dot(full_query, first, ((0,), (1,))) + q_bias.reshape(width, 1)).astype(BF)
    mixed_t, lse = attn_forward(scal, q_t, kv_all, 4, with_length)
    residual = inputs + dot(mixed_t, full_mixer, ((0,), (0,))) + m_bias
    unit2, rstd2 = norm_stats(residual)
    second = (unit2 * ffgain + ffshift).astype(BF)

    token_pos = (z * 2 + x) * seg + jnp.arange(seg, dtype=jnp.int32)
    valid = (token_pos[None, :] < lengths[:, None]).astype(F32).reshape(rows, 1)
    d_out = cotangent.reshape(rows, width).astype(F32) * valid
    d_down = d_out.astype(BF)

    down_all = gather_plane(d_down)
    d_second, out_parts, down_part, up_part, ubias_part = ffn(
        second,
        jnp.concatenate(down_all, axis=0),
        up_mine,
        up_bias_mine.astype(F32),
        down_mine,
        length,
    )
    output = residual + scatter_plane([out_parts[i] for i in range(4)]) + d_bias
    layer_out = output.astype(BF).reshape(tokens.shape)
    down_grad = scatter_line(down_part.reshape(length, hidden_block, width), z, length)
    ubias_grad = scatter_line(ubias_part.reshape(length, hidden_block), z, length)
    out_rows = width // (8 * length)
    up_sum = scatter_line(up_part, z, length).astype(BF)
    up_rows = lax.all_to_all(
        up_sum.reshape(8, out_rows, hidden_mine), ("y", "c", "x"), 0, 0, tiled=True
    )
    up_grad = (
        up_rows.reshape(4, 2, out_rows, length, hidden_block)
        .transpose(2, 0, 3, 1, 4)
        .reshape(out_rows, hidden)
        .astype(F32)
    )

    d_residual = d_out + norm_backward(d_second, unit2, rstd2, ffgain)
    d_mix = d_residual.astype(BF)
    d_mixed_t = dot(full_mixer, d_mix, ((1,), (1,))).astype(BF)
    where = (y, c, z, x)
    sizes = (length, width)
    mixer_all = scatter_all(
        mixed_t.T,
        d_mix,
        (
            jnp.sum(d_mix.astype(F32), axis=0),
            jnp.sum(d_second * unit2, axis=0),
            jnp.sum(d_second, axis=0),
            jnp.sum(d_out, axis=0),
        ),
        where,
        sizes,
    )

    dq_t, dkv = attn_backward(scal, q_t, kv_all, mixed_t, d_mixed_t, lse, 4, with_length)
    dkv = dkv.reshape(slots, length, 2, seg, 2 * head_dim)
    running = None
    for step in range(length - 1, -1, -1):
        term = dkv[:, step]
        term = pick(term, x, 1) + swap(pick(term, 1 - x, 1).astype(BF), "x").astype(F32)
        if running is not None:
            term = term + lax.ppermute(
                running.astype(BF), "z", [(i, i - 1) for i in range(1, length)]
            ).astype(F32)
        running = term
    d_keyvals = running.reshape(rows, 2 * head_dim).astype(BF)
    d_first = dot(dq_t, full_query, ((0,), (1,))) + dot(d_keyvals, full_keyval, ((1,), (1,)))
    tokens_grad = (d_residual + norm_backward(d_first, unit1, rstd1, gain)).astype(BF)
    d_queries = dq_t.T
    devices = 8 * length
    vbias = jnp.sum(d_keyvals[:, head_dim:].astype(F32), axis=0)
    vbias = jnp.pad(
        vbias.reshape(devices, head_dim // devices),
        ((0, 0), (0, out_rows - head_dim // devices)),
    ).reshape(width)
    query_all = scatter_all(
        first,
        jnp.concatenate([d_queries, d_keyvals], axis=1),
        (
            jnp.sum(d_first * unit1, axis=0),
            jnp.sum(d_first, axis=0),
            jnp.sum(d_queries.astype(F32), axis=0),
            vbias,
        ),
        where,
        sizes,
    )
    kv_end = width + 2 * head_dim
    return (
        layer_out,
        tokens_grad.reshape(tokens.shape),
        query_all[:, kv_end],
        query_all[:, kv_end + 1],
        query_all[:, :width],
        query_all[:, kv_end + 2],
        query_all[:, width:kv_end],
        query_all[: head_dim // devices, kv_end + 3],
        mixer_all[:, :width],
        mixer_all[:, width],
        mixer_all[:, width + 1],
        mixer_all[:, width + 2],
        up_grad,
        ubias_grad,
        down_grad,
        mixer_all[:, width + 3],
    )


def solution(mesh):
    ctx = mesh.shape["ctx"]
    fine = Mesh(mesh.devices.reshape(2, 2, ctx // 2, 2), ("y", "c", "z", "x"))
    fsdp, both, every = ("y", "c"), ("z", "x"), ("y", "c", "z", "x")
    return jax.shard_map(
        body,
        mesh=fine,
        in_specs=(
            P(fsdp, both, None),
            P(fsdp),
            P(fsdp, both, None),
            P(fsdp),
            P(fsdp),
            P(fsdp, None),
            P(fsdp),
            P(fsdp, None),
            P(fsdp),
            P(fsdp, None),
            P(fsdp),
            P(fsdp),
            P(fsdp),
            P(fsdp, None),
            P(fsdp),
            P(fsdp, None),
            P(fsdp),
        ),
        out_specs=(
            P(fsdp, both, None),
            P(fsdp, both, None),
            P(every),
            P(every),
            P(every, None),
            P(every),
            P(every, None),
            P(every),
            P(every, None),
            P(every),
            P(every),
            P(every),
            P(every, None),
            P(every),
            P(every, None),
            P(every),
        ),
        check_vma=False,
    )
```

```python
import functools

import jax
import jax.numpy as jnp
from jax import lax
from jax.experimental import pallas as pl
from jax.experimental.pallas import tpu as pltpu
from jax.sharding import Mesh, PartitionSpec as P

EPSILON = 1e-05
NEG_LARGE = -1e30
MIN_LEN = 1024
BF = jnp.bfloat16
F32 = jnp.float32
GELU_K = 0.7978845608028654
GELU_C = 0.044715


def dot(left_side, right_side, dims=((1,), (0,))):
    return lax.dot_general(left_side, right_side, (dims, ((), ())), preferred_element_type=F32)


def swap(values, axis):
    return lax.ppermute(values, axis, [(0, 1), (1, 0)])


def pick(values, index, axis):
    return lax.dynamic_index_in_dim(values, index, axis, keepdims=False)


def stack_heads(block, head_dim):
    heads = block.shape[0] // head_dim
    return jnp.concatenate([block[h * head_dim : (h + 1) * head_dim] for h in range(heads)], axis=1)


def unstack_heads(stacked, seg):
    heads = stacked.shape[1] // seg
    return jnp.concatenate([stacked[:, h * seg : (h + 1) * seg] for h in range(heads)], axis=0)


def masked_scores(scal_ref, queries, keys, step, seg, heads, with_length, first_block):
    scores = dot(keys, queries) * (keys.shape[1] ** (-0.5))
    pair = keys.shape[0]
    if not (with_length or first_block):
        return scores
    key_pos = lax.broadcasted_iota(jnp.int32, (pair, seg), 0)
    allowed = None
    if first_block:
        query_pos = lax.broadcasted_iota(jnp.int32, (pair, seg), 1) + scal_ref[1] * seg
        allowed = key_pos <= query_pos
    if with_length:
        length = scal_ref[2 + pl.program_id(0)]
        inside = key_pos + (scal_ref[0] - step) * pair < length
        allowed = inside if allowed is None else allowed & inside
    bias = jnp.where(allowed, 0.0, NEG_LARGE).astype(F32)
    return scores + jnp.concatenate([bias] * heads, axis=1)


def attn_fwd_kernel(scal_ref, q_ref, kv_ref, out_ref, lse_ref, *, with_length):
    head_dim = kv_ref.shape[-1] // 2
    seg = q_ref.shape[1]
    heads = q_ref.shape[0] // head_dim
    queries = stack_heads(q_ref[...], head_dim)

    def block(step, state, first_block):
        top, total, accum = state
        keys = kv_ref[0, step, :, :head_dim]
        values = kv_ref[0, step, :, head_dim:]
        scores = masked_scores(scal_ref, queries, keys, step, seg, heads, with_length, first_block)
        new_top = jnp.maximum(top, jnp.max(scores, axis=0, keepdims=True))
        terms = jnp.exp(scores - new_top)
        fade = jnp.exp(top - new_top)
        total = total * fade + jnp.sum(terms, axis=0, keepdims=True)
        accum = accum * fade + dot(values, terms.astype(BF), ((0,), (0,)))
        return new_top, total, accum

    lanes = heads * seg
    state = (
        jnp.full((1, lanes), NEG_LARGE, F32),
        jnp.zeros((1, lanes), F32),
        jnp.zeros((head_dim, lanes), F32),
    )
    state = block(0, state, True)
    top, total, accum = lax.fori_loop(1, scal_ref[0] + 1, lambda t, s: block(t, s, False), state)
    out_ref[...] = unstack_heads(accum / total, seg).astype(BF)
    lse_ref[0, 0] = top + jnp.log(total)


def attn_bwd_kernel(scal_ref, q_ref, kv_ref, out_ref, dout_ref, lse_ref, dq_ref, dkv_ref, *, with_length):
    head_dim = kv_ref.shape[-1] // 2
    seg = q_ref.shape[1]
    heads = q_ref.shape[0] // head_dim
    scale = head_dim ** (-0.5)
    queries = stack_heads(q_ref[...], head_dim)
    d_mixed = stack_heads(dout_ref[...], head_dim)
    mixed = stack_heads(out_ref[...], head_dim)
    delta = jnp.sum(mixed.astype(F32) * d_mixed.astype(F32), axis=0, keepdims=True)
    lse = lse_ref[0, 0]

    @pl.when(pl.program_id(1) == 0)
    def clear():
        dkv_ref[...] = jnp.zeros_like(dkv_ref)

    def block(step, accum, first_block):
        keys = kv_ref[0, step, :, :head_dim]
        values = kv_ref[0, step, :, head_dim:]
        scores = masked_scores(scal_ref, queries, keys, step, seg, heads, with_length, first_block)
        probs = jnp.exp(scores - lse)
        d_probs = dot(values, d_mixed)
        d_scores = (probs * (d_probs - delta)).astype(BF)
        dkv_ref[0, step, :, :head_dim] += dot(d_scores, queries, ((1,), (1,))) * scale
        dkv_ref[0, step, :, head_dim:] += dot(probs.astype(BF), d_mixed, ((1,), (1,)))
        return accum + dot(keys, d_scores, ((0,), (0,)))

    accum = block(0, jnp.zeros((head_dim, heads * seg), F32), True)
    accum = lax.fori_loop(1, scal_ref[0] + 1, lambda t, s: block(t, s, False), accum)
    dq_ref[...] = (unstack_heads(accum, seg) * scale).astype(BF)


def attn_specs(slots, steps, pair, seg, rows, groups, head_dim):
    lanes = rows // groups // head_dim * seg
    scal = pl.BlockSpec(memory_space=pltpu.SMEM)
    feat = pl.BlockSpec((rows // groups, seg), lambda s, g: (g, s))
    kv = pl.BlockSpec((1, steps, pair, 2 * head_dim), lambda s, g: (s, 0, 0, 0))
    lse = pl.BlockSpec((1, 1, 1, lanes), lambda s, g: (s, g, 0, 0))
    return scal, feat, kv, lse, lanes


def attn_forward(scal, q_t, kv, groups, with_length):
    slots, steps, pair, width = kv.shape
    rows, cols = q_t.shape
    seg = cols // slots
    scal_s, feat, kv_s, lse_s, lanes = attn_specs(slots, steps, pair, seg, rows, groups, width // 2)
    return pl.pallas_call(
        functools.partial(attn_fwd_kernel, with_length=with_length),
        grid=(slots, groups),
        in_specs=[scal_s, feat, kv_s],
        out_specs=[feat, lse_s],
        out_shape=[
            jax.ShapeDtypeStruct((rows, cols), BF),
            jax.ShapeDtypeStruct((slots, groups, 1, lanes), F32),
        ],
        compiler_params=pltpu.CompilerParams(vmem_limit_bytes=40 << 20),
        cost_estimate=pl.CostEstimate(
            flops=4 * rows * cols * steps * pair, bytes_accessed=6 << 20, transcendentals=0
        ),
    )(scal, q_t, kv)


def attn_backward(scal, q_t, kv, out_t, dout_t, lse, groups, with_length):
    slots, steps, pair, width = kv.shape
    rows, cols = q_t.shape
    seg = cols // slots
    scal_s, feat, kv_s, lse_s, lanes = attn_specs(slots, steps, pair, seg, rows, groups, width // 2)
    return pl.pallas_call(
        functools.partial(attn_bwd_kernel, with_length=with_length),
        grid=(slots, groups),
        in_specs=[scal_s, feat, kv_s, feat, feat, lse_s],
        out_specs=[feat, kv_s],
        out_shape=[
            jax.ShapeDtypeStruct((rows, cols), BF),
            jax.ShapeDtypeStruct(kv.shape, F32),
        ],
        compiler_params=pltpu.CompilerParams(vmem_limit_bytes=48 << 20),
        cost_estimate=pl.CostEstimate(
            flops=10 * rows * cols * steps * pair, bytes_accessed=9 << 20, transcendentals=0
        ),
    )(scal, q_t, kv, out_t, dout_t, lse)


def norm_stats(values):
    center = values - jnp.mean(values, axis=-1, keepdims=True)
    spread = jnp.mean(center * center, axis=-1, keepdims=True)
    rstd = lax.rsqrt(spread + EPSILON)
    return center * rstd, rstd


def norm_backward(d_values, unit, rstd, gain):
    scaled = d_values * gain
    return rstd * (
        scaled
        - jnp.mean(scaled, axis=-1, keepdims=True)
        - unit * jnp.mean(scaled * unit, axis=-1, keepdims=True)
    )


def gather_rows(shard, x, place):
    rows = shard.shape[0]
    half = rows // 2
    mine = lax.dynamic_slice_in_dim(shard, x * half, half, 0)
    direct = swap(mine, "y")
    other = swap(direct, "x")
    sib = swap(shard, "c")
    sib_direct = swap(direct, "c")
    sib_other = swap(other, "c")
    full = jnp.zeros((4 * rows,) + shard.shape[1:], shard.dtype)
    far = place ^ 2
    pieces = (
        (shard, place * rows),
        (sib, (place ^ 1) * rows),
        (direct, far * rows + x * half),
        (other, far * rows + (1 - x) * half),
        (sib_direct, (far ^ 1) * rows + x * half),
        (sib_other, (far ^ 1) * rows + (1 - x) * half),
    )
    for piece, start in pieces:
        full = lax.dynamic_update_slice_in_dim(full, piece, start, 0)
    return full


def gather_plane(block):
    half = block.shape[0] // 2
    from_x = swap(block, "x")
    from_y = swap(block, "y")
    diag = jnp.concatenate([swap(from_y[:half], "x"), swap(from_x[half:], "y")], axis=0)
    return [
        jnp.concatenate([part, swap(part, "c")], axis=0) for part in (block, from_x, from_y, diag)
    ]


def scatter_plane(parts):
    rows = parts[0].shape[0] // 2
    half = rows // 2
    own, to_x, to_y, diag = [
        part[:rows].astype(F32) + swap(part[rows:].astype(BF), "c").astype(F32) for part in parts
    ]
    via_x = swap(diag[:half].astype(BF), "x").astype(F32)
    via_y = swap(diag[half:].astype(BF), "y").astype(F32)
    to_y = jnp.concatenate([to_y[:half] + via_x, to_y[half:]], axis=0)
    to_x = jnp.concatenate([to_x[:half], to_x[half:] + via_y], axis=0)
    return own + swap(to_x.astype(BF), "x").astype(F32) + swap(to_y.astype(BF), "y").astype(F32)


def scatter_line(parts, z, length):
    def block(index):
        return pick(parts, jnp.clip(index, 0, length - 1), 0).astype(F32)

    from_left = from_right = None
    for step in range(1, length):
        up = block(length - step + z)
        down = block(z - length + step)
        if from_left is not None:
            up, down = up + from_left, down + from_right
        from_left = lax.ppermute(up.astype(BF), "z", [(i, i + 1) for i in range(step)]).astype(F32)
        from_right = lax.ppermute(
            down.astype(BF), "z", [(i, i - 1) for i in range(length - step, length)]
        ).astype(F32)
    return block(z) + from_left + from_right


def scatter_all(left_side, right_side, vectors, place_yczx, sizes):
    y, c, z, x = place_yczx
    length, width = sizes
    tokens = left_side.shape[0]
    block = width // (8 * length)
    left_parts = left_side.reshape(tokens, 2, 2, width // 4)
    left_mine = pick(left_parts, c, 2).reshape(tokens, width // 2)
    left_sib = swap(pick(left_parts, 1 - c, 2), "c").reshape(tokens, width // 2)
    right_sib = swap(right_side, "c")
    partial = dot(
        jnp.concatenate([left_mine, left_sib], axis=0),
        jnp.concatenate([right_side, right_sib], axis=0),
        ((0,), (0,)),
    )
    extra = jnp.pad(jnp.stack(vectors, axis=1), ((0, 0), (0, 128 - len(vectors))))
    extra = extra.reshape(2, 2, width // 4, 128)
    extra = pick(extra, c, 1) + swap(pick(extra, 1 - c, 1).astype(BF), "c").astype(F32)
    partial = jnp.concatenate([partial, extra.reshape(width // 2, 128)], axis=1)
    cols = partial.shape[1]
    partial = partial.reshape(2, length, 2, block, cols)
    cut = (cols // 256) * 128
    side_a, side_b = partial[..., :cut], partial[..., cut:]
    side_a = pick(side_a, y, 0) + swap(pick(side_a, 1 - y, 0).astype(BF), "y").astype(F32)
    side_b = pick(side_b, x, 2) + swap(pick(side_b, 1 - x, 2).astype(BF), "x").astype(F32)
    side_a = pick(side_a, x, 1) + swap(pick(side_a, 1 - x, 1).astype(BF), "x").astype(F32)
    side_b = pick(side_b, y, 0) + swap(pick(side_b, 1 - y, 0).astype(BF), "y").astype(F32)
    return scatter_line(jnp.concatenate([side_a, side_b], axis=-1), z, length)


MESH = pl.DeviceIdType.MESH


def remote(src, dst, send_sems, recv_sems, index, device):
    return pltpu.make_async_remote_copy(
        src_ref=src,
        dst_ref=dst,
        send_sem=send_sems.at[index],
        recv_sem=recv_sems.at[index],
        device_id=device,
        device_id_type=MESH,
    )


def greet(devices):
    barrier = pltpu.get_barrier_semaphore()
    for device in devices:
        pl.semaphore_signal(barrier, inc=1, device_id=device, device_id_type=MESH)
    pl.semaphore_wait(barrier, len(devices))


def tiles(count, size):
    def over(fn):
        @pl.loop(0, count)
        def step(index):
            fn(pl.ds(pl.multiple_of(index * size, size), size), index)

    return over


def gelu_pair(upper):
    inner = jnp.tanh(upper * (GELU_K + (GELU_K * GELU_C) * (upper * upper)))
    half = 0.5 + 0.5 * inner
    slope = half + (0.5 * upper) * (1.0 - inner * inner) * (
        GELU_K + (3.0 * GELU_K * GELU_C) * (upper * upper)
    )
    return upper * half, slope


def ffn_kernel(
    second_ref,
    down_all_ref,
    up_ref,
    ubias_ref,
    down_ref,
    dsecond_ref,
    out_parts_ref,
    down_part_ref,
    up_part_ref,
    ubias_part_ref,
    tokens_v,
    cots_v,
    up_v,
    down_v,
    active_v,
    dupper_v,
    sib_out,
    sib_in,
    chip_out,
    chip_in,
    acc_v,
    stage_v,
    load_sem,
    stage_sem,
    gs_send,
    gs_recv,
    rs_send,
    rs_recv,
    *,
    length,
):
    rows, width = second_ref.shape
    hidden = up_ref.shape[1]
    half = rows // 2
    chunk = 2 * rows
    y, c, x = [lax.axis_index(name) for name in ("y", "c", "x")]
    sib, to_x, to_y = {"c": 1 - c}, {"x": 1 - x}, {"y": 1 - y}
    diag = {"x": 1 - x, "y": 1 - y}
    chips = (None, to_x, to_y, diag)

    loads = [
        pltpu.make_async_copy(second_ref, tokens_v.at[0, pl.ds(0, rows)], load_sem.at[0]),
        pltpu.make_async_copy(down_ref, down_v, load_sem.at[1]),
        pltpu.make_async_copy(down_all_ref, cots_v, load_sem.at[2]),
        pltpu.make_async_copy(up_ref, up_v, load_sem.at[3]),
    ]
    for load in loads:
        load.start()
    greet((sib, to_x, to_y, diag))
    loads[0].wait()

    same, other = pl.ds(0, rows), pl.ds(rows, rows)
    top, bottom = pl.ds(0, half), pl.ds(half, half)

    def gather(index, chip, span_src, chip_dst, span_dst, device):
        return remote(
            tokens_v.at[chip, span_src], tokens_v.at[chip_dst, span_dst], gs_send, gs_recv, index, device
        )

    send_x = gather(0, 0, same, 1, same, to_x)
    send_y = gather(1, 0, same, 2, same, to_y)
    share = [gather(2 + k, k, same, k, other, sib) for k in range(4)]
    diag_x = gather(6, 2, top, 3, top, to_x)
    diag_y = gather(7, 1, bottom, 3, bottom, to_y)
    send_x.start()
    send_y.start()
    share[0].start()

    loads[1].wait()
    loads[2].wait()

    @tiles(4 * chunk // 512, 512)
    def grad_active(span, index):
        @tiles(hidden // 512, 512)
        def columns(cols, _):
            dupper_v[span, cols] = dot(cots_v[span, :], down_v[cols, :], ((1,), (1,))).astype(BF)

    loads[3].wait()

    def chip_work(k):
        @tiles(hidden // 256, 256)
        def columns(cols, _):
            block = pl.ds(k * chunk, chunk)
            upper = dot(tokens_v[k], up_v[:, cols]) + ubias_ref[:, cols]
            active, slope = gelu_pair(upper)
            active_v[block, cols] = active.astype(BF)
            d_upper = (dupper_v[block, cols].astype(F32) * slope).astype(BF)
            dupper_v[block, cols] = d_upper
            part = jnp.sum(d_upper.astype(F32), axis=0, keepdims=True)
            if k == 0:
                ubias_part_ref[:, cols] = part
            else:
                ubias_part_ref[:, cols] += part

        @tiles(width // 512, 512)
        def to_sibling(cols, _):
            sib_out[k, :, cols] = dot(
                dupper_v[pl.ds(k * chunk + rows, rows), :], up_v[cols, :], ((1,), (1,))
            ).astype(BF)

        pair = remote(sib_out.at[k], sib_in.at[k], rs_send, rs_recv, k, sib)
        pair.start()

        @tiles(width // 512, 512)
        def keep(cols, _):
            acc_v[:, cols] = dot(dupper_v[pl.ds(k * chunk, rows), :], up_v[cols, :], ((1,), (1,)))

        pair.wait_recv()
        if k == 0:
            dsecond_ref[...] = acc_v[...] + sib_in[0].astype(F32)
            return [pair]
        chip_out[k - 1] = (acc_v[...] + sib_in[k].astype(F32)).astype(BF)
        far = remote(chip_out.at[k - 1], chip_in.at[k - 1], rs_send, rs_recv, 3 + k, chips[k])
        far.start()
        return [pair, far]

    share[0].wait_recv()
    sent = chip_work(0)
    send_x.wait_recv()
    share[1].start()
    diag_y.start()
    send_y.wait_recv()
    share[2].start()
    diag_x.start()
    share[1].wait_recv()
    sent += chip_work(1)
    share[2].wait_recv()
    sent += chip_work(2)
    diag_x.wait_recv()
    diag_y.wait_recv()
    share[3].start()
    share[3].wait_recv()
    sent += chip_work(3)

    def staged(slot, value, target):
        stage_v[slot] = value.astype(BF)
        copy = pltpu.make_async_copy(stage_v.at[slot], target, stage_sem.at[slot])
        copy.start()
        return copy

    @pl.loop(0, 4)
    def outputs(k):
        block = pl.ds(pl.multiple_of(k * chunk, chunk), chunk)
        copies = []
        for j in range(width // 512):
            cols = pl.ds(j * 512, 512)
            copies.append(
                staged(j, dot(active_v[block, :], down_v[:, cols]), out_parts_ref.at[k, :, cols])
            )
        for copy in copies:
            copy.wait()

    @pl.loop(0, hidden // 512)
    def downs(r):
        block = pl.ds(pl.multiple_of(r * 512, 512), 512)
        copies = []
        for j in range(width // 512):
            cols = pl.ds(j * 512, 512)
            copies.append(
                staged(
                    j,
                    dot(active_v[:, block], cots_v[:, cols], ((0,), (0,))),
                    down_part_ref.at[block, cols],
                )
            )
        for copy in copies:
            copy.wait()

    quarter = width // 4
    piece = quarter // length

    @pl.loop(0, hidden // 512)
    def ups(r):
        cols = pl.ds(pl.multiple_of(r * 512, 512), 512)
        copies = []
        for f in range(4):
            value = None
            for k in range(4):
                term = dot(
                    tokens_v[k, :, f * quarter : (f + 1) * quarter],
                    dupper_v[k * chunk : (k + 1) * chunk, cols],
                    ((0,), (0,)),
                )
                value = term if value is None else value + term
            stage_v[f] = value.astype(BF)
            for level in range(length):
                copy = pltpu.make_async_copy(
                    stage_v.at[f, pl.ds(level * piece, piece)],
                    up_part_ref.at[level, f, :, cols],
                    stage_sem.at[4 + f * length + level],
                )
                copy.start()
                copies.append(copy)
        for copy in copies:
            copy.wait()

    for k in range(3):
        remote(chip_out.at[k], chip_in.at[k], rs_send, rs_recv, 4 + k, chips[k + 1]).wait_recv()
    dsecond_ref[...] += (
        chip_in[0].astype(F32) + chip_in[1].astype(F32) + chip_in[2].astype(F32)
    )
    for copy in [send_x, send_y, diag_x, diag_y] + share + sent:
        copy.wait_send()


def ffn(second, down_all, up_mine, ubias, down_mine, length):
    rows, width = second.shape
    hidden = up_mine.shape[1]
    hbm = pl.BlockSpec(memory_space=pltpu.HBM)
    vmem = pl.BlockSpec(memory_space=pltpu.VMEM)
    sems = pltpu.SemaphoreType.DMA
    return pl.pallas_call(
        functools.partial(ffn_kernel, length=length),
        in_specs=[hbm, hbm, hbm, vmem, hbm],
        out_specs=[vmem, hbm, hbm, hbm, vmem],
        out_shape=[
            jax.ShapeDtypeStruct((rows, width), F32),
            jax.ShapeDtypeStruct((4, 2 * rows, width), BF),
            jax.ShapeDtypeStruct((hidden, width), BF),
            jax.ShapeDtypeStruct((length, 4, width // 4 // length, hidden), BF),
            jax.ShapeDtypeStruct((1, hidden), F32),
        ],
        scratch_shapes=[
            pltpu.VMEM((4, 2 * rows, width), BF),
            pltpu.VMEM((8 * rows, width), BF),
            pltpu.VMEM((width, hidden), BF),
            pltpu.VMEM((hidden, width), BF),
            pltpu.VMEM((8 * rows, hidden), BF),
            pltpu.VMEM((8 * rows, hidden), BF),
            pltpu.VMEM((4, rows, width), BF),
            pltpu.VMEM((4, rows, width), BF),
            pltpu.VMEM((3, rows, width), BF),
            pltpu.VMEM((3, rows, width), BF),
            pltpu.VMEM((rows, width), F32),
            pltpu.VMEM((4, 512, 512), BF),
            sems((4,)),
            sems((4 + 4 * length,)),
            sems((8,)),
            sems((8,)),
            sems((7,)),
            sems((7,)),
        ],
        compiler_params=pltpu.CompilerParams(
            collective_id=1, has_side_effects=True, vmem_limit_bytes=60 << 20
        ),
        cost_estimate=pl.CostEstimate(
            flops=12 * 8 * rows * width * hidden, bytes_accessed=40 << 20, transcendentals=0
        ),
    )(second, down_all, up_mine, ubias, down_mine)


ROW_TILE = 32


def for_rows(total, fn):
    @pl.loop(0, total // ROW_TILE)
    def step(index):
        fn(pl.ds(pl.multiple_of(index * ROW_TILE, ROW_TILE), ROW_TILE))


def norm_rows(values):
    center = values - jnp.mean(values, axis=-1, keepdims=True)
    spread = jnp.mean(center * center, axis=-1, keepdims=True)
    rstd = lax.rsqrt(spread + EPSILON)
    return center * rstd, rstd


class Gathered:
    def __init__(self, shard_ref, full_ref, sems, base, where):
        self.y, self.c, self.x = where
        self.shard, self.full, self.sems, self.base = shard_ref, full_ref, sems, base
        self.rows = shard_ref.shape[0]
        self.half = self.rows // 2
        self.step = self.half // 4
        self.place = self.y * 2 + self.c

    def copy(self, src, dst, index, device):
        send_sems, recv_sems = self.sems
        return remote(src, dst, send_sems, recv_sems, self.base + index, device)

    def span(self, place, side, i):
        start = place * self.rows + side * self.half + i * self.step
        return self.full.at[pl.ds(pl.multiple_of(start, self.step), self.step)]

    def over_y(self, i):
        start = pl.multiple_of(self.x * self.half + i * self.step, self.step)
        return self.copy(
            self.shard.at[pl.ds(start, self.step)], self.span(self.place, self.x, i), i, {"y": 1 - self.y}
        )

    def over_x(self, i):
        ref = self.span(self.place ^ 2, self.x, i)
        return self.copy(ref, ref, 4 + i, {"x": 1 - self.x})

    def over_c(self, i, side):
        ref = self.span(self.place ^ 2, self.x if side == 0 else 1 - self.x, i)
        return self.copy(ref, ref, 8 + 4 * side + i, {"c": 1 - self.c})

    def own_c(self):
        start = pl.multiple_of(self.place * self.rows, self.rows)
        return self.copy(self.shard, self.full.at[pl.ds(start, self.rows)], 16, {"c": 1 - self.c})

    def own(self, sem):
        start = pl.multiple_of(self.place * self.rows, self.rows)
        return pltpu.make_async_copy(self.shard, self.full.at[pl.ds(start, self.rows)], sem)


class Stream:
    def __init__(self, weights):
        self.order = [(w, i) for w in weights for i in range(4)]
        self.next = 0
        self.sent = []

    def begin(self, copy):
        copy.start()
        self.sent.append(copy)

    def start(self):
        for n in range(2):
            w, i = self.order[n]
            self.begin(w.over_y(i))

    def event(self):
        n = self.next
        self.next += 1
        if n < len(self.order):
            w, i = self.order[n]
            w.over_y(i).wait_recv()
            if n + 2 < len(self.order):
                w2, i2 = self.order[n + 2]
                self.begin(w2.over_y(i2))
            self.begin(w.over_x(i))
            self.begin(w.over_c(i, 0))
        if n >= 1:
            w, i = self.order[n - 1]
            w.over_x(i).wait_recv()
            self.begin(w.over_c(i, 1))

    def settle(self, weight):
        weight.own_c().wait_recv()
        for i in range(4):
            weight.over_c(i, 0).wait_recv()
            weight.over_c(i, 1).wait_recv()


def front_kernel(
    lengths_ref,
    tokens_v,
    smalls_ref,
    kvw_ref,
    qw_ref,
    mw_ref,
    up_ref,
    cot_ref,
    second_ref,
    residual_ref,
    first_v,
    q_v,
    kv_v,
    mixed_v,
    lse_ref,
    vec_v,
    wq_out,
    wm_out,
    wkv_v,
    up_out,
    cots_out,
    wq_v,
    wm_v,
    smalls_v,
    local_sem,
    w_send,
    w_recv,
    s_send,
    s_recv,
    k_send,
    k_recv,
    u_send,
    u_recv,
    uz_send,
    uz_recv,
    c_send,
    c_recv,
    *,
    length,
    slots,
    with_length,
    aligned,
):
    rows, width = tokens_v.shape
    seg = rows // slots
    head_dim = kvw_ref.shape[1] // 2
    heads = width // head_dim
    group = 4
    quarter = width // 4
    y, c, z, x = [lax.axis_index(name) for name in ("y", "c", "z", "x")]
    place = y * 2 + c
    sib, to_x, to_y = {"c": 1 - c}, {"x": 1 - x}, {"y": 1 - y}
    cross, diag = {"y": 1 - y, "c": 1 - c}, {"x": 1 - x, "y": 1 - y}

    weights = [
        Gathered(ref, full, (w_send, w_recv), 17 * n, (y, c, x))
        for n, (ref, full) in enumerate(((qw_ref, wq_v), (mw_ref, wm_v)))
    ]
    query_w, mixer_w = weights
    locals_ = [query_w.own(local_sem.at[0]), mixer_w.own(local_sem.at[1])]
    kv_rows = pl.ds(pl.multiple_of(place * quarter, quarter), quarter)
    locals_.append(pltpu.make_async_copy(kvw_ref, wkv_v.at[kv_rows], local_sem.at[2]))
    locals_.append(pltpu.make_async_copy(smalls_ref, smalls_v.at[place], local_sem.at[3]))
    for copy in locals_:
        copy.start()

    barrier = pltpu.get_barrier_semaphore()
    for device in (sib, to_x, to_y, cross, diag):
        pl.semaphore_signal(barrier, inc=1, device_id=device, device_id_type=MESH)
    for other in range(length):
        @pl.when(other != z)
        def hello():
            pl.semaphore_signal(barrier, inc=1, device_id={"z": other}, device_id_type=MESH)
    pl.semaphore_wait(barrier, 5 + length - 1)

    sent = []

    def begin(copy):
        copy.start()
        sent.append(copy)
        return copy

    small_copies = [
        begin(remote(smalls_ref, smalls_v.at[place], s_send, s_recv, n, device))
        for n, device in enumerate((sib, to_y, cross))
    ]
    kv_near = begin(remote(kvw_ref, wkv_v.at[kv_rows], s_send, s_recv, 3, sib))
    kv_far = begin(remote(kvw_ref, wkv_v.at[kv_rows], s_send, s_recv, 4, to_y))
    stream = Stream(weights)
    stream.start()
    for weight in weights:
        begin(weight.own_c())

    for copy in small_copies:
        copy.wait_recv()
    locals_[3].wait()
    vec_v[...] = jnp.concatenate([smalls_v[f].astype(F32) for f in range(4)], axis=1)

    def first_norm(span):
        unit, _ = norm_rows(tokens_v[span, :].astype(F32))
        first_v[span, :] = (unit * vec_v[0:1, :] + vec_v[1:2, :]).astype(BF)

    for_rows(rows, first_norm)

    kv_far.wait_recv()
    far_rows = wkv_v.at[pl.ds(pl.multiple_of((place ^ 2) * quarter, quarter), quarter)]
    kv_pass = begin(remote(far_rows, far_rows, s_send, s_recv, 5, sib))
    stream.event()
    kv_near.wait_recv()
    locals_[2].wait()
    kv_pass.wait_recv()
    v_bias = (
        vec_v[7:8, 0:head_dim]
        + vec_v[7:8, quarter : quarter + head_dim]
        + vec_v[7:8, 2 * quarter : 2 * quarter + head_dim]
        + vec_v[7:8, 3 * quarter : 3 * quarter + head_dim]
    )
    keyvals = dot(first_v[...], wkv_v[...]) + jnp.concatenate([jnp.zeros_like(v_bias), v_bias], axis=1)
    mine = pl.ds(pl.multiple_of(x * seg, seg), seg)
    for s in range(slots):
        kv_v[s, 0, mine, :] = keyvals[s * seg : (s + 1) * seg].astype(BF)

    def kv_up(t):
        return remote(kv_v.at[:, t - 1, mine], kv_v.at[:, t, mine], k_send, k_recv, t, {"z": z + 1})

    def kv_side(t):
        ref = kv_v.at[:, t, mine]
        return remote(ref, ref, k_send, k_recv, length + t, to_x)

    def kv_step(t):
        if t:
            @pl.when(z >= t)
            def arrive():
                kv_up(t).wait_recv()

        @pl.when(z >= t)
        def side():
            kv_side(t).start()

        if t + 1 < length:
            @pl.when((z >= t) & (z < length - 1))
            def onward():
                kv_up(t + 1).start()

    part = quarter // length
    hidden = up_out.shape[1]
    block = hidden // length

    def up_copies(index, flip, span, device):
        target = place ^ flip
        dst_rows = pl.ds(pl.multiple_of(place * quarter + span[0], span[1]), span[1])
        copies = []
        for b in range(length if aligned else 1):
            if aligned:
                start = target * (hidden * 2) + (2 * b + x) * block
                src = up_ref.at[pl.ds(span[0], span[1]), pl.ds(pl.multiple_of(start, block), block)]
                dst = up_out.at[dst_rows, pl.ds(b * block, block)]
            else:
                src = up_ref.at[target, pl.ds(span[0], span[1])]
                dst = up_out.at[dst_rows]
            n = index * length + b
            if device is None:
                copies.append(pltpu.make_async_copy(src, dst, u_send.at[n]))
            else:
                copies.append(remote(src, dst, u_send, u_recv, n, device))
        return copies

    up_local = up_copies(0, 0, (0, quarter), None)
    up_near = up_copies(1, 1, (0, quarter), sib)
    z_part = (pl.multiple_of(z * part, part), part)
    up_far = up_copies(2, 2, z_part, to_y) + up_copies(3, 3, z_part, cross)

    def up_share(k, source, target):
        start = (place ^ (2 + k)) * quarter + source * part
        ref = up_out.at[pl.ds(pl.multiple_of(start, part), part)]
        return pltpu.make_async_remote_copy(
            src_ref=ref,
            dst_ref=ref,
            send_sem=uz_send.at[k, target],
            recv_sem=uz_recv.at[k, source],
            device_id={"z": target},
            device_id_type=MESH,
        )

    for copy in up_local:
        copy.start()
    for copy in up_near:
        begin(copy)

    for t in range(length):
        kv_step(t)
        if t < 3:
            stream.event()

    same, other_half = pl.ds(0, rows), pl.ds(rows, rows)
    top, bottom = pl.ds(0, rows // 2), pl.ds(rows // 2, rows // 2)
    cot_local = pltpu.make_async_copy(cot_ref, cots_out.at[0, same], local_sem.at[4])
    cot_local.start()
    cot_x = remote(cot_ref, cots_out.at[1, same], c_send, c_recv, 0, to_x)
    cot_y = remote(cot_ref, cots_out.at[2, same], c_send, c_recv, 1, to_y)
    cot_share = [
        remote(cot_ref if k == 0 else cots_out.at[k, same], cots_out.at[k, other_half], c_send, c_recv, 2 + k, sib)
        for k in range(4)
    ]
    cot_dx = remote(cots_out.at[2, top], cots_out.at[3, top], c_send, c_recv, 6, to_x)
    cot_dy = remote(cots_out.at[1, bottom], cots_out.at[3, bottom], c_send, c_recv, 7, to_y)

    stream.event()
    locals_[0].wait()
    stream.settle(query_w)

    @tiles(width // 512, 512)
    def project(cols, _):
        q_v[:, cols] = (dot(first_v[...], wq_v[:, cols]) + vec_v[2:3, cols]).astype(BF)

    wq_copy = pltpu.make_async_copy(wq_v, wq_out, local_sem.at[5])
    wq_copy.start()
    for t in range(length):
        @pl.when(z >= t)
        def arrived():
            kv_side(t).wait_recv()
            kv_side(t).wait_send()

        if t:
            @pl.when((z >= t - 1) & (z < length - 1))
            def gone():
                kv_up(t).wait_send()

    scale = head_dim ** (-0.5)

    def attend(s, g):
        lanes = pl.ds(pl.multiple_of(g * group * head_dim, group * head_dim), group * head_dim)
        wide = q_v[pl.ds(s * seg, seg), lanes]
        queries = jnp.concatenate(
            [wide[:, h * head_dim : (h + 1) * head_dim] for h in range(group)], axis=0
        )

        def step(t, state, diagonal):
            top_, total, accum = state
            keys = kv_v[s, t, :, :head_dim]
            values = kv_v[s, t, :, head_dim:]
            scores = dot(keys, queries, ((1,), (1,))) * scale
            if diagonal or with_length:
                key_pos = lax.broadcasted_iota(jnp.int32, (2 * seg, seg), 0)
                allowed = None
                if diagonal:
                    query_pos = lax.broadcasted_iota(jnp.int32, (2 * seg, seg), 1) + x * seg
                    allowed = key_pos <= query_pos
                if with_length:
                    inside = key_pos + (z - t) * (2 * seg) < lengths_ref[s]
                    allowed = inside if allowed is None else allowed & inside
                bias = jnp.where(allowed, 0.0, NEG_LARGE).astype(F32)
                scores = scores + jnp.concatenate([bias] * group, axis=1)
            new_top = jnp.maximum(top_, jnp.max(scores, axis=0, keepdims=True))
            terms = jnp.exp(scores - new_top)
            fade = jnp.exp(top_ - new_top)
            total = total * fade + jnp.sum(terms, axis=0, keepdims=True)
            accum = accum * fade + dot(values, terms.astype(BF), ((0,), (0,)))
            return new_top, total, accum

        span = group * seg
        state = (
            jnp.full((1, span), NEG_LARGE, F32),
            jnp.zeros((1, span), F32),
            jnp.zeros((head_dim, span), F32),
        )
        state = step(0, state, True)
        top_, total, accum = lax.fori_loop(1, z + 1, lambda t, st: step(t, st, False), state)
        out = accum / total
        mixed_v[pl.ds(s * seg, seg), lanes] = jnp.concatenate(
            [out[:, h * seg : (h + 1) * seg].T for h in range(group)], axis=1
        ).astype(BF)
        lse_ref[s, g] = top_ + jnp.log(total)

    for s in range(slots):
        @pl.loop(0, heads // group)
        def over_groups(g):
            attend(s, g)

        stream.event()
        stream.event()

    locals_[1].wait()
    while stream.next <= len(stream.order):
        stream.event()
    for copy in up_far:
        begin(copy)
    begin(cot_x)
    begin(cot_y)
    begin(cot_share[0])
    stream.settle(mixer_w)
    wm_copy = pltpu.make_async_copy(wm_v, wm_out, local_sem.at[6])
    wm_copy.start()

    @tiles(width // 512, 512)
    def mix(cols, _):
        residual_ref[:, cols] = (
            tokens_v[:, cols].astype(F32) + dot(mixed_v[...], wm_v[:, cols]) + vec_v[3:4, cols]
        )

    def second_norm(span):
        unit, _ = norm_rows(residual_ref[span, :])
        second_ref[span, :] = (unit * vec_v[4:5, :] + vec_v[5:6, :]).astype(BF)

    for_rows(rows, second_norm)

    for copy in up_far:
        copy.wait_recv()
    for target in range(length):
        @pl.when(target != z)
        def share():
            for k in range(2):
                up_share(k, z, target).start()

    cot_x.wait_recv()
    cot_y.wait_recv()
    begin(cot_share[1])
    begin(cot_share[2])
    begin(cot_dx)
    begin(cot_dy)
    cot_dx.wait_recv()
    cot_dy.wait_recv()
    begin(cot_share[3])
    for copy in cot_share + up_near:
        copy.wait_recv()
    for copy in up_local:
        copy.wait()
    for target in range(length):
        @pl.when(target != z)
        def shared():
            for k in range(2):
                up_share(k, z, target).wait_send()
                up_share(k, target, z).wait_recv()
    for copy in sent + stream.sent:
        copy.wait_send()
    for copy in (cot_local, wq_copy, wm_copy):
        copy.wait()


def front(lengths, tokens, smalls, kvw, qw, mw, up, cot, slots, length, with_length, aligned, hidden):
    rows, width = tokens.shape
    seg = rows // slots
    both = kvw.shape[1]
    groups = width // (both // 2) // 4
    hbm = pl.BlockSpec(memory_space=pltpu.HBM)
    vmem = pl.BlockSpec(memory_space=pltpu.VMEM)
    sems = pltpu.SemaphoreType.DMA
    return pl.pallas_call(
        functools.partial(
            front_kernel, length=length, slots=slots, with_length=with_length, aligned=aligned
        ),
        in_specs=[pl.BlockSpec(memory_space=pltpu.SMEM), vmem, hbm, hbm, hbm, hbm, hbm, hbm],
        out_specs=[vmem] * 8 + [hbm, hbm, vmem, hbm, hbm],
        out_shape=[
            jax.ShapeDtypeStruct((rows, width), BF),
            jax.ShapeDtypeStruct((rows, width), F32),
            jax.ShapeDtypeStruct((rows, width), BF),
            jax.ShapeDtypeStruct((rows, width), BF),
            jax.ShapeDtypeStruct((slots, length, 2 * seg, both), BF),
            jax.ShapeDtypeStruct((rows, width), BF),
            jax.ShapeDtypeStruct((slots, groups, 1, 4 * seg), F32),
            jax.ShapeDtypeStruct((16, width), F32),
            jax.ShapeDtypeStruct((width, width), BF),
            jax.ShapeDtypeStruct((width, width), BF),
            jax.ShapeDtypeStruct((width, both), BF),
            jax.ShapeDtypeStruct((width, hidden), BF),
            jax.ShapeDtypeStruct((4, 2 * rows, width), BF),
        ],
        scratch_shapes=[
            pltpu.VMEM((width, width), BF),
            pltpu.VMEM((width, width), BF),
            pltpu.VMEM((4, 16, width // 4), BF),
            sems((7,)),
            sems((34,)),
            sems((34,)),
            sems((6,)),
            sems((6,)),
            sems((2 * length,)),
            sems((2 * length,)),
            sems((4 * length,)),
            sems((4 * length,)),
            sems((2, length)),
            sems((2, length)),
            sems((8,)),
            sems((8,)),
        ],
        compiler_params=pltpu.CompilerParams(
            collective_id=2, has_side_effects=True, vmem_limit_bytes=60 << 20
        ),
        cost_estimate=pl.CostEstimate(
            flops=6 * rows * width * width, bytes_accessed=40 << 20, transcendentals=0
        ),
    )(lengths, tokens, smalls, kvw, qw, mw, up, cot)


def body(
    tokens,
    lengths,
    cotangent,
    norm_gain,
    norm_shift,
    query_weight,
    query_bias,
    keyval_weight,
    value_bias,
    mixer_weight,
    mixer_bias,
    ffnorm_gain,
    ffnorm_shift,
    up_weight,
    up_bias,
    down_weight,
    down_bias,
):
    y, c, z, x = [lax.axis_index(name) for name in ("y", "c", "z", "x")]
    length = lax.axis_size("z")
    place = y * 2 + c
    slots, seg, width = tokens.shape
    rows = slots * seg
    head_dim = value_bias.shape[0] * 4
    hidden = up_weight.shape[1]
    hidden_block = hidden // (8 * length)
    hidden_mine = hidden // 8
    with_length = 2 * length * seg > MIN_LEN
    scal = jnp.concatenate([jnp.stack([z, x]).astype(jnp.int32), lengths])

    quarter = width // 4
    v_part = value_bias.shape[0]
    v_place = lax.dynamic_update_slice(jnp.zeros((quarter,), BF), value_bias, (place * v_part,))
    small = jnp.stack(
        [norm_gain, norm_shift, query_bias, mixer_bias, ffnorm_gain, ffnorm_shift, down_bias, v_place]
    )
    small = jnp.concatenate([small, jnp.zeros_like(small)], axis=0)

    down_mine = pick(down_weight.reshape(length, 2, hidden_block, width), x, 1).reshape(
        hidden_mine, width
    )
    up_bias_mine = pick(up_bias.reshape(length, 2, hidden_block), x, 1).reshape(1, hidden_mine)
    aligned = hidden_block % 128 == 0
    up_given = up_weight
    if not aligned:
        up_given = pick(up_weight.reshape(quarter, 4, length, 2, hidden_block), x, 3)
        up_given = up_given.reshape(quarter, 4, hidden_mine).transpose(1, 0, 2)

    token_pos = (z * 2 + x) * seg + jnp.arange(seg, dtype=jnp.int32)
    valid = (token_pos[None, :] < lengths[:, None]).astype(F32).reshape(rows, 1)
    d_down = cotangent.reshape(rows, width)
    if with_length:
        d_down = (d_down.astype(F32) * valid).astype(BF)
    d_out = d_down.astype(F32)

    flat = tokens.reshape(rows, width)
    (
        second,
        residual,
        first,
        queries,
        kv_all,
        mixed,
        lse,
        vectors,
        full_query,
        full_mixer,
        full_keyval,
        up_mine,
        down_all,
    ) = front(
        lengths,
        flat,
        small,
        keyval_weight,
        query_weight,
        mixer_weight,
        up_given,
        d_down,
        slots,
        length,
        with_length,
        aligned,
        hidden_mine,
    )
    inputs = flat.astype(F32)
    gain, ffgain, d_bias = vectors[0:1], vectors[4:5], vectors[6:7]
    unit1, rstd1 = norm_stats(inputs)
    unit2, rstd2 = norm_stats(residual)
    q_t, mixed_t = queries.T, mixed.T

    d_second, out_parts, down_part, up_part, ubias_part = ffn(
        second,
        down_all.reshape(8 * rows, width),
        up_mine,
        up_bias_mine.astype(F32),
        down_mine,
        length,
    )
    output = residual + scatter_plane([out_parts[i] for i in range(4)]) + d_bias
    layer_out = output.astype(BF).reshape(tokens.shape)
    down_grad = scatter_line(down_part.reshape(length, hidden_block, width), z, length)
    ubias_grad = scatter_line(ubias_part.reshape(length, hidden_block), z, length)
    out_rows = width // (8 * length)
    up_sum = scatter_line(up_part, z, length).astype(BF)
    up_rows = lax.all_to_all(
        up_sum.reshape(8, out_rows, hidden_mine), ("y", "c", "x"), 0, 0, tiled=True
    )
    up_grad = (
        up_rows.reshape(4, 2, out_rows, length, hidden_block)
        .transpose(2, 0, 3, 1, 4)
        .reshape(out_rows, hidden)
        .astype(F32)
    )

    d_residual = d_out + norm_backward(d_second, unit2, rstd2, ffgain)
    d_mix = d_residual.astype(BF)
    d_mixed_t = dot(full_mixer, d_mix, ((1,), (1,))).astype(BF)
    where = (y, c, z, x)
    sizes = (length, width)
    mixer_all = scatter_all(
        mixed,
        d_mix,
        (
            jnp.sum(d_mix.astype(F32), axis=0),
            jnp.sum(d_second * unit2, axis=0),
            jnp.sum(d_second, axis=0),
            jnp.sum(d_out, axis=0),
        ),
        where,
        sizes,
    )

    dq_t, dkv = attn_backward(scal, q_t, kv_all, mixed_t, d_mixed_t, lse, 4, with_length)
    dkv = dkv.reshape(slots, length, 2, seg, 2 * head_dim)
    running = None
    for step in range(length - 1, -1, -1):
        term = dkv[:, step]
        term = pick(term, x, 1) + swap(pick(term, 1 - x, 1).astype(BF), "x").astype(F32)
        if running is not None:
            term = term + lax.ppermute(
                running.astype(BF), "z", [(i, i - 1) for i in range(1, length)]
            ).astype(F32)
        running = term
    d_keyvals = running.reshape(rows, 2 * head_dim).astype(BF)
    d_first = dot(dq_t, full_query, ((0,), (1,))) + dot(d_keyvals, full_keyval, ((1,), (1,)))
    tokens_grad = (d_residual + norm_backward(d_first, unit1, rstd1, gain)).astype(BF)
    d_queries = dq_t.T
    devices = 8 * length
    vbias = jnp.sum(d_keyvals[:, head_dim:].astype(F32), axis=0)
    vbias = jnp.pad(
        vbias.reshape(devices, head_dim // devices),
        ((0, 0), (0, out_rows - head_dim // devices)),
    ).reshape(width)
    query_all = scatter_all(
        first,
        jnp.concatenate([d_queries, d_keyvals], axis=1),
        (
            jnp.sum(d_first * unit1, axis=0),
            jnp.sum(d_first, axis=0),
            jnp.sum(d_queries.astype(F32), axis=0),
            vbias,
        ),
        where,
        sizes,
    )
    kv_end = width + 2 * head_dim
    return (
        layer_out,
        tokens_grad.reshape(tokens.shape),
        query_all[:, kv_end],
        query_all[:, kv_end + 1],
        query_all[:, :width],
        query_all[:, kv_end + 2],
        query_all[:, width:kv_end],
        query_all[: head_dim // devices, kv_end + 3],
        mixer_all[:, :width],
        mixer_all[:, width],
        mixer_all[:, width + 1],
        mixer_all[:, width + 2],
        up_grad,
        ubias_grad,
        down_grad,
        mixer_all[:, width + 3],
    )


def solution(mesh):
    ctx = mesh.shape["ctx"]
    fine = Mesh(mesh.devices.reshape(2, 2, ctx // 2, 2), ("y", "c", "z", "x"))
    fsdp, both, every = ("y", "c"), ("z", "x"), ("y", "c", "z", "x")
    return jax.shard_map(
        body,
        mesh=fine,
        in_specs=(
            P(fsdp, both, None),
            P(fsdp),
            P(fsdp, both, None),
            P(fsdp),
            P(fsdp),
            P(fsdp, None),
            P(fsdp),
            P(fsdp, None),
            P(fsdp),
            P(fsdp, None),
            P(fsdp),
            P(fsdp),
            P(fsdp),
            P(fsdp, None),
            P(fsdp),
            P(fsdp, None),
            P(fsdp),
        ),
        out_specs=(
            P(fsdp, both, None),
            P(fsdp, both, None),
            P(every),
            P(every),
            P(every, None),
            P(every),
            P(every, None),
            P(every),
            P(every, None),
            P(every),
            P(every),
            P(every),
            P(every, None),
            P(every),
            P(every, None),
            P(every),
        ),
        check_vma=False,
    )
```

```python
import functools

import jax
import jax.numpy as jnp
from jax import lax
from jax.experimental import pallas as pl
from jax.experimental.pallas import tpu as pltpu
from jax.sharding import Mesh, PartitionSpec as P

EPSILON = 1e-05
NEG_LARGE = -1e30
MIN_LEN = 1024
BF = jnp.bfloat16
F32 = jnp.float32
GELU_K = 0.7978845608028654
GELU_C = 0.044715


def dot(left_side, right_side, dims=((1,), (0,))):
    return lax.dot_general(left_side, right_side, (dims, ((), ())), preferred_element_type=F32)


def swap(values, axis):
    return lax.ppermute(values, axis, [(0, 1), (1, 0)])


def pick(values, index, axis):
    return lax.dynamic_index_in_dim(values, index, axis, keepdims=False)


def stack_heads(block, head_dim):
    heads = block.shape[0] // head_dim
    return jnp.concatenate([block[h * head_dim : (h + 1) * head_dim] for h in range(heads)], axis=1)


def unstack_heads(stacked, seg):
    heads = stacked.shape[1] // seg
    return jnp.concatenate([stacked[:, h * seg : (h + 1) * seg] for h in range(heads)], axis=0)


def masked_scores(scal_ref, queries, keys, step, seg, heads, with_length, first_block):
    scores = dot(keys, queries) * (keys.shape[1] ** (-0.5))
    pair = keys.shape[0]
    if not (with_length or first_block):
        return scores
    key_pos = lax.broadcasted_iota(jnp.int32, (pair, seg), 0)
    allowed = None
    if first_block:
        query_pos = lax.broadcasted_iota(jnp.int32, (pair, seg), 1) + scal_ref[1] * seg
        allowed = key_pos <= query_pos
    if with_length:
        length = scal_ref[2 + pl.program_id(0)]
        inside = key_pos + (scal_ref[0] - step) * pair < length
        allowed = inside if allowed is None else allowed & inside
    bias = jnp.where(allowed, 0.0, NEG_LARGE).astype(F32)
    return scores + jnp.concatenate([bias] * heads, axis=1)


def attn_fwd_kernel(scal_ref, q_ref, kv_ref, out_ref, lse_ref, *, with_length):
    head_dim = kv_ref.shape[-1] // 2
    seg = q_ref.shape[1]
    heads = q_ref.shape[0] // head_dim
    queries = stack_heads(q_ref[...], head_dim)

    def block(step, state, first_block):
        top, total, accum = state
        keys = kv_ref[0, step, :, :head_dim]
        values = kv_ref[0, step, :, head_dim:]
        scores = masked_scores(scal_ref, queries, keys, step, seg, heads, with_length, first_block)
        new_top = jnp.maximum(top, jnp.max(scores, axis=0, keepdims=True))
        terms = jnp.exp(scores - new_top)
        fade = jnp.exp(top - new_top)
        total = total * fade + jnp.sum(terms, axis=0, keepdims=True)
        accum = accum * fade + dot(values, terms.astype(BF), ((0,), (0,)))
        return new_top, total, accum

    lanes = heads * seg
    state = (
        jnp.full((1, lanes), NEG_LARGE, F32),
        jnp.zeros((1, lanes), F32),
        jnp.zeros((head_dim, lanes), F32),
    )
    state = block(0, state, True)
    top, total, accum = lax.fori_loop(1, scal_ref[0] + 1, lambda t, s: block(t, s, False), state)
    out_ref[...] = unstack_heads(accum / total, seg).astype(BF)
    lse_ref[0, 0] = top + jnp.log(total)


def attn_bwd_kernel(scal_ref, q_ref, kv_ref, out_ref, dout_ref, lse_ref, dq_ref, dkv_ref, *, with_length):
    head_dim = kv_ref.shape[-1] // 2
    seg = q_ref.shape[1]
    heads = q_ref.shape[0] // head_dim
    scale = head_dim ** (-0.5)
    queries = stack_heads(q_ref[...], head_dim)
    d_mixed = stack_heads(dout_ref[...], head_dim)
    mixed = stack_heads(out_ref[...], head_dim)
    delta = jnp.sum(mixed.astype(F32) * d_mixed.astype(F32), axis=0, keepdims=True)
    lse = lse_ref[0, 0]

    @pl.when(pl.program_id(1) == 0)
    def clear():
        dkv_ref[...] = jnp.zeros_like(dkv_ref)

    def block(step, accum, first_block):
        keys = kv_ref[0, step, :, :head_dim]
        values = kv_ref[0, step, :, head_dim:]
        scores = masked_scores(scal_ref, queries, keys, step, seg, heads, with_length, first_block)
        probs = jnp.exp(scores - lse)
        d_probs = dot(values, d_mixed)
        d_scores = (probs * (d_probs - delta)).astype(BF)
        dkv_ref[0, step, :, :head_dim] += dot(d_scores, queries, ((1,), (1,))) * scale
        dkv_ref[0, step, :, head_dim:] += dot(probs.astype(BF), d_mixed, ((1,), (1,)))
        return accum + dot(keys, d_scores, ((0,), (0,)))

    accum = block(0, jnp.zeros((head_dim, heads * seg), F32), True)
    accum = lax.fori_loop(1, scal_ref[0] + 1, lambda t, s: block(t, s, False), accum)
    dq_ref[...] = (unstack_heads(accum, seg) * scale).astype(BF)


def attn_specs(slots, steps, pair, seg, rows, groups, head_dim):
    lanes = rows // groups // head_dim * seg
    scal = pl.BlockSpec(memory_space=pltpu.SMEM)
    feat = pl.BlockSpec((rows // groups, seg), lambda s, g: (g, s))
    kv = pl.BlockSpec((1, steps, pair, 2 * head_dim), lambda s, g: (s, 0, 0, 0))
    lse = pl.BlockSpec((1, 1, 1, lanes), lambda s, g: (s, g, 0, 0))
    return scal, feat, kv, lse, lanes


def attn_forward(scal, q_t, kv, groups, with_length):
    slots, steps, pair, width = kv.shape
    rows, cols = q_t.shape
    seg = cols // slots
    scal_s, feat, kv_s, lse_s, lanes = attn_specs(slots, steps, pair, seg, rows, groups, width // 2)
    return pl.pallas_call(
        functools.partial(attn_fwd_kernel, with_length=with_length),
        grid=(slots, groups),
        in_specs=[scal_s, feat, kv_s],
        out_specs=[feat, lse_s],
        out_shape=[
            jax.ShapeDtypeStruct((rows, cols), BF),
            jax.ShapeDtypeStruct((slots, groups, 1, lanes), F32),
        ],
        compiler_params=pltpu.CompilerParams(vmem_limit_bytes=40 << 20),
        cost_estimate=pl.CostEstimate(
            flops=4 * rows * cols * steps * pair, bytes_accessed=6 << 20, transcendentals=0
        ),
    )(scal, q_t, kv)


def attn_backward(scal, q_t, kv, out_t, dout_t, lse, groups, with_length):
    slots, steps, pair, width = kv.shape
    rows, cols = q_t.shape
    seg = cols // slots
    scal_s, feat, kv_s, lse_s, lanes = attn_specs(slots, steps, pair, seg, rows, groups, width // 2)
    return pl.pallas_call(
        functools.partial(attn_bwd_kernel, with_length=with_length),
        grid=(slots, groups),
        in_specs=[scal_s, feat, kv_s, feat, feat, lse_s],
        out_specs=[feat, kv_s],
        out_shape=[
            jax.ShapeDtypeStruct((rows, cols), BF),
            jax.ShapeDtypeStruct(kv.shape, F32),
        ],
        compiler_params=pltpu.CompilerParams(vmem_limit_bytes=48 << 20),
        cost_estimate=pl.CostEstimate(
            flops=10 * rows * cols * steps * pair, bytes_accessed=9 << 20, transcendentals=0
        ),
    )(scal, q_t, kv, out_t, dout_t, lse)


def norm_stats(values):
    center = values - jnp.mean(values, axis=-1, keepdims=True)
    spread = jnp.mean(center * center, axis=-1, keepdims=True)
    rstd = lax.rsqrt(spread + EPSILON)
    return center * rstd, rstd


def norm_backward(d_values, unit, rstd, gain):
    scaled = d_values * gain
    return rstd * (
        scaled
        - jnp.mean(scaled, axis=-1, keepdims=True)
        - unit * jnp.mean(scaled * unit, axis=-1, keepdims=True)
    )


def gather_rows(shard, x, place):
    rows = shard.shape[0]
    half = rows // 2
    mine = lax.dynamic_slice_in_dim(shard, x * half, half, 0)
    direct = swap(mine, "y")
    other = swap(direct, "x")
    sib = swap(shard, "c")
    sib_direct = swap(direct, "c")
    sib_other = swap(other, "c")
    full = jnp.zeros((4 * rows,) + shard.shape[1:], shard.dtype)
    far = place ^ 2
    pieces = (
        (shard, place * rows),
        (sib, (place ^ 1) * rows),
        (direct, far * rows + x * half),
        (other, far * rows + (1 - x) * half),
        (sib_direct, (far ^ 1) * rows + x * half),
        (sib_other, (far ^ 1) * rows + (1 - x) * half),
    )
    for piece, start in pieces:
        full = lax.dynamic_update_slice_in_dim(full, piece, start, 0)
    return full


def gather_plane(block):
    half = block.shape[0] // 2
    from_x = swap(block, "x")
    from_y = swap(block, "y")
    diag = jnp.concatenate([swap(from_y[:half], "x"), swap(from_x[half:], "y")], axis=0)
    return [
        jnp.concatenate([part, swap(part, "c")], axis=0) for part in (block, from_x, from_y, diag)
    ]


def scatter_plane(parts):
    rows = parts[0].shape[0] // 2
    half = rows // 2
    own, to_x, to_y, diag = [
        part[:rows].astype(F32) + swap(part[rows:].astype(BF), "c").astype(F32) for part in parts
    ]
    via_x = swap(diag[:half].astype(BF), "x").astype(F32)
    via_y = swap(diag[half:].astype(BF), "y").astype(F32)
    to_y = jnp.concatenate([to_y[:half] + via_x, to_y[half:]], axis=0)
    to_x = jnp.concatenate([to_x[:half], to_x[half:] + via_y], axis=0)
    return own + swap(to_x.astype(BF), "x").astype(F32) + swap(to_y.astype(BF), "y").astype(F32)


def scatter_line(parts, z, length):
    def block(index):
        return pick(parts, jnp.clip(index, 0, length - 1), 0).astype(F32)

    from_left = from_right = None
    for step in range(1, length):
        up = block(length - step + z)
        down = block(z - length + step)
        if from_left is not None:
            up, down = up + from_left, down + from_right
        from_left = lax.ppermute(up.astype(BF), "z", [(i, i + 1) for i in range(step)]).astype(F32)
        from_right = lax.ppermute(
            down.astype(BF), "z", [(i, i - 1) for i in range(length - step, length)]
        ).astype(F32)
    return block(z) + from_left + from_right


def scatter_all(left_side, right_side, vectors, place_yczx, sizes):
    y, c, z, x = place_yczx
    length, width = sizes
    tokens = left_side.shape[0]
    block = width // (8 * length)
    left_parts = left_side.reshape(tokens, 2, 2, width // 4)
    left_mine = pick(left_parts, c, 2).reshape(tokens, width // 2)
    left_sib = swap(pick(left_parts, 1 - c, 2), "c").reshape(tokens, width // 2)
    right_sib = swap(right_side, "c")
    partial = dot(
        jnp.concatenate([left_mine, left_sib], axis=0),
        jnp.concatenate([right_side, right_sib], axis=0),
        ((0,), (0,)),
    )
    extra = jnp.pad(jnp.stack(vectors, axis=1), ((0, 0), (0, 128 - len(vectors))))
    extra = extra.reshape(2, 2, width // 4, 128)
    extra = pick(extra, c, 1) + swap(pick(extra, 1 - c, 1).astype(BF), "c").astype(F32)
    partial = jnp.concatenate([partial, extra.reshape(width // 2, 128)], axis=1)
    cols = partial.shape[1]
    partial = partial.reshape(2, length, 2, block, cols)
    cut = (cols // 256) * 128
    side_a, side_b = partial[..., :cut], partial[..., cut:]
    side_a = pick(side_a, y, 0) + swap(pick(side_a, 1 - y, 0).astype(BF), "y").astype(F32)
    side_b = pick(side_b, x, 2) + swap(pick(side_b, 1 - x, 2).astype(BF), "x").astype(F32)
    side_a = pick(side_a, x, 1) + swap(pick(side_a, 1 - x, 1).astype(BF), "x").astype(F32)
    side_b = pick(side_b, y, 0) + swap(pick(side_b, 1 - y, 0).astype(BF), "y").astype(F32)
    return scatter_line(jnp.concatenate([side_a, side_b], axis=-1), z, length)


MESH = pl.DeviceIdType.MESH


def remote(src, dst, send_sems, recv_sems, index, device):
    return pltpu.make_async_remote_copy(
        src_ref=src,
        dst_ref=dst,
        send_sem=send_sems.at[index],
        recv_sem=recv_sems.at[index],
        device_id=device,
        device_id_type=MESH,
    )


def greet(devices):
    barrier = pltpu.get_barrier_semaphore()
    for device in devices:
        pl.semaphore_signal(barrier, inc=1, device_id=device, device_id_type=MESH)
    pl.semaphore_wait(barrier, len(devices))


def tiles(count, size):
    def over(fn):
        @pl.loop(0, count)
        def step(index):
            fn(pl.ds(pl.multiple_of(index * size, size), size), index)

    return over


def gelu_pair(upper):
    inner = jnp.tanh(upper * (GELU_K + (GELU_K * GELU_C) * (upper * upper)))
    half = 0.5 + 0.5 * inner
    slope = half + (0.5 * upper) * (1.0 - inner * inner) * (
        GELU_K + (3.0 * GELU_K * GELU_C) * (upper * upper)
    )
    return upper * half, slope


def ffn_kernel(
    second_ref,
    down_all_ref,
    up_ref,
    ubias_ref,
    down_ref,
    dsecond_ref,
    out_parts_ref,
    down_part_ref,
    up_part_ref,
    ubias_part_ref,
    tokens_v,
    cots_v,
    up_v,
    down_v,
    active_v,
    dupper_v,
    sib_out,
    sib_in,
    chip_out,
    chip_in,
    acc_v,
    stage_v,
    load_sem,
    stage_sem,
    gs_send,
    gs_recv,
    rs_send,
    rs_recv,
    *,
    length,
):
    rows, width = second_ref.shape
    hidden = up_ref.shape[1]
    half = rows // 2
    chunk = 2 * rows
    y, c, x = [lax.axis_index(name) for name in ("y", "c", "x")]
    sib, to_x, to_y = {"c": 1 - c}, {"x": 1 - x}, {"y": 1 - y}
    diag = {"x": 1 - x, "y": 1 - y}
    chips = (None, to_x, to_y, diag)

    loads = [
        pltpu.make_async_copy(second_ref, tokens_v.at[0, pl.ds(0, rows)], load_sem.at[0]),
        pltpu.make_async_copy(down_ref, down_v, load_sem.at[1]),
        pltpu.make_async_copy(down_all_ref, cots_v, load_sem.at[2]),
        pltpu.make_async_copy(up_ref, up_v, load_sem.at[3]),
    ]
    for load in loads:
        load.start()
    greet((sib, to_x, to_y, diag))
    loads[0].wait()

    same, other = pl.ds(0, rows), pl.ds(rows, rows)
    top, bottom = pl.ds(0, half), pl.ds(half, half)

    def gather(index, chip, span_src, chip_dst, span_dst, device):
        return remote(
            tokens_v.at[chip, span_src], tokens_v.at[chip_dst, span_dst], gs_send, gs_recv, index, device
        )

    send_x = gather(0, 0, same, 1, same, to_x)
    send_y = gather(1, 0, same, 2, same, to_y)
    share = [gather(2 + k, k, same, k, other, sib) for k in range(4)]
    diag_x = gather(6, 2, top, 3, top, to_x)
    diag_y = gather(7, 1, bottom, 3, bottom, to_y)
    send_x.start()
    send_y.start()
    share[0].start()

    loads[1].wait()
    loads[2].wait()

    @tiles(4 * chunk // 512, 512)
    def grad_active(span, index):
        @tiles(hidden // 512, 512)
        def columns(cols, _):
            dupper_v[span, cols] = dot(cots_v[span, :], down_v[cols, :], ((1,), (1,))).astype(BF)

    loads[3].wait()

    def chip_work(k):
        @tiles(hidden // 256, 256)
        def columns(cols, _):
            block = pl.ds(k * chunk, chunk)
            upper = dot(tokens_v[k], up_v[:, cols]) + ubias_ref[:, cols]
            active, slope = gelu_pair(upper)
            active_v[block, cols] = active.astype(BF)
            d_upper = (dupper_v[block, cols].astype(F32) * slope).astype(BF)
            dupper_v[block, cols] = d_upper
            part = jnp.sum(d_upper.astype(F32), axis=0, keepdims=True)
            if k == 0:
                ubias_part_ref[:, cols] = part
            else:
                ubias_part_ref[:, cols] += part

        @tiles(width // 512, 512)
        def to_sibling(cols, _):
            sib_out[k, :, cols] = dot(
                dupper_v[pl.ds(k * chunk + rows, rows), :], up_v[cols, :], ((1,), (1,))
            ).astype(BF)

        pair = remote(sib_out.at[k], sib_in.at[k], rs_send, rs_recv, k, sib)
        pair.start()

        @tiles(width // 512, 512)
        def keep(cols, _):
            acc_v[:, cols] = dot(dupper_v[pl.ds(k * chunk, rows), :], up_v[cols, :], ((1,), (1,)))

        pair.wait_recv()
        if k == 0:
            dsecond_ref[...] = acc_v[...] + sib_in[0].astype(F32)
            return [pair]
        chip_out[k - 1] = (acc_v[...] + sib_in[k].astype(F32)).astype(BF)
        far = remote(chip_out.at[k - 1], chip_in.at[k - 1], rs_send, rs_recv, 3 + k, chips[k])
        far.start()
        return [pair, far]

    share[0].wait_recv()
    sent = chip_work(0)
    send_x.wait_recv()
    share[1].start()
    diag_y.start()
    send_y.wait_recv()
    share[2].start()
    diag_x.start()
    share[1].wait_recv()
    sent += chip_work(1)
    share[2].wait_recv()
    sent += chip_work(2)
    diag_x.wait_recv()
    diag_y.wait_recv()
    share[3].start()
    share[3].wait_recv()
    sent += chip_work(3)

    def staged(slot, value, target):
        stage_v[slot] = value.astype(BF)
        copy = pltpu.make_async_copy(stage_v.at[slot], target, stage_sem.at[slot])
        copy.start()
        return copy

    @pl.loop(0, 4)
    def outputs(k):
        block = pl.ds(pl.multiple_of(k * chunk, chunk), chunk)
        copies = []
        for j in range(width // 512):
            cols = pl.ds(j * 512, 512)
            copies.append(
                staged(j, dot(active_v[block, :], down_v[:, cols]), out_parts_ref.at[k, :, cols])
            )
        for copy in copies:
            copy.wait()

    @pl.loop(0, hidden // 512)
    def downs(r):
        block = pl.ds(pl.multiple_of(r * 512, 512), 512)
        copies = []
        for j in range(width // 512):
            cols = pl.ds(j * 512, 512)
            copies.append(
                staged(
                    j,
                    dot(active_v[:, block], cots_v[:, cols], ((0,), (0,))),
                    down_part_ref.at[block, cols],
                )
            )
        for copy in copies:
            copy.wait()

    quarter = width // 4
    piece = quarter // length

    @pl.loop(0, hidden // 512)
    def ups(r):
        cols = pl.ds(pl.multiple_of(r * 512, 512), 512)
        copies = []
        for f in range(4):
            value = None
            for k in range(4):
                term = dot(
                    tokens_v[k, :, f * quarter : (f + 1) * quarter],
                    dupper_v[k * chunk : (k + 1) * chunk, cols],
                    ((0,), (0,)),
                )
                value = term if value is None else value + term
            stage_v[f] = value.astype(BF)
            for level in range(length):
                copy = pltpu.make_async_copy(
                    stage_v.at[f, pl.ds(level * piece, piece)],
                    up_part_ref.at[level, f, :, cols],
                    stage_sem.at[4 + f * length + level],
                )
                copy.start()
                copies.append(copy)
        for copy in copies:
            copy.wait()

    for k in range(3):
        remote(chip_out.at[k], chip_in.at[k], rs_send, rs_recv, 4 + k, chips[k + 1]).wait_recv()
    dsecond_ref[...] += (
        chip_in[0].astype(F32) + chip_in[1].astype(F32) + chip_in[2].astype(F32)
    )
    for copy in [send_x, send_y, diag_x, diag_y] + share + sent:
        copy.wait_send()


def ffn(second, down_all, up_mine, ubias, down_mine, length):
    rows, width = second.shape
    hidden = up_mine.shape[1]
    hbm = pl.BlockSpec(memory_space=pltpu.HBM)
    vmem = pl.BlockSpec(memory_space=pltpu.VMEM)
    sems = pltpu.SemaphoreType.DMA
    return pl.pallas_call(
        functools.partial(ffn_kernel, length=length),
        in_specs=[hbm, hbm, hbm, vmem, hbm],
        out_specs=[vmem, hbm, hbm, hbm, vmem],
        out_shape=[
            jax.ShapeDtypeStruct((rows, width), F32),
            jax.ShapeDtypeStruct((4, 2 * rows, width), BF),
            jax.ShapeDtypeStruct((hidden, width), BF),
            jax.ShapeDtypeStruct((length, 4, width // 4 // length, hidden), BF),
            jax.ShapeDtypeStruct((1, hidden), F32),
        ],
        scratch_shapes=[
            pltpu.VMEM((4, 2 * rows, width), BF),
            pltpu.VMEM((8 * rows, width), BF),
            pltpu.VMEM((width, hidden), BF),
            pltpu.VMEM((hidden, width), BF),
            pltpu.VMEM((8 * rows, hidden), BF),
            pltpu.VMEM((8 * rows, hidden), BF),
            pltpu.VMEM((4, rows, width), BF),
            pltpu.VMEM((4, rows, width), BF),
            pltpu.VMEM((3, rows, width), BF),
            pltpu.VMEM((3, rows, width), BF),
            pltpu.VMEM((rows, width), F32),
            pltpu.VMEM((4, 512, 512), BF),
            sems((4,)),
            sems((4 + 4 * length,)),
            sems((8,)),
            sems((8,)),
            sems((7,)),
            sems((7,)),
        ],
        compiler_params=pltpu.CompilerParams(
            collective_id=1, has_side_effects=True, vmem_limit_bytes=60 << 20
        ),
        cost_estimate=pl.CostEstimate(
            flops=12 * 8 * rows * width * hidden, bytes_accessed=40 << 20, transcendentals=0
        ),
    )(second, down_all, up_mine, ubias, down_mine)


ROW_TILE = 32


def for_rows(total, fn):
    @pl.loop(0, total // ROW_TILE)
    def step(index):
        fn(pl.ds(pl.multiple_of(index * ROW_TILE, ROW_TILE), ROW_TILE))


def norm_rows(values):
    center = values - jnp.mean(values, axis=-1, keepdims=True)
    spread = jnp.mean(center * center, axis=-1, keepdims=True)
    rstd = lax.rsqrt(spread + EPSILON)
    return center * rstd, rstd


class Gathered:
    def __init__(self, shard_ref, full_ref, sems, base, where):
        self.y, self.c, self.x = where
        self.shard, self.full, self.sems, self.base = shard_ref, full_ref, sems, base
        self.rows = shard_ref.shape[0]
        self.half = self.rows // 2
        self.step = self.half // 4
        self.place = self.y * 2 + self.c

    def copy(self, src, dst, index, device):
        send_sems, recv_sems = self.sems
        return remote(src, dst, send_sems, recv_sems, self.base + index, device)

    def span(self, place, side, i):
        start = place * self.rows + side * self.half + i * self.step
        return self.full.at[pl.ds(pl.multiple_of(start, self.step), self.step)]

    def over_y(self, i):
        start = pl.multiple_of(self.x * self.half + i * self.step, self.step)
        return self.copy(
            self.shard.at[pl.ds(start, self.step)], self.span(self.place, self.x, i), i, {"y": 1 - self.y}
        )

    def over_x(self, i):
        ref = self.span(self.place ^ 2, self.x, i)
        return self.copy(ref, ref, 4 + i, {"x": 1 - self.x})

    def over_c(self, i, side):
        ref = self.span(self.place ^ 2, self.x if side == 0 else 1 - self.x, i)
        return self.copy(ref, ref, 8 + 4 * side + i, {"c": 1 - self.c})

    def own_c(self):
        start = pl.multiple_of(self.place * self.rows, self.rows)
        return self.copy(self.shard, self.full.at[pl.ds(start, self.rows)], 16, {"c": 1 - self.c})

    def own(self, sem):
        start = pl.multiple_of(self.place * self.rows, self.rows)
        return pltpu.make_async_copy(self.shard, self.full.at[pl.ds(start, self.rows)], sem)


class Stream:
    def __init__(self, weights):
        self.order = [(w, i) for w in weights for i in range(4)]
        self.next = 0
        self.sent = []

    def begin(self, copy):
        copy.start()
        self.sent.append(copy)

    def start(self):
        for n in range(2):
            w, i = self.order[n]
            self.begin(w.over_y(i))

    def event(self):
        n = self.next
        self.next += 1
        if n < len(self.order):
            w, i = self.order[n]
            w.over_y(i).wait_recv()
            if n + 2 < len(self.order):
                w2, i2 = self.order[n + 2]
                self.begin(w2.over_y(i2))
            self.begin(w.over_x(i))
            self.begin(w.over_c(i, 0))
        if n >= 1:
            w, i = self.order[n - 1]
            w.over_x(i).wait_recv()
            self.begin(w.over_c(i, 1))

    def settle(self, weight):
        weight.own_c().wait_recv()
        for i in range(4):
            weight.over_c(i, 0).wait_recv()
            weight.over_c(i, 1).wait_recv()


def front_kernel(
    lengths_ref,
    tokens_v,
    smalls_ref,
    kvw_ref,
    qw_ref,
    mw_ref,
    up_ref,
    cot_ref,
    second_ref,
    residual_ref,
    first_v,
    q_v,
    kv_v,
    mixed_v,
    lse_ref,
    vec_v,
    wq_out,
    wm_out,
    wkv_v,
    up_out,
    cots_out,
    wq_v,
    wm_v,
    smalls_v,
    local_sem,
    w_send,
    w_recv,
    s_send,
    s_recv,
    k_send,
    k_recv,
    u_send,
    u_recv,
    uz_send,
    uz_recv,
    c_send,
    c_recv,
    *,
    length,
    slots,
    with_length,
    aligned,
):
    rows, width = tokens_v.shape
    seg = rows // slots
    head_dim = kvw_ref.shape[1] // 2
    heads = width // head_dim
    group = 4
    quarter = width // 4
    y, c, z, x = [lax.axis_index(name) for name in ("y", "c", "z", "x")]
    place = y * 2 + c
    sib, to_x, to_y = {"c": 1 - c}, {"x": 1 - x}, {"y": 1 - y}
    cross, diag = {"y": 1 - y, "c": 1 - c}, {"x": 1 - x, "y": 1 - y}

    weights = [
        Gathered(ref, full, (w_send, w_recv), 17 * n, (y, c, x))
        for n, (ref, full) in enumerate(((qw_ref, wq_v), (mw_ref, wm_v)))
    ]
    query_w, mixer_w = weights
    locals_ = [query_w.own(local_sem.at[0]), mixer_w.own(local_sem.at[1])]
    kv_rows = pl.ds(pl.multiple_of(place * quarter, quarter), quarter)
    locals_.append(pltpu.make_async_copy(kvw_ref, wkv_v.at[kv_rows], local_sem.at[2]))
    locals_.append(pltpu.make_async_copy(smalls_ref, smalls_v.at[place], local_sem.at[3]))
    for copy in locals_:
        copy.start()

    barrier = pltpu.get_barrier_semaphore()
    for device in (sib, to_x, to_y, cross, diag):
        pl.semaphore_signal(barrier, inc=1, device_id=device, device_id_type=MESH)
    for other in range(length):
        @pl.when(other != z)
        def hello():
            pl.semaphore_signal(barrier, inc=1, device_id={"z": other}, device_id_type=MESH)
    pl.semaphore_wait(barrier, 5 + length - 1)

    sent = []

    def begin(copy):
        copy.start()
        sent.append(copy)
        return copy

    small_copies = [
        begin(remote(smalls_ref, smalls_v.at[place], s_send, s_recv, n, device))
        for n, device in enumerate((sib, to_y, cross))
    ]
    kv_near = begin(remote(kvw_ref, wkv_v.at[kv_rows], s_send, s_recv, 3, sib))
    kv_far = begin(remote(kvw_ref, wkv_v.at[kv_rows], s_send, s_recv, 4, to_y))
    stream = Stream(weights)
    stream.start()
    for weight in weights:
        begin(weight.own_c())

    for copy in small_copies:
        copy.wait_recv()
    locals_[3].wait()
    vec_v[...] = jnp.concatenate([smalls_v[f].astype(F32) for f in range(4)], axis=1)

    def first_norm(span):
        unit, _ = norm_rows(tokens_v[span, :].astype(F32))
        first_v[span, :] = (unit * vec_v[0:1, :] + vec_v[1:2, :]).astype(BF)

    for_rows(rows, first_norm)

    kv_far.wait_recv()
    far_rows = wkv_v.at[pl.ds(pl.multiple_of((place ^ 2) * quarter, quarter), quarter)]
    kv_pass = begin(remote(far_rows, far_rows, s_send, s_recv, 5, sib))
    stream.event()
    kv_near.wait_recv()
    locals_[2].wait()
    kv_pass.wait_recv()
    v_bias = (
        vec_v[7:8, 0:head_dim]
        + vec_v[7:8, quarter : quarter + head_dim]
        + vec_v[7:8, 2 * quarter : 2 * quarter + head_dim]
        + vec_v[7:8, 3 * quarter : 3 * quarter + head_dim]
    )
    keyvals = dot(first_v[...], wkv_v[...]) + jnp.concatenate([jnp.zeros_like(v_bias), v_bias], axis=1)
    mine = pl.ds(pl.multiple_of(x * seg, seg), seg)
    for s in range(slots):
        kv_v[s, 0, mine, :] = keyvals[s * seg : (s + 1) * seg].astype(BF)

    def kv_up(t):
        return remote(kv_v.at[:, t - 1, mine], kv_v.at[:, t, mine], k_send, k_recv, t, {"z": z + 1})

    def kv_side(t):
        ref = kv_v.at[:, t, mine]
        return remote(ref, ref, k_send, k_recv, length + t, to_x)

    def kv_step(t):
        if t:
            @pl.when(z >= t)
            def arrive():
                kv_up(t).wait_recv()

        @pl.when(z >= t)
        def side():
            kv_side(t).start()

        if t + 1 < length:
            @pl.when((z >= t) & (z < length - 1))
            def onward():
                kv_up(t + 1).start()

    part = quarter // length
    hidden = up_out.shape[1]
    block = hidden // length

    def up_copies(index, flip, span, device):
        target = place ^ flip
        dst_rows = pl.ds(pl.multiple_of(place * quarter + span[0], span[1]), span[1])
        copies = []
        for b in range(length if aligned else 1):
            if aligned:
                start = target * (hidden * 2) + (2 * b + x) * block
                src = up_ref.at[pl.ds(span[0], span[1]), pl.ds(pl.multiple_of(start, block), block)]
                dst = up_out.at[dst_rows, pl.ds(b * block, block)]
            else:
                src = up_ref.at[target, pl.ds(span[0], span[1])]
                dst = up_out.at[dst_rows]
            n = index * length + b
            if device is None:
                copies.append(pltpu.make_async_copy(src, dst, u_send.at[n]))
            else:
                copies.append(remote(src, dst, u_send, u_recv, n, device))
        return copies

    up_local = up_copies(0, 0, (0, quarter), None)
    up_near = up_copies(1, 1, (0, quarter), sib)
    z_part = (pl.multiple_of(z * part, part), part)
    up_far = up_copies(2, 2, z_part, to_y) + up_copies(3, 3, z_part, cross)

    def up_share(k, source, target):
        start = (place ^ (2 + k)) * quarter + source * part
        ref = up_out.at[pl.ds(pl.multiple_of(start, part), part)]
        return pltpu.make_async_remote_copy(
            src_ref=ref,
            dst_ref=ref,
            send_sem=uz_send.at[k, target],
            recv_sem=uz_recv.at[k, source],
            device_id={"z": target},
            device_id_type=MESH,
        )

    for copy in up_local:
        copy.start()
    for copy in up_near:
        begin(copy)

    for t in range(length):
        kv_step(t)
        if t < 3:
            stream.event()

    same, other_half = pl.ds(0, rows), pl.ds(rows, rows)
    top, bottom = pl.ds(0, rows // 2), pl.ds(rows // 2, rows // 2)
    cot_local = pltpu.make_async_copy(cot_ref, cots_out.at[0, same], local_sem.at[4])
    cot_local.start()
    cot_x = remote(cot_ref, cots_out.at[1, same], c_send, c_recv, 0, to_x)
    cot_y = remote(cot_ref, cots_out.at[2, same], c_send, c_recv, 1, to_y)
    cot_share = [
        remote(cot_ref if k == 0 else cots_out.at[k, same], cots_out.at[k, other_half], c_send, c_recv, 2 + k, sib)
        for k in range(4)
    ]
    cot_dx = remote(cots_out.at[2, top], cots_out.at[3, top], c_send, c_recv, 6, to_x)
    cot_dy = remote(cots_out.at[1, bottom], cots_out.at[3, bottom], c_send, c_recv, 7, to_y)

    stream.event()
    locals_[0].wait()
    stream.settle(query_w)

    @tiles(width // 512, 512)
    def project(cols, _):
        q_v[:, cols] = (dot(first_v[...], wq_v[:, cols]) + vec_v[2:3, cols]).astype(BF)

    wq_copy = pltpu.make_async_copy(wq_v, wq_out, local_sem.at[5])
    wq_copy.start()
    for t in range(length):
        @pl.when(z >= t)
        def arrived():
            kv_side(t).wait_recv()
            kv_side(t).wait_send()

        if t:
            @pl.when((z >= t - 1) & (z < length - 1))
            def gone():
                kv_up(t).wait_send()

    scale = head_dim ** (-0.5)

    def attend(s, g):
        lanes = pl.ds(pl.multiple_of(g * group * head_dim, group * head_dim), group * head_dim)
        wide = q_v[pl.ds(s * seg, seg), lanes]
        queries = jnp.concatenate(
            [wide[:, h * head_dim : (h + 1) * head_dim] for h in range(group)], axis=0
        )

        def step(t, state, diagonal):
            top_, total, accum = state
            keys = kv_v[s, t, :, :head_dim]
            values = kv_v[s, t, :, head_dim:]
            scores = dot(keys, queries, ((1,), (1,))) * scale
            if diagonal or with_length:
                key_pos = lax.broadcasted_iota(jnp.int32, (2 * seg, seg), 0)
                allowed = None
                if diagonal:
                    query_pos = lax.broadcasted_iota(jnp.int32, (2 * seg, seg), 1) + x * seg
                    allowed = key_pos <= query_pos
                if with_length:
                    inside = key_pos + (z - t) * (2 * seg) < lengths_ref[s]
                    allowed = inside if allowed is None else allowed & inside
                bias = jnp.where(allowed, 0.0, NEG_LARGE).astype(F32)
                scores = scores + jnp.concatenate([bias] * group, axis=1)
            new_top = jnp.maximum(top_, jnp.max(scores, axis=0, keepdims=True))
            terms = jnp.exp(scores - new_top)
            fade = jnp.exp(top_ - new_top)
            total = total * fade + jnp.sum(terms, axis=0, keepdims=True)
            accum = accum * fade + dot(values, terms.astype(BF), ((0,), (0,)))
            return new_top, total, accum

        span = group * seg
        state = (
            jnp.full((1, span), NEG_LARGE, F32),
            jnp.zeros((1, span), F32),
            jnp.zeros((head_dim, span), F32),
        )
        state = step(0, state, True)
        top_, total, accum = lax.fori_loop(1, z + 1, lambda t, st: step(t, st, False), state)
        out = accum / total
        mixed_v[pl.ds(s * seg, seg), lanes] = jnp.concatenate(
            [out[:, h * seg : (h + 1) * seg].T for h in range(group)], axis=1
        ).astype(BF)
        lse_ref[s, g] = top_ + jnp.log(total)

    for s in range(slots):
        @pl.loop(0, heads // group)
        def over_groups(g):
            attend(s, g)

        stream.event()
        stream.event()

    locals_[1].wait()
    while stream.next <= len(stream.order):
        stream.event()
    for copy in up_far:
        begin(copy)
    begin(cot_x)
    begin(cot_y)
    begin(cot_share[0])
    stream.settle(mixer_w)
    wm_copy = pltpu.make_async_copy(wm_v, wm_out, local_sem.at[6])
    wm_copy.start()

    @tiles(width // 512, 512)
    def mix(cols, _):
        residual_ref[:, cols] = (
            tokens_v[:, cols].astype(F32) + dot(mixed_v[...], wm_v[:, cols]) + vec_v[3:4, cols]
        )

    def second_norm(span):
        unit, _ = norm_rows(residual_ref[span, :])
        second_ref[span, :] = (unit * vec_v[4:5, :] + vec_v[5:6, :]).astype(BF)

    for_rows(rows, second_norm)

    for copy in up_far:
        copy.wait_recv()
    for target in range(length):
        @pl.when(target != z)
        def share():
            for k in range(2):
                up_share(k, z, target).start()

    cot_x.wait_recv()
    cot_y.wait_recv()
    begin(cot_share[1])
    begin(cot_share[2])
    begin(cot_dx)
    begin(cot_dy)
    cot_dx.wait_recv()
    cot_dy.wait_recv()
    begin(cot_share[3])
    for copy in cot_share + up_near:
        copy.wait_recv()
    for copy in up_local:
        copy.wait()
    for target in range(length):
        @pl.when(target != z)
        def shared():
            for k in range(2):
                up_share(k, z, target).wait_send()
                up_share(k, target, z).wait_recv()
    for copy in sent + stream.sent:
        copy.wait_send()
    for copy in (cot_local, wq_copy, wm_copy):
        copy.wait()


def front(lengths, tokens, smalls, kvw, qw, mw, up, cot, slots, length, with_length, aligned, hidden):
    rows, width = tokens.shape
    seg = rows // slots
    both = kvw.shape[1]
    groups = width // (both // 2) // 4
    hbm = pl.BlockSpec(memory_space=pltpu.HBM)
    vmem = pl.BlockSpec(memory_space=pltpu.VMEM)
    sems = pltpu.SemaphoreType.DMA
    return pl.pallas_call(
        functools.partial(
            front_kernel, length=length, slots=slots, with_length=with_length, aligned=aligned
        ),
        in_specs=[pl.BlockSpec(memory_space=pltpu.SMEM), vmem, hbm, hbm, hbm, hbm, hbm, hbm],
        out_specs=[vmem] * 8 + [hbm, hbm, vmem, hbm, hbm],
        out_shape=[
            jax.ShapeDtypeStruct((rows, width), BF),
            jax.ShapeDtypeStruct((rows, width), F32),
            jax.ShapeDtypeStruct((rows, width), BF),
            jax.ShapeDtypeStruct((rows, width), BF),
            jax.ShapeDtypeStruct((slots, length, 2 * seg, both), BF),
            jax.ShapeDtypeStruct((rows, width), BF),
            jax.ShapeDtypeStruct((slots, groups, 1, 4 * seg), F32),
            jax.ShapeDtypeStruct((16, width), F32),
            jax.ShapeDtypeStruct((width, width), BF),
            jax.ShapeDtypeStruct((width, width), BF),
            jax.ShapeDtypeStruct((width, both), BF),
            jax.ShapeDtypeStruct((width, hidden), BF),
            jax.ShapeDtypeStruct((4, 2 * rows, width), BF),
        ],
        scratch_shapes=[
            pltpu.VMEM((width, width), BF),
            pltpu.VMEM((width, width), BF),
            pltpu.VMEM((4, 16, width // 4), BF),
            sems((7,)),
            sems((34,)),
            sems((34,)),
            sems((6,)),
            sems((6,)),
            sems((2 * length,)),
            sems((2 * length,)),
            sems((4 * length,)),
            sems((4 * length,)),
            sems((2, length)),
            sems((2, length)),
            sems((8,)),
            sems((8,)),
        ],
        compiler_params=pltpu.CompilerParams(
            collective_id=2, has_side_effects=True, vmem_limit_bytes=60 << 20
        ),
        cost_estimate=pl.CostEstimate(
            flops=6 * rows * width * width, bytes_accessed=40 << 20, transcendentals=0
        ),
    )(lengths, tokens, smalls, kvw, qw, mw, up, cot)


def feed_kernel(
    second_ref,
    down_all_ref,
    up_ref,
    ubias_ref,
    residual_ref,
    vec_ref,
    down_ref,
    dres_ref,
    red_ref,
    down_part_ref,
    up_part_ref,
    ubias_part_ref,
    vsum_ref,
    tokens_v,
    cots_v,
    up_v,
    down_v,
    active_v,
    dupper_v,
    sib_out,
    sib_in,
    red_in,
    chip_out,
    chip_in,
    acc_v,
    stage_v,
    load_sem,
    stage_sem,
    gs_send,
    gs_recv,
    rs_send,
    rs_recv,
    *,
    length,
):
    rows, width = second_ref.shape
    hidden = up_ref.shape[1]
    half = rows // 2
    chunk = 2 * rows
    y, c, x = [lax.axis_index(name) for name in ("y", "c", "x")]
    sib, to_x, to_y = {"c": 1 - c}, {"x": 1 - x}, {"y": 1 - y}
    diag = {"x": 1 - x, "y": 1 - y}
    chips = (None, to_x, to_y, diag)

    loads = [
        pltpu.make_async_copy(second_ref, tokens_v.at[0, pl.ds(0, rows)], load_sem.at[0]),
        pltpu.make_async_copy(down_all_ref, cots_v, load_sem.at[1]),
        pltpu.make_async_copy(up_ref, up_v, load_sem.at[2]),
    ]
    block = hidden // length
    downs_in = [
        pltpu.make_async_copy(
            down_ref.at[pl.ds(pl.multiple_of((2 * b + x) * block, block), block)],
            down_v.at[pl.ds(b * block, block)],
            load_sem.at[4 + b],
        )
        for b in range(length)
    ]
    for load in loads + downs_in:
        load.start()
    greet((sib, to_x, to_y, diag))
    loads[0].wait()

    same, other = pl.ds(0, rows), pl.ds(rows, rows)
    top, bottom = pl.ds(0, half), pl.ds(half, half)

    def gather(index, chip, span_src, chip_dst, span_dst, device):
        return remote(
            tokens_v.at[chip, span_src], tokens_v.at[chip_dst, span_dst], gs_send, gs_recv, index, device
        )

    send_x = gather(0, 0, same, 1, same, to_x)
    send_y = gather(1, 0, same, 2, same, to_y)
    share = [gather(2 + k, k, same, k, other, sib) for k in range(4)]
    diag_x = gather(6, 2, top, 3, top, to_x)
    diag_y = gather(7, 1, bottom, 3, bottom, to_y)
    send_x.start()
    send_y.start()
    share[0].start()

    loads[1].wait()
    for load in downs_in:
        load.wait()

    @tiles(4 * chunk // 512, 512)
    def grad_active(span, index):
        @tiles(hidden // 512, 512)
        def columns(cols, _):
            dupper_v[span, cols] = dot(cots_v[span, :], down_v[cols, :], ((1,), (1,))).astype(BF)

    loads[2].wait()

    def chip_work(k):
        @tiles(hidden // 256, 256)
        def columns(cols, _):
            block = pl.ds(k * chunk, chunk)
            upper = dot(tokens_v[k], up_v[:, cols]) + ubias_ref[:, cols]
            active, slope = gelu_pair(upper)
            active_v[block, cols] = active.astype(BF)
            d_upper = (dupper_v[block, cols].astype(F32) * slope).astype(BF)
            dupper_v[block, cols] = d_upper
            part = jnp.sum(d_upper.astype(F32), axis=0, keepdims=True)
            if k == 0:
                ubias_part_ref[:, cols] = part
            else:
                ubias_part_ref[:, cols] += part

        @tiles(width // 512, 512)
        def to_sibling(cols, _):
            sib_out[k, :, cols] = dot(
                dupper_v[pl.ds(k * chunk + rows, rows), :], up_v[cols, :], ((1,), (1,))
            ).astype(BF)

        pair = remote(sib_out.at[k], sib_in.at[k], rs_send, rs_recv, k, sib)
        pair.start()

        @tiles(width // 512, 512)
        def keep(cols, _):
            dres_ref[:, cols] = dot(dupper_v[pl.ds(k * chunk, rows), :], up_v[cols, :], ((1,), (1,)))

        pair.wait_recv()

        def total(span):
            value = dres_ref[span, :] + sib_in[k, span, :].astype(F32)
            if k == 0:
                acc_v[span, :] = value
            else:
                chip_out[k - 1, span, :] = value.astype(BF)

        for_rows(rows, total)
        if k == 0:
            return [pair]
        far = remote(chip_out.at[k - 1], chip_in.at[k - 1], rs_send, rs_recv, 3 + k, chips[k])
        far.start()
        return [pair, far]

    share[0].wait_recv()
    sent = chip_work(0)
    send_x.wait_recv()
    share[1].start()
    diag_y.start()
    send_y.wait_recv()
    share[2].start()
    diag_x.start()
    share[1].wait_recv()
    sent += chip_work(1)
    share[2].wait_recv()
    sent += chip_work(2)
    diag_x.wait_recv()
    diag_y.wait_recv()
    share[3].start()
    share[3].wait_recv()
    sent += chip_work(3)

    def staged(slot, value, target):
        stage_v[slot] = value.astype(BF)
        copy = pltpu.make_async_copy(stage_v.at[slot], target, stage_sem.at[slot])
        copy.start()
        return copy

    pairs = []
    for k in range(4):
        sent[0 if k == 0 else 2 * k - 1].wait_send()

        @tiles(width // 512, 512)
        def to_sibling(cols, _):
            sib_out[k, :, cols] = dot(
                active_v[pl.ds(k * chunk + rows, rows), :], down_v[:, cols]
            ).astype(BF)

        pair = remote(sib_out.at[k], red_in.at[k], rs_send, rs_recv, 7 + k, sib)
        pair.start()
        pairs.append(pair)

    for k in range(4):

        @tiles(width // 512, 512)
        def keep(cols, _):
            dres_ref[:, cols] = dot(active_v[pl.ds(k * chunk, rows), :], down_v[:, cols])

        pairs[k].wait_recv()

        def total(span):
            red_in[k, span, :] = (dres_ref[span, :] + red_in[k, span, :].astype(F32)).astype(BF)

        for_rows(rows, total)
    red_copy = pltpu.make_async_copy(red_in, red_ref, load_sem.at[3])
    red_copy.start()

    @pl.loop(0, hidden // 512)
    def downs(r):
        block = pl.ds(pl.multiple_of(r * 512, 512), 512)
        copies = []
        for j in range(width // 512):
            cols = pl.ds(j * 512, 512)
            copies.append(
                staged(
                    j,
                    dot(active_v[:, block], cots_v[:, cols], ((0,), (0,))),
                    down_part_ref.at[block, cols],
                )
            )
        for copy in copies:
            copy.wait()

    quarter = width // 4
    piece = quarter // length

    @pl.loop(0, hidden // 512)
    def ups(r):
        first = pl.multiple_of(r * 512, 512)
        cols = pl.ds(first, 512)
        copies = []
        for f in range(4):
            value = None
            for k in range(4):
                term = dot(
                    tokens_v[k, :, f * quarter : (f + 1) * quarter],
                    dupper_v[k * chunk : (k + 1) * chunk, cols],
                    ((0,), (0,)),
                )
                value = term if value is None else value + term
            stage_v[f] = value.astype(BF)
            for level in range(length):
                copy = pltpu.make_async_copy(
                    stage_v.at[f, pl.ds(level * piece, piece)],
                    up_part_ref.at[
                        level, pl.ds((f % 2) * piece, piece), pl.ds((f // 2) * hidden + first, 512)
                    ],
                    stage_sem.at[4 + f * length + level],
                )
                copy.start()
                copies.append(copy)
        for copy in copies:
            copy.wait()

    for k in range(3):
        remote(chip_out.at[k], chip_in.at[k], rs_send, rs_recv, 4 + k, chips[k + 1]).wait_recv()
    vsum_ref[...] = jnp.zeros(vsum_ref.shape, F32)

    def norm_back(span):
        d_second = acc_v[span, :]
        for k in range(3):
            d_second = d_second + chip_in[k, span, :].astype(F32)
        unit, rstd = norm_rows(residual_ref[span, :])
        d_out = cots_v[span, :].astype(F32)
        d_residual = d_out + norm_backward(d_second, unit, rstd, vec_ref[4:5, :])
        dres_ref[span, :] = d_residual
        vsum_ref[0:1, :] += jnp.sum(d_second * unit, axis=0, keepdims=True)
        vsum_ref[1:2, :] += jnp.sum(d_second, axis=0, keepdims=True)
        vsum_ref[2:3, :] += jnp.sum(d_residual.astype(BF).astype(F32), axis=0, keepdims=True)
        vsum_ref[3:4, :] += jnp.sum(d_out, axis=0, keepdims=True)

    for_rows(rows, norm_back)
    red_copy.wait()
    for copy in [send_x, send_y, diag_x, diag_y] + share + pairs + sent[2::2]:
        copy.wait_send()


def feed(second, down_all, up_mine, ubias, residual, vectors, down_weight, length):
    rows, width = second.shape
    hidden = up_mine.shape[1]
    hbm = pl.BlockSpec(memory_space=pltpu.HBM)
    vmem = pl.BlockSpec(memory_space=pltpu.VMEM)
    sems = pltpu.SemaphoreType.DMA
    return pl.pallas_call(
        functools.partial(feed_kernel, length=length),
        in_specs=[hbm, hbm, hbm, vmem, vmem, vmem, hbm],
        out_specs=[vmem, hbm, hbm, hbm, vmem, vmem],
        out_shape=[
            jax.ShapeDtypeStruct((rows, width), F32),
            jax.ShapeDtypeStruct((4, rows, width), BF),
            jax.ShapeDtypeStruct((hidden, width), BF),
            jax.ShapeDtypeStruct((length, hidden // length, width), BF),
            jax.ShapeDtypeStruct((1, hidden), F32),
            jax.ShapeDtypeStruct((8, width), F32),
        ],
        scratch_shapes=[
            pltpu.VMEM((4, 2 * rows, width), BF),
            pltpu.VMEM((8 * rows, width), BF),
            pltpu.VMEM((width, hidden), BF),
            pltpu.VMEM((hidden, width), BF),
            pltpu.VMEM((8 * rows, hidden), BF),
            pltpu.VMEM((8 * rows, hidden), BF),
            pltpu.VMEM((4, rows, width), BF),
            pltpu.VMEM((4, rows, width), BF),
            pltpu.VMEM((4, rows, width), BF),
            pltpu.VMEM((3, rows, width), BF),
            pltpu.VMEM((3, rows, width), BF),
            pltpu.VMEM((rows, width), F32),
            pltpu.VMEM((4, 512, 512), BF),
            sems((4 + length,)),
            sems((4 + 4 * length,)),
            sems((8,)),
            sems((8,)),
            sems((11,)),
            sems((11,)),
        ],
        compiler_params=pltpu.CompilerParams(
            collective_id=4, has_side_effects=True, vmem_limit_bytes=62 << 20
        ),
        cost_estimate=pl.CostEstimate(
            flops=12 * 8 * rows * width * hidden, bytes_accessed=40 << 20, transcendentals=0
        ),
    )(second, down_all, up_mine, ubias, residual, vectors, down_weight)


class Links:
    def __init__(self, send_sems, recv_sems, count):
        self.send_sems, self.recv_sems, self.count = send_sems, recv_sems, count
        self.used = 0

    def copy(self, src, dst, device):
        index = self.used
        self.used += 1
        assert index < self.count
        return self.again(src, dst, device, index)

    def again(self, src, dst, device, index):
        return remote(src, dst, self.send_sems, self.recv_sems, index, device)


class LineSum:
    def __init__(self, links, z, length, parts, landing):
        self.z, self.length, self.parts, self.landing = z, length, parts, landing
        self.copies = {}
        self.links = links

    def position(self, way):
        return self.z if way == 0 else self.length - 1 - self.z

    def block(self, way, t):
        index = self.length - t + self.position(way)
        index = index if way == 0 else self.length - 1 - index
        return jnp.clip(index, 0, self.length - 1)

    def clear(self):
        last = self.length - 1
        for way in range(2):
            @pl.when(self.position(way) == 0)
            def zero():
                ref = self.landing(way, last)
                ref[...] = jnp.zeros(ref.shape, ref.dtype)

    def step(self, t):
        if t > 1:
            self.settle(t - 1)
        for way in range(2):
            pos = self.position(way)
            device = {"z": self.z + (1 if way == 0 else -1)}
            part = self.parts.at[self.block(way, t)]
            index = self.links.used
            direct = self.links.copy(part, self.landing(way, t), device)
            self.copies[way, t] = direct

            @pl.when(pos == 0)
            def first():
                direct.start()

            if t > 1:
                ref = self.landing(way, t - 1)
                passed = self.links.again(ref, self.landing(way, t), device, index)

                @pl.when((pos >= 1) & (pos <= t - 1))
                def onward():
                    self.copies[way, t - 1].wait_recv()
                    add_rows(ref, part)
                    passed.start()

    def finish(self, own, out):
        last = self.length - 1
        for way in range(2):
            @pl.when(self.position(way) >= 1)
            def arrive():
                self.copies[way, last].wait_recv()

        right, left = self.landing(0, last), self.landing(1, last)
        rows = out.shape[0]
        tile = min(rows, ROW_TILE)

        @pl.loop(0, rows // tile)
        def add(index):
            span = pl.ds(pl.multiple_of(index * tile, tile), tile)
            out[span, :] = (
                own[span, :].astype(F32) + right[span, :].astype(F32) + left[span, :].astype(F32)
            ).astype(out.dtype)

    def settle(self, t):
        for way in range(2):
            @pl.when((self.position(way) <= t - 1) & (self.position(way) < self.length - 1))
            def sent():
                self.copies[way, t].wait_send()

    def drain(self):
        self.settle(self.length - 1)


def add_rows(ref, term):
    rows = ref.shape[0]
    tile = min(rows, ROW_TILE)

    @pl.loop(0, rows // tile)
    def add(index):
        span = pl.ds(pl.multiple_of(index * tile, tile), tile)
        ref[span, :] = (ref[span, :].astype(F32) + term[span, :].astype(F32)).astype(ref.dtype)


class GradSum:
    def __init__(self, links, where, length, width, cols, left, right, bufs):
        self.y, self.c, self.z, self.x = where
        self.length, self.width, self.half = length, width, cols // 2
        self.left, self.right = left, right
        self.cols = cols
        (
            self.left_own,
            self.left_out,
            self.left_in,
            self.right_in,
            self.send1,
            self.recv1,
            self.send2,
            self.recv2,
            self.hold,
            self.zpart,
            self.zland,
        ) = bufs
        self.links = links
        self.sent = []

    def begin(self, copy):
        copy.start()
        self.sent.append(copy)
        return copy

    def all_cols(self, ref):
        return ref.at[..., pl.ds(0, self.cols)] if ref.shape[-1] != self.cols else ref

    def half_cols(self, ref):
        return ref.at[..., pl.ds(0, self.half)] if ref.shape[-1] != self.half else ref

    def share(self):
        quarter = self.width // 4
        block = quarter // (2 * self.length)
        for core, target in ((1 - self.c, self.left_out), (self.c, self.left_own)):
            for y_part in range(2):
                lanes = pl.ds(pl.multiple_of((y_part * 2 + core) * quarter, quarter), quarter)
                turned = self.left[:, lanes].astype(F32).T.astype(BF)
                for x_part in range(2):
                    for level in range(self.length):
                        start = (level * 2 + x_part) * block
                        target[y_part * 2 + x_part, level * block : (level + 1) * block, :] = turned[
                            start : start + block
                        ]
        sib = {"c": 1 - self.c}
        self.left_copy = self.begin(self.links.copy(self.left_out, self.left_in, sib))
        self.right_copy = self.begin(self.links.copy(self.right, self.all_cols(self.right_in), sib))

    def term(self, y_part, x_part, cols):
        g = y_part * 2 + x_part
        return dot(self.left_own[g], self.right[:, cols]) + dot(self.left_in[g], self.right_in[:, cols])

    def columns(self, side, fn):
        count = self.half // 128
        size = 128 * max(n for n in range(1, 5) if count % n == 0)
        for j in range(self.half // size):
            fn(pl.ds(side * self.half + j * size, size), pl.ds(j * size, size))

    def first(self):
        self.left_copy.wait_recv()
        self.right_copy.wait_recv()
        for n in range(2):

            def over_y(cols, local):
                self.send1[0, n, :, local] = self.term(1 - self.y, n, cols).astype(BF)

            def over_x(cols, local):
                self.send1[1, n, :, local] = self.term(n, 1 - self.x, cols).astype(BF)

            self.columns(0, over_y)
            self.columns(1, over_x)
        self.copies1 = [
            self.begin(
                self.links.copy(self.half_cols(self.send1.at[side]), self.half_cols(self.recv1.at[side]), device)
            )
            for side, device in ((0, {"y": 1 - self.y}), (1, {"x": 1 - self.x}))
        ]

    def second(self):
        for copy in self.copies1:
            copy.wait_recv()

        def a_out(cols, local):
            term = self.term(self.y, 1 - self.x, cols) + self.recv1[0, 1 - self.x, :, local].astype(F32)
            self.send2[0, :, local] = term.astype(BF)

        def b_out(cols, local):
            term = self.term(1 - self.y, self.x, cols) + self.recv1[1, 1 - self.y, :, local].astype(F32)
            self.send2[1, :, local] = term.astype(BF)

        def a_keep(cols, local):
            self.hold[:, cols] = self.term(self.y, self.x, cols) + self.recv1[0, self.x, :, local].astype(F32)

        def b_keep(cols, local):
            self.hold[:, cols] = self.term(self.y, self.x, cols) + self.recv1[1, self.y, :, local].astype(F32)

        self.columns(0, a_out)
        self.columns(1, b_out)
        self.copies2 = [
            self.begin(
                self.links.copy(self.half_cols(self.send2.at[side]), self.half_cols(self.recv2.at[side]), device)
            )
            for side, device in ((0, {"x": 1 - self.x}), (1, {"y": 1 - self.y}))
        ]
        self.columns(0, a_keep)
        self.columns(1, b_keep)

    def third(self, out):
        for copy in self.copies2:
            copy.wait_recv()
        block = self.hold.shape[0] // self.length
        for side in range(2):

            def add(cols, local):
                total = self.hold[:, cols] + self.recv2[side, :, local].astype(F32)
                self.hold[:, cols] = total
                for level in range(self.length):
                    self.zpart[level, :, cols] = total[level * block : (level + 1) * block].astype(BF)

            self.columns(side, add)
        rows = pl.ds(pl.multiple_of(self.z * block, block), block)
        out[...] = self.all_cols(self.hold)[rows, :]
        self.line = LineSum(
            self.links,
            self.z,
            self.length,
            self.all_cols(self.zpart),
            lambda way, t: self.all_cols(self.zland.at[way, t - 1]),
        )

    def finish(self, out):
        self.line.finish(out, out)

    def drain(self):
        for copy in self.sent:
            copy.wait_send()
        self.line.drain()


def back_kernel(
    lengths_ref,
    tokens_v,
    dres_ref,
    first_ref,
    q_ref,
    kv_ref,
    mixed_ref,
    lse_ref,
    vec_ref,
    wkv_ref,
    vsum_ref,
    ubias_ref,
    wq_ref,
    wm_ref,
    red_ref,
    down_part,
    up_part,
    tgrad_ref,
    query_ref,
    mixer_ref,
    up_ref,
    down_ref,
    vectors_ref,
    far_ref,
    w_v,
    dmix_v,
    dmixed_v,
    right_v,
    dfirst_v,
    dkv_v,
    keep_v,
    xsend_v,
    xrecv_v,
    csend_v,
    crecv_v,
    line_v,
    land_v,
    last_v,
    upsend_v,
    uprecv_v,
    vsend_v,
    vrecv_v,
    left_own,
    left_out,
    left_in,
    right_in,
    send1,
    recv1,
    send2,
    recv2,
    hold,
    zpart,
    zland,
    load_sem,
    credit,
    send_sems,
    recv_sems,
    *,
    length,
    slots,
    with_length,
    count,
):
    rows, width = tokens_v.shape
    seg = rows // slots
    both = wkv_ref.shape[1]
    head_dim = both // 2
    heads = width // head_dim
    group = 4
    y, c, z, x = [lax.axis_index(name) for name in ("y", "c", "z", "x")]
    place = y * 2 + c
    sib, to_x, to_y, diag = {"c": 1 - c}, {"x": 1 - x}, {"y": 1 - y}, {"x": 1 - x, "y": 1 - y}
    links = Links(send_sems, recv_sems, count)
    scale = head_dim ** (-0.5)

    def load(src, dst, n):
        copy = pltpu.make_async_copy(src, dst, load_sem.at[n])
        copy.start()
        return copy

    load_down = load(down_part, line_v, 0)
    load_wm = load(wm_ref, w_v, 1)

    down_line = LineSum(links, z, length, line_v, lambda way, t: land_v.at[way, t - 1] if t < length - 1 else last_v.at[0, way])
    up_line = LineSum(links, z, length, line_v, lambda way, t: land_v.at[way, t - 1] if t < length - 1 else last_v.at[1, way])
    bufs = (left_own, left_out, left_in, right_in, send1, recv1, send2, recv2, hold, zpart, zland)
    where = (y, c, z, x)
    mixer = GradSum(links, where, length, width, width, mixed_ref, dmix_v, bufs)
    query = GradSum(links, where, length, width, width + both, first_ref, right_v, bufs)
    down_line.clear()
    up_line.clear()
    for way, edge in ((0, 0), (1, length - 1)):
        @pl.when(z == edge)
        def clear_edge():
            zland[way, length - 2] = jnp.zeros(zland.shape[2:], BF)

    @pl.when(z == length - 1)
    def clear_hops():
        crecv_v[...] = jnp.zeros(crecv_v.shape, BF)

    barrier = pltpu.get_barrier_semaphore()
    plane = []
    for flip in range(1, 8):
        device = {"y": y ^ (flip // 4), "c": c ^ (flip // 2 % 2), "x": x ^ (flip % 2)}
        plane.append(device)
    for device in plane:
        pl.semaphore_signal(barrier, inc=1, device_id=device, device_id_type=MESH)
    for other in range(length):
        @pl.when(other != z)
        def hello():
            pl.semaphore_signal(barrier, inc=1, device_id={"z": other}, device_id_type=MESH)
    pl.semaphore_wait(barrier, 7 + length - 1)

    sent = []

    def begin(copy):
        copy.start()
        sent.append(copy)
        return copy

    def hand_over(base):
        for way, step in ((0, 1), (1, -1)):
            @pl.when((z + step >= 0) & (z + step < length))
            def free():
                pl.semaphore_signal(
                    credit.at[base + way], inc=1, device_id={"z": z + step}, device_id_type=MESH
                )

        for way, step in ((0, 1), (1, -1)):
            @pl.when((z - step >= 0) & (z - step < length))
            def freed():
                pl.semaphore_wait(credit.at[base + way], 1)

    load_down.wait()
    down_line.step(1)

    def to_bf(span):
        dmix_v[span, :] = dres_ref[span, :].astype(BF)

    for_rows(rows, to_bf)
    mixer.share()
    load_wm.wait()

    @tiles(width // 512, 512)
    def mix_back(cols, _):
        dmixed_v[:, cols] = dot(dmix_v[...], w_v[cols, :], ((1,), (1,))).astype(BF)

    load_wq = load(wq_ref, w_v, 1)
    far = [
        begin(links.copy(red_ref.at[k + 1], far_ref.at[k], device))
        for k, device in enumerate((to_x, to_y, diag))
    ]

    def attend(s, g):
        lanes = pl.ds(pl.multiple_of(g * group * head_dim, group * head_dim), group * head_dim)
        span = pl.ds(s * seg, seg)

        def stack(wide):
            return jnp.concatenate(
                [wide[:, h * head_dim : (h + 1) * head_dim] for h in range(group)], axis=0
            )

        queries = stack(q_ref[span, lanes])
        d_mixed = stack(dmixed_v[span, lanes])
        inner = mixed_ref[span, lanes].astype(F32) * dmixed_v[span, lanes].astype(F32)
        delta = jnp.concatenate(
            [
                jnp.sum(inner[:, h * head_dim : (h + 1) * head_dim].T, axis=0, keepdims=True)
                for h in range(group)
            ],
            axis=1,
        )
        lse = lse_ref[s, g]

        def step(t, accum, diagonal):
            keys = kv_ref[s, t, :, :head_dim]
            values = kv_ref[s, t, :, head_dim:]
            scores = dot(keys, queries, ((1,), (1,))) * scale
            if diagonal or with_length:
                key_pos = lax.broadcasted_iota(jnp.int32, (2 * seg, seg), 0)
                allowed = None
                if diagonal:
                    query_pos = lax.broadcasted_iota(jnp.int32, (2 * seg, seg), 1) + x * seg
                    allowed = key_pos <= query_pos
                if with_length:
                    inside = key_pos + (z - t) * (2 * seg) < lengths_ref[s]
                    allowed = inside if allowed is None else allowed & inside
                bias = jnp.where(allowed, 0.0, NEG_LARGE).astype(F32)
                scores = scores + jnp.concatenate([bias] * group, axis=1)
            probs = jnp.exp(scores - lse)
            d_probs = dot(values, d_mixed, ((1,), (1,)))
            d_scores = (probs * (d_probs - delta)).astype(BF)
            dkv_v[t, :, :head_dim] += dot(d_scores, queries) * scale
            dkv_v[t, :, head_dim:] += dot(probs.astype(BF), d_mixed)
            return accum + dot(keys, d_scores, ((0,), (0,)))

        accum = step(0, jnp.zeros((head_dim, group * seg), F32), True)
        accum = lax.fori_loop(1, z + 1, lambda t, a: step(t, a, False), accum)
        right_v[span, lanes] = (
            jnp.concatenate([accum[:, h * seg : (h + 1) * seg].T for h in range(group)], axis=1) * scale
        ).astype(BF)

    x_copies = []
    for s in range(slots):
        for t in range(length):
            dkv_v[t] = jnp.zeros(dkv_v.shape[1:], F32)

        @pl.loop(0, heads // group)
        def over_groups(g):
            attend(s, g)

        for t in range(length):
            keep_v[s, t] = dkv_v[t, pl.ds(pl.multiple_of(x * seg, seg), seg), :].astype(BF)
            xsend_v[s, t] = dkv_v[t, pl.ds(pl.multiple_of((1 - x) * seg, seg), seg), :].astype(BF)
        x_copies.append(begin(links.copy(xsend_v.at[s], xrecv_v.at[s], to_x)))

    down_line.step(2)
    mixer.first()

    for copy in x_copies:
        copy.wait_recv()
    hops = [links.copy(csend_v.at[t - 1], crecv_v.at[t - 1], {"z": z - 1}) for t in range(1, length)]
    for t in range(length - 1, -1, -1):
        @pl.when(t <= z)
        def hop():
            if t + 1 < length:
                @pl.when(z < length - 1)
                def arrive():
                    hops[t].wait_recv()

            total = keep_v[:, t].astype(F32) + xrecv_v[:, t].astype(F32)
            if t + 1 < length:
                total = total + crecv_v[t].astype(F32)
            if t:
                csend_v[t - 1] = total.astype(BF)
                hops[t - 1].start()
            else:
                for s in range(slots):
                    right_v[s * seg : (s + 1) * seg, width:] = total[s].astype(BF)

    mixer.second()

    load_wq.wait()

    @tiles(width // 512, 512)
    def first_back(cols, _):
        dfirst_v[:, cols] = dot(right_v[:, :width], w_v[cols, :], ((1,), (1,))) + dot(
            right_v[:, width:], wkv_ref[cols, :], ((1,), (1,))
        )

    mixer.third(mixer_ref)
    mixer_line = mixer.line
    mixer_line.step(1)
    down_line.step(3) if length > 3 else None
    neighbours = ((0, sib), (1, to_y), (2, to_x))
    for n, device in neighbours:
        pl.semaphore_signal(credit.at[n], inc=1, device_id=device, device_id_type=MESH)
    for n, _ in neighbours:
        pl.semaphore_wait(credit.at[n], 1)
    for copy in mixer.sent:
        copy.wait_send()
    query.share()

    vsend_v[0] = jnp.zeros(vsend_v.shape[1:], F32)

    def first_norm_back(span):
        unit, rstd = norm_rows(tokens_v[span, :].astype(F32))
        d_first = dfirst_v[span, :]
        tgrad_ref[span, :] = (
            dres_ref[span, :] + norm_backward(d_first, unit, rstd, vec_ref[0:1, :])
        ).astype(BF)
        vsend_v[0, 0:1, :] += jnp.sum(d_first * unit, axis=0, keepdims=True)
        vsend_v[0, 1:2, :] += jnp.sum(d_first, axis=0, keepdims=True)
        d_right = right_v[span, :].astype(F32)
        vsend_v[0, 2:3, :] += jnp.sum(d_right[:, :width], axis=0, keepdims=True)
        vsend_v[0, 3:4, 0:both] += jnp.sum(d_right[:, width:], axis=0, keepdims=True)

    query.first()
    for_rows(rows, first_norm_back)
    vsend_v[0, 4:8, :] = vsum_ref[0:4, :]
    vsend_v[0, 8:9, 0 : ubias_ref.shape[1]] = ubias_ref[...]

    partners = [(sib, 8), (to_x, 8), (to_y, 8)]
    bit = 1
    while bit < length:
        partners.append(({"z": z ^ bit}, 16))
        bit *= 2

    def exchange(n):
        device, high = partners[n]
        copy = begin(links.copy(vsend_v.at[n, pl.ds(0, high)], vrecv_v.at[n, pl.ds(0, high)], device))

        def land():
            copy.wait_recv()
            out = vectors_ref if n + 1 == len(partners) else vsend_v.at[n + 1]
            out[0:high, :] = vsend_v[n, 0:high, :] + vrecv_v[n, 0:high, :]
            if high == 8:
                out[8:16, :] = vsend_v[n, 8:16, :]

        return land

    land = exchange(0)
    mixer_line.step(2)
    query.second()
    land()
    land = exchange(1)
    down_line.finish(line_v.at[z], down_ref)
    down_line.drain()
    load_up = load(up_part, line_v, 0)
    hand_over(5)
    load_up.wait()
    up_line.step(1)
    land()
    land = exchange(2)
    for t in range(3, length):
        mixer_line.step(t)
    mixer.finish(mixer_ref)
    mixer_line.drain()
    hand_over(3)

    query.third(query_ref)
    up_line.step(2)
    land()
    land = exchange(3)
    query.line.step(1)
    query.line.step(2)
    land()
    for n in range(4, len(partners)):
        land = exchange(n)
        land()
    for t in range(3, length):
        query.line.step(t)
    for t in range(3, length):
        up_line.step(t)
    query.finish(query_ref)

    upsum_v = dmixed_v
    up_line.finish(line_v.at[z], upsum_v)
    hidden = upsum_v.shape[1] // 2
    piece = upsum_v.shape[0] // 2
    block = piece // 2
    for f in range(4):
        for x_part in range(2):
            start = (f % 2) * piece + x_part * block
            lanes = slice((f // 2) * hidden, (f // 2 + 1) * hidden)
            upsend_v[f * 2 + x_part] = upsum_v[start : start + block, lanes]
    mine = place * 2 + x
    up_copies = []
    for flip, device in zip(range(1, 8), plane):
        target = mine ^ flip
        copy = links.copy(upsend_v.at[target], uprecv_v.at[flip], device)
        begin(copy)
        up_copies.append(copy)
    out_block = hidden // length

    def place_up(flip, ref):
        source = mine ^ flip
        base = (source // 2) * (2 * hidden) + (source % 2) * out_block
        for level in range(length):
            lanes = pl.ds(pl.multiple_of(base + level * 2 * out_block, out_block), out_block)
            up_ref[:, lanes] = ref[:, level * out_block : (level + 1) * out_block].astype(up_ref.dtype)

    place_up(0, upsend_v.at[mine])
    for flip, copy in zip(range(1, 8), up_copies):
        copy.wait_recv()
        place_up(flip, uprecv_v.at[flip])
    for copy in far:
        copy.wait_recv()
    for copy in sent:
        copy.wait_send()
    query.drain()
    up_line.drain()
    for t in range(1, length):
        @pl.when(t <= z)
        def hopped():
            hops[t - 1].wait_send()


def back(lengths, vmem_args, hbm_args, slots, length, with_length):
    tokens, kv, wkv = vmem_args[0], vmem_args[4], vmem_args[8]
    rows, width = tokens.shape
    seg = rows // slots
    both = wkv.shape[1]
    cols = width + both
    hidden = width // 2
    block = width // (8 * length)
    stages = 3 + (length - 1).bit_length()
    count = 96 + 12 * length
    hbm = pl.BlockSpec(memory_space=pltpu.HBM)
    vmem = pl.BlockSpec(memory_space=pltpu.VMEM)
    sems = pltpu.SemaphoreType.DMA

    def half(*dims):
        return pltpu.VMEM(dims, BF)

    return pl.pallas_call(
        functools.partial(
            back_kernel, length=length, slots=slots, with_length=with_length, count=count
        ),
        in_specs=[pl.BlockSpec(memory_space=pltpu.SMEM)]
        + [vmem] * len(vmem_args)
        + [hbm] * len(hbm_args),
        out_specs=[vmem] * 6 + [hbm],
        out_shape=[
            jax.ShapeDtypeStruct((rows, width), BF),
            jax.ShapeDtypeStruct((block, cols), F32),
            jax.ShapeDtypeStruct((block, width), F32),
            jax.ShapeDtypeStruct((block, 8 * hidden), BF),
            jax.ShapeDtypeStruct((8 * hidden // (8 * length), width), F32),
            jax.ShapeDtypeStruct((16, width), F32),
            jax.ShapeDtypeStruct((3, rows, width), BF),
        ],
        scratch_shapes=[
            half(width, width),
            half(rows, width),
            half(rows, width),
            half(rows, cols),
            pltpu.VMEM((rows, width), F32),
            pltpu.VMEM((length, 2 * seg, both), F32),
            half(slots, length, seg, both),
            half(slots, length, seg, both),
            half(slots, length, seg, both),
            half(length - 1, slots, seg, both),
            half(length - 1, slots, seg, both),
            half(length, hidden // length, width),
            half(2, length - 2, hidden // length, width),
            half(2, 2, hidden // length, width),
            half(8, block, hidden),
            half(8, block, hidden),
            pltpu.VMEM((stages, 16, width), F32),
            pltpu.VMEM((stages, 16, width), F32),
            half(4, width // 8, rows),
            half(4, width // 8, rows),
            half(4, width // 8, rows),
            half(rows, cols),
            half(2, 2, width // 8, cols // 2),
            half(2, 2, width // 8, cols // 2),
            half(2, width // 8, cols // 2),
            half(2, width // 8, cols // 2),
            pltpu.VMEM((width // 8, cols), F32),
            half(length, block, cols),
            half(2, length - 1, block, cols),
            sems((2,)),
            pltpu.SemaphoreType.REGULAR((7,)),
            sems((count,)),
            sems((count,)),
        ],
        compiler_params=pltpu.CompilerParams(
            collective_id=3, has_side_effects=True, vmem_limit_bytes=62 << 20
        ),
        cost_estimate=pl.CostEstimate(
            flops=12 * rows * width * width, bytes_accessed=40 << 20, transcendentals=0
        ),
    )(lengths, *vmem_args, *hbm_args)


def finish_fast(given, kept, weights):
    tokens, lengths, down_weight, up_bias, where, slots, length, with_length = given
    second, residual, first, queries, kv_all, mixed, lse, vectors = kept
    full_query, full_mixer, full_keyval, up_mine, down_all = weights
    y, c, z, x = where
    rows, width = second.shape
    flat = tokens.reshape(rows, width)
    d_residual, reduced, down_part, up_part, ubias_part, vsum = feed(
        second, down_all, up_mine, up_bias, residual, vectors, down_weight, length
    )
    tokens_grad, query_all, mixer_grad, up_grad, down_grad, sums, far = back(
        lengths,
        (flat, d_residual, first, queries, kv_all, mixed, lse, vectors, full_keyval, vsum, ubias_part),
        (full_query, full_mixer, reduced, down_part.reshape(length, -1, width), up_part),
        slots,
        length,
        with_length,
    )
    output = residual + vectors[6:7]
    for term in (reduced[0], far[0], far[1], far[2]):
        output = output + term.astype(F32)
    layer_out = output.astype(BF).reshape(tokens.shape)
    devices = 8 * length
    index = (y * 2 + c) * 2 * length + z * 2 + x
    block = width // devices
    mine = lax.dynamic_slice_in_dim(sums[:8], index * block, block, 1)
    head_dim = full_keyval.shape[1] // 2
    v_block = head_dim // devices
    vbias = lax.dynamic_slice_in_dim(sums[3], head_dim + index * v_block, v_block, 0)
    u_block = up_bias.shape[1] // length
    ubias = lax.dynamic_slice_in_dim(sums[8], z * u_block, u_block, 0)
    return (
        layer_out,
        tokens_grad.reshape(tokens.shape),
        mine[0],
        mine[1],
        query_all[:, :width],
        mine[2],
        query_all[:, width:],
        vbias,
        mixer_grad,
        mine[6],
        mine[4],
        mine[5],
        up_grad.astype(F32),
        ubias,
        down_grad,
        mine[7],
    )


def body(
    tokens,
    lengths,
    cotangent,
    norm_gain,
    norm_shift,
    query_weight,
    query_bias,
    keyval_weight,
    value_bias,
    mixer_weight,
    mixer_bias,
    ffnorm_gain,
    ffnorm_shift,
    up_weight,
    up_bias,
    down_weight,
    down_bias,
):
    y, c, z, x = [lax.axis_index(name) for name in ("y", "c", "z", "x")]
    length = lax.axis_size("z")
    place = y * 2 + c
    slots, seg, width = tokens.shape
    rows = slots * seg
    head_dim = value_bias.shape[0] * 4
    hidden = up_weight.shape[1]
    hidden_block = hidden // (8 * length)
    hidden_mine = hidden // 8
    with_length = 2 * length * seg > MIN_LEN
    scal = jnp.concatenate([jnp.stack([z, x]).astype(jnp.int32), lengths])

    quarter = width // 4
    v_part = value_bias.shape[0]
    v_place = lax.dynamic_update_slice(jnp.zeros((quarter,), BF), value_bias, (place * v_part,))
    small = jnp.stack(
        [norm_gain, norm_shift, query_bias, mixer_bias, ffnorm_gain, ffnorm_shift, down_bias, v_place]
    )
    small = jnp.concatenate([small, jnp.zeros_like(small)], axis=0)

    down_mine = pick(down_weight.reshape(length, 2, hidden_block, width), x, 1).reshape(
        hidden_mine, width
    )
    up_bias_mine = pick(up_bias.reshape(length, 2, hidden_block), x, 1).reshape(1, hidden_mine)
    aligned = hidden_block % 128 == 0
    up_given = up_weight
    if not aligned:
        up_given = pick(up_weight.reshape(quarter, 4, length, 2, hidden_block), x, 3)
        up_given = up_given.reshape(quarter, 4, hidden_mine).transpose(1, 0, 2)

    token_pos = (z * 2 + x) * seg + jnp.arange(seg, dtype=jnp.int32)
    valid = (token_pos[None, :] < lengths[:, None]).astype(F32).reshape(rows, 1)
    d_down = cotangent.reshape(rows, width)
    if with_length:
        d_down = (d_down.astype(F32) * valid).astype(BF)
    d_out = d_down.astype(F32)

    flat = tokens.reshape(rows, width)
    (
        second,
        residual,
        first,
        queries,
        kv_all,
        mixed,
        lse,
        vectors,
        full_query,
        full_mixer,
        full_keyval,
        up_mine,
        down_all,
    ) = front(
        lengths,
        flat,
        small,
        keyval_weight,
        query_weight,
        mixer_weight,
        up_given,
        d_down,
        slots,
        length,
        with_length,
        aligned,
        hidden_mine,
    )
    if aligned and length == 4:
        return finish_fast(
            (tokens, lengths, down_weight, up_bias_mine.astype(F32), (y, c, z, x), slots, length, with_length),
            (second, residual, first, queries, kv_all, mixed, lse, vectors),
            (full_query, full_mixer, full_keyval, up_mine, down_all.reshape(8 * rows, width)),
        )
    inputs = flat.astype(F32)
    gain, ffgain, d_bias = vectors[0:1], vectors[4:5], vectors[6:7]
    unit1, rstd1 = norm_stats(inputs)
    unit2, rstd2 = norm_stats(residual)
    q_t, mixed_t = queries.T, mixed.T

    d_second, out_parts, down_part, up_part, ubias_part = ffn(
        second,
        down_all.reshape(8 * rows, width),
        up_mine,
        up_bias_mine.astype(F32),
        down_mine,
        length,
    )
    output = residual + scatter_plane([out_parts[i] for i in range(4)]) + d_bias
    layer_out = output.astype(BF).reshape(tokens.shape)
    down_grad = scatter_line(down_part.reshape(length, hidden_block, width), z, length)
    ubias_grad = scatter_line(ubias_part.reshape(length, hidden_block), z, length)
    out_rows = width // (8 * length)
    up_sum = scatter_line(up_part, z, length).astype(BF)
    up_rows = lax.all_to_all(
        up_sum.reshape(8, out_rows, hidden_mine), ("y", "c", "x"), 0, 0, tiled=True
    )
    up_grad = (
        up_rows.reshape(4, 2, out_rows, length, hidden_block)
        .transpose(2, 0, 3, 1, 4)
        .reshape(out_rows, hidden)
        .astype(F32)
    )

    d_residual = d_out + norm_backward(d_second, unit2, rstd2, ffgain)
    d_mix = d_residual.astype(BF)
    d_mixed_t = dot(full_mixer, d_mix, ((1,), (1,))).astype(BF)
    where = (y, c, z, x)
    sizes = (length, width)
    mixer_all = scatter_all(
        mixed,
        d_mix,
        (
            jnp.sum(d_mix.astype(F32), axis=0),
            jnp.sum(d_second * unit2, axis=0),
            jnp.sum(d_second, axis=0),
            jnp.sum(d_out, axis=0),
        ),
        where,
        sizes,
    )

    dq_t, dkv = attn_backward(scal, q_t, kv_all, mixed_t, d_mixed_t, lse, 4, with_length)
    dkv = dkv.reshape(slots, length, 2, seg, 2 * head_dim)
    running = None
    for step in range(length - 1, -1, -1):
        term = dkv[:, step]
        term = pick(term, x, 1) + swap(pick(term, 1 - x, 1).astype(BF), "x").astype(F32)
        if running is not None:
            term = term + lax.ppermute(
                running.astype(BF), "z", [(i, i - 1) for i in range(1, length)]
            ).astype(F32)
        running = term
    d_keyvals = running.reshape(rows, 2 * head_dim).astype(BF)
    d_first = dot(dq_t, full_query, ((0,), (1,))) + dot(d_keyvals, full_keyval, ((1,), (1,)))
    tokens_grad = (d_residual + norm_backward(d_first, unit1, rstd1, gain)).astype(BF)
    d_queries = dq_t.T
    devices = 8 * length
    vbias = jnp.sum(d_keyvals[:, head_dim:].astype(F32), axis=0)
    vbias = jnp.pad(
        vbias.reshape(devices, head_dim // devices),
        ((0, 0), (0, out_rows - head_dim // devices)),
    ).reshape(width)
    query_all = scatter_all(
        first,
        jnp.concatenate([d_queries, d_keyvals], axis=1),
        (
            jnp.sum(d_first * unit1, axis=0),
            jnp.sum(d_first, axis=0),
            jnp.sum(d_queries.astype(F32), axis=0),
            vbias,
        ),
        where,
        sizes,
    )
    kv_end = width + 2 * head_dim
    return (
        layer_out,
        tokens_grad.reshape(tokens.shape),
        query_all[:, kv_end],
        query_all[:, kv_end + 1],
        query_all[:, :width],
        query_all[:, kv_end + 2],
        query_all[:, width:kv_end],
        query_all[: head_dim // devices, kv_end + 3],
        mixer_all[:, :width],
        mixer_all[:, width],
        mixer_all[:, width + 1],
        mixer_all[:, width + 2],
        up_grad,
        ubias_grad,
        down_grad,
        mixer_all[:, width + 3],
    )


def solution(mesh):
    ctx = mesh.shape["ctx"]
    fine = Mesh(mesh.devices.reshape(2, 2, ctx // 2, 2), ("y", "c", "z", "x"))
    fsdp, both, every = ("y", "c"), ("z", "x"), ("y", "c", "z", "x")
    return jax.shard_map(
        body,
        mesh=fine,
        in_specs=(
            P(fsdp, both, None),
            P(fsdp),
            P(fsdp, both, None),
            P(fsdp),
            P(fsdp),
            P(fsdp, None),
            P(fsdp),
            P(fsdp, None),
            P(fsdp),
            P(fsdp, None),
            P(fsdp),
            P(fsdp),
            P(fsdp),
            P(fsdp, None),
            P(fsdp),
            P(fsdp, None),
            P(fsdp),
        ),
        out_specs=(
            P(fsdp, both, None),
            P(fsdp, both, None),
            P(every),
            P(every),
            P(every, None),
            P(every),
            P(every, None),
            P(every),
            P(every, None),
            P(every),
            P(every),
            P(every),
            P(every, None),
            P(every),
            P(every, None),
            P(every),
        ),
        check_vma=False,
    )
```

```python
import functools

import jax
import jax.numpy as jnp
from jax import lax
from jax.experimental import pallas as pl
from jax.experimental.pallas import tpu as pltpu
from jax.sharding import Mesh, PartitionSpec as P

EPSILON = 1e-05
NEG_LARGE = -1e30
MIN_LEN = 1024
BF = jnp.bfloat16
F32 = jnp.float32
GELU_K = 0.7978845608028654
GELU_C = 0.044715


def dot(left_side, right_side, dims=((1,), (0,))):
    return lax.dot_general(left_side, right_side, (dims, ((), ())), preferred_element_type=F32)


def swap(values, axis):
    return lax.ppermute(values, axis, [(0, 1), (1, 0)])


def pick(values, index, axis):
    return lax.dynamic_index_in_dim(values, index, axis, keepdims=False)


def stack_heads(block, head_dim):
    heads = block.shape[0] // head_dim
    return jnp.concatenate([block[h * head_dim : (h + 1) * head_dim] for h in range(heads)], axis=1)


def unstack_heads(stacked, seg):
    heads = stacked.shape[1] // seg
    return jnp.concatenate([stacked[:, h * seg : (h + 1) * seg] for h in range(heads)], axis=0)


def masked_scores(scal_ref, queries, keys, step, seg, heads, with_length, first_block):
    scores = dot(keys, queries) * (keys.shape[1] ** (-0.5))
    pair = keys.shape[0]
    if not (with_length or first_block):
        return scores
    key_pos = lax.broadcasted_iota(jnp.int32, (pair, seg), 0)
    allowed = None
    if first_block:
        query_pos = lax.broadcasted_iota(jnp.int32, (pair, seg), 1) + scal_ref[1] * seg
        allowed = key_pos <= query_pos
    if with_length:
        length = scal_ref[2 + pl.program_id(0)]
        inside = key_pos + (scal_ref[0] - step) * pair < length
        allowed = inside if allowed is None else allowed & inside
    bias = jnp.where(allowed, 0.0, NEG_LARGE).astype(F32)
    return scores + jnp.concatenate([bias] * heads, axis=1)


def attn_fwd_kernel(scal_ref, q_ref, kv_ref, out_ref, lse_ref, *, with_length):
    head_dim = kv_ref.shape[-1] // 2
    seg = q_ref.shape[1]
    heads = q_ref.shape[0] // head_dim
    queries = stack_heads(q_ref[...], head_dim)

    def block(step, state, first_block):
        top, total, accum = state
        keys = kv_ref[0, step, :, :head_dim]
        values = kv_ref[0, step, :, head_dim:]
        scores = masked_scores(scal_ref, queries, keys, step, seg, heads, with_length, first_block)
        new_top = jnp.maximum(top, jnp.max(scores, axis=0, keepdims=True))
        terms = jnp.exp(scores - new_top)
        fade = jnp.exp(top - new_top)
        total = total * fade + jnp.sum(terms, axis=0, keepdims=True)
        accum = accum * fade + dot(values, terms.astype(BF), ((0,), (0,)))
        return new_top, total, accum

    lanes = heads * seg
    state = (
        jnp.full((1, lanes), NEG_LARGE, F32),
        jnp.zeros((1, lanes), F32),
        jnp.zeros((head_dim, lanes), F32),
    )
    state = block(0, state, True)
    top, total, accum = lax.fori_loop(1, scal_ref[0] + 1, lambda t, s: block(t, s, False), state)
    out_ref[...] = unstack_heads(accum / total, seg).astype(BF)
    lse_ref[0, 0] = top + jnp.log(total)


def attn_bwd_kernel(scal_ref, q_ref, kv_ref, out_ref, dout_ref, lse_ref, dq_ref, dkv_ref, *, with_length):
    head_dim = kv_ref.shape[-1] // 2
    seg = q_ref.shape[1]
    heads = q_ref.shape[0] // head_dim
    scale = head_dim ** (-0.5)
    queries = stack_heads(q_ref[...], head_dim)
    d_mixed = stack_heads(dout_ref[...], head_dim)
    mixed = stack_heads(out_ref[...], head_dim)
    delta = jnp.sum(mixed.astype(F32) * d_mixed.astype(F32), axis=0, keepdims=True)
    lse = lse_ref[0, 0]

    @pl.when(pl.program_id(1) == 0)
    def clear():
        dkv_ref[...] = jnp.zeros_like(dkv_ref)

    def block(step, accum, first_block):
        keys = kv_ref[0, step, :, :head_dim]
        values = kv_ref[0, step, :, head_dim:]
        scores = masked_scores(scal_ref, queries, keys, step, seg, heads, with_length, first_block)
        probs = jnp.exp(scores - lse)
        d_probs = dot(values, d_mixed)
        d_scores = (probs * (d_probs - delta)).astype(BF)
        dkv_ref[0, step, :, :head_dim] += dot(d_scores, queries, ((1,), (1,))) * scale
        dkv_ref[0, step, :, head_dim:] += dot(probs.astype(BF), d_mixed, ((1,), (1,)))
        return accum + dot(keys, d_scores, ((0,), (0,)))

    accum = block(0, jnp.zeros((head_dim, heads * seg), F32), True)
    accum = lax.fori_loop(1, scal_ref[0] + 1, lambda t, s: block(t, s, False), accum)
    dq_ref[...] = (unstack_heads(accum, seg) * scale).astype(BF)


def attn_specs(slots, steps, pair, seg, rows, groups, head_dim):
    lanes = rows // groups // head_dim * seg
    scal = pl.BlockSpec(memory_space=pltpu.SMEM)
    feat = pl.BlockSpec((rows // groups, seg), lambda s, g: (g, s))
    kv = pl.BlockSpec((1, steps, pair, 2 * head_dim), lambda s, g: (s, 0, 0, 0))
    lse = pl.BlockSpec((1, 1, 1, lanes), lambda s, g: (s, g, 0, 0))
    return scal, feat, kv, lse, lanes


def attn_forward(scal, q_t, kv, groups, with_length):
    slots, steps, pair, width = kv.shape
    rows, cols = q_t.shape
    seg = cols // slots
    scal_s, feat, kv_s, lse_s, lanes = attn_specs(slots, steps, pair, seg, rows, groups, width // 2)
    return pl.pallas_call(
        functools.partial(attn_fwd_kernel, with_length=with_length),
        grid=(slots, groups),
        in_specs=[scal_s, feat, kv_s],
        out_specs=[feat, lse_s],
        out_shape=[
            jax.ShapeDtypeStruct((rows, cols), BF),
            jax.ShapeDtypeStruct((slots, groups, 1, lanes), F32),
        ],
        compiler_params=pltpu.CompilerParams(vmem_limit_bytes=40 << 20),
        cost_estimate=pl.CostEstimate(
            flops=4 * rows * cols * steps * pair, bytes_accessed=6 << 20, transcendentals=0
        ),
    )(scal, q_t, kv)


def attn_backward(scal, q_t, kv, out_t, dout_t, lse, groups, with_length):
    slots, steps, pair, width = kv.shape
    rows, cols = q_t.shape
    seg = cols // slots
    scal_s, feat, kv_s, lse_s, lanes = attn_specs(slots, steps, pair, seg, rows, groups, width // 2)
    return pl.pallas_call(
        functools.partial(attn_bwd_kernel, with_length=with_length),
        grid=(slots, groups),
        in_specs=[scal_s, feat, kv_s, feat, feat, lse_s],
        out_specs=[feat, kv_s],
        out_shape=[
            jax.ShapeDtypeStruct((rows, cols), BF),
            jax.ShapeDtypeStruct(kv.shape, F32),
        ],
        compiler_params=pltpu.CompilerParams(vmem_limit_bytes=48 << 20),
        cost_estimate=pl.CostEstimate(
            flops=10 * rows * cols * steps * pair, bytes_accessed=9 << 20, transcendentals=0
        ),
    )(scal, q_t, kv, out_t, dout_t, lse)


def norm_stats(values):
    center = values - jnp.mean(values, axis=-1, keepdims=True)
    spread = jnp.mean(center * center, axis=-1, keepdims=True)
    rstd = lax.rsqrt(spread + EPSILON)
    return center * rstd, rstd


def norm_backward(d_values, unit, rstd, gain):
    scaled = d_values * gain
    return rstd * (
        scaled
        - jnp.mean(scaled, axis=-1, keepdims=True)
        - unit * jnp.mean(scaled * unit, axis=-1, keepdims=True)
    )


def gather_rows(shard, x, place):
    rows = shard.shape[0]
    half = rows // 2
    mine = lax.dynamic_slice_in_dim(shard, x * half, half, 0)
    direct = swap(mine, "y")
    other = swap(direct, "x")
    sib = swap(shard, "c")
    sib_direct = swap(direct, "c")
    sib_other = swap(other, "c")
    full = jnp.zeros((4 * rows,) + shard.shape[1:], shard.dtype)
    far = place ^ 2
    pieces = (
        (shard, place * rows),
        (sib, (place ^ 1) * rows),
        (direct, far * rows + x * half),
        (other, far * rows + (1 - x) * half),
        (sib_direct, (far ^ 1) * rows + x * half),
        (sib_other, (far ^ 1) * rows + (1 - x) * half),
    )
    for piece, start in pieces:
        full = lax.dynamic_update_slice_in_dim(full, piece, start, 0)
    return full


def gather_plane(block):
    half = block.shape[0] // 2
    from_x = swap(block, "x")
    from_y = swap(block, "y")
    diag = jnp.concatenate([swap(from_y[:half], "x"), swap(from_x[half:], "y")], axis=0)
    return [
        jnp.concatenate([part, swap(part, "c")], axis=0) for part in (block, from_x, from_y, diag)
    ]


def scatter_plane(parts):
    rows = parts[0].shape[0] // 2
    half = rows // 2
    own, to_x, to_y, diag = [
        part[:rows].astype(F32) + swap(part[rows:].astype(BF), "c").astype(F32) for part in parts
    ]
    via_x = swap(diag[:half].astype(BF), "x").astype(F32)
    via_y = swap(diag[half:].astype(BF), "y").astype(F32)
    to_y = jnp.concatenate([to_y[:half] + via_x, to_y[half:]], axis=0)
    to_x = jnp.concatenate([to_x[:half], to_x[half:] + via_y], axis=0)
    return own + swap(to_x.astype(BF), "x").astype(F32) + swap(to_y.astype(BF), "y").astype(F32)


def scatter_line(parts, z, length):
    def block(index):
        return pick(parts, jnp.clip(index, 0, length - 1), 0).astype(F32)

    from_left = from_right = None
    for step in range(1, length):
        up = block(length - step + z)
        down = block(z - length + step)
        if from_left is not None:
            up, down = up + from_left, down + from_right
        from_left = lax.ppermute(up.astype(BF), "z", [(i, i + 1) for i in range(step)]).astype(F32)
        from_right = lax.ppermute(
            down.astype(BF), "z", [(i, i - 1) for i in range(length - step, length)]
        ).astype(F32)
    return block(z) + from_left + from_right


def scatter_all(left_side, right_side, vectors, place_yczx, sizes):
    y, c, z, x = place_yczx
    length, width = sizes
    tokens = left_side.shape[0]
    block = width // (8 * length)
    left_parts = left_side.reshape(tokens, 2, 2, width // 4)
    left_mine = pick(left_parts, c, 2).reshape(tokens, width // 2)
    left_sib = swap(pick(left_parts, 1 - c, 2), "c").reshape(tokens, width // 2)
    right_sib = swap(right_side, "c")
    partial = dot(
        jnp.concatenate([left_mine, left_sib], axis=0),
        jnp.concatenate([right_side, right_sib], axis=0),
        ((0,), (0,)),
    )
    extra = jnp.pad(jnp.stack(vectors, axis=1), ((0, 0), (0, 128 - len(vectors))))
    extra = extra.reshape(2, 2, width // 4, 128)
    extra = pick(extra, c, 1) + swap(pick(extra, 1 - c, 1).astype(BF), "c").astype(F32)
    partial = jnp.concatenate([partial, extra.reshape(width // 2, 128)], axis=1)
    cols = partial.shape[1]
    partial = partial.reshape(2, length, 2, block, cols)
    cut = (cols // 256) * 128
    side_a, side_b = partial[..., :cut], partial[..., cut:]
    side_a = pick(side_a, y, 0) + swap(pick(side_a, 1 - y, 0).astype(BF), "y").astype(F32)
    side_b = pick(side_b, x, 2) + swap(pick(side_b, 1 - x, 2).astype(BF), "x").astype(F32)
    side_a = pick(side_a, x, 1) + swap(pick(side_a, 1 - x, 1).astype(BF), "x").astype(F32)
    side_b = pick(side_b, y, 0) + swap(pick(side_b, 1 - y, 0).astype(BF), "y").astype(F32)
    return scatter_line(jnp.concatenate([side_a, side_b], axis=-1), z, length)


MESH = pl.DeviceIdType.MESH


def remote(src, dst, send_sems, recv_sems, index, device):
    return pltpu.make_async_remote_copy(
        src_ref=src,
        dst_ref=dst,
        send_sem=send_sems.at[index],
        recv_sem=recv_sems.at[index],
        device_id=device,
        device_id_type=MESH,
    )


def greet(devices):
    barrier = pltpu.get_barrier_semaphore()
    for device in devices:
        pl.semaphore_signal(barrier, inc=1, device_id=device, device_id_type=MESH)
    pl.semaphore_wait(barrier, len(devices))


def tiles(count, size):
    def over(fn):
        @pl.loop(0, count)
        def step(index):
            fn(pl.ds(pl.multiple_of(index * size, size), size), index)

    return over


def gelu_pair(upper):
    inner = jnp.tanh(upper * (GELU_K + (GELU_K * GELU_C) * (upper * upper)))
    half = 0.5 + 0.5 * inner
    slope = half + (0.5 * upper) * (1.0 - inner * inner) * (
        GELU_K + (3.0 * GELU_K * GELU_C) * (upper * upper)
    )
    return upper * half, slope


def ffn_kernel(
    second_ref,
    down_all_ref,
    up_ref,
    ubias_ref,
    down_ref,
    dsecond_ref,
    out_parts_ref,
    down_part_ref,
    up_part_ref,
    ubias_part_ref,
    tokens_v,
    cots_v,
    up_v,
    down_v,
    active_v,
    dupper_v,
    sib_out,
    sib_in,
    chip_out,
    chip_in,
    acc_v,
    stage_v,
    load_sem,
    stage_sem,
    gs_send,
    gs_recv,
    rs_send,
    rs_recv,
    *,
    length,
):
    rows, width = second_ref.shape
    hidden = up_ref.shape[1]
    half = rows // 2
    chunk = 2 * rows
    y, c, x = [lax.axis_index(name) for name in ("y", "c", "x")]
    sib, to_x, to_y = {"c": 1 - c}, {"x": 1 - x}, {"y": 1 - y}
    diag = {"x": 1 - x, "y": 1 - y}
    chips = (None, to_x, to_y, diag)

    loads = [
        pltpu.make_async_copy(second_ref, tokens_v.at[0, pl.ds(0, rows)], load_sem.at[0]),
        pltpu.make_async_copy(down_ref, down_v, load_sem.at[1]),
        pltpu.make_async_copy(down_all_ref, cots_v, load_sem.at[2]),
        pltpu.make_async_copy(up_ref, up_v, load_sem.at[3]),
    ]
    for load in loads:
        load.start()
    greet((sib, to_x, to_y, diag))
    loads[0].wait()

    same, other = pl.ds(0, rows), pl.ds(rows, rows)
    top, bottom = pl.ds(0, half), pl.ds(half, half)

    def gather(index, chip, span_src, chip_dst, span_dst, device):
        return remote(
            tokens_v.at[chip, span_src], tokens_v.at[chip_dst, span_dst], gs_send, gs_recv, index, device
        )

    send_x = gather(0, 0, same, 1, same, to_x)
    send_y = gather(1, 0, same, 2, same, to_y)
    share = [gather(2 + k, k, same, k, other, sib) for k in range(4)]
    diag_x = gather(6, 2, top, 3, top, to_x)
    diag_y = gather(7, 1, bottom, 3, bottom, to_y)
    send_x.start()
    send_y.start()
    share[0].start()

    loads[1].wait()
    loads[2].wait()

    @tiles(4 * chunk // 512, 512)
    def grad_active(span, index):
        @tiles(hidden // 512, 512)
        def columns(cols, _):
            dupper_v[span, cols] = dot(cots_v[span, :], down_v[cols, :], ((1,), (1,))).astype(BF)

    loads[3].wait()

    def chip_work(k):
        @tiles(hidden // 256, 256)
        def columns(cols, _):
            block = pl.ds(k * chunk, chunk)
            upper = dot(tokens_v[k], up_v[:, cols]) + ubias_ref[:, cols]
            active, slope = gelu_pair(upper)
            active_v[block, cols] = active.astype(BF)
            d_upper = (dupper_v[block, cols].astype(F32) * slope).astype(BF)
            dupper_v[block, cols] = d_upper
            part = jnp.sum(d_upper.astype(F32), axis=0, keepdims=True)
            if k == 0:
                ubias_part_ref[:, cols] = part
            else:
                ubias_part_ref[:, cols] += part

        @tiles(width // 512, 512)
        def to_sibling(cols, _):
            sib_out[k, :, cols] = dot(
                dupper_v[pl.ds(k * chunk + rows, rows), :], up_v[cols, :], ((1,), (1,))
            ).astype(BF)

        pair = remote(sib_out.at[k], sib_in.at[k], rs_send, rs_recv, k, sib)
        pair.start()

        @tiles(width // 512, 512)
        def keep(cols, _):
            acc_v[:, cols] = dot(dupper_v[pl.ds(k * chunk, rows), :], up_v[cols, :], ((1,), (1,)))

        pair.wait_recv()
        if k == 0:
            dsecond_ref[...] = acc_v[...] + sib_in[0].astype(F32)
            return [pair]
        chip_out[k - 1] = (acc_v[...] + sib_in[k].astype(F32)).astype(BF)
        far = remote(chip_out.at[k - 1], chip_in.at[k - 1], rs_send, rs_recv, 3 + k, chips[k])
        far.start()
        return [pair, far]

    share[0].wait_recv()
    sent = chip_work(0)
    send_x.wait_recv()
    share[1].start()
    diag_y.start()
    send_y.wait_recv()
    share[2].start()
    diag_x.start()
    share[1].wait_recv()
    sent += chip_work(1)
    share[2].wait_recv()
    sent += chip_work(2)
    diag_x.wait_recv()
    diag_y.wait_recv()
    share[3].start()
    share[3].wait_recv()
    sent += chip_work(3)

    def staged(slot, value, target):
        stage_v[slot] = value.astype(BF)
        copy = pltpu.make_async_copy(stage_v.at[slot], target, stage_sem.at[slot])
        copy.start()
        return copy

    @pl.loop(0, 4)
    def outputs(k):
        block = pl.ds(pl.multiple_of(k * chunk, chunk), chunk)
        copies = []
        for j in range(width // 512):
            cols = pl.ds(j * 512, 512)
            copies.append(
                staged(j, dot(active_v[block, :], down_v[:, cols]), out_parts_ref.at[k, :, cols])
            )
        for copy in copies:
            copy.wait()

    @pl.loop(0, hidden // 512)
    def downs(r):
        block = pl.ds(pl.multiple_of(r * 512, 512), 512)
        copies = []
        for j in range(width // 512):
            cols = pl.ds(j * 512, 512)
            copies.append(
                staged(
                    j,
                    dot(active_v[:, block], cots_v[:, cols], ((0,), (0,))),
                    down_part_ref.at[block, cols],
                )
            )
        for copy in copies:
            copy.wait()

    quarter = width // 4
    piece = quarter // length

    @pl.loop(0, hidden // 512)
    def ups(r):
        cols = pl.ds(pl.multiple_of(r * 512, 512), 512)
        copies = []
        for f in range(4):
            value = None
            for k in range(4):
                term = dot(
                    tokens_v[k, :, f * quarter : (f + 1) * quarter],
                    dupper_v[k * chunk : (k + 1) * chunk, cols],
                    ((0,), (0,)),
                )
                value = term if value is None else value + term
            stage_v[f] = value.astype(BF)
            for level in range(length):
                copy = pltpu.make_async_copy(
                    stage_v.at[f, pl.ds(level * piece, piece)],
                    up_part_ref.at[level, f, :, cols],
                    stage_sem.at[4 + f * length + level],
                )
                copy.start()
                copies.append(copy)
        for copy in copies:
            copy.wait()

    for k in range(3):
        remote(chip_out.at[k], chip_in.at[k], rs_send, rs_recv, 4 + k, chips[k + 1]).wait_recv()
    dsecond_ref[...] += (
        chip_in[0].astype(F32) + chip_in[1].astype(F32) + chip_in[2].astype(F32)
    )
    for copy in [send_x, send_y, diag_x, diag_y] + share + sent:
        copy.wait_send()


def ffn(second, down_all, up_mine, ubias, down_mine, length):
    rows, width = second.shape
    hidden = up_mine.shape[1]
    hbm = pl.BlockSpec(memory_space=pltpu.HBM)
    vmem = pl.BlockSpec(memory_space=pltpu.VMEM)
    sems = pltpu.SemaphoreType.DMA
    return pl.pallas_call(
        functools.partial(ffn_kernel, length=length),
        in_specs=[hbm, hbm, hbm, vmem, hbm],
        out_specs=[vmem, hbm, hbm, hbm, vmem],
        out_shape=[
            jax.ShapeDtypeStruct((rows, width), F32),
            jax.ShapeDtypeStruct((4, 2 * rows, width), BF),
            jax.ShapeDtypeStruct((hidden, width), BF),
            jax.ShapeDtypeStruct((length, 4, width // 4 // length, hidden), BF),
            jax.ShapeDtypeStruct((1, hidden), F32),
        ],
        scratch_shapes=[
            pltpu.VMEM((4, 2 * rows, width), BF),
            pltpu.VMEM((8 * rows, width), BF),
            pltpu.VMEM((width, hidden), BF),
            pltpu.VMEM((hidden, width), BF),
            pltpu.VMEM((8 * rows, hidden), BF),
            pltpu.VMEM((8 * rows, hidden), BF),
            pltpu.VMEM((4, rows, width), BF),
            pltpu.VMEM((4, rows, width), BF),
            pltpu.VMEM((3, rows, width), BF),
            pltpu.VMEM((3, rows, width), BF),
            pltpu.VMEM((rows, width), F32),
            pltpu.VMEM((4, 512, 512), BF),
            sems((4,)),
            sems((4 + 4 * length,)),
            sems((8,)),
            sems((8,)),
            sems((7,)),
            sems((7,)),
        ],
        compiler_params=pltpu.CompilerParams(
            collective_id=1, has_side_effects=True, vmem_limit_bytes=60 << 20
        ),
        cost_estimate=pl.CostEstimate(
            flops=12 * 8 * rows * width * hidden, bytes_accessed=40 << 20, transcendentals=0
        ),
    )(second, down_all, up_mine, ubias, down_mine)


ROW_TILE = 32


def for_rows(total, fn):
    @pl.loop(0, total // ROW_TILE)
    def step(index):
        fn(pl.ds(pl.multiple_of(index * ROW_TILE, ROW_TILE), ROW_TILE))


def norm_rows(values):
    center = values - jnp.mean(values, axis=-1, keepdims=True)
    spread = jnp.mean(center * center, axis=-1, keepdims=True)
    rstd = lax.rsqrt(spread + EPSILON)
    return center * rstd, rstd


class Gathered:
    def __init__(self, shard_ref, full_ref, sems, base, where):
        self.y, self.c, self.x = where
        self.shard, self.full, self.sems, self.base = shard_ref, full_ref, sems, base
        self.rows = shard_ref.shape[0]
        self.half = self.rows // 2
        self.step = self.half // 4
        self.place = self.y * 2 + self.c

    def copy(self, src, dst, index, device):
        send_sems, recv_sems = self.sems
        return remote(src, dst, send_sems, recv_sems, self.base + index, device)

    def span(self, place, side, i):
        start = place * self.rows + side * self.half + i * self.step
        return self.full.at[pl.ds(pl.multiple_of(start, self.step), self.step)]

    def over_y(self, i):
        start = pl.multiple_of(self.x * self.half + i * self.step, self.step)
        return self.copy(
            self.shard.at[pl.ds(start, self.step)], self.span(self.place, self.x, i), i, {"y": 1 - self.y}
        )

    def over_x(self, i):
        ref = self.span(self.place ^ 2, self.x, i)
        return self.copy(ref, ref, 4 + i, {"x": 1 - self.x})

    def over_c(self, i, side):
        ref = self.span(self.place ^ 2, self.x if side == 0 else 1 - self.x, i)
        return self.copy(ref, ref, 8 + 4 * side + i, {"c": 1 - self.c})

    def own_c(self):
        start = pl.multiple_of(self.place * self.rows, self.rows)
        return self.copy(self.shard, self.full.at[pl.ds(start, self.rows)], 16, {"c": 1 - self.c})

    def settle(self):
        self.own_c().wait_recv()
        for i in range(4):
            self.over_c(i, 0).wait_recv()
            self.over_c(i, 1).wait_recv()

    def own(self, sem):
        start = pl.multiple_of(self.place * self.rows, self.rows)
        return pltpu.make_async_copy(self.shard, self.full.at[pl.ds(start, self.rows)], sem)


class WeightStep:
    def __init__(self, weight, i):
        self.weight, self.i = weight, i

    def start(self, begin):
        begin(self.weight.over_y(self.i))

    def arrive(self):
        self.weight.over_y(self.i).wait_recv()

    def follow(self, begin):
        begin(self.weight.over_x(self.i))
        begin(self.weight.over_c(self.i, 0))

    def late(self, begin):
        self.weight.over_x(self.i).wait_recv()
        begin(self.weight.over_c(self.i, 1))


class Stream:
    def __init__(self, order, begin):
        self.order, self.begin = order, begin
        self.next = 0
        self.behind = None
        for step in order[:2]:
            step.start(begin)

    def event(self):
        n = self.next
        self.next += 1
        step = self.order[n]
        step.arrive()
        if n + 2 < len(self.order):
            self.order[n + 2].start(self.begin)
        step.follow(self.begin)
        self.late()
        self.behind = step

    def late(self):
        if self.behind is not None:
            self.behind.late(self.begin)
        self.behind = None


def front_kernel(
    lengths_ref,
    tokens_v,
    smalls_ref,
    kvw_ref,
    qw_ref,
    mw_ref,
    up_ref,
    cot_ref,
    second_ref,
    residual_ref,
    first_v,
    q_v,
    kv_v,
    mixed_v,
    lse_ref,
    vec_v,
    wq_out,
    wm_out,
    wkv_v,
    up_out,
    cots_out,
    wq_v,
    wm_v,
    smalls_v,
    local_sem,
    w_send,
    w_recv,
    s_send,
    s_recv,
    k_send,
    k_recv,
    u_send,
    u_recv,
    uz_send,
    uz_recv,
    c_send,
    c_recv,
    *,
    length,
    slots,
    with_length,
    aligned,
):
    rows, width = tokens_v.shape
    seg = rows // slots
    head_dim = kvw_ref.shape[1] // 2
    heads = width // head_dim
    group = 4
    quarter = width // 4
    y, c, z, x = [lax.axis_index(name) for name in ("y", "c", "z", "x")]
    place = y * 2 + c
    sib, to_x, to_y = {"c": 1 - c}, {"x": 1 - x}, {"y": 1 - y}
    cross, diag = {"y": 1 - y, "c": 1 - c}, {"x": 1 - x, "y": 1 - y}

    weights = [
        Gathered(ref, full, (w_send, w_recv), 17 * n, (y, c, x))
        for n, (ref, full) in enumerate(((qw_ref, wq_v), (mw_ref, wm_v)))
    ]
    query_w, mixer_w = weights
    locals_ = [query_w.own(local_sem.at[0]), mixer_w.own(local_sem.at[1])]
    kv_rows = pl.ds(pl.multiple_of(place * quarter, quarter), quarter)
    locals_.append(pltpu.make_async_copy(kvw_ref, wkv_v.at[kv_rows], local_sem.at[2]))
    locals_.append(pltpu.make_async_copy(smalls_ref, smalls_v.at[place], local_sem.at[3]))
    for copy in locals_:
        copy.start()

    barrier = pltpu.get_barrier_semaphore()
    for device in (sib, to_x, to_y, cross, diag):
        pl.semaphore_signal(barrier, inc=1, device_id=device, device_id_type=MESH)
    for other in range(length):
        @pl.when(other != z)
        def hello():
            pl.semaphore_signal(barrier, inc=1, device_id={"z": other}, device_id_type=MESH)
    pl.semaphore_wait(barrier, 5 + length - 1)

    sent = []

    def begin(copy):
        copy.start()
        sent.append(copy)
        return copy

    small_copies = [
        begin(remote(smalls_ref, smalls_v.at[place], s_send, s_recv, n, device))
        for n, device in enumerate((sib, to_y, cross))
    ]
    kv_near = begin(remote(kvw_ref, wkv_v.at[kv_rows], s_send, s_recv, 3, sib))
    kv_far = begin(remote(kvw_ref, wkv_v.at[kv_rows], s_send, s_recv, 4, to_y))
    part = quarter // length
    hidden = up_out.shape[1]
    block = hidden // length

    def up_copies(index, flip, span, device):
        target = place ^ flip
        dst_rows = pl.ds(pl.multiple_of(place * quarter + span[0], span[1]), span[1])
        copies = []
        for b in range(length if aligned else 1):
            if aligned:
                start = target * (hidden * 2) + (2 * b + x) * block
                src = up_ref.at[pl.ds(span[0], span[1]), pl.ds(pl.multiple_of(start, block), block)]
                dst = up_out.at[dst_rows, pl.ds(b * block, block)]
            else:
                src = up_ref.at[target, pl.ds(span[0], span[1])]
                dst = up_out.at[dst_rows]
            n = index * length + b
            if device is None:
                copies.append(pltpu.make_async_copy(src, dst, u_send.at[n]))
            else:
                copies.append(remote(src, dst, u_send, u_recv, n, device))
        return copies

    up_local = [] if aligned else up_copies(0, 0, (0, quarter), None)
    up_near = up_copies(1, 1, (0, quarter), sib)
    z_part = (pl.multiple_of(z * part, part), part)
    up_far = up_copies(2, 2, z_part, to_y) + up_copies(3, 3, z_part, cross)

    def up_share(k, source, target):
        start = (place ^ (2 + k)) * quarter + source * part
        ref = up_out.at[pl.ds(pl.multiple_of(start, part), part)]
        return pltpu.make_async_remote_copy(
            src_ref=ref,
            dst_ref=ref,
            send_sem=uz_send.at[k, target],
            recv_sem=uz_recv.at[k, source],
            device_id={"z": target},
            device_id_type=MESH,
        )

    class UpStep:
        def start(self, begin):
            for copy in up_far:
                begin(copy)

        def arrive(self):
            for copy in up_far:
                copy.wait_recv()

        def follow(self, begin):
            for target in range(length):
                @pl.when(target != z)
                def share():
                    for k in range(2):
                        up_share(k, z, target).start()

        def late(self, begin):
            pass

    stream = Stream(
        [WeightStep(query_w, i) for i in range(4)] + [UpStep()] + [WeightStep(mixer_w, i) for i in range(4)],
        begin,
    )
    for weight in weights:
        begin(weight.own_c())

    for copy in small_copies:
        copy.wait_recv()
    locals_[3].wait()
    vec_v[...] = jnp.concatenate([smalls_v[f].astype(F32) for f in range(4)], axis=1)

    def first_norm(span):
        unit, _ = norm_rows(tokens_v[span, :].astype(F32))
        first_v[span, :] = (unit * vec_v[0:1, :] + vec_v[1:2, :]).astype(BF)

    for_rows(rows, first_norm)

    kv_far.wait_recv()
    far_rows = wkv_v.at[pl.ds(pl.multiple_of((place ^ 2) * quarter, quarter), quarter)]
    kv_pass = begin(remote(far_rows, far_rows, s_send, s_recv, 5, sib))
    stream.event()
    kv_near.wait_recv()
    locals_[2].wait()
    kv_pass.wait_recv()
    v_bias = (
        vec_v[7:8, 0:head_dim]
        + vec_v[7:8, quarter : quarter + head_dim]
        + vec_v[7:8, 2 * quarter : 2 * quarter + head_dim]
        + vec_v[7:8, 3 * quarter : 3 * quarter + head_dim]
    )
    keyvals = dot(first_v[...], wkv_v[...]) + jnp.concatenate([jnp.zeros_like(v_bias), v_bias], axis=1)
    mine = pl.ds(pl.multiple_of(x * seg, seg), seg)
    for s in range(slots):
        kv_v[s, 0, mine, :] = keyvals[s * seg : (s + 1) * seg].astype(BF)

    def kv_up(t):
        return remote(kv_v.at[:, t - 1, mine], kv_v.at[:, t, mine], k_send, k_recv, t, {"z": z + 1})

    def kv_side(t):
        ref = kv_v.at[:, t, mine]
        return remote(ref, ref, k_send, k_recv, length + t, to_x)

    def kv_step(t):
        if t:
            @pl.when(z >= t)
            def arrive():
                kv_up(t).wait_recv()

        @pl.when(z >= t)
        def side():
            kv_side(t).start()

        if t + 1 < length:
            @pl.when((z >= t) & (z < length - 1))
            def onward():
                kv_up(t + 1).start()

    for copy in up_local:
        copy.start()
    for copy in up_near:
        begin(copy)

    for t in range(length):
        kv_step(t)
        if t < 3:
            stream.event()

    same, other_half = pl.ds(0, rows), pl.ds(rows, rows)
    top, bottom = pl.ds(0, rows // 2), pl.ds(rows // 2, rows // 2)
    if not aligned:
        cot_local = pltpu.make_async_copy(cot_ref, cots_out.at[0, same], local_sem.at[4])
        cot_local.start()
    cot_x = remote(cot_ref, cots_out.at[1, same], c_send, c_recv, 0, to_x)
    cot_y = remote(cot_ref, cots_out.at[2, same], c_send, c_recv, 1, to_y)
    cot_share = [
        remote(cot_ref if k == 0 else cots_out.at[k, same], cots_out.at[k, other_half], c_send, c_recv, 2 + k, sib)
        for k in range(4)
    ]
    cot_dx = remote(cots_out.at[2, top], cots_out.at[3, top], c_send, c_recv, 6, to_x)
    cot_dy = remote(cots_out.at[1, bottom], cots_out.at[3, bottom], c_send, c_recv, 7, to_y)

    stream.late()
    locals_[0].wait()
    query_w.settle()

    @tiles(width // 512, 512)
    def project(cols, _):
        q_v[:, cols] = (dot(first_v[...], wq_v[:, cols]) + vec_v[2:3, cols]).astype(BF)

    wq_copy = pltpu.make_async_copy(wq_v, wq_out, local_sem.at[5])
    wq_copy.start()
    for t in range(length):
        @pl.when(z >= t)
        def arrived():
            kv_side(t).wait_recv()
            kv_side(t).wait_send()

        if t:
            @pl.when((z >= t - 1) & (z < length - 1))
            def gone():
                kv_up(t).wait_send()

    scale = head_dim ** (-0.5)

    def attend(s, g):
        lanes = pl.ds(pl.multiple_of(g * group * head_dim, group * head_dim), group * head_dim)
        wide = q_v[pl.ds(s * seg, seg), lanes]
        queries = jnp.concatenate(
            [wide[:, h * head_dim : (h + 1) * head_dim] for h in range(group)], axis=0
        )

        def step(t, state, diagonal):
            top_, total, accum = state
            keys = kv_v[s, t, :, :head_dim]
            values = kv_v[s, t, :, head_dim:]
            scores = dot(keys, queries, ((1,), (1,))) * scale
            if diagonal or with_length:
                key_pos = lax.broadcasted_iota(jnp.int32, (2 * seg, seg), 0)
                allowed = None
                if diagonal:
                    query_pos = lax.broadcasted_iota(jnp.int32, (2 * seg, seg), 1) + x * seg
                    allowed = key_pos <= query_pos
                if with_length:
                    inside = key_pos + (z - t) * (2 * seg) < lengths_ref[s]
                    allowed = inside if allowed is None else allowed & inside
                bias = jnp.where(allowed, 0.0, NEG_LARGE).astype(F32)
                scores = scores + jnp.concatenate([bias] * group, axis=1)
            new_top = jnp.maximum(top_, jnp.max(scores, axis=0, keepdims=True))
            terms = jnp.exp(scores - new_top)
            fade = jnp.exp(top_ - new_top)
            total = total * fade + jnp.sum(terms, axis=0, keepdims=True)
            accum = accum * fade + dot(values, terms.astype(BF), ((0,), (0,)))
            return new_top, total, accum

        span = group * seg
        state = (
            jnp.full((1, span), NEG_LARGE, F32),
            jnp.zeros((1, span), F32),
            jnp.zeros((head_dim, span), F32),
        )
        state = step(0, state, True)
        top_, total, accum = lax.fori_loop(1, z + 1, lambda t, st: step(t, st, False), state)
        out = accum / total
        mixed_v[pl.ds(s * seg, seg), lanes] = jnp.concatenate(
            [out[:, h * seg : (h + 1) * seg].T for h in range(group)], axis=1
        ).astype(BF)
        lse_ref[s, g] = top_ + jnp.log(total)

    for s in range(slots):
        for g in range(heads // group):
            attend(s, g)
            if stream.next < len(stream.order):
                stream.event()
                if stream.next == len(stream.order) - 1:
                    begin(cot_x)
                    begin(cot_y)
                    begin(cot_share[0])

    stream.late()
    locals_[1].wait()
    mixer_w.settle()
    wm_copy = pltpu.make_async_copy(wm_v, wm_out, local_sem.at[6])
    wm_copy.start()

    @tiles(width // 512, 512)
    def mix(cols, _):
        residual_ref[:, cols] = (
            tokens_v[:, cols].astype(F32) + dot(mixed_v[...], wm_v[:, cols]) + vec_v[3:4, cols]
        )

    def second_norm(span):
        unit, _ = norm_rows(residual_ref[span, :])
        second_ref[span, :] = (unit * vec_v[4:5, :] + vec_v[5:6, :]).astype(BF)

    for_rows(rows, second_norm)

    cot_x.wait_recv()
    cot_y.wait_recv()
    begin(cot_share[1])
    begin(cot_share[2])
    if not aligned:
        begin(cot_dx)
        begin(cot_dy)
        cot_dx.wait_recv()
        cot_dy.wait_recv()
        begin(cot_share[3])
    for copy in cot_share[: 3 if aligned else 4] + up_near:
        copy.wait_recv()
    for copy in up_local:
        copy.wait()
    for target in range(length):
        @pl.when(target != z)
        def shared():
            for k in range(2):
                up_share(k, z, target).wait_send()
                up_share(k, target, z).wait_recv()
    for copy in sent:
        copy.wait_send()
    for copy in (wq_copy, wm_copy) + (() if aligned else (cot_local,)):
        copy.wait()


def front(lengths, tokens, smalls, kvw, qw, mw, up, cot, slots, length, with_length, aligned, hidden):
    rows, width = tokens.shape
    seg = rows // slots
    both = kvw.shape[1]
    groups = width // (both // 2) // 4
    hbm = pl.BlockSpec(memory_space=pltpu.HBM)
    vmem = pl.BlockSpec(memory_space=pltpu.VMEM)
    sems = pltpu.SemaphoreType.DMA
    return pl.pallas_call(
        functools.partial(
            front_kernel, length=length, slots=slots, with_length=with_length, aligned=aligned
        ),
        in_specs=[pl.BlockSpec(memory_space=pltpu.SMEM), vmem, hbm, hbm, hbm, hbm, hbm, hbm],
        out_specs=[vmem] * 8 + [hbm, hbm, vmem, hbm, hbm],
        out_shape=[
            jax.ShapeDtypeStruct((rows, width), BF),
            jax.ShapeDtypeStruct((rows, width), F32),
            jax.ShapeDtypeStruct((rows, width), BF),
            jax.ShapeDtypeStruct((rows, width), BF),
            jax.ShapeDtypeStruct((slots, length, 2 * seg, both), BF),
            jax.ShapeDtypeStruct((rows, width), BF),
            jax.ShapeDtypeStruct((slots, groups, 1, 4 * seg), F32),
            jax.ShapeDtypeStruct((16, width), F32),
            jax.ShapeDtypeStruct((width, width), BF),
            jax.ShapeDtypeStruct((width, width), BF),
            jax.ShapeDtypeStruct((width, both), BF),
            jax.ShapeDtypeStruct((width, hidden), BF),
            jax.ShapeDtypeStruct((4, 2 * rows, width), BF),
        ],
        scratch_shapes=[
            pltpu.VMEM((width, width), BF),
            pltpu.VMEM((width, width), BF),
            pltpu.VMEM((4, 16, width // 4), BF),
            sems((7,)),
            sems((34,)),
            sems((34,)),
            sems((6,)),
            sems((6,)),
            sems((2 * length,)),
            sems((2 * length,)),
            sems((4 * length,)),
            sems((4 * length,)),
            sems((2, length)),
            sems((2, length)),
            sems((8,)),
            sems((8,)),
        ],
        compiler_params=pltpu.CompilerParams(
            collective_id=2, has_side_effects=True, vmem_limit_bytes=60 << 20
        ),
        cost_estimate=pl.CostEstimate(
            flops=6 * rows * width * width, bytes_accessed=40 << 20, transcendentals=0
        ),
    )(lengths, tokens, smalls, kvw, qw, mw, up, cot)


def feed_kernel(
    second_ref,
    cot_ref,
    down_all_ref,
    up_ref,
    upw_ref,
    ubias_ref,
    residual_ref,
    vec_ref,
    down_ref,
    dres_ref,
    red_ref,
    down_part_ref,
    up_part_ref,
    ubias_part_ref,
    vsum_ref,
    tokens_v,
    cots_v,
    up_v,
    down_v,
    active_v,
    dupper_v,
    sib_out,
    sib_in,
    red_in,
    chip_out,
    chip_in,
    acc_v,
    stage_v,
    load_sem,
    stage_sem,
    gs_send,
    gs_recv,
    rs_send,
    rs_recv,
    *,
    length,
):
    rows, width = second_ref.shape
    hidden = up_ref.shape[1]
    half = rows // 2
    chunk = 2 * rows
    y, c, x = [lax.axis_index(name) for name in ("y", "c", "x")]
    sib, to_x, to_y = {"c": 1 - c}, {"x": 1 - x}, {"y": 1 - y}
    diag = {"x": 1 - x, "y": 1 - y}
    chips = (None, to_x, to_y, diag)

    loads = [
        pltpu.make_async_copy(second_ref, tokens_v.at[0, pl.ds(0, rows)], load_sem.at[0]),
        pltpu.make_async_copy(cot_ref, cots_v.at[pl.ds(0, rows)], load_sem.at[1]),
        pltpu.make_async_copy(
            down_all_ref.at[pl.ds(rows, 5 * rows)], cots_v.at[pl.ds(rows, 5 * rows)], load_sem.at[2]
        ),
    ]
    block = hidden // length
    quarter = width // 4
    place = y * 2 + c
    ups_in = []
    for flip in range(1, 4):
        span = pl.ds(pl.multiple_of((place ^ flip) * quarter, quarter), quarter)
        ups_in.append(pltpu.make_async_copy(up_ref.at[span], up_v.at[span], load_sem.at[3 + flip]))
    own_rows = pl.ds(pl.multiple_of(place * quarter, quarter), quarter)
    for b in range(length):
        start = place * (2 * hidden) + (2 * b + x) * block
        ups_in.append(
            pltpu.make_async_copy(
                upw_ref.at[:, pl.ds(pl.multiple_of(start, block), block)],
                up_v.at[own_rows, pl.ds(b * block, block)],
                load_sem.at[7 + length + b],
            )
        )
    downs_in = [
        pltpu.make_async_copy(
            down_ref.at[pl.ds(pl.multiple_of((2 * b + x) * block, block), block)],
            down_v.at[pl.ds(b * block, block)],
            load_sem.at[7 + b],
        )
        for b in range(length)
    ]
    for load in loads + downs_in + ups_in:
        load.start()
    greet((sib, to_x, to_y, diag))
    loads[0].wait()

    same, other = pl.ds(0, rows), pl.ds(rows, rows)
    top, bottom = pl.ds(0, half), pl.ds(half, half)

    def gather(index, chip, span_src, chip_dst, span_dst, device):
        return remote(
            tokens_v.at[chip, span_src], tokens_v.at[chip_dst, span_dst], gs_send, gs_recv, index, device
        )

    send_x = gather(0, 0, same, 1, same, to_x)
    send_y = gather(1, 0, same, 2, same, to_y)
    share = [gather(2 + k, k, same, k, other, sib) for k in range(4)]
    diag_x = gather(6, 2, top, 3, top, to_x)
    diag_y = gather(7, 1, bottom, 3, bottom, to_y)
    send_x.start()
    send_y.start()
    share[0].start()

    loads[1].wait()
    loads[2].wait()
    for load in downs_in:
        load.wait()

    def cot_part(chip, start, size):
        return cots_v.at[pl.ds(chip * chunk + start, size)]

    cot_dx = remote(cot_part(2, 0, half), cot_part(3, 0, half), gs_send, gs_recv, 8, to_x)
    cot_dy = remote(cot_part(1, half, half), cot_part(3, half, half), gs_send, gs_recv, 9, to_y)
    cot_dc = remote(cot_part(3, 0, rows), cot_part(3, rows, rows), gs_send, gs_recv, 10, sib)
    cot_dx.start()
    cot_dy.start()

    def grad_active(span, index):
        @tiles(hidden // 512, 512)
        def columns(cols, _):
            dupper_v[span, cols] = dot(cots_v[span, :], down_v[cols, :], ((1,), (1,))).astype(BF)

    @pl.loop(0, 3)
    def near_grads(k):
        grad_active(pl.ds(pl.multiple_of(k * chunk, chunk), chunk), k)

    for load in ups_in:
        load.wait()

    def chip_work(k):
        @tiles(hidden // 256, 256)
        def columns(cols, _):
            block = pl.ds(k * chunk, chunk)
            upper = dot(tokens_v[k], up_v[:, cols]) + ubias_ref[:, cols]
            active, slope = gelu_pair(upper)
            active_v[block, cols] = active.astype(BF)
            d_upper = (dupper_v[block, cols].astype(F32) * slope).astype(BF)
            dupper_v[block, cols] = d_upper
            part = jnp.sum(d_upper.astype(F32), axis=0, keepdims=True)
            if k == 0:
                ubias_part_ref[:, cols] = part
            else:
                ubias_part_ref[:, cols] += part

        @tiles(width // 512, 512)
        def to_sibling(cols, _):
            sib_out[k, :, cols] = dot(
                dupper_v[pl.ds(k * chunk + rows, rows), :], up_v[cols, :], ((1,), (1,))
            ).astype(BF)

        pair = remote(sib_out.at[k], sib_in.at[k], rs_send, rs_recv, k, sib)
        pair.start()

        @tiles(width // 512, 512)
        def keep(cols, _):
            dres_ref[:, cols] = dot(dupper_v[pl.ds(k * chunk, rows), :], up_v[cols, :], ((1,), (1,)))

        pair.wait_recv()

        def total(span):
            value = dres_ref[span, :] + sib_in[k, span, :].astype(F32)
            if k == 0:
                acc_v[span, :] = value
            else:
                chip_out[k - 1, span, :] = value.astype(BF)

        for_rows(rows, total)
        if k == 0:
            return [pair]
        far = remote(chip_out.at[k - 1], chip_in.at[k - 1], rs_send, rs_recv, 3 + k, chips[k])
        far.start()
        return [pair, far]

    share[0].wait_recv()
    sent = chip_work(0)
    send_x.wait_recv()
    share[1].start()
    diag_y.start()
    send_y.wait_recv()
    share[2].start()
    diag_x.start()
    share[1].wait_recv()
    sent += chip_work(1)
    share[2].wait_recv()
    sent += chip_work(2)
    diag_x.wait_recv()
    diag_y.wait_recv()
    share[3].start()
    cot_dx.wait_recv()
    cot_dy.wait_recv()
    cot_dc.start()
    cot_dc.wait_recv()
    grad_active(pl.ds(3 * chunk, chunk), 3)
    share[3].wait_recv()
    sent += chip_work(3)

    def staged(slot, value, target):
        stage_v[slot] = value.astype(BF)
        copy = pltpu.make_async_copy(stage_v.at[slot], target, stage_sem.at[slot])
        copy.start()
        return copy

    pairs = []
    for k in range(4):
        sent[0 if k == 0 else 2 * k - 1].wait_send()

        @tiles(width // 512, 512)
        def to_sibling(cols, _):
            sib_out[k, :, cols] = dot(
                active_v[pl.ds(k * chunk + rows, rows), :], down_v[:, cols]
            ).astype(BF)

        pair = remote(sib_out.at[k], red_in.at[k], rs_send, rs_recv, 7 + k, sib)
        pair.start()
        pairs.append(pair)

    for k in range(4):

        @tiles(width // 512, 512)
        def keep(cols, _):
            dres_ref[:, cols] = dot(active_v[pl.ds(k * chunk, rows), :], down_v[:, cols])

        pairs[k].wait_recv()

        def total(span):
            red_in[k, span, :] = (dres_ref[span, :] + red_in[k, span, :].astype(F32)).astype(BF)

        for_rows(rows, total)
    red_copy = pltpu.make_async_copy(red_in, red_ref, load_sem.at[3])
    red_copy.start()

    @pl.loop(0, hidden // 512)
    def downs(r):
        block = pl.ds(pl.multiple_of(r * 512, 512), 512)
        copies = []
        for j in range(width // 512):
            cols = pl.ds(j * 512, 512)
            copies.append(
                staged(
                    j,
                    dot(active_v[:, block], cots_v[:, cols], ((0,), (0,))),
                    down_part_ref.at[block, cols],
                )
            )
        for copy in copies:
            copy.wait()

    piece = quarter // length

    @pl.loop(0, hidden // 512)
    def ups(r):
        first = pl.multiple_of(r * 512, 512)
        cols = pl.ds(first, 512)
        copies = []
        for f in range(4):
            value = None
            for k in range(4):
                term = dot(
                    tokens_v[k, :, f * quarter : (f + 1) * quarter],
                    dupper_v[k * chunk : (k + 1) * chunk, cols],
                    ((0,), (0,)),
                )
                value = term if value is None else value + term
            stage_v[f] = value.astype(BF)
            for level in range(length):
                copy = pltpu.make_async_copy(
                    stage_v.at[f, pl.ds(level * piece, piece)],
                    up_part_ref.at[
                        level, pl.ds((f % 2) * piece, piece), pl.ds((f // 2) * hidden + first, 512)
                    ],
                    stage_sem.at[4 + f * length + level],
                )
                copy.start()
                copies.append(copy)
        for copy in copies:
            copy.wait()

    for k in range(3):
        remote(chip_out.at[k], chip_in.at[k], rs_send, rs_recv, 4 + k, chips[k + 1]).wait_recv()
    vsum_ref[...] = jnp.zeros(vsum_ref.shape, F32)

    def norm_back(span):
        d_second = acc_v[span, :]
        for k in range(3):
            d_second = d_second + chip_in[k, span, :].astype(F32)
        unit, rstd = norm_rows(residual_ref[span, :])
        d_out = cots_v[span, :].astype(F32)
        d_residual = d_out + norm_backward(d_second, unit, rstd, vec_ref[4:5, :])
        dres_ref[span, :] = d_residual
        vsum_ref[0:1, :] += jnp.sum(d_second * unit, axis=0, keepdims=True)
        vsum_ref[1:2, :] += jnp.sum(d_second, axis=0, keepdims=True)
        vsum_ref[2:3, :] += jnp.sum(d_residual.astype(BF).astype(F32), axis=0, keepdims=True)
        vsum_ref[3:4, :] += jnp.sum(d_out, axis=0, keepdims=True)

    for_rows(rows, norm_back)
    red_copy.wait()
    for copy in [send_x, send_y, diag_x, diag_y, cot_dx, cot_dy, cot_dc] + share + pairs + sent[2::2]:
        copy.wait_send()


def feed(second, d_down, down_all, up_mine, up_weight, ubias, residual, vectors, down_weight, length):
    rows, width = second.shape
    hidden = up_mine.shape[1]
    hbm = pl.BlockSpec(memory_space=pltpu.HBM)
    vmem = pl.BlockSpec(memory_space=pltpu.VMEM)
    sems = pltpu.SemaphoreType.DMA
    return pl.pallas_call(
        functools.partial(feed_kernel, length=length),
        in_specs=[hbm, hbm, hbm, hbm, hbm, vmem, vmem, vmem, hbm],
        out_specs=[vmem, hbm, hbm, hbm, vmem, vmem],
        out_shape=[
            jax.ShapeDtypeStruct((rows, width), F32),
            jax.ShapeDtypeStruct((4, rows, width), BF),
            jax.ShapeDtypeStruct((hidden, width), BF),
            jax.ShapeDtypeStruct((length, hidden // length, width), BF),
            jax.ShapeDtypeStruct((1, hidden), F32),
            jax.ShapeDtypeStruct((8, width), F32),
        ],
        scratch_shapes=[
            pltpu.VMEM((4, 2 * rows, width), BF),
            pltpu.VMEM((8 * rows, width), BF),
            pltpu.VMEM((width, hidden), BF),
            pltpu.VMEM((hidden, width), BF),
            pltpu.VMEM((8 * rows, hidden), BF),
            pltpu.VMEM((8 * rows, hidden), BF),
            pltpu.VMEM((4, rows, width), BF),
            pltpu.VMEM((4, rows, width), BF),
            pltpu.VMEM((4, rows, width), BF),
            pltpu.VMEM((3, rows, width), BF),
            pltpu.VMEM((3, rows, width), BF),
            pltpu.VMEM((rows, width), F32),
            pltpu.VMEM((4, 512, 512), BF),
            sems((7 + 2 * length,)),
            sems((4 + 4 * length,)),
            sems((11,)),
            sems((11,)),
            sems((11,)),
            sems((11,)),
        ],
        compiler_params=pltpu.CompilerParams(
            collective_id=4, has_side_effects=True, vmem_limit_bytes=62 << 20
        ),
        cost_estimate=pl.CostEstimate(
            flops=12 * 8 * rows * width * hidden, bytes_accessed=40 << 20, transcendentals=0
        ),
    )(second, d_down, down_all, up_mine, up_weight, ubias, residual, vectors, down_weight)


class Links:
    def __init__(self, send_sems, recv_sems, count):
        self.send_sems, self.recv_sems, self.count = send_sems, recv_sems, count
        self.used = 0

    def copy(self, src, dst, device):
        index = self.used
        self.used += 1
        assert index < self.count
        return self.again(src, dst, device, index)

    def again(self, src, dst, device, index):
        return remote(src, dst, self.send_sems, self.recv_sems, index, device)


class LineSum:
    def __init__(self, links, z, length, parts, landing):
        self.z, self.length, self.parts, self.landing = z, length, parts, landing
        self.copies = {}
        self.links = links

    def position(self, way):
        return self.z if way == 0 else self.length - 1 - self.z

    def block(self, way, t):
        index = self.length - t + self.position(way)
        index = index if way == 0 else self.length - 1 - index
        return jnp.clip(index, 0, self.length - 1)

    def clear(self):
        last = self.length - 1
        for way in range(2):
            @pl.when(self.position(way) == 0)
            def zero():
                ref = self.landing(way, last)
                ref[...] = jnp.zeros(ref.shape, ref.dtype)

    def step(self, t):
        if t > 1:
            self.settle(t - 1)
        for way in range(2):
            pos = self.position(way)
            device = {"z": self.z + (1 if way == 0 else -1)}
            part = self.parts.at[self.block(way, t)]
            index = self.links.used
            direct = self.links.copy(part, self.landing(way, t), device)
            self.copies[way, t] = direct

            @pl.when(pos == 0)
            def first():
                direct.start()

            if t > 1:
                ref = self.landing(way, t - 1)
                passed = self.links.again(ref, self.landing(way, t), device, index)

                @pl.when((pos >= 1) & (pos <= t - 1))
                def onward():
                    self.copies[way, t - 1].wait_recv()
                    add_rows(ref, part)
                    passed.start()

    def finish(self, own, out):
        last = self.length - 1
        for way in range(2):
            @pl.when(self.position(way) >= 1)
            def arrive():
                self.copies[way, last].wait_recv()

        right, left = self.landing(0, last), self.landing(1, last)
        rows = out.shape[0]
        tile = min(rows, ROW_TILE)

        @pl.loop(0, rows // tile)
        def add(index):
            span = pl.ds(pl.multiple_of(index * tile, tile), tile)
            out[span, :] = (
                own[span, :].astype(F32) + right[span, :].astype(F32) + left[span, :].astype(F32)
            ).astype(out.dtype)

    def settle(self, t):
        for way in range(2):
            @pl.when((self.position(way) <= t - 1) & (self.position(way) < self.length - 1))
            def sent():
                self.copies[way, t].wait_send()

    def drain(self):
        self.settle(self.length - 1)


def add_rows(ref, term):
    rows = ref.shape[0]
    tile = min(rows, ROW_TILE)

    @pl.loop(0, rows // tile)
    def add(index):
        span = pl.ds(pl.multiple_of(index * tile, tile), tile)
        ref[span, :] = (ref[span, :].astype(F32) + term[span, :].astype(F32)).astype(ref.dtype)


class GradSum:
    def __init__(self, links, where, length, width, cols, left, right, bufs):
        self.y, self.c, self.z, self.x = where
        self.length, self.width, self.half = length, width, cols // 2
        self.left, self.right = left, right
        self.cols = cols
        (
            self.left_own,
            self.left_out,
            self.left_in,
            self.right_in,
            self.send1,
            self.recv1,
            self.send2,
            self.recv2,
            self.hold,
            self.zpart,
            self.zland,
        ) = bufs
        self.links = links
        self.sent = []

    def begin(self, copy):
        copy.start()
        self.sent.append(copy)
        return copy

    def all_cols(self, ref):
        return ref.at[..., pl.ds(0, self.cols)] if ref.shape[-1] != self.cols else ref

    def half_cols(self, ref):
        return ref.at[..., pl.ds(0, self.half)] if ref.shape[-1] != self.half else ref

    def share(self):
        quarter = self.width // 4
        block = quarter // (2 * self.length)
        for core, target in ((1 - self.c, self.left_out), (self.c, self.left_own)):
            for y_part in range(2):
                lanes = pl.ds(pl.multiple_of((y_part * 2 + core) * quarter, quarter), quarter)
                turned = self.left[:, lanes].astype(F32).T.astype(BF)
                for x_part in range(2):
                    for level in range(self.length):
                        start = (level * 2 + x_part) * block
                        target[y_part * 2 + x_part, level * block : (level + 1) * block, :] = turned[
                            start : start + block
                        ]
        sib = {"c": 1 - self.c}
        self.left_copy = self.begin(self.links.copy(self.left_out, self.left_in, sib))
        self.right_copy = self.begin(self.links.copy(self.right, self.all_cols(self.right_in), sib))

    def term(self, y_part, x_part, cols):
        g = y_part * 2 + x_part
        return dot(self.left_own[g], self.right[:, cols]) + dot(self.left_in[g], self.right_in[:, cols])

    def columns(self, side, fn):
        count = self.half // 128
        size = 128 * max(n for n in range(1, 5) if count % n == 0)
        for j in range(self.half // size):
            fn(pl.ds(side * self.half + j * size, size), pl.ds(j * size, size))

    def first(self):
        self.left_copy.wait_recv()
        self.right_copy.wait_recv()
        for n in range(2):

            def over_y(cols, local):
                self.send1[0, n, :, local] = self.term(1 - self.y, n, cols).astype(BF)

            def over_x(cols, local):
                self.send1[1, n, :, local] = self.term(n, 1 - self.x, cols).astype(BF)

            self.columns(0, over_y)
            self.columns(1, over_x)
        self.copies1 = [
            self.begin(
                self.links.copy(self.half_cols(self.send1.at[side]), self.half_cols(self.recv1.at[side]), device)
            )
            for side, device in ((0, {"y": 1 - self.y}), (1, {"x": 1 - self.x}))
        ]

    def second(self):
        for copy in self.copies1:
            copy.wait_recv()

        def a_out(cols, local):
            term = self.term(self.y, 1 - self.x, cols) + self.recv1[0, 1 - self.x, :, local].astype(F32)
            self.send2[0, :, local] = term.astype(BF)

        def b_out(cols, local):
            term = self.term(1 - self.y, self.x, cols) + self.recv1[1, 1 - self.y, :, local].astype(F32)
            self.send2[1, :, local] = term.astype(BF)

        def a_keep(cols, local):
            self.hold[:, cols] = self.term(self.y, self.x, cols) + self.recv1[0, self.x, :, local].astype(F32)

        def b_keep(cols, local):
            self.hold[:, cols] = self.term(self.y, self.x, cols) + self.recv1[1, self.y, :, local].astype(F32)

        self.columns(0, a_out)
        self.columns(1, b_out)
        self.copies2 = [
            self.begin(
                self.links.copy(self.half_cols(self.send2.at[side]), self.half_cols(self.recv2.at[side]), device)
            )
            for side, device in ((0, {"x": 1 - self.x}), (1, {"y": 1 - self.y}))
        ]
        self.columns(0, a_keep)
        self.columns(1, b_keep)

    def third(self, out):
        for copy in self.copies2:
            copy.wait_recv()
        block = self.hold.shape[0] // self.length
        for side in range(2):

            def add(cols, local):
                total = self.hold[:, cols] + self.recv2[side, :, local].astype(F32)
                self.hold[:, cols] = total
                for level in range(self.length):
                    self.zpart[level, :, cols] = total[level * block : (level + 1) * block].astype(BF)

            self.columns(side, add)
        rows = pl.ds(pl.multiple_of(self.z * block, block), block)
        out[...] = self.all_cols(self.hold)[rows, :]
        self.line = LineSum(
            self.links,
            self.z,
            self.length,
            self.all_cols(self.zpart),
            lambda way, t: self.all_cols(self.zland.at[way, t - 1]),
        )

    def finish(self, out):
        self.line.finish(out, out)

    def drain(self):
        for copy in self.sent:
            copy.wait_send()
        self.line.drain()


def back_kernel(
    lengths_ref,
    tokens_v,
    dres_ref,
    first_ref,
    q_ref,
    kv_ref,
    mixed_ref,
    lse_ref,
    vec_ref,
    wkv_ref,
    vsum_ref,
    ubias_ref,
    wq_ref,
    wm_ref,
    red_ref,
    down_part,
    up_part,
    tgrad_ref,
    query_ref,
    mixer_ref,
    up_ref,
    vectors_ref,
    far_ref,
    down_last,
    w_v,
    dmix_v,
    dmixed_v,
    right_v,
    dfirst_v,
    dkv_v,
    keep_v,
    xsend_v,
    xrecv_v,
    csend_v,
    crecv_v,
    line_v,
    land_v,
    last_v,
    upsend_v,
    uprecv_v,
    vsend_v,
    vrecv_v,
    left_own,
    left_out,
    left_in,
    right_in,
    send1,
    recv1,
    send2,
    recv2,
    hold,
    zpart,
    zland,
    load_sem,
    credit,
    send_sems,
    recv_sems,
    *,
    length,
    slots,
    with_length,
    count,
):
    rows, width = tokens_v.shape
    seg = rows // slots
    both = wkv_ref.shape[1]
    head_dim = both // 2
    heads = width // head_dim
    group = 4
    y, c, z, x = [lax.axis_index(name) for name in ("y", "c", "z", "x")]
    place = y * 2 + c
    sib, to_x, to_y, diag = {"c": 1 - c}, {"x": 1 - x}, {"y": 1 - y}, {"x": 1 - x, "y": 1 - y}
    links = Links(send_sems, recv_sems, count)
    scale = head_dim ** (-0.5)

    def load(src, dst, n):
        copy = pltpu.make_async_copy(src, dst, load_sem.at[n])
        copy.start()
        return copy

    load_up = load(up_part, line_v.at[0], 0)
    load_down = load(down_part, line_v.at[1], 1)
    strip = w_v.shape[1]

    class Strips:
        def __init__(self, ref):
            self.ref, self.loads = ref, {}

        def start(self, j):
            if (j + 1) * strip <= width:
                self.loads[j] = load(self.ref.at[pl.ds(j * strip, strip)], w_v.at[j % 2], 2 + j % 2)

        def over(self, fn):
            for j in range(width // strip):
                self.loads[j].wait()
                fn(pl.ds(j * strip, strip), w_v.at[j % 2])
                self.start(j + 2)

    mixer_strips, query_strips = Strips(wm_ref), Strips(wq_ref)
    mixer_strips.start(0)
    mixer_strips.start(1)

    def landing(n, final):
        return lambda way, t: land_v.at[n, way, t - 1] if t < length - 1 else final.at[way]

    up_line = LineSum(links, z, length, line_v.at[0], landing(0, last_v))
    down_line = LineSum(links, z, length, line_v.at[1], landing(1, down_last))
    bufs = (left_own, left_out, left_in, right_in, send1, recv1, send2, recv2, hold, zpart, zland)
    where = (y, c, z, x)
    mixer = GradSum(links, where, length, width, width, mixed_ref, dmix_v, bufs)
    query = GradSum(links, where, length, width, width + both, first_ref, right_v, bufs)
    up_line.clear()
    for way, edge in ((0, 0), (1, length - 1)):
        @pl.when(z == edge)
        def clear_edge():
            zland[way, length - 2] = jnp.zeros(zland.shape[2:], BF)

    @pl.when(z == length - 1)
    def clear_hops():
        crecv_v[...] = jnp.zeros(crecv_v.shape, BF)

    barrier = pltpu.get_barrier_semaphore()
    plane = []
    for flip in range(1, 8):
        device = {"y": y ^ (flip // 4), "c": c ^ (flip // 2 % 2), "x": x ^ (flip % 2)}
        plane.append(device)
    for device in plane:
        pl.semaphore_signal(barrier, inc=1, device_id=device, device_id_type=MESH)
    for other in range(length):
        @pl.when(other != z)
        def hello():
            pl.semaphore_signal(barrier, inc=1, device_id={"z": other}, device_id_type=MESH)
    pl.semaphore_wait(barrier, 7 + length - 1)

    sent = []

    def begin(copy):
        copy.start()
        sent.append(copy)
        return copy

    def hand_over(base):
        for way, step in ((0, 1), (1, -1)):
            @pl.when((z + step >= 0) & (z + step < length))
            def free():
                pl.semaphore_signal(
                    credit.at[base + way], inc=1, device_id={"z": z + step}, device_id_type=MESH
                )

        for way, step in ((0, 1), (1, -1)):
            @pl.when((z - step >= 0) & (z - step < length))
            def freed():
                pl.semaphore_wait(credit.at[base + way], 1)

    load_up.wait()
    up_line.step(1)
    far = [
        links.copy(red_ref.at[k + 1], far_ref.at[k], device)
        for k, device in enumerate((to_x, to_y, diag))
    ]
    begin(far[0])
    begin(far[1])

    def to_bf(span):
        dmix_v[span, :] = dres_ref[span, :].astype(BF)

    for_rows(rows, to_bf)

    def mix_back(cols, strip_v):
        dmixed_v[:, cols] = dot(dmix_v[...], strip_v[...], ((1,), (1,))).astype(BF)

    mixer_strips.over(mix_back)
    query_strips.start(0)
    query_strips.start(1)

    def attend(s, g):
        lanes = pl.ds(pl.multiple_of(g * group * head_dim, group * head_dim), group * head_dim)
        span = pl.ds(s * seg, seg)

        def stack(wide):
            return jnp.concatenate(
                [wide[:, h * head_dim : (h + 1) * head_dim] for h in range(group)], axis=0
            )

        queries = stack(q_ref[span, lanes])
        d_mixed = stack(dmixed_v[span, lanes])
        inner = mixed_ref[span, lanes].astype(F32) * dmixed_v[span, lanes].astype(F32)
        delta = jnp.concatenate(
            [
                jnp.sum(inner[:, h * head_dim : (h + 1) * head_dim].T, axis=0, keepdims=True)
                for h in range(group)
            ],
            axis=1,
        )
        lse = lse_ref[s, g]

        def step(t, accum, diagonal):
            keys = kv_ref[s, t, :, :head_dim]
            values = kv_ref[s, t, :, head_dim:]
            scores = dot(keys, queries, ((1,), (1,))) * scale
            if diagonal or with_length:
                key_pos = lax.broadcasted_iota(jnp.int32, (2 * seg, seg), 0)
                allowed = None
                if diagonal:
                    query_pos = lax.broadcasted_iota(jnp.int32, (2 * seg, seg), 1) + x * seg
                    allowed = key_pos <= query_pos
                if with_length:
                    inside = key_pos + (z - t) * (2 * seg) < lengths_ref[s]
                    allowed = inside if allowed is None else allowed & inside
                bias = jnp.where(allowed, 0.0, NEG_LARGE).astype(F32)
                scores = scores + jnp.concatenate([bias] * group, axis=1)
            probs = jnp.exp(scores - lse)
            d_probs = dot(values, d_mixed, ((1,), (1,)))
            d_scores = (probs * (d_probs - delta)).astype(BF)
            dkv_v[t, :, :head_dim] += dot(d_scores, queries) * scale
            dkv_v[t, :, head_dim:] += dot(probs.astype(BF), d_mixed)
            return accum + dot(keys, d_scores, ((0,), (0,)))

        accum = step(0, jnp.zeros((head_dim, group * seg), F32), True)
        accum = lax.fori_loop(1, z + 1, lambda t, a: step(t, a, False), accum)
        right_v[span, lanes] = (
            jnp.concatenate([accum[:, h * seg : (h + 1) * seg].T for h in range(group)], axis=1) * scale
        ).astype(BF)

    x_copies = []
    for s in range(slots):
        for t in range(length):
            dkv_v[t] = jnp.zeros(dkv_v.shape[1:], F32)

        @pl.loop(0, heads // group)
        def over_groups(g):
            attend(s, g)

        for t in range(length):
            keep_v[s, t] = dkv_v[t, pl.ds(pl.multiple_of(x * seg, seg), seg), :].astype(BF)
            xsend_v[s, t] = dkv_v[t, pl.ds(pl.multiple_of((1 - x) * seg, seg), seg), :].astype(BF)
        x_copies.append(begin(links.copy(xsend_v.at[s], xrecv_v.at[s], to_x)))
        if s == 0:
            load_down.wait()
            down_line.step(1)
            mixer.share()

    up_line.step(2)
    mixer.first()
    begin(far[2])

    for copy in x_copies:
        copy.wait_recv()
    hops = [links.copy(csend_v.at[t - 1], crecv_v.at[t - 1], {"z": z - 1}) for t in range(1, length)]
    for t in range(length - 1, -1, -1):
        @pl.when(t <= z)
        def hop():
            if t + 1 < length:
                @pl.when(z < length - 1)
                def arrive():
                    hops[t].wait_recv()

            total = keep_v[:, t].astype(F32) + xrecv_v[:, t].astype(F32)
            if t + 1 < length:
                total = total + crecv_v[t].astype(F32)
            if t:
                csend_v[t - 1] = total.astype(BF)
                hops[t - 1].start()
            else:
                for s in range(slots):
                    right_v[s * seg : (s + 1) * seg, width:] = total[s].astype(BF)

    def first_back(cols, strip_v):
        dfirst_v[:, cols] = dot(right_v[:, :width], strip_v[...], ((1,), (1,))) + dot(
            right_v[:, width:], wkv_ref[cols, :], ((1,), (1,))
        )

    query_strips.over(first_back)
    mixer.second()
    down_line.step(2)

    mixer.third(mixer_ref)
    mixer.line.step(1)
    neighbours = ((0, sib), (1, to_y), (2, to_x))
    for n, device in neighbours:
        pl.semaphore_signal(credit.at[n], inc=1, device_id=device, device_id_type=MESH)
    for n, _ in neighbours:
        pl.semaphore_wait(credit.at[n], 1)
    for copy in mixer.sent:
        copy.wait_send()
    query.share()
    query.first()

    vsend_v[0] = jnp.zeros(vsend_v.shape[1:], F32)

    def first_norm_back(span):
        unit, rstd = norm_rows(tokens_v[span, :].astype(F32))
        d_first = dfirst_v[span, :]
        tgrad_ref[span, :] = (
            dres_ref[span, :] + norm_backward(d_first, unit, rstd, vec_ref[0:1, :])
        ).astype(BF)
        vsend_v[0, 0:1, :] += jnp.sum(d_first * unit, axis=0, keepdims=True)
        vsend_v[0, 1:2, :] += jnp.sum(d_first, axis=0, keepdims=True)
        d_right = right_v[span, :].astype(F32)
        vsend_v[0, 2:3, :] += jnp.sum(d_right[:, :width], axis=0, keepdims=True)
        vsend_v[0, 3:4, 0:both] += jnp.sum(d_right[:, width:], axis=0, keepdims=True)

    for_rows(rows, first_norm_back)
    vsend_v[0, 4:8, :] = vsum_ref[0:4, :]
    vsend_v[0, 8:9, 0 : ubias_ref.shape[1]] = ubias_ref[...]

    partners = [(sib, 8), (to_x, 8), (to_y, 8)]
    bit = 1
    while bit < length:
        partners.append(({"z": z ^ bit}, 16))
        bit *= 2

    def exchange(n):
        device, high = partners[n]
        copy = begin(links.copy(vsend_v.at[n, pl.ds(0, high)], vrecv_v.at[n, pl.ds(0, high)], device))

        def land():
            copy.wait_recv()
            out = vectors_ref if n + 1 == len(partners) else vsend_v.at[n + 1]
            out[0:high, :] = vsend_v[n, 0:high, :] + vrecv_v[n, 0:high, :]
            if high == 8:
                out[8:16, :] = vsend_v[n, 8:16, :]

        return land

    land = exchange(0)
    up_line.step(3)
    land()
    land = exchange(1)
    mixer.line.step(2)
    land()
    land = exchange(2)
    query.second()
    land()
    land = exchange(3)
    down_line.step(3)
    for t in range(3, length):
        mixer.line.step(t)
    land()
    land = exchange(4)
    mixer.finish(mixer_ref)
    mixer.line.drain()
    hand_over(3)
    query.third(query_ref)
    query.line.step(1)
    land()

    upsum_v = dmixed_v
    up_line.finish(line_v.at[0, z], upsum_v)
    hidden = upsum_v.shape[1] // 2
    piece = upsum_v.shape[0] // 2
    block = piece // 2
    for f in range(4):
        for x_part in range(2):
            start = (f % 2) * piece + x_part * block
            lanes = slice((f // 2) * hidden, (f // 2 + 1) * hidden)
            upsend_v[f * 2 + x_part] = upsum_v[start : start + block, lanes]
    mine = place * 2 + x
    up_copies = []
    for flip, device in zip(range(1, 8), plane):
        up_copies.append(begin(links.copy(upsend_v.at[mine ^ flip], uprecv_v.at[flip], device)))
    out_block = hidden // length

    def place_up(flip, ref):
        source = mine ^ flip
        base = (source // 2) * (2 * hidden) + (source % 2) * out_block
        for level in range(length):
            lanes = pl.ds(pl.multiple_of(base + level * 2 * out_block, out_block), out_block)
            up_ref[:, lanes] = ref[:, level * out_block : (level + 1) * out_block].astype(up_ref.dtype)

    query.line.step(2)
    place_up(0, upsend_v.at[mine])
    for flip, copy in zip(range(1, 8), up_copies):
        copy.wait_recv()
        place_up(flip, uprecv_v.at[flip])
    for t in range(3, length):
        query.line.step(t)
    for copy in far:
        copy.wait_recv()
    query.finish(query_ref)
    for way in range(2):
        @pl.when(down_line.position(way) >= 1)
        def down_landed():
            down_line.copies[way, length - 1].wait_recv()
    for copy in sent:
        copy.wait_send()
    query.drain()
    up_line.drain()
    down_line.drain()
    for t in range(1, length):
        @pl.when(t <= z)
        def hopped():
            hops[t - 1].wait_send()


def back(lengths, vmem_args, hbm_args, slots, length, with_length):
    tokens, kv, wkv = vmem_args[0], vmem_args[4], vmem_args[8]
    rows, width = tokens.shape
    seg = rows // slots
    both = wkv.shape[1]
    cols = width + both
    hidden = width // 2
    block = width // (8 * length)
    stages = 3 + (length - 1).bit_length()
    count = 96 + 12 * length
    hbm = pl.BlockSpec(memory_space=pltpu.HBM)
    vmem = pl.BlockSpec(memory_space=pltpu.VMEM)
    sems = pltpu.SemaphoreType.DMA

    def half(*dims):
        return pltpu.VMEM(dims, BF)

    return pl.pallas_call(
        functools.partial(
            back_kernel, length=length, slots=slots, with_length=with_length, count=count
        ),
        in_specs=[pl.BlockSpec(memory_space=pltpu.SMEM)]
        + [vmem] * len(vmem_args)
        + [hbm] * len(hbm_args),
        out_specs=[vmem] * 5 + [hbm, hbm],
        out_shape=[
            jax.ShapeDtypeStruct((rows, width), BF),
            jax.ShapeDtypeStruct((block, cols), F32),
            jax.ShapeDtypeStruct((block, width), F32),
            jax.ShapeDtypeStruct((block, 8 * hidden), BF),
            jax.ShapeDtypeStruct((16, width), F32),
            jax.ShapeDtypeStruct((3, rows, width), BF),
            jax.ShapeDtypeStruct((2, hidden // length, width), BF),
        ],
        scratch_shapes=[
            half(2, width // 4, width),
            half(rows, width),
            half(rows, width),
            half(rows, cols),
            pltpu.VMEM((rows, width), F32),
            pltpu.VMEM((length, 2 * seg, both), F32),
            half(slots, length, seg, both),
            half(slots, length, seg, both),
            half(slots, length, seg, both),
            half(length - 1, slots, seg, both),
            half(length - 1, slots, seg, both),
            half(2, length, hidden // length, width),
            half(2, 2, length - 2, hidden // length, width),
            half(2, hidden // length, width),
            half(8, block, hidden),
            half(8, block, hidden),
            pltpu.VMEM((stages, 16, width), F32),
            pltpu.VMEM((stages, 16, width), F32),
            half(4, width // 8, rows),
            half(4, width // 8, rows),
            half(4, width // 8, rows),
            half(rows, cols),
            half(2, 2, width // 8, cols // 2),
            half(2, 2, width // 8, cols // 2),
            half(2, width // 8, cols // 2),
            half(2, width // 8, cols // 2),
            pltpu.VMEM((width // 8, cols), F32),
            half(length, block, cols),
            half(2, length - 1, block, cols),
            sems((4,)),
            pltpu.SemaphoreType.REGULAR((5,)),
            sems((count,)),
            sems((count,)),
        ],
        compiler_params=pltpu.CompilerParams(
            collective_id=3, has_side_effects=True, vmem_limit_bytes=62 << 20
        ),
        cost_estimate=pl.CostEstimate(
            flops=12 * rows * width * width, bytes_accessed=40 << 20, transcendentals=0
        ),
    )(lengths, *vmem_args, *hbm_args)


def finish_fast(given, kept, weights):
    tokens, lengths, d_down, up_weight, down_weight, up_bias, where, slots, length, with_length = given
    second, residual, first, queries, kv_all, mixed, lse, vectors = kept
    full_query, full_mixer, full_keyval, up_mine, down_all = weights
    y, c, z, x = where
    rows, width = second.shape
    flat = tokens.reshape(rows, width)
    d_residual, reduced, down_part, up_part, ubias_part, vsum = feed(
        second, d_down, down_all, up_mine, up_weight, up_bias, residual, vectors, down_weight, length
    )
    tokens_grad, query_all, mixer_grad, up_grad, sums, far, down_last = back(
        lengths,
        (flat, d_residual, first, queries, kv_all, mixed, lse, vectors, full_keyval, vsum, ubias_part),
        (full_query, full_mixer, reduced, down_part.reshape(length, -1, width), up_part),
        slots,
        length,
        with_length,
    )
    down_grad = pick(down_part.reshape(length, -1, width), z, 0).astype(F32)
    down_grad = down_grad + jnp.where(z > 0, down_last[0].astype(F32), 0.0)
    down_grad = down_grad + jnp.where(z < length - 1, down_last[1].astype(F32), 0.0)
    output = residual + vectors[6:7]
    for term in (reduced[0], far[0], far[1], far[2]):
        output = output + term.astype(F32)
    layer_out = output.astype(BF).reshape(tokens.shape)
    devices = 8 * length
    index = (y * 2 + c) * 2 * length + z * 2 + x
    block = width // devices
    mine = lax.dynamic_slice_in_dim(sums[:8], index * block, block, 1)
    head_dim = full_keyval.shape[1] // 2
    v_block = head_dim // devices
    vbias = lax.dynamic_slice_in_dim(sums[3], head_dim + index * v_block, v_block, 0)
    u_block = up_bias.shape[1] // length
    ubias = lax.dynamic_slice_in_dim(sums[8], z * u_block, u_block, 0)
    return (
        layer_out,
        tokens_grad.reshape(tokens.shape),
        mine[0],
        mine[1],
        query_all[:, :width],
        mine[2],
        query_all[:, width:],
        vbias,
        mixer_grad,
        mine[6],
        mine[4],
        mine[5],
        up_grad.astype(F32),
        ubias,
        down_grad,
        mine[7],
    )


def body(
    tokens,
    lengths,
    cotangent,
    norm_gain,
    norm_shift,
    query_weight,
    query_bias,
    keyval_weight,
    value_bias,
    mixer_weight,
    mixer_bias,
    ffnorm_gain,
    ffnorm_shift,
    up_weight,
    up_bias,
    down_weight,
    down_bias,
):
    y, c, z, x = [lax.axis_index(name) for name in ("y", "c", "z", "x")]
    length = lax.axis_size("z")
    place = y * 2 + c
    slots, seg, width = tokens.shape
    rows = slots * seg
    head_dim = value_bias.shape[0] * 4
    hidden = up_weight.shape[1]
    hidden_block = hidden // (8 * length)
    hidden_mine = hidden // 8
    with_length = 2 * length * seg > MIN_LEN
    scal = jnp.concatenate([jnp.stack([z, x]).astype(jnp.int32), lengths])

    quarter = width // 4
    v_part = value_bias.shape[0]
    v_place = lax.dynamic_update_slice(jnp.zeros((quarter,), BF), value_bias, (place * v_part,))
    small = jnp.stack(
        [norm_gain, norm_shift, query_bias, mixer_bias, ffnorm_gain, ffnorm_shift, down_bias, v_place]
    )
    small = jnp.concatenate([small, jnp.zeros_like(small)], axis=0)

    down_mine = pick(down_weight.reshape(length, 2, hidden_block, width), x, 1).reshape(
        hidden_mine, width
    )
    up_bias_mine = pick(up_bias.reshape(length, 2, hidden_block), x, 1).reshape(1, hidden_mine)
    aligned = hidden_block % 128 == 0
    up_given = up_weight
    if not aligned:
        up_given = pick(up_weight.reshape(quarter, 4, length, 2, hidden_block), x, 3)
        up_given = up_given.reshape(quarter, 4, hidden_mine).transpose(1, 0, 2)

    token_pos = (z * 2 + x) * seg + jnp.arange(seg, dtype=jnp.int32)
    valid = (token_pos[None, :] < lengths[:, None]).astype(F32).reshape(rows, 1)
    d_down = cotangent.reshape(rows, width)
    if with_length:
        d_down = (d_down.astype(F32) * valid).astype(BF)
    d_out = d_down.astype(F32)

    flat = tokens.reshape(rows, width)
    (
        second,
        residual,
        first,
        queries,
        kv_all,
        mixed,
        lse,
        vectors,
        full_query,
        full_mixer,
        full_keyval,
        up_mine,
        down_all,
    ) = front(
        lengths,
        flat,
        small,
        keyval_weight,
        query_weight,
        mixer_weight,
        up_given,
        d_down,
        slots,
        length,
        with_length,
        aligned,
        hidden_mine,
    )
    if aligned and length == 4:
        return finish_fast(
            (
                tokens,
                lengths,
                d_down,
                up_weight,
                down_weight,
                up_bias_mine.astype(F32),
                (y, c, z, x),
                slots,
                length,
                with_length,
            ),
            (second, residual, first, queries, kv_all, mixed, lse, vectors),
            (full_query, full_mixer, full_keyval, up_mine, down_all.reshape(8 * rows, width)),
        )
    inputs = flat.astype(F32)
    gain, ffgain, d_bias = vectors[0:1], vectors[4:5], vectors[6:7]
    unit1, rstd1 = norm_stats(inputs)
    unit2, rstd2 = norm_stats(residual)
    q_t, mixed_t = queries.T, mixed.T

    d_second, out_parts, down_part, up_part, ubias_part = ffn(
        second,
        down_all.reshape(8 * rows, width),
        up_mine,
        up_bias_mine.astype(F32),
        down_mine,
        length,
    )
    output = residual + scatter_plane([out_parts[i] for i in range(4)]) + d_bias
    layer_out = output.astype(BF).reshape(tokens.shape)
    down_grad = scatter_line(down_part.reshape(length, hidden_block, width), z, length)
    ubias_grad = scatter_line(ubias_part.reshape(length, hidden_block), z, length)
    out_rows = width // (8 * length)
    up_sum = scatter_line(up_part, z, length).astype(BF)
    up_rows = lax.all_to_all(
        up_sum.reshape(8, out_rows, hidden_mine), ("y", "c", "x"), 0, 0, tiled=True
    )
    up_grad = (
        up_rows.reshape(4, 2, out_rows, length, hidden_block)
        .transpose(2, 0, 3, 1, 4)
        .reshape(out_rows, hidden)
        .astype(F32)
    )

    d_residual = d_out + norm_backward(d_second, unit2, rstd2, ffgain)
    d_mix = d_residual.astype(BF)
    d_mixed_t = dot(full_mixer, d_mix, ((1,), (1,))).astype(BF)
    where = (y, c, z, x)
    sizes = (length, width)
    mixer_all = scatter_all(
        mixed,
        d_mix,
        (
            jnp.sum(d_mix.astype(F32), axis=0),
            jnp.sum(d_second * unit2, axis=0),
            jnp.sum(d_second, axis=0),
            jnp.sum(d_out, axis=0),
        ),
        where,
        sizes,
    )

    dq_t, dkv = attn_backward(scal, q_t, kv_all, mixed_t, d_mixed_t, lse, 4, with_length)
    dkv = dkv.reshape(slots, length, 2, seg, 2 * head_dim)
    running = None
    for step in range(length - 1, -1, -1):
        term = dkv[:, step]
        term = pick(term, x, 1) + swap(pick(term, 1 - x, 1).astype(BF), "x").astype(F32)
        if running is not None:
            term = term + lax.ppermute(
                running.astype(BF), "z", [(i, i - 1) for i in range(1, length)]
            ).astype(F32)
        running = term
    d_keyvals = running.reshape(rows, 2 * head_dim).astype(BF)
    d_first = dot(dq_t, full_query, ((0,), (1,))) + dot(d_keyvals, full_keyval, ((1,), (1,)))
    tokens_grad = (d_residual + norm_backward(d_first, unit1, rstd1, gain)).astype(BF)
    d_queries = dq_t.T
    devices = 8 * length
    vbias = jnp.sum(d_keyvals[:, head_dim:].astype(F32), axis=0)
    vbias = jnp.pad(
        vbias.reshape(devices, head_dim // devices),
        ((0, 0), (0, out_rows - head_dim // devices)),
    ).reshape(width)
    query_all = scatter_all(
        first,
        jnp.concatenate([d_queries, d_keyvals], axis=1),
        (
            jnp.sum(d_first * unit1, axis=0),
            jnp.sum(d_first, axis=0),
            jnp.sum(d_queries.astype(F32), axis=0),
            vbias,
        ),
        where,
        sizes,
    )
    kv_end = width + 2 * head_dim
    return (
        layer_out,
        tokens_grad.reshape(tokens.shape),
        query_all[:, kv_end],
        query_all[:, kv_end + 1],
        query_all[:, :width],
        query_all[:, kv_end + 2],
        query_all[:, width:kv_end],
        query_all[: head_dim // devices, kv_end + 3],
        mixer_all[:, :width],
        mixer_all[:, width],
        mixer_all[:, width + 1],
        mixer_all[:, width + 2],
        up_grad,
        ubias_grad,
        down_grad,
        mixer_all[:, width + 3],
    )


def solution(mesh):
    ctx = mesh.shape["ctx"]
    fine = Mesh(mesh.devices.reshape(2, 2, ctx // 2, 2), ("y", "c", "z", "x"))
    fsdp, both, every = ("y", "c"), ("z", "x"), ("y", "c", "z", "x")
    return jax.shard_map(
        body,
        mesh=fine,
        in_specs=(
            P(fsdp, both, None),
            P(fsdp),
            P(fsdp, both, None),
            P(fsdp),
            P(fsdp),
            P(fsdp, None),
            P(fsdp),
            P(fsdp, None),
            P(fsdp),
            P(fsdp, None),
            P(fsdp),
            P(fsdp),
            P(fsdp),
            P(fsdp, None),
            P(fsdp),
            P(fsdp, None),
            P(fsdp),
        ),
        out_specs=(
            P(fsdp, both, None),
            P(fsdp, both, None),
            P(every),
            P(every),
            P(every, None),
            P(every),
            P(every, None),
            P(every),
            P(every, None),
            P(every),
            P(every),
            P(every),
            P(every, None),
            P(every),
            P(every, None),
            P(every),
        ),
        check_vma=False,
    )
```

```python
import functools

import jax
import jax.numpy as jnp
from jax import lax
from jax.experimental import pallas as pl
from jax.experimental.pallas import tpu as pltpu
from jax.sharding import Mesh, PartitionSpec as P

EPSILON = 1e-05
NEG_LARGE = -1e30
MIN_LEN = 1024
BF = jnp.bfloat16
F32 = jnp.float32
GELU_K = 0.7978845608028654
GELU_C = 0.044715


def dot(left_side, right_side, dims=((1,), (0,))):
    return lax.dot_general(left_side, right_side, (dims, ((), ())), preferred_element_type=F32)


def swap(values, axis):
    return lax.ppermute(values, axis, [(0, 1), (1, 0)])


def pick(values, index, axis):
    return lax.dynamic_index_in_dim(values, index, axis, keepdims=False)


def stack_heads(block, head_dim):
    heads = block.shape[0] // head_dim
    return jnp.concatenate([block[h * head_dim : (h + 1) * head_dim] for h in range(heads)], axis=1)


def unstack_heads(stacked, seg):
    heads = stacked.shape[1] // seg
    return jnp.concatenate([stacked[:, h * seg : (h + 1) * seg] for h in range(heads)], axis=0)


def masked_scores(scal_ref, queries, keys, step, seg, heads, with_length, first_block):
    scores = dot(keys, queries) * (keys.shape[1] ** (-0.5))
    pair = keys.shape[0]
    if not (with_length or first_block):
        return scores
    key_pos = lax.broadcasted_iota(jnp.int32, (pair, seg), 0)
    allowed = None
    if first_block:
        query_pos = lax.broadcasted_iota(jnp.int32, (pair, seg), 1) + scal_ref[1] * seg
        allowed = key_pos <= query_pos
    if with_length:
        length = scal_ref[2 + pl.program_id(0)]
        inside = key_pos + (scal_ref[0] - step) * pair < length
        allowed = inside if allowed is None else allowed & inside
    bias = jnp.where(allowed, 0.0, NEG_LARGE).astype(F32)
    return scores + jnp.concatenate([bias] * heads, axis=1)


def attn_fwd_kernel(scal_ref, q_ref, kv_ref, out_ref, lse_ref, *, with_length):
    head_dim = kv_ref.shape[-1] // 2
    seg = q_ref.shape[1]
    heads = q_ref.shape[0] // head_dim
    queries = stack_heads(q_ref[...], head_dim)

    def block(step, state, first_block):
        top, total, accum = state
        keys = kv_ref[0, step, :, :head_dim]
        values = kv_ref[0, step, :, head_dim:]
        scores = masked_scores(scal_ref, queries, keys, step, seg, heads, with_length, first_block)
        new_top = jnp.maximum(top, jnp.max(scores, axis=0, keepdims=True))
        terms = jnp.exp(scores - new_top)
        fade = jnp.exp(top - new_top)
        total = total * fade + jnp.sum(terms, axis=0, keepdims=True)
        accum = accum * fade + dot(values, terms.astype(BF), ((0,), (0,)))
        return new_top, total, accum

    lanes = heads * seg
    state = (
        jnp.full((1, lanes), NEG_LARGE, F32),
        jnp.zeros((1, lanes), F32),
        jnp.zeros((head_dim, lanes), F32),
    )
    state = block(0, state, True)
    top, total, accum = lax.fori_loop(1, scal_ref[0] + 1, lambda t, s: block(t, s, False), state)
    out_ref[...] = unstack_heads(accum / total, seg).astype(BF)
    lse_ref[0, 0] = top + jnp.log(total)


def attn_bwd_kernel(scal_ref, q_ref, kv_ref, out_ref, dout_ref, lse_ref, dq_ref, dkv_ref, *, with_length):
    head_dim = kv_ref.shape[-1] // 2
    seg = q_ref.shape[1]
    heads = q_ref.shape[0] // head_dim
    scale = head_dim ** (-0.5)
    queries = stack_heads(q_ref[...], head_dim)
    d_mixed = stack_heads(dout_ref[...], head_dim)
    mixed = stack_heads(out_ref[...], head_dim)
    delta = jnp.sum(mixed.astype(F32) * d_mixed.astype(F32), axis=0, keepdims=True)
    lse = lse_ref[0, 0]

    @pl.when(pl.program_id(1) == 0)
    def clear():
        dkv_ref[...] = jnp.zeros_like(dkv_ref)

    def block(step, accum, first_block):
        keys = kv_ref[0, step, :, :head_dim]
        values = kv_ref[0, step, :, head_dim:]
        scores = masked_scores(scal_ref, queries, keys, step, seg, heads, with_length, first_block)
        probs = jnp.exp(scores - lse)
        d_probs = dot(values, d_mixed)
        d_scores = (probs * (d_probs - delta)).astype(BF)
        dkv_ref[0, step, :, :head_dim] += dot(d_scores, queries, ((1,), (1,))) * scale
        dkv_ref[0, step, :, head_dim:] += dot(probs.astype(BF), d_mixed, ((1,), (1,)))
        return accum + dot(keys, d_scores, ((0,), (0,)))

    accum = block(0, jnp.zeros((head_dim, heads * seg), F32), True)
    accum = lax.fori_loop(1, scal_ref[0] + 1, lambda t, s: block(t, s, False), accum)
    dq_ref[...] = (unstack_heads(accum, seg) * scale).astype(BF)


def attn_specs(slots, steps, pair, seg, rows, groups, head_dim):
    lanes = rows // groups // head_dim * seg
    scal = pl.BlockSpec(memory_space=pltpu.SMEM)
    feat = pl.BlockSpec((rows // groups, seg), lambda s, g: (g, s))
    kv = pl.BlockSpec((1, steps, pair, 2 * head_dim), lambda s, g: (s, 0, 0, 0))
    lse = pl.BlockSpec((1, 1, 1, lanes), lambda s, g: (s, g, 0, 0))
    return scal, feat, kv, lse, lanes


def attn_forward(scal, q_t, kv, groups, with_length):
    slots, steps, pair, width = kv.shape
    rows, cols = q_t.shape
    seg = cols // slots
    scal_s, feat, kv_s, lse_s, lanes = attn_specs(slots, steps, pair, seg, rows, groups, width // 2)
    return pl.pallas_call(
        functools.partial(attn_fwd_kernel, with_length=with_length),
        grid=(slots, groups),
        in_specs=[scal_s, feat, kv_s],
        out_specs=[feat, lse_s],
        out_shape=[
            jax.ShapeDtypeStruct((rows, cols), BF),
            jax.ShapeDtypeStruct((slots, groups, 1, lanes), F32),
        ],
        compiler_params=pltpu.CompilerParams(vmem_limit_bytes=40 << 20),
        cost_estimate=pl.CostEstimate(
            flops=4 * rows * cols * steps * pair, bytes_accessed=6 << 20, transcendentals=0
        ),
    )(scal, q_t, kv)


def attn_backward(scal, q_t, kv, out_t, dout_t, lse, groups, with_length):
    slots, steps, pair, width = kv.shape
    rows, cols = q_t.shape
    seg = cols // slots
    scal_s, feat, kv_s, lse_s, lanes = attn_specs(slots, steps, pair, seg, rows, groups, width // 2)
    return pl.pallas_call(
        functools.partial(attn_bwd_kernel, with_length=with_length),
        grid=(slots, groups),
        in_specs=[scal_s, feat, kv_s, feat, feat, lse_s],
        out_specs=[feat, kv_s],
        out_shape=[
            jax.ShapeDtypeStruct((rows, cols), BF),
            jax.ShapeDtypeStruct(kv.shape, F32),
        ],
        compiler_params=pltpu.CompilerParams(vmem_limit_bytes=48 << 20),
        cost_estimate=pl.CostEstimate(
            flops=10 * rows * cols * steps * pair, bytes_accessed=9 << 20, transcendentals=0
        ),
    )(scal, q_t, kv, out_t, dout_t, lse)


def norm_stats(values):
    center = values - jnp.mean(values, axis=-1, keepdims=True)
    spread = jnp.mean(center * center, axis=-1, keepdims=True)
    rstd = lax.rsqrt(spread + EPSILON)
    return center * rstd, rstd


def norm_backward(d_values, unit, rstd, gain):
    scaled = d_values * gain
    return rstd * (
        scaled
        - jnp.mean(scaled, axis=-1, keepdims=True)
        - unit * jnp.mean(scaled * unit, axis=-1, keepdims=True)
    )


def gather_rows(shard, x, place):
    rows = shard.shape[0]
    half = rows // 2
    mine = lax.dynamic_slice_in_dim(shard, x * half, half, 0)
    direct = swap(mine, "y")
    other = swap(direct, "x")
    sib = swap(shard, "c")
    sib_direct = swap(direct, "c")
    sib_other = swap(other, "c")
    full = jnp.zeros((4 * rows,) + shard.shape[1:], shard.dtype)
    far = place ^ 2
    pieces = (
        (shard, place * rows),
        (sib, (place ^ 1) * rows),
        (direct, far * rows + x * half),
        (other, far * rows + (1 - x) * half),
        (sib_direct, (far ^ 1) * rows + x * half),
        (sib_other, (far ^ 1) * rows + (1 - x) * half),
    )
    for piece, start in pieces:
        full = lax.dynamic_update_slice_in_dim(full, piece, start, 0)
    return full


def gather_plane(block):
    half = block.shape[0] // 2
    from_x = swap(block, "x")
    from_y = swap(block, "y")
    diag = jnp.concatenate([swap(from_y[:half], "x"), swap(from_x[half:], "y")], axis=0)
    return [
        jnp.concatenate([part, swap(part, "c")], axis=0) for part in (block, from_x, from_y, diag)
    ]


def scatter_plane(parts):
    rows = parts[0].shape[0] // 2
    half = rows // 2
    own, to_x, to_y, diag = [
        part[:rows].astype(F32) + swap(part[rows:].astype(BF), "c").astype(F32) for part in parts
    ]
    via_x = swap(diag[:half].astype(BF), "x").astype(F32)
    via_y = swap(diag[half:].astype(BF), "y").astype(F32)
    to_y = jnp.concatenate([to_y[:half] + via_x, to_y[half:]], axis=0)
    to_x = jnp.concatenate([to_x[:half], to_x[half:] + via_y], axis=0)
    return own + swap(to_x.astype(BF), "x").astype(F32) + swap(to_y.astype(BF), "y").astype(F32)


def scatter_line(parts, z, length):
    def block(index):
        return pick(parts, jnp.clip(index, 0, length - 1), 0).astype(F32)

    from_left = from_right = None
    for step in range(1, length):
        up = block(length - step + z)
        down = block(z - length + step)
        if from_left is not None:
            up, down = up + from_left, down + from_right
        from_left = lax.ppermute(up.astype(BF), "z", [(i, i + 1) for i in range(step)]).astype(F32)
        from_right = lax.ppermute(
            down.astype(BF), "z", [(i, i - 1) for i in range(length - step, length)]
        ).astype(F32)
    return block(z) + from_left + from_right


def scatter_all(left_side, right_side, vectors, place_yczx, sizes):
    y, c, z, x = place_yczx
    length, width = sizes
    tokens = left_side.shape[0]
    block = width // (8 * length)
    left_parts = left_side.reshape(tokens, 2, 2, width // 4)
    left_mine = pick(left_parts, c, 2).reshape(tokens, width // 2)
    left_sib = swap(pick(left_parts, 1 - c, 2), "c").reshape(tokens, width // 2)
    right_sib = swap(right_side, "c")
    partial = dot(
        jnp.concatenate([left_mine, left_sib], axis=0),
        jnp.concatenate([right_side, right_sib], axis=0),
        ((0,), (0,)),
    )
    extra = jnp.pad(jnp.stack(vectors, axis=1), ((0, 0), (0, 128 - len(vectors))))
    extra = extra.reshape(2, 2, width // 4, 128)
    extra = pick(extra, c, 1) + swap(pick(extra, 1 - c, 1).astype(BF), "c").astype(F32)
    partial = jnp.concatenate([partial, extra.reshape(width // 2, 128)], axis=1)
    cols = partial.shape[1]
    partial = partial.reshape(2, length, 2, block, cols)
    cut = (cols // 256) * 128
    side_a, side_b = partial[..., :cut], partial[..., cut:]
    side_a = pick(side_a, y, 0) + swap(pick(side_a, 1 - y, 0).astype(BF), "y").astype(F32)
    side_b = pick(side_b, x, 2) + swap(pick(side_b, 1 - x, 2).astype(BF), "x").astype(F32)
    side_a = pick(side_a, x, 1) + swap(pick(side_a, 1 - x, 1).astype(BF), "x").astype(F32)
    side_b = pick(side_b, y, 0) + swap(pick(side_b, 1 - y, 0).astype(BF), "y").astype(F32)
    return scatter_line(jnp.concatenate([side_a, side_b], axis=-1), z, length)


MESH = pl.DeviceIdType.MESH


def remote(src, dst, send_sems, recv_sems, index, device):
    return pltpu.make_async_remote_copy(
        src_ref=src,
        dst_ref=dst,
        send_sem=send_sems.at[index],
        recv_sem=recv_sems.at[index],
        device_id=device,
        device_id_type=MESH,
    )


def greet(devices):
    barrier = pltpu.get_barrier_semaphore()
    for device in devices:
        pl.semaphore_signal(barrier, inc=1, device_id=device, device_id_type=MESH)
    pl.semaphore_wait(barrier, len(devices))


def tiles(count, size):
    def over(fn):
        @pl.loop(0, count)
        def step(index):
            fn(pl.ds(pl.multiple_of(index * size, size), size), index)

    return over


def gelu_pair(upper):
    inner = jnp.tanh(upper * (GELU_K + (GELU_K * GELU_C) * (upper * upper)))
    half = 0.5 + 0.5 * inner
    slope = half + (0.5 * upper) * (1.0 - inner * inner) * (
        GELU_K + (3.0 * GELU_K * GELU_C) * (upper * upper)
    )
    return upper * half, slope


def ffn_kernel(
    second_ref,
    down_all_ref,
    up_ref,
    ubias_ref,
    down_ref,
    dsecond_ref,
    out_parts_ref,
    down_part_ref,
    up_part_ref,
    ubias_part_ref,
    tokens_v,
    cots_v,
    up_v,
    down_v,
    active_v,
    dupper_v,
    sib_out,
    sib_in,
    chip_out,
    chip_in,
    acc_v,
    stage_v,
    load_sem,
    stage_sem,
    gs_send,
    gs_recv,
    rs_send,
    rs_recv,
    *,
    length,
):
    rows, width = second_ref.shape
    hidden = up_ref.shape[1]
    half = rows // 2
    chunk = 2 * rows
    y, c, x = [lax.axis_index(name) for name in ("y", "c", "x")]
    sib, to_x, to_y = {"c": 1 - c}, {"x": 1 - x}, {"y": 1 - y}
    diag = {"x": 1 - x, "y": 1 - y}
    chips = (None, to_x, to_y, diag)

    loads = [
        pltpu.make_async_copy(second_ref, tokens_v.at[0, pl.ds(0, rows)], load_sem.at[0]),
        pltpu.make_async_copy(down_ref, down_v, load_sem.at[1]),
        pltpu.make_async_copy(down_all_ref, cots_v, load_sem.at[2]),
        pltpu.make_async_copy(up_ref, up_v, load_sem.at[3]),
    ]
    for load in loads:
        load.start()
    greet((sib, to_x, to_y, diag))
    loads[0].wait()

    same, other = pl.ds(0, rows), pl.ds(rows, rows)
    top, bottom = pl.ds(0, half), pl.ds(half, half)

    def gather(index, chip, span_src, chip_dst, span_dst, device):
        return remote(
            tokens_v.at[chip, span_src], tokens_v.at[chip_dst, span_dst], gs_send, gs_recv, index, device
        )

    send_x = gather(0, 0, same, 1, same, to_x)
    send_y = gather(1, 0, same, 2, same, to_y)
    share = [gather(2 + k, k, same, k, other, sib) for k in range(4)]
    diag_x = gather(6, 2, top, 3, top, to_x)
    diag_y = gather(7, 1, bottom, 3, bottom, to_y)
    send_x.start()
    send_y.start()
    share[0].start()

    loads[1].wait()
    loads[2].wait()

    @tiles(4 * chunk // 512, 512)
    def grad_active(span, index):
        @tiles(hidden // 512, 512)
        def columns(cols, _):
            dupper_v[span, cols] = dot(cots_v[span, :], down_v[cols, :], ((1,), (1,))).astype(BF)

    loads[3].wait()

    def chip_work(k):
        @tiles(hidden // 256, 256)
        def columns(cols, _):
            block = pl.ds(k * chunk, chunk)
            upper = dot(tokens_v[k], up_v[:, cols]) + ubias_ref[:, cols]
            active, slope = gelu_pair(upper)
            active_v[block, cols] = active.astype(BF)
            d_upper = (dupper_v[block, cols].astype(F32) * slope).astype(BF)
            dupper_v[block, cols] = d_upper
            part = jnp.sum(d_upper.astype(F32), axis=0, keepdims=True)
            if k == 0:
                ubias_part_ref[:, cols] = part
            else:
                ubias_part_ref[:, cols] += part

        @tiles(width // 512, 512)
        def to_sibling(cols, _):
            sib_out[k, :, cols] = dot(
                dupper_v[pl.ds(k * chunk + rows, rows), :], up_v[cols, :], ((1,), (1,))
            ).astype(BF)

        pair = remote(sib_out.at[k], sib_in.at[k], rs_send, rs_recv, k, sib)
        pair.start()

        @tiles(width // 512, 512)
        def keep(cols, _):
            acc_v[:, cols] = dot(dupper_v[pl.ds(k * chunk, rows), :], up_v[cols, :], ((1,), (1,)))

        pair.wait_recv()
        if k == 0:
            dsecond_ref[...] = acc_v[...] + sib_in[0].astype(F32)
            return [pair]
        chip_out[k - 1] = (acc_v[...] + sib_in[k].astype(F32)).astype(BF)
        far = remote(chip_out.at[k - 1], chip_in.at[k - 1], rs_send, rs_recv, 3 + k, chips[k])
        far.start()
        return [pair, far]

    share[0].wait_recv()
    sent = chip_work(0)
    send_x.wait_recv()
    share[1].start()
    diag_y.start()
    send_y.wait_recv()
    share[2].start()
    diag_x.start()
    share[1].wait_recv()
    sent += chip_work(1)
    share[2].wait_recv()
    sent += chip_work(2)
    diag_x.wait_recv()
    diag_y.wait_recv()
    share[3].start()
    share[3].wait_recv()
    sent += chip_work(3)

    def staged(slot, value, target):
        stage_v[slot] = value.astype(BF)
        copy = pltpu.make_async_copy(stage_v.at[slot], target, stage_sem.at[slot])
        copy.start()
        return copy

    @pl.loop(0, 4)
    def outputs(k):
        block = pl.ds(pl.multiple_of(k * chunk, chunk), chunk)
        copies = []
        for j in range(width // 512):
            cols = pl.ds(j * 512, 512)
            copies.append(
                staged(j, dot(active_v[block, :], down_v[:, cols]), out_parts_ref.at[k, :, cols])
            )
        for copy in copies:
            copy.wait()

    @pl.loop(0, hidden // 512)
    def downs(r):
        block = pl.ds(pl.multiple_of(r * 512, 512), 512)
        copies = []
        for j in range(width // 512):
            cols = pl.ds(j * 512, 512)
            copies.append(
                staged(
                    j,
                    dot(active_v[:, block], cots_v[:, cols], ((0,), (0,))),
                    down_part_ref.at[block, cols],
                )
            )
        for copy in copies:
            copy.wait()

    quarter = width // 4
    piece = quarter // length

    @pl.loop(0, hidden // 512)
    def ups(r):
        cols = pl.ds(pl.multiple_of(r * 512, 512), 512)
        copies = []
        for f in range(4):
            value = None
            for k in range(4):
                term = dot(
                    tokens_v[k, :, f * quarter : (f + 1) * quarter],
                    dupper_v[k * chunk : (k + 1) * chunk, cols],
                    ((0,), (0,)),
                )
                value = term if value is None else value + term
            stage_v[f] = value.astype(BF)
            for level in range(length):
                copy = pltpu.make_async_copy(
                    stage_v.at[f, pl.ds(level * piece, piece)],
                    up_part_ref.at[level, f, :, cols],
                    stage_sem.at[4 + f * length + level],
                )
                copy.start()
                copies.append(copy)
        for copy in copies:
            copy.wait()

    for k in range(3):
        remote(chip_out.at[k], chip_in.at[k], rs_send, rs_recv, 4 + k, chips[k + 1]).wait_recv()
    dsecond_ref[...] += (
        chip_in[0].astype(F32) + chip_in[1].astype(F32) + chip_in[2].astype(F32)
    )
    for copy in [send_x, send_y, diag_x, diag_y] + share + sent:
        copy.wait_send()


def ffn(second, down_all, up_mine, ubias, down_mine, length):
    rows, width = second.shape
    hidden = up_mine.shape[1]
    hbm = pl.BlockSpec(memory_space=pltpu.HBM)
    vmem = pl.BlockSpec(memory_space=pltpu.VMEM)
    sems = pltpu.SemaphoreType.DMA
    return pl.pallas_call(
        functools.partial(ffn_kernel, length=length),
        in_specs=[hbm, hbm, hbm, vmem, hbm],
        out_specs=[vmem, hbm, hbm, hbm, vmem],
        out_shape=[
            jax.ShapeDtypeStruct((rows, width), F32),
            jax.ShapeDtypeStruct((4, 2 * rows, width), BF),
            jax.ShapeDtypeStruct((hidden, width), BF),
            jax.ShapeDtypeStruct((length, 4, width // 4 // length, hidden), BF),
            jax.ShapeDtypeStruct((1, hidden), F32),
        ],
        scratch_shapes=[
            pltpu.VMEM((4, 2 * rows, width), BF),
            pltpu.VMEM((8 * rows, width), BF),
            pltpu.VMEM((width, hidden), BF),
            pltpu.VMEM((hidden, width), BF),
            pltpu.VMEM((8 * rows, hidden), BF),
            pltpu.VMEM((8 * rows, hidden), BF),
            pltpu.VMEM((4, rows, width), BF),
            pltpu.VMEM((4, rows, width), BF),
            pltpu.VMEM((3, rows, width), BF),
            pltpu.VMEM((3, rows, width), BF),
            pltpu.VMEM((rows, width), F32),
            pltpu.VMEM((4, 512, 512), BF),
            sems((4,)),
            sems((4 + 4 * length,)),
            sems((8,)),
            sems((8,)),
            sems((7,)),
            sems((7,)),
        ],
        compiler_params=pltpu.CompilerParams(
            collective_id=1, has_side_effects=True, vmem_limit_bytes=60 << 20
        ),
        cost_estimate=pl.CostEstimate(
            flops=12 * 8 * rows * width * hidden, bytes_accessed=40 << 20, transcendentals=0
        ),
    )(second, down_all, up_mine, ubias, down_mine)


ROW_TILE = 32


def for_rows(total, fn):
    @pl.loop(0, total // ROW_TILE)
    def step(index):
        fn(pl.ds(pl.multiple_of(index * ROW_TILE, ROW_TILE), ROW_TILE))


def norm_rows(values):
    center = values - jnp.mean(values, axis=-1, keepdims=True)
    spread = jnp.mean(center * center, axis=-1, keepdims=True)
    rstd = lax.rsqrt(spread + EPSILON)
    return center * rstd, rstd


class Gathered:
    def __init__(self, shard_ref, full_ref, sems, base, where):
        self.y, self.c, self.x = where
        self.shard, self.full, self.sems, self.base = shard_ref, full_ref, sems, base
        self.rows = shard_ref.shape[0]
        self.half = self.rows // 2
        self.step = self.half // 4
        self.place = self.y * 2 + self.c

    def copy(self, src, dst, index, device):
        send_sems, recv_sems = self.sems
        return remote(src, dst, send_sems, recv_sems, self.base + index, device)

    def span(self, place, side, i):
        start = place * self.rows + side * self.half + i * self.step
        return self.full.at[pl.ds(pl.multiple_of(start, self.step), self.step)]

    def over_y(self, i):
        start = pl.multiple_of(self.x * self.half + i * self.step, self.step)
        return self.copy(
            self.shard.at[pl.ds(start, self.step)], self.span(self.place, self.x, i), i, {"y": 1 - self.y}
        )

    def over_x(self, i):
        ref = self.span(self.place ^ 2, self.x, i)
        return self.copy(ref, ref, 4 + i, {"x": 1 - self.x})

    def over_c(self, i, side):
        ref = self.span(self.place ^ 2, self.x if side == 0 else 1 - self.x, i)
        return self.copy(ref, ref, 8 + 4 * side + i, {"c": 1 - self.c})

    def own_c(self):
        start = pl.multiple_of(self.place * self.rows, self.rows)
        return self.copy(self.shard, self.full.at[pl.ds(start, self.rows)], 16, {"c": 1 - self.c})

    def settle(self):
        self.own_c().wait_recv()
        for i in range(4):
            self.over_c(i, 0).wait_recv()
            self.over_c(i, 1).wait_recv()

    def own(self, sem):
        start = pl.multiple_of(self.place * self.rows, self.rows)
        return pltpu.make_async_copy(self.shard, self.full.at[pl.ds(start, self.rows)], sem)


class Arrivals:
    def __init__(self, order, begin):
        self.order, self.begin = order, begin
        self.next = 0
        self.behind = None

    def event(self):
        if self.next == len(self.order):
            return
        weight, i = self.order[self.next]
        self.next += 1
        weight.over_y(i).wait_recv()
        self.begin(weight.over_x(i))
        self.begin(weight.over_c(i, 0))
        self.late()
        self.behind = (weight, i)

    def late(self):
        if self.behind is not None:
            weight, i = self.behind
            weight.over_x(i).wait_recv()
            self.begin(weight.over_c(i, 1))
        self.behind = None


def front_kernel(
    lengths_ref,
    tokens_v,
    smalls_ref,
    kvw_ref,
    qw_ref,
    mw_ref,
    up_ref,
    cot_ref,
    second_ref,
    residual_ref,
    first_v,
    q_v,
    kv_v,
    mixed_v,
    lse_ref,
    vec_v,
    wq_out,
    wm_out,
    wkv_v,
    up_out,
    cots_out,
    wq_v,
    wm_v,
    smalls_v,
    local_sem,
    w_send,
    w_recv,
    s_send,
    s_recv,
    k_send,
    k_recv,
    u_send,
    u_recv,
    uz_send,
    uz_recv,
    c_send,
    c_recv,
    *,
    length,
    slots,
    with_length,
    aligned,
):
    rows, width = tokens_v.shape
    seg = rows // slots
    head_dim = kvw_ref.shape[1] // 2
    heads = width // head_dim
    group = 4
    quarter = width // 4
    y, c, z, x = [lax.axis_index(name) for name in ("y", "c", "z", "x")]
    place = y * 2 + c
    sib, to_x, to_y = {"c": 1 - c}, {"x": 1 - x}, {"y": 1 - y}
    cross, diag = {"y": 1 - y, "c": 1 - c}, {"x": 1 - x, "y": 1 - y}

    weights = [
        Gathered(ref, full, (w_send, w_recv), 17 * n, (y, c, x))
        for n, (ref, full) in enumerate(((qw_ref, wq_v), (mw_ref, wm_v)))
    ]
    query_w, mixer_w = weights
    locals_ = [query_w.own(local_sem.at[0]), mixer_w.own(local_sem.at[1])]
    kv_rows = pl.ds(pl.multiple_of(place * quarter, quarter), quarter)
    locals_.append(pltpu.make_async_copy(kvw_ref, wkv_v.at[kv_rows], local_sem.at[2]))
    locals_.append(pltpu.make_async_copy(smalls_ref, smalls_v.at[place], local_sem.at[3]))
    for copy in locals_:
        copy.start()

    barrier = pltpu.get_barrier_semaphore()
    for device in (sib, to_x, to_y, cross, diag):
        pl.semaphore_signal(barrier, inc=1, device_id=device, device_id_type=MESH)
    for other in range(length):
        @pl.when(other != z)
        def hello():
            pl.semaphore_signal(barrier, inc=1, device_id={"z": other}, device_id_type=MESH)
    pl.semaphore_wait(barrier, 5 + length - 1)

    sent = []

    def begin(copy):
        copy.start()
        sent.append(copy)
        return copy

    small_copies = [
        begin(remote(smalls_ref, smalls_v.at[place], s_send, s_recv, n, device))
        for n, device in enumerate((sib, to_y, cross))
    ]
    kv_near = begin(remote(kvw_ref, wkv_v.at[kv_rows], s_send, s_recv, 3, sib))
    kv_far = begin(remote(kvw_ref, wkv_v.at[kv_rows], s_send, s_recv, 4, to_y))
    part = quarter // length
    hidden = up_out.shape[1]
    block = hidden // length

    def up_copies(index, flip, span, device):
        target = place ^ flip
        dst_rows = pl.ds(pl.multiple_of(place * quarter + span[0], span[1]), span[1])
        copies = []
        for b in range(length if aligned else 1):
            if aligned:
                start = target * (hidden * 2) + (2 * b + x) * block
                src = up_ref.at[pl.ds(span[0], span[1]), pl.ds(pl.multiple_of(start, block), block)]
                dst = up_out.at[dst_rows, pl.ds(b * block, block)]
            else:
                src = up_ref.at[target, pl.ds(span[0], span[1])]
                dst = up_out.at[dst_rows]
            n = index * length + b
            if device is None:
                copies.append(pltpu.make_async_copy(src, dst, u_send.at[n]))
            else:
                copies.append(remote(src, dst, u_send, u_recv, n, device))
        return copies

    up_local = [] if aligned else up_copies(0, 0, (0, quarter), None)
    up_near = up_copies(1, 1, (0, quarter), sib)
    z_part = (pl.multiple_of(z * part, part), part)
    up_far = up_copies(2, 2, z_part, to_y) + up_copies(3, 3, z_part, cross)

    def up_share(k, source, target):
        start = (place ^ (2 + k)) * quarter + source * part
        ref = up_out.at[pl.ds(pl.multiple_of(start, part), part)]
        return pltpu.make_async_remote_copy(
            src_ref=ref,
            dst_ref=ref,
            send_sem=uz_send.at[k, target],
            recv_sem=uz_recv.at[k, source],
            device_id={"z": target},
            device_id_type=MESH,
        )

    same, other_half = pl.ds(0, rows), pl.ds(rows, rows)
    for copy in up_far:
        begin(copy)
    for i in range(4):
        begin(query_w.over_y(i))
    for i in range(4):
        begin(mixer_w.over_y(i))
    cot_y = begin(remote(cot_ref, cots_out.at[2, same], c_send, c_recv, 1, to_y))
    cot_x = begin(remote(cot_ref, cots_out.at[1, same], c_send, c_recv, 0, to_x))
    stream = Arrivals([(query_w, i) for i in range(4)] + [(mixer_w, i) for i in range(4)], begin)
    begin(query_w.own_c())

    for copy in small_copies:
        copy.wait_recv()
    locals_[3].wait()
    vec_v[...] = jnp.concatenate([smalls_v[f] for f in range(4)], axis=1)

    def first_norm(span):
        unit, _ = norm_rows(tokens_v[span, :].astype(F32))
        first_v[span, :] = (unit * vec_v[0:1, :] + vec_v[1:2, :]).astype(BF)

    for_rows(rows, first_norm)

    kv_far.wait_recv()
    far_rows = wkv_v.at[pl.ds(pl.multiple_of((place ^ 2) * quarter, quarter), quarter)]
    kv_pass = begin(remote(far_rows, far_rows, s_send, s_recv, 5, sib))
    kv_near.wait_recv()
    locals_[2].wait()
    kv_pass.wait_recv()
    v_bias = (
        vec_v[7:8, 0:head_dim]
        + vec_v[7:8, quarter : quarter + head_dim]
        + vec_v[7:8, 2 * quarter : 2 * quarter + head_dim]
        + vec_v[7:8, 3 * quarter : 3 * quarter + head_dim]
    )
    keyvals = dot(first_v[...], wkv_v[...]) + jnp.concatenate([jnp.zeros_like(v_bias), v_bias], axis=1)
    mine = pl.ds(pl.multiple_of(x * seg, seg), seg)
    for s in range(slots):
        kv_v[s, 0, mine, :] = keyvals[s * seg : (s + 1) * seg].astype(BF)

    def kv_up(t):
        return remote(kv_v.at[:, t - 1, mine], kv_v.at[:, t, mine], k_send, k_recv, t, {"z": z + 1})

    def kv_side(t):
        ref = kv_v.at[:, t, mine]
        return remote(ref, ref, k_send, k_recv, length + t, to_x)

    def kv_step(t):
        if t:
            @pl.when(z >= t)
            def arrive():
                kv_up(t).wait_recv()

        @pl.when(z >= t)
        def side():
            kv_side(t).start()

        if t + 1 < length:
            @pl.when((z >= t) & (z < length - 1))
            def onward():
                kv_up(t + 1).start()

    for t in range(length):
        kv_step(t)
    for copy in up_far:
        copy.wait_recv()
    for target in range(length):
        @pl.when(target != z)
        def share():
            for k in range(2):
                up_share(k, z, target).start()

    while stream.next < 4:
        stream.event()

    top, bottom = pl.ds(0, rows // 2), pl.ds(rows // 2, rows // 2)
    if not aligned:
        cot_local = pltpu.make_async_copy(cot_ref, cots_out.at[0, same], local_sem.at[4])
        cot_local.start()
    cot_share = [
        remote(cot_ref if k == 0 else cots_out.at[k, same], cots_out.at[k, other_half], c_send, c_recv, 2 + k, sib)
        for k in range(3 if aligned else 4)
    ]

    for copy in up_local:
        copy.start()
    for copy in up_near:
        begin(copy)
    begin(mixer_w.own_c())
    begin(cot_share[0])
    stream.late()
    locals_[0].wait()
    query_w.settle()

    @tiles(width // 512, 512)
    def project(cols, _):
        q_v[:, cols] = (dot(first_v[...], wq_v[:, cols]) + vec_v[2:3, cols]).astype(BF)

    wq_copy = pltpu.make_async_copy(wq_v, wq_out, local_sem.at[5])
    wq_copy.start()
    for t in range(length):
        @pl.when(z >= t)
        def arrived():
            kv_side(t).wait_recv()
            kv_side(t).wait_send()

        if t:
            @pl.when((z >= t - 1) & (z < length - 1))
            def gone():
                kv_up(t).wait_send()

    scale = head_dim ** (-0.5)

    def attend(s, g):
        lanes = pl.ds(pl.multiple_of(g * group * head_dim, group * head_dim), group * head_dim)
        wide = q_v[pl.ds(s * seg, seg), lanes]
        queries = jnp.concatenate(
            [wide[:, h * head_dim : (h + 1) * head_dim] for h in range(group)], axis=0
        )

        def step(t, state, diagonal):
            top_, total, accum = state
            keys = kv_v[s, t, :, :head_dim]
            values = kv_v[s, t, :, head_dim:]
            scores = dot(keys, queries, ((1,), (1,))) * scale
            if diagonal or with_length:
                key_pos = lax.broadcasted_iota(jnp.int32, (2 * seg, seg), 0)
                allowed = None
                if diagonal:
                    query_pos = lax.broadcasted_iota(jnp.int32, (2 * seg, seg), 1) + x * seg
                    allowed = key_pos <= query_pos
                if with_length:
                    inside = key_pos + (z - t) * (2 * seg) < lengths_ref[s]
                    allowed = inside if allowed is None else allowed & inside
                bias = jnp.where(allowed, 0.0, NEG_LARGE).astype(F32)
                scores = scores + jnp.concatenate([bias] * group, axis=1)
            new_top = jnp.maximum(top_, jnp.max(scores, axis=0, keepdims=True))
            terms = jnp.exp(scores - new_top)
            fade = jnp.exp(top_ - new_top)
            total = total * fade + jnp.sum(terms, axis=0, keepdims=True)
            accum = accum * fade + dot(values, terms.astype(BF), ((0,), (0,)))
            return new_top, total, accum

        span = group * seg
        state = (
            jnp.full((1, span), NEG_LARGE, F32),
            jnp.zeros((1, span), F32),
            jnp.zeros((head_dim, span), F32),
        )
        state = step(0, state, True)
        top_, total, accum = lax.fori_loop(1, z + 1, lambda t, st: step(t, st, False), state)
        out = accum / total
        mixed_v[pl.ds(s * seg, seg), lanes] = jnp.concatenate(
            [out[:, h * seg : (h + 1) * seg].T for h in range(group)], axis=1
        ).astype(BF)
        lse_ref[s, g] = top_ + jnp.log(total)

    for s in range(slots):
        for g in range(heads // group):
            attend(s, g)
            stream.event()

    stream.late()
    locals_[1].wait()
    mixer_w.settle()
    wm_copy = pltpu.make_async_copy(wm_v, wm_out, local_sem.at[6])
    wm_copy.start()

    @tiles(width // 512, 512)
    def mix(cols, _):
        residual_ref[:, cols] = (
            tokens_v[:, cols].astype(F32) + dot(mixed_v[...], wm_v[:, cols]) + vec_v[3:4, cols]
        )

    def second_norm(span):
        unit, _ = norm_rows(residual_ref[span, :])
        second_ref[span, :] = (unit * vec_v[4:5, :] + vec_v[5:6, :]).astype(BF)

    for_rows(rows, second_norm)

    cot_x.wait_recv()
    cot_y.wait_recv()
    begin(cot_share[1])
    begin(cot_share[2])
    if not aligned:
        cot_dx = begin(remote(cots_out.at[2, top], cots_out.at[3, top], c_send, c_recv, 6, to_x))
        cot_dy = begin(remote(cots_out.at[1, bottom], cots_out.at[3, bottom], c_send, c_recv, 7, to_y))
        cot_dx.wait_recv()
        cot_dy.wait_recv()
        begin(cot_share[3])
    for copy in cot_share + up_near:
        copy.wait_recv()
    for copy in up_local:
        copy.wait()
    for target in range(length):
        @pl.when(target != z)
        def shared():
            for k in range(2):
                up_share(k, z, target).wait_send()
                up_share(k, target, z).wait_recv()
    for copy in sent:
        copy.wait_send()
    for copy in (wq_copy, wm_copy) + (() if aligned else (cot_local,)):
        copy.wait()


def front(lengths, tokens, smalls, kvw, qw, mw, up, cot, slots, length, with_length, aligned, hidden):
    rows, width = tokens.shape
    seg = rows // slots
    both = kvw.shape[1]
    groups = width // (both // 2) // 4
    hbm = pl.BlockSpec(memory_space=pltpu.HBM)
    vmem = pl.BlockSpec(memory_space=pltpu.VMEM)
    sems = pltpu.SemaphoreType.DMA
    return pl.pallas_call(
        functools.partial(
            front_kernel, length=length, slots=slots, with_length=with_length, aligned=aligned
        ),
        in_specs=[pl.BlockSpec(memory_space=pltpu.SMEM), vmem, hbm, hbm, hbm, hbm, hbm, hbm],
        out_specs=[vmem] * 8 + [hbm, hbm, vmem, hbm, hbm],
        out_shape=[
            jax.ShapeDtypeStruct((rows, width), BF),
            jax.ShapeDtypeStruct((rows, width), F32),
            jax.ShapeDtypeStruct((rows, width), BF),
            jax.ShapeDtypeStruct((rows, width), BF),
            jax.ShapeDtypeStruct((slots, length, 2 * seg, both), BF),
            jax.ShapeDtypeStruct((rows, width), BF),
            jax.ShapeDtypeStruct((slots, groups, 1, 4 * seg), F32),
            jax.ShapeDtypeStruct((8, width), F32),
            jax.ShapeDtypeStruct((width, width), BF),
            jax.ShapeDtypeStruct((width, width), BF),
            jax.ShapeDtypeStruct((width, both), BF),
            jax.ShapeDtypeStruct((width, hidden), BF),
            jax.ShapeDtypeStruct((4, 2 * rows, width), BF),
        ],
        scratch_shapes=[
            pltpu.VMEM((width, width), BF),
            pltpu.VMEM((width, width), BF),
            pltpu.VMEM((4, 8, width // 4), F32),
            sems((7,)),
            sems((34,)),
            sems((34,)),
            sems((6,)),
            sems((6,)),
            sems((2 * length,)),
            sems((2 * length,)),
            sems((4 * length,)),
            sems((4 * length,)),
            sems((2, length)),
            sems((2, length)),
            sems((8,)),
            sems((8,)),
        ],
        compiler_params=pltpu.CompilerParams(
            collective_id=2, has_side_effects=True, vmem_limit_bytes=60 << 20
        ),
        cost_estimate=pl.CostEstimate(
            flops=6 * rows * width * width, bytes_accessed=40 << 20, transcendentals=0
        ),
    )(lengths, tokens, smalls, kvw, qw, mw, up, cot)


def feed_kernel(
    second_ref,
    cot_ref,
    down_all_ref,
    up_ref,
    upw_ref,
    ubias_ref,
    residual_ref,
    vec_ref,
    down_ref,
    dres_ref,
    red_ref,
    down_part_ref,
    up_part_ref,
    ubias_part_ref,
    vsum_ref,
    first_ref,
    tokens_v,
    cots_v,
    up_v,
    down_v,
    active_v,
    dupper_v,
    sib_out,
    sib_in,
    chip_out,
    chip_in,
    acc_v,
    stage_v,
    credit,
    load_sem,
    stage_sem,
    gs_send,
    gs_recv,
    rs_send,
    rs_recv,
    *,
    length,
):
    rows, width = second_ref.shape
    hidden = up_ref.shape[1]
    half = rows // 2
    chunk = 2 * rows
    y, c, z, x = [lax.axis_index(name) for name in ("y", "c", "z", "x")]
    sib, to_x, to_y = {"c": 1 - c}, {"x": 1 - x}, {"y": 1 - y}
    diag = {"x": 1 - x, "y": 1 - y}
    chips = (None, to_x, to_y, diag)

    loads = [
        pltpu.make_async_copy(second_ref, tokens_v.at[pl.ds(0, rows)], load_sem.at[0]),
        pltpu.make_async_copy(cot_ref, cots_v.at[pl.ds(0, rows)], load_sem.at[1]),
        pltpu.make_async_copy(
            down_all_ref.at[pl.ds(rows, 5 * rows)], cots_v.at[pl.ds(rows, 5 * rows)], load_sem.at[2]
        ),
    ]
    block = hidden // length
    quarter = width // 4
    place = y * 2 + c
    ups_in = []
    for flip in range(1, 4):
        span = pl.ds(pl.multiple_of((place ^ flip) * quarter, quarter), quarter)
        ups_in.append(pltpu.make_async_copy(up_ref.at[span], up_v.at[span], load_sem.at[3 + flip]))
    own_rows = pl.ds(pl.multiple_of(place * quarter, quarter), quarter)
    for b in range(length):
        start = place * (2 * hidden) + (2 * b + x) * block
        ups_in.append(
            pltpu.make_async_copy(
                upw_ref.at[:, pl.ds(pl.multiple_of(start, block), block)],
                up_v.at[own_rows, pl.ds(b * block, block)],
                load_sem.at[7 + length + b],
            )
        )
    downs_in = [
        pltpu.make_async_copy(
            down_ref.at[pl.ds(pl.multiple_of((2 * b + x) * block, block), block)],
            down_v.at[pl.ds(b * block, block)],
            load_sem.at[7 + b],
        )
        for b in range(length)
    ]
    for load in loads + downs_in + ups_in:
        load.start()
    barrier = pltpu.get_barrier_semaphore()
    for device in (sib, to_x, to_y, diag):
        pl.semaphore_signal(barrier, inc=1, device_id=device, device_id_type=MESH)
    for step in (-1, 1):
        @pl.when((z + step >= 0) & (z + step < length))
        def hello():
            pl.semaphore_signal(barrier, inc=1, device_id={"z": z + step}, device_id_type=MESH)
    inner = (z > 0).astype(jnp.int32) + (z < length - 1).astype(jnp.int32)
    pl.semaphore_wait(barrier, 4 + inner)
    loads[0].wait()

    same, other = (0, rows), (rows, rows)
    top, bottom = (0, half), (half, half)

    def gather(index, chip, span_src, chip_dst, span_dst, device):
        src = tokens_v.at[pl.ds(chip * chunk + span_src[0], span_src[1])]
        dst = tokens_v.at[pl.ds(chip_dst * chunk + span_dst[0], span_dst[1])]
        return remote(src, dst, gs_send, gs_recv, index, device)

    send_x = gather(0, 0, same, 1, same, to_x)
    send_y = gather(1, 0, same, 2, same, to_y)
    share = [gather(2 + k, k, same, k, other, sib) for k in range(4)]
    diag_x = gather(6, 2, top, 3, top, to_x)
    diag_y = gather(7, 1, bottom, 3, bottom, to_y)
    send_x.start()
    send_y.start()
    share[0].start()

    loads[1].wait()
    loads[2].wait()
    for load in downs_in:
        load.wait()

    def cot_part(chip, start, size):
        return cots_v.at[pl.ds(chip * chunk + start, size)]

    cot_dx = remote(cot_part(2, 0, half), cot_part(3, 0, half), gs_send, gs_recv, 8, to_x)
    cot_dy = remote(cot_part(1, half, half), cot_part(3, half, half), gs_send, gs_recv, 9, to_y)
    cot_dc = remote(cot_part(3, 0, rows), cot_part(3, rows, rows), gs_send, gs_recv, 10, sib)

    def grad_active(span, index):
        dupper_v[span, :] = dot(cots_v[span, :], down_v[...], ((1,), (1,))).astype(BF)

    @pl.loop(0, 3)
    def near_grads(k):
        grad_active(pl.ds(pl.multiple_of(k * chunk, chunk), chunk), k)

    for load in ups_in:
        load.wait()

    def chip_work(k):
        block = pl.ds(k * chunk, chunk)

        @tiles(hidden // 512, 512)
        def columns(cols, _):
            if k < 3:
                upper = dot(tokens_v[block, :], up_v[:, cols]) + ubias_ref[:, cols]
                active, slope = gelu_pair(upper)
                active_v[block, cols] = active.astype(BF)
                d_upper = (dupper_v[block, cols].astype(F32) * slope).astype(BF)
            else:
                d_active = dot(cots_v[block, :], down_v[cols, :], ((1,), (1,)))
                d_upper = (d_active * dupper_v[block, cols].astype(F32)).astype(BF)
            dupper_v[block, cols] = d_upper
            part = jnp.sum(d_upper.astype(F32), axis=0, keepdims=True)
            if k == 0:
                ubias_part_ref[:, cols] = part
            else:
                ubias_part_ref[:, cols] += part

        theirs, mine = pl.ds(k * chunk + rows, rows), pl.ds(k * chunk, rows)

        @tiles(width // 1024, 1024)
        def to_sibling(cols, _):
            sib_out[k, :, cols] = dot(dupper_v[theirs, :], up_v[cols, :], ((1,), (1,))).astype(BF)

        pair = remote(sib_out.at[k], sib_in.at[k], rs_send, rs_recv, k, sib)
        pair.start()

        @tiles(width // 1024, 1024)
        def keep(cols, _):
            dres_ref[:, cols] = dot(dupper_v[mine, :], up_v[cols, :], ((1,), (1,)))

        pair.wait_recv()

        def total(span):
            value = dres_ref[span, :] + sib_in[k, span, :].astype(F32)
            if k == 0:
                acc_v[span, :] = value
            else:
                chip_out[k - 1, span, :] = value.astype(BF)

        for_rows(rows, total)
        if k == 0:
            return [pair]
        far = remote(chip_out.at[k - 1], chip_in.at[k - 1], rs_send, rs_recv, 3 + k, chips[k])
        far.start()
        return [pair, far]

    share[0].wait_recv()
    sent = chip_work(0)
    send_x.wait_recv()
    share[1].start()
    diag_y.start()
    send_y.wait_recv()
    share[2].start()
    diag_x.start()
    cot_dx.start()
    cot_dy.start()
    share[1].wait_recv()
    sent += chip_work(1)
    share[2].wait_recv()
    sent += chip_work(2)
    diag_x.wait_recv()
    diag_y.wait_recv()
    share[3].start()
    share[3].wait_recv()

    @tiles(hidden // 512, 512)
    def last_slopes(cols, _):
        block = pl.ds(3 * chunk, chunk)
        upper = dot(tokens_v[block, :], up_v[:, cols]) + ubias_ref[:, cols]
        active, slope = gelu_pair(upper)
        active_v[block, cols] = active.astype(BF)
        dupper_v[block, cols] = slope.astype(BF)

    cot_dx.wait_recv()
    cot_dy.wait_recv()
    cot_dc.start()
    cot_dc.wait_recv()

    @pl.loop(0, 2)
    def downs(n):
        block = pl.ds(pl.multiple_of(n * 512, 512), 512)
        copies = []
        for m in range(2):
            cols = pl.ds(m * (width // 2), width // 2)
            stage_v[m] = dot(active_v[:, block], cots_v[:, cols], ((0,), (0,))).astype(BF)
            copy = pltpu.make_async_copy(
                stage_v.at[m], down_part_ref.at[block, cols], stage_sem.at[m * length]
            )
            copy.start()
            copies.append(copy)
        for copy in copies:
            copy.wait()

    line_block = hidden // length
    ends = []
    for n in range(2):
        for way, device in ((0, {"z": z + 1}), (1, {"z": z - 1})):
            b = length - 1 if way == 0 else 0
            part = down_part_ref.at[pl.ds(b * line_block, line_block)] if n else up_part_ref.at[b]
            ends.append(remote(part, first_ref.at[n, way], rs_send, rs_recv, 11 + 2 * n + way, device))

    def send_ends(n):
        for way, edge in ((0, 0), (1, length - 1)):
            @pl.when(z == edge)
            def send_end():
                ends[2 * n + way].start()

    send_ends(1)
    sent += chip_work(3)

    pl.semaphore_signal(credit, inc=1, device_id=sib, device_id_type=MESH)
    pl.semaphore_wait(credit, 1)

    piece = quarter // length

    @pl.loop(0, 2)
    def ups(lane_half):
        lanes = pl.ds(pl.multiple_of(lane_half * hidden, hidden), hidden)
        copies = []
        for n in range(2):
            cols = pl.ds(pl.multiple_of((lane_half * 2 + n) * quarter, quarter), quarter)
            stage_v[n] = dot(tokens_v[:, cols], dupper_v[...], ((0,), (0,))).astype(BF)
            for level in range(length):
                copy = pltpu.make_async_copy(
                    stage_v.at[n, pl.ds(level * piece, piece)],
                    up_part_ref.at[level, pl.ds(n * piece, piece), lanes],
                    stage_sem.at[n * length + level],
                )
                copy.start()
                copies.append(copy)
        for copy in copies:
            copy.wait()

    send_ends(0)

    for k in range(4):
        sent[0 if k == 0 else 2 * k - 1].wait_send()

    def out_pair(k):
        return remote(sib_out.at[k], sib_in.at[k], rs_send, rs_recv, 7 + k, sib)

    @pl.loop(0, 4)
    def outs_away(k):
        theirs = pl.ds(pl.multiple_of(k * chunk + rows, rows), rows)

        @tiles(width // 1024, 1024)
        def columns(cols, _):
            sib_out[k, :, cols] = dot(active_v[theirs, :], down_v[:, cols]).astype(BF)

        out_pair(k).start()

    @pl.loop(0, 4)
    def outs_here(k):
        mine = pl.ds(pl.multiple_of(k * chunk, rows), rows)

        @tiles(width // 1024, 1024)
        def columns(cols, _):
            dres_ref[:, cols] = dot(active_v[mine, :], down_v[:, cols])

        out_pair(k).wait_recv()

        def total(span):
            sib_in[k, span, :] = (dres_ref[span, :] + sib_in[k, span, :].astype(F32)).astype(BF)

        for_rows(rows, total)

    red_copy = pltpu.make_async_copy(sib_in, red_ref, load_sem.at[3])
    red_copy.start()

    for k in range(3):
        remote(chip_out.at[k], chip_in.at[k], rs_send, rs_recv, 4 + k, chips[k + 1]).wait_recv()
    vsum_ref[...] = jnp.zeros(vsum_ref.shape, F32)

    def norm_back(span):
        d_second = acc_v[span, :]
        for k in range(3):
            d_second = d_second + chip_in[k, span, :].astype(F32)
        unit, rstd = norm_rows(residual_ref[span, :])
        d_out = cots_v[span, :].astype(F32)
        d_residual = d_out + norm_backward(d_second, unit, rstd, vec_ref[4:5, :])
        dres_ref[span, :] = d_residual
        vsum_ref[0:1, :] += jnp.sum(d_second * unit, axis=0, keepdims=True)
        vsum_ref[1:2, :] += jnp.sum(d_second, axis=0, keepdims=True)
        vsum_ref[2:3, :] += jnp.sum(d_residual.astype(BF).astype(F32), axis=0, keepdims=True)
        vsum_ref[3:4, :] += jnp.sum(d_out, axis=0, keepdims=True)

    for_rows(rows, norm_back)
    red_copy.wait()
    for n in range(2):
        for way, edge in ((0, 0), (1, length - 1)):
            @pl.when(z == edge)
            def end_sent():
                ends[2 * n + way].wait_send()

            @pl.when(z == (1 if way == 0 else length - 2))
            def end_here():
                ends[2 * n + way].wait_recv()

    for k in range(4):
        out_pair(k).wait_send()
    for copy in [send_x, send_y, diag_x, diag_y, cot_dx, cot_dy, cot_dc] + share + sent[2::2]:
        copy.wait_send()


def feed(second, d_down, down_all, up_mine, up_weight, ubias, residual, vectors, down_weight, length):
    rows, width = second.shape
    hidden = up_mine.shape[1]
    hbm = pl.BlockSpec(memory_space=pltpu.HBM)
    vmem = pl.BlockSpec(memory_space=pltpu.VMEM)
    sems = pltpu.SemaphoreType.DMA
    return pl.pallas_call(
        functools.partial(feed_kernel, length=length),
        in_specs=[hbm, hbm, hbm, hbm, hbm, vmem, vmem, vmem, hbm],
        out_specs=[vmem, hbm, hbm, hbm, vmem, vmem, hbm],
        out_shape=[
            jax.ShapeDtypeStruct((rows, width), F32),
            jax.ShapeDtypeStruct((4, rows, width), BF),
            jax.ShapeDtypeStruct((hidden, width), BF),
            jax.ShapeDtypeStruct((length, hidden // length, width), BF),
            jax.ShapeDtypeStruct((1, hidden), F32),
            jax.ShapeDtypeStruct((8, width), F32),
            jax.ShapeDtypeStruct((2, 2, hidden // length, width), BF),
        ],
        scratch_shapes=[
            pltpu.VMEM((8 * rows, width), BF),
            pltpu.VMEM((8 * rows, width), BF),
            pltpu.VMEM((width, hidden), BF),
            pltpu.VMEM((hidden, width), BF),
            pltpu.VMEM((8 * rows, hidden), BF),
            pltpu.VMEM((8 * rows, hidden), BF),
            pltpu.VMEM((4, rows, width), BF),
            pltpu.VMEM((4, rows, width), BF),
            pltpu.VMEM((3, rows, width), BF),
            pltpu.VMEM((3, rows, width), BF),
            pltpu.VMEM((rows, width), F32),
            pltpu.VMEM((2, 512, 1024), BF),
            pltpu.SemaphoreType.REGULAR,
            sems((7 + 2 * length,)),
            sems((2 * length,)),
            sems((11,)),
            sems((11,)),
            sems((15,)),
            sems((15,)),
        ],
        compiler_params=pltpu.CompilerParams(
            collective_id=4, has_side_effects=True, vmem_limit_bytes=62 << 20
        ),
        cost_estimate=pl.CostEstimate(
            flops=12 * 8 * rows * width * hidden, bytes_accessed=40 << 20, transcendentals=0
        ),
    )(second, d_down, down_all, up_mine, up_weight, ubias, residual, vectors, down_weight)


class Links:
    def __init__(self, send_sems, recv_sems, count):
        self.send_sems, self.recv_sems, self.count = send_sems, recv_sems, count
        self.used = 0

    def copy(self, src, dst, device):
        index = self.used
        self.used += 1
        assert index < self.count
        return self.again(src, dst, device, index)

    def again(self, src, dst, device, index):
        return remote(src, dst, self.send_sems, self.recv_sems, index, device)


class LineSum:
    def __init__(self, links, z, length, parts, landing, source=None, given=None):
        self.z, self.length, self.parts, self.landing = z, length, parts, landing
        self.source = parts if source is None else source
        self.given = given
        self.copies, self.indices = {}, {}
        self.links = links

    def position(self, way):
        return self.z if way == 0 else self.length - 1 - self.z

    def block(self, way, t):
        index = self.length - t + self.position(way)
        index = index if way == 0 else self.length - 1 - index
        return jnp.clip(index, 0, self.length - 1)

    def clear(self):
        last = self.length - 1
        for way in range(2):
            @pl.when(self.position(way) == 0)
            def zero():
                ref = self.landing(way, last)
                ref[...] = jnp.zeros(ref.shape, ref.dtype)

    def direct(self, t, ways=(0, 1)):
        for way in ways:
            device = {"z": self.z + (1 if way == 0 else -1)}
            index = self.links.used
            copy = self.links.copy(
                self.source.at[self.block(way, t)], self.landing(way, t), device
            )
            self.copies[way, t] = copy
            self.indices[way, t] = index

            @pl.when(self.position(way) == 0)
            def first():
                copy.start()

    def onward(self, t):
        for way in range(2):
            pos = self.position(way)
            device = {"z": self.z + (1 if way == 0 else -1)}
            ref = self.landing(way, t - 1)
            passed = self.links.again(ref, self.landing(way, t), device, self.indices[way, t])

            @pl.when((pos >= 1) & (pos <= t - 1))
            def add():
                if t == 2 and self.given is not None:
                    self.given[way].wait()
                else:
                    self.copies[way, t - 1].wait_recv()
                add_rows(ref, self.parts.at[self.block(way, t)])
                passed.start()

    def step(self, t):
        self.direct(t)
        if t > 1:
            self.onward(t)

    def finish(self, own, out):
        last = self.length - 1
        for way in range(2):
            @pl.when(self.position(way) >= 1)
            def arrive():
                self.copies[way, last].wait_recv()

        right, left = self.landing(0, last), self.landing(1, last)
        rows = out.shape[0]
        tile = min(rows, ROW_TILE)

        @pl.loop(0, rows // tile)
        def add(index):
            span = pl.ds(pl.multiple_of(index * tile, tile), tile)
            out[span, :] = (
                own[span, :].astype(F32) + right[span, :].astype(F32) + left[span, :].astype(F32)
            ).astype(out.dtype)

    def settle(self, t):
        for way in range(2):
            @pl.when((self.position(way) <= t - 1) & (self.position(way) < self.length - 1))
            def sent():
                self.copies[way, t].wait_send()

    def drain(self):
        for t in range(1 if self.given is None else 2, self.length):
            self.settle(t)


def add_rows(ref, term):
    rows = ref.shape[0]
    tile = min(rows, ROW_TILE)

    @pl.loop(0, rows // tile)
    def add(index):
        span = pl.ds(pl.multiple_of(index * tile, tile), tile)
        ref[span, :] = (ref[span, :].astype(F32) + term[span, :].astype(F32)).astype(ref.dtype)


class GradSum:
    def __init__(self, links, where, length, width, cols, left, right, bufs):
        self.y, self.c, self.z, self.x = where
        self.length, self.width, self.half = length, width, cols // 2
        self.left, self.right = left, right
        self.cols = cols
        (
            self.left_own,
            self.left_out,
            self.left_in,
            self.right_in,
            self.send1,
            self.recv1,
            self.send2,
            self.recv2,
            self.hold,
            self.zpart,
            self.zland,
        ) = bufs
        self.links = links
        self.sent = []
        self.left_copy = self.sum_copy = None

    def begin(self, copy):
        copy.start()
        self.sent.append(copy)
        return copy

    def share(self):
        quarter = self.width // 4
        block = quarter // (2 * self.length)
        for core, target in ((1 - self.c, self.left_out), (self.c, self.left_own)):
            for y_part in range(2):
                lanes = pl.ds(pl.multiple_of((y_part * 2 + core) * quarter, quarter), quarter)
                turned = self.left[:, lanes].astype(F32).T.astype(BF)
                for x_part in range(2):
                    for level in range(self.length):
                        start = (level * 2 + x_part) * block
                        target[y_part * 2 + x_part, level * block : (level + 1) * block, :] = turned[
                            start : start + block
                        ]
        sib = {"c": 1 - self.c}
        self.left_copy = self.begin(self.links.copy(self.left_out, self.left_in, sib))
        self.share_right()

    def share_right(self):
        sib = {"c": 1 - self.c}
        self.right_copy = self.begin(self.links.copy(self.right, self.right_in, sib))

    def share_sums(self, sums, own, out, landing):
        self.sum_own, self.sum_in = own, landing
        quarter = self.width // 4
        block = quarter // (2 * self.length)
        for core, target in ((1 - self.c, out), (self.c, own)):
            for y_part in range(2):
                lanes = pl.ds(pl.multiple_of((y_part * 2 + core) * quarter, quarter), quarter)
                filler = jnp.zeros((own.shape[2] - sums.shape[0], quarter), F32)
                turned = jnp.concatenate([sums[:, lanes], filler], axis=0).T.astype(BF)
                for x_part in range(2):
                    for level in range(self.length):
                        start = (level * 2 + x_part) * block
                        target[y_part * 2 + x_part, level * block : (level + 1) * block, :] = turned[
                            start : start + block
                        ]
        self.sum_copy = self.begin(self.links.copy(out, landing, {"c": 1 - self.c}))

    def term(self, y_part, x_part, cols):
        g = y_part * 2 + x_part
        if cols.start >= self.right.shape[1]:
            total = self.sum_own[g].astype(F32) + self.sum_in[g].astype(F32)
            return jnp.concatenate([total, jnp.zeros((total.shape[0], cols.size - total.shape[1]), F32)], axis=1)
        return dot(self.left_own[g], self.right[:, cols]) + dot(self.left_in[g], self.right_in[:, cols])

    def columns(self, side, fn):
        count = self.half // 128
        size = 128 * max(n for n in range(1, 5) if count % n == 0)
        for j in range(self.half // size):
            fn(pl.ds(side * self.half + j * size, size), pl.ds(j * size, size))

    def first(self):
        if self.left_copy is not None:
            self.left_copy.wait_recv()
        self.right_copy.wait_recv()
        if self.sum_copy is not None:
            self.sum_copy.wait_recv()
        for n in range(2):

            def over_y(cols, local):
                self.send1[0, n, :, local] = self.term(1 - self.y, n, cols).astype(BF)

            def over_x(cols, local):
                self.send1[1, n, :, local] = self.term(n, 1 - self.x, cols).astype(BF)

            self.columns(0, over_y)
            self.columns(1, over_x)
        self.copies1 = [
            self.begin(
                self.links.copy(self.send1.at[side], self.recv1.at[side], device)
            )
            for side, device in ((0, {"y": 1 - self.y}), (1, {"x": 1 - self.x}))
        ]

    def second(self):
        for copy in self.copies1:
            copy.wait_recv()

        def a_out(cols, local):
            term = self.term(self.y, 1 - self.x, cols) + self.recv1[0, 1 - self.x, :, local].astype(F32)
            self.send2[0, :, local] = term.astype(BF)

        def b_out(cols, local):
            term = self.term(1 - self.y, self.x, cols) + self.recv1[1, 1 - self.y, :, local].astype(F32)
            self.send2[1, :, local] = term.astype(BF)

        def a_keep(cols, local):
            self.hold[:, cols] = self.term(self.y, self.x, cols) + self.recv1[0, self.x, :, local].astype(F32)

        def b_keep(cols, local):
            self.hold[:, cols] = self.term(self.y, self.x, cols) + self.recv1[1, self.y, :, local].astype(F32)

        self.columns(0, a_out)
        self.columns(1, b_out)
        self.copies2 = [
            self.begin(
                self.links.copy(self.send2.at[side], self.recv2.at[side], device)
            )
            for side, device in ((0, {"x": 1 - self.x}), (1, {"y": 1 - self.y}))
        ]
        self.columns(0, a_keep)
        self.columns(1, b_keep)

    def third(self, out):
        for copy in self.copies2:
            copy.wait_recv()
        block = self.hold.shape[0] // self.length
        for side in range(2):

            def add(cols, local):
                total = self.hold[:, cols] + self.recv2[side, :, local].astype(F32)
                self.hold[:, cols] = total
                for level in range(self.length):
                    self.zpart[level, :, cols] = total[level * block : (level + 1) * block].astype(BF)

            self.columns(side, add)
        rows = pl.ds(pl.multiple_of(self.z * block, block), block)
        out[...] = self.hold[rows, :]
        self.line = LineSum(
            self.links,
            self.z,
            self.length,
            self.zpart,
            lambda way, t: self.zland.at[way, t - 1],
        )

    def finish(self, out):
        self.line.finish(out, out)

    def drain(self):
        for copy in self.sent:
            copy.wait_send()
        self.line.drain()


def back_kernel(
    lengths_ref,
    dres_ref,
    q_ref,
    kv_ref,
    mixed_ref,
    lse_ref,
    vec_ref,
    wkv_ref,
    vsum_ref,
    ubias_ref,
    tokens_ref,
    first_ref,
    wq_ref,
    wm_ref,
    red_ref,
    down_part,
    up_part,
    first_ref_z,
    tgrad_ref,
    query_ref,
    keyval_ref,
    mixer_ref,
    up_ref,
    ubias_out,
    far_ref,
    down_last,
    w_v,
    dmix_v,
    dmixed_v,
    right_v,
    dfirst_v,
    dkv_v,
    keep_v,
    xsend_v,
    xrecv_v,
    csend_v,
    crecv_v,
    line_v,
    land_v,
    last_v,
    upsend_v,
    uprecv_v,
    sums_v,
    s_own,
    s_out,
    s_in,
    ub_part,
    ub_land,
    left_own,
    left_out,
    left_in,
    right_in,
    send1,
    recv1,
    send2,
    recv2,
    hold,
    zpart,
    zland,
    zpart_q,
    zland_q,
    pair_v,
    k_right,
    k_send1,
    k_recv1,
    k_send2,
    k_recv2,
    k_hold,
    k_zpart,
    k_zland,
    load_sem,
    credit,
    send_sems,
    recv_sems,
    *,
    length,
    slots,
    with_length,
    count,
):
    rows, width = dres_ref.shape
    seg = rows // slots
    both = wkv_ref.shape[1]
    head_dim = both // 2
    heads = width // head_dim
    group = 4
    y, c, z, x = [lax.axis_index(name) for name in ("y", "c", "z", "x")]
    place = y * 2 + c
    sib, to_x, to_y, diag = {"c": 1 - c}, {"x": 1 - x}, {"y": 1 - y}, {"x": 1 - x, "y": 1 - y}
    links = Links(send_sems, recv_sems, count)
    scale = head_dim ** (-0.5)

    def load(src, dst, n):
        copy = pltpu.make_async_copy(src, dst, load_sem.at[n])
        copy.start()
        return copy

    load_up = load(up_part, line_v.at[0], 0)
    load_down = load(down_part, line_v.at[1], 1)
    strip = w_v.shape[1]

    class Strips:
        def __init__(self, ref):
            self.ref, self.loads = ref, {}

        def start(self, j):
            if (j + 1) * strip <= width:
                self.loads[j] = load(self.ref.at[pl.ds(j * strip, strip)], w_v.at[j % 2], 2 + j % 2)

        def over(self, fn):
            for j in range(width // strip):
                self.loads[j].wait()
                fn(pl.ds(j * strip, strip), w_v.at[j % 2])
                self.start(j + 2)

    mixer_strips, query_strips = Strips(wm_ref), Strips(wq_ref)
    mixer_strips.start(0)
    mixer_strips.start(1)

    def landing(n, final):
        return lambda way, t: land_v.at[n, way, t - 1] if t < length - 1 else final.at[way]

    given = [
        [
            pltpu.make_async_copy(first_ref_z.at[n, way], land_v.at[n, way, 0], load_sem.at[4 + 2 * n + way])
            for way in range(2)
        ]
        for n in range(2)
    ]
    for way, inner in ((0, 1), (1, length - 2)):
        @pl.when(z == inner)
        def load_first():
            given[0][way].start()
            given[1][way].start()

    up_line = LineSum(links, z, length, line_v.at[0], landing(0, last_v), up_part, given[0])
    down_line = LineSum(links, z, length, line_v.at[1], landing(1, down_last), down_part, given[1])
    lanes = ubias_ref.shape[1] // length
    for level in range(length):
        ub_part[level] = jnp.broadcast_to(ubias_ref[:, level * lanes : (level + 1) * lanes], ub_part.shape[1:])
    ubias_line = LineSum(links, z, length, ub_part, lambda way, t: ub_land.at[way, t - 1])
    bufs = (left_own, left_out, left_in, right_in, send1, recv1, send2, recv2, hold)
    where = (y, c, z, x)
    mixer = GradSum(links, where, length, width, width, mixed_ref, dmix_v, bufs + (zpart, zland))
    query = GradSum(links, where, length, width, width, dmix_v, right_v, bufs + (zpart_q, zland_q))
    keyval = GradSum(
        links,
        where,
        length,
        width,
        2 * both,
        dmix_v,
        pair_v,
        (left_own, left_out, left_in)
        + (k_right, k_send1, k_recv1, k_send2, k_recv2, k_hold, k_zpart, k_zland),
    )
    up_line.clear()
    for way, edge in ((0, 0), (1, length - 1)):
        @pl.when(z == edge)
        def clear_edge():
            zland[way, length - 2] = jnp.zeros(zland.shape[2:], BF)
            zland_q[way, length - 2] = jnp.zeros(zland_q.shape[2:], BF)
            k_zland[way, length - 2] = jnp.zeros(k_zland.shape[2:], BF)
            ub_land[way, length - 2] = jnp.zeros(ub_land.shape[2:], F32)

    @pl.when(z == length - 1)
    def clear_hops():
        crecv_v[...] = jnp.zeros(crecv_v.shape, BF)

    barrier = pltpu.get_barrier_semaphore()
    plane = []
    for flip in range(1, 8):
        device = {"y": y ^ (flip // 4), "c": c ^ (flip // 2 % 2), "x": x ^ (flip % 2)}
        plane.append(device)
    for device in plane:
        pl.semaphore_signal(barrier, inc=1, device_id=device, device_id_type=MESH)
    for other in range(length):
        @pl.when(other != z)
        def hello():
            pl.semaphore_signal(barrier, inc=1, device_id={"z": other}, device_id_type=MESH)
    pl.semaphore_wait(barrier, 7 + length - 1)

    sent = []

    def begin(copy):
        copy.start()
        sent.append(copy)
        return copy

    far = [
        links.copy(red_ref.at[k + 1], far_ref.at[k], device)
        for k, device in enumerate((to_x, to_y, diag))
    ]
    ubias_line.direct(1)
    ubias_line.direct(2)
    ubias_line.direct(3)
    up_line.direct(2)
    down_line.direct(2)

    def to_bf(span):
        dmix_v[span, :] = dres_ref[span, :].astype(BF)

    for_rows(rows, to_bf)
    mixer.share()
    ubias_line.onward(2)
    load_up.wait()
    up_line.onward(2)
    load_down.wait()
    down_line.onward(2)

    def mix_back(cols, strip_v):
        dmixed_v[:, cols] = dot(dmix_v[...], strip_v[...], ((1,), (1,))).astype(BF)

    mixer_strips.over(mix_back)
    query_strips.start(0)
    query_strips.start(1)
    mixer.first()

    def attend(s, g):
        lanes = pl.ds(pl.multiple_of(g * group * head_dim, group * head_dim), group * head_dim)
        span = pl.ds(s * seg, seg)

        def stack(wide):
            return jnp.concatenate(
                [wide[:, h * head_dim : (h + 1) * head_dim] for h in range(group)], axis=0
            )

        queries = stack(q_ref[span, lanes])
        d_mixed = stack(dmixed_v[span, lanes])
        inner = mixed_ref[span, lanes].astype(F32) * dmixed_v[span, lanes].astype(F32)
        delta = jnp.concatenate(
            [
                jnp.sum(inner[:, h * head_dim : (h + 1) * head_dim].T, axis=0, keepdims=True)
                for h in range(group)
            ],
            axis=1,
        )
        lse = lse_ref[s, g]

        def step(t, accum, diagonal):
            keys = kv_ref[s, t, :, :head_dim]
            values = kv_ref[s, t, :, head_dim:]
            scores = dot(keys, queries, ((1,), (1,))) * scale
            if diagonal or with_length:
                key_pos = lax.broadcasted_iota(jnp.int32, (2 * seg, seg), 0)
                allowed = None
                if diagonal:
                    query_pos = lax.broadcasted_iota(jnp.int32, (2 * seg, seg), 1) + x * seg
                    allowed = key_pos <= query_pos
                if with_length:
                    inside = key_pos + (z - t) * (2 * seg) < lengths_ref[s]
                    allowed = inside if allowed is None else allowed & inside
                bias = jnp.where(allowed, 0.0, NEG_LARGE).astype(F32)
                scores = scores + jnp.concatenate([bias] * group, axis=1)
            probs = jnp.exp(scores - lse)
            d_probs = dot(values, d_mixed, ((1,), (1,)))
            d_scores = (probs * (d_probs - delta)).astype(BF)
            dkv_v[t, :, :head_dim] += dot(d_scores, queries) * scale
            dkv_v[t, :, head_dim:] += dot(probs.astype(BF), d_mixed)
            return accum + dot(keys, d_scores, ((0,), (0,)))

        accum = step(0, jnp.zeros((head_dim, group * seg), F32), True)
        accum = lax.fori_loop(1, z + 1, lambda t, a: step(t, a, False), accum)
        right_v[span, lanes] = (
            jnp.concatenate([accum[:, h * seg : (h + 1) * seg].T for h in range(group)], axis=1) * scale
        ).astype(BF)

    x_copies = []
    for s in range(slots):
        for t in range(length):
            dkv_v[t] = jnp.zeros(dkv_v.shape[1:], F32)

        @pl.loop(0, heads // group)
        def over_groups(g):
            attend(s, g)

        for t in range(length):
            keep_v[s, t] = dkv_v[t, pl.ds(pl.multiple_of(x * seg, seg), seg), :].astype(BF)
            xsend_v[s, t] = dkv_v[t, pl.ds(pl.multiple_of((1 - x) * seg, seg), seg), :].astype(BF)
        x_copies.append(begin(links.copy(xsend_v.at[s], xrecv_v.at[s], to_x)))
    load_tokens = load(tokens_ref, dmixed_v, 8)
    mixer.second()

    neighbours = ((0, sib), (1, to_y), (2, to_x))
    for n, device in neighbours:
        pl.semaphore_signal(credit.at[n], inc=1, device_id=device, device_id_type=MESH)
    for copy in mixer.sent[:4]:
        copy.wait_send()
    load_first = load(first_ref, dmix_v, 9)
    for n, _ in neighbours:
        pl.semaphore_wait(credit.at[n], 1)
    load_first.wait()
    query.share()
    query.first()
    mixer.third(mixer_ref)
    for n, device in neighbours[1:]:
        pl.semaphore_signal(credit.at[2 + n], inc=1, device_id=device, device_id_type=MESH)

    for copy in x_copies:
        copy.wait_recv()
    hops = [links.copy(csend_v.at[t - 1], crecv_v.at[t - 1], {"z": z - 1}) for t in range(1, length)]
    for t in range(length - 1, -1, -1):
        @pl.when(t <= z)
        def hop():
            if t + 1 < length:
                @pl.when(z < length - 1)
                def arrive():
                    hops[t].wait_recv()

            total = keep_v[:, t].astype(F32) + xrecv_v[:, t].astype(F32)
            if t + 1 < length:
                total = total + crecv_v[t].astype(F32)
            if t:
                csend_v[t - 1] = total.astype(BF)
                hops[t - 1].start()
            else:
                for s in range(slots):
                    pair_v[s * seg : (s + 1) * seg, :] = total[s].astype(BF)

    keyval.share_right()
    up_line.direct(3)
    down_line.direct(3)
    for t in range(1, length):
        mixer.line.direct(t)
    up_line.onward(3)
    ubias_line.onward(3)

    def first_back(cols, strip_v):
        dfirst_v[:, cols] = dot(right_v[...], strip_v[...], ((1,), (1,))) + dot(
            pair_v[...], wkv_ref[cols, :], ((1,), (1,))
        )

    query_strips.over(first_back)
    load_tokens.wait()

    sums_v[...] = jnp.zeros(sums_v.shape, F32)

    def first_norm_back(span):
        unit, rstd = norm_rows(dmixed_v[span, :].astype(F32))
        d_first = dfirst_v[span, :]
        dmixed_v[span, :] = (
            dres_ref[span, :] + norm_backward(d_first, unit, rstd, vec_ref[0:1, :])
        ).astype(BF)
        sums_v[0:1, :] += jnp.sum(d_first * unit, axis=0, keepdims=True)
        sums_v[1:2, :] += jnp.sum(d_first, axis=0, keepdims=True)
        sums_v[2:3, :] += jnp.sum(right_v[span, :].astype(F32), axis=0, keepdims=True)

    for_rows(rows, first_norm_back)
    tgrad_copy = load(dmixed_v, tgrad_ref, 0)
    sums_v[4:8, :] = vsum_ref[0:4, :]

    devices = 8 * length
    entries, span = head_dim // devices, width // devices
    v_sum = jnp.sum(pair_v[:, head_dim:].astype(F32), axis=0, keepdims=True)
    v_rows = jnp.broadcast_to(v_sum, (8, head_dim)).astype(BF)
    for j in range(width // 256):
        entry = lax.broadcasted_iota(jnp.int32, (head_dim, 256), 0)
        target = lax.broadcasted_iota(jnp.int32, (head_dim, 256), 1) + j * 256
        spread = (target // span == entry // entries) & (target % span == entry % entries)
        sums_v[3:4, j * 256 : (j + 1) * 256] = dot(v_rows, jnp.where(spread, 1.0, 0.0).astype(BF))[0:1]
    keyval.share_sums(sums_v, s_own, s_out, s_in)

    for copy in mixer.sent[4:]:
        copy.wait_send()
    for n, _ in neighbours[1:]:
        pl.semaphore_wait(credit.at[2 + n], 1)
    query.second()
    keyval.first()
    down_line.onward(3)
    query.third(query_ref)
    for t in range(1, length):
        query.line.direct(t)
    keyval.second()

    tgrad_copy.wait()
    upsum_v = dmixed_v
    up_line.finish(line_v.at[0, z], upsum_v)
    hidden = upsum_v.shape[1] // 2
    piece = upsum_v.shape[0] // 2
    block = piece // 2
    for f in range(4):
        for x_part in range(2):
            start = (f % 2) * piece + x_part * block
            lanes = slice((f // 2) * hidden, (f // 2 + 1) * hidden)
            upsend_v[f * 2 + x_part] = upsum_v[start : start + block, lanes]
    mine = place * 2 + x
    up_copies = []
    for flip, device in zip(range(1, 8), plane):
        up_copies.append(begin(links.copy(upsend_v.at[mine ^ flip], uprecv_v.at[flip], device)))
    for copy in far:
        begin(copy)
    keyval.third(keyval_ref)
    for t in range(1, length):
        keyval.line.direct(t)
    for t in range(2, length):
        mixer.line.onward(t)
        query.line.onward(t)
        keyval.line.onward(t)
    out_block = hidden // length

    def place_up(flip, ref):
        source = mine ^ flip
        base = (source // 2) * (2 * hidden) + (source % 2) * out_block
        for level in range(length):
            lanes = pl.ds(pl.multiple_of(base + level * 2 * out_block, out_block), out_block)
            up_ref[:, lanes] = ref[:, level * out_block : (level + 1) * out_block].astype(up_ref.dtype)

    place_up(0, upsend_v.at[mine])
    for flip, copy in zip(range(1, 8), up_copies):
        copy.wait_recv()
        place_up(flip, uprecv_v.at[flip])
    mixer.finish(mixer_ref)
    for copy in far:
        copy.wait_recv()
    query.finish(query_ref)
    keyval.finish(keyval_ref)
    ubias_line.finish(ub_part.at[z], ubias_out)
    for way in range(2):
        @pl.when(down_line.position(way) >= 1)
        def down_landed():
            down_line.copies[way, length - 1].wait_recv()
    for copy in sent:
        copy.wait_send()
    mixer.line.drain()
    ubias_line.drain()
    query.drain()
    keyval.drain()
    up_line.drain()
    down_line.drain()
    for t in range(1, length):
        @pl.when(t <= z)
        def hopped():
            hops[t - 1].wait_send()


def back(lengths, vmem_args, hbm_args, slots, length, with_length):
    d_residual, kv, wkv = vmem_args[0], vmem_args[2], vmem_args[6]
    rows, width = d_residual.shape
    seg = rows // slots
    both = wkv.shape[1]
    cols = width
    hidden = width // 2
    block = width // (8 * length)
    count = 96 + 16 * length
    hbm = pl.BlockSpec(memory_space=pltpu.HBM)
    vmem = pl.BlockSpec(memory_space=pltpu.VMEM)
    sems = pltpu.SemaphoreType.DMA

    def half(*dims):
        return pltpu.VMEM(dims, BF)

    return pl.pallas_call(
        functools.partial(
            back_kernel, length=length, slots=slots, with_length=with_length, count=count
        ),
        in_specs=[pl.BlockSpec(memory_space=pltpu.SMEM)]
        + [vmem] * len(vmem_args)
        + [hbm] * len(hbm_args),
        out_specs=[hbm] + [vmem] * 5 + [hbm, hbm],
        out_shape=[
            jax.ShapeDtypeStruct((rows, width), BF),
            jax.ShapeDtypeStruct((block, cols), F32),
            jax.ShapeDtypeStruct((block, 2 * both), F32),
            jax.ShapeDtypeStruct((block, width), F32),
            jax.ShapeDtypeStruct((block, 8 * hidden), BF),
            jax.ShapeDtypeStruct((8, hidden // length), F32),
            jax.ShapeDtypeStruct((3, rows, width), BF),
            jax.ShapeDtypeStruct((2, hidden // length, width), BF),
        ],
        scratch_shapes=[
            half(2, width // 4, width),
            half(rows, width),
            half(rows, width),
            half(rows, cols),
            pltpu.VMEM((rows, width), F32),
            pltpu.VMEM((length, 2 * seg, both), F32),
            half(slots, length, seg, both),
            half(slots, length, seg, both),
            half(slots, length, seg, both),
            half(length - 1, slots, seg, both),
            half(length - 1, slots, seg, both),
            half(2, length, hidden // length, width),
            half(2, 2, length - 2, hidden // length, width),
            half(2, hidden // length, width),
            half(8, block, hidden),
            half(8, block, hidden),
            pltpu.VMEM((8, width), F32),
            half(4, width // 8, 128),
            half(4, width // 8, 128),
            half(4, width // 8, 128),
            pltpu.VMEM((length, 8, hidden // length), F32),
            pltpu.VMEM((2, length - 1, 8, hidden // length), F32),
            half(4, width // 8, rows),
            half(4, width // 8, rows),
            half(4, width // 8, rows),
            half(rows, cols),
            half(2, 2, width // 8, cols // 2),
            half(2, 2, width // 8, cols // 2),
            half(2, width // 8, cols // 2),
            half(2, width // 8, cols // 2),
            pltpu.VMEM((width // 8, cols), F32),
            half(length, block, width),
            half(2, length - 1, block, width),
            half(length, block, cols),
            half(2, length - 1, block, cols),
            half(rows, both),
            half(rows, both),
            half(2, 2, width // 8, both),
            half(2, 2, width // 8, both),
            half(2, width // 8, both),
            half(2, width // 8, both),
            pltpu.VMEM((width // 8, 2 * both), F32),
            half(length, block, 2 * both),
            half(2, length - 1, block, 2 * both),
            sems((10,)),
            pltpu.SemaphoreType.REGULAR((5,)),
            sems((count,)),
            sems((count,)),
        ],
        compiler_params=pltpu.CompilerParams(
            collective_id=3, has_side_effects=True, vmem_limit_bytes=125 << 19
        ),
        cost_estimate=pl.CostEstimate(
            flops=12 * rows * width * width, bytes_accessed=40 << 20, transcendentals=0
        ),
    )(lengths, *vmem_args, *hbm_args)


def finish_fast(given, kept, weights):
    tokens, lengths, d_down, up_weight, down_weight, up_bias, where, slots, length, with_length = given
    second, residual, first, queries, kv_all, mixed, lse, vectors = kept
    full_query, full_mixer, full_keyval, up_mine, down_all = weights
    y, c, z, x = where
    rows, width = second.shape
    flat = tokens.reshape(rows, width)
    d_residual, reduced, down_part, up_part, ubias_part, vsum, ends = feed(
        second, d_down, down_all, up_mine, up_weight, up_bias, residual, vectors, down_weight, length
    )
    tokens_grad, query_grad, keyval_all, mixer_grad, up_grad, ubias, far, down_last = back(
        lengths,
        (d_residual, queries, kv_all, mixed, lse, vectors, full_keyval, vsum, ubias_part),
        (flat, first, full_query, full_mixer, reduced, down_part.reshape(length, -1, width), up_part, ends),
        slots,
        length,
        with_length,
    )
    down_grad = pick(down_part.reshape(length, -1, width), z, 0).astype(F32)
    down_grad = down_grad + jnp.where(z > 0, down_last[0].astype(F32), 0.0)
    down_grad = down_grad + jnp.where(z < length - 1, down_last[1].astype(F32), 0.0)
    output = residual + vectors[6:7]
    for term in (reduced[0], far[0], far[1], far[2]):
        output = output + term.astype(F32)
    layer_out = output.astype(BF).reshape(tokens.shape)
    both = full_keyval.shape[1]
    v_block = both // 2 // (8 * length)
    mine = keyval_all[:, both : both + 8].T
    return (
        layer_out,
        tokens_grad.reshape(tokens.shape),
        mine[0],
        mine[1],
        query_grad,
        mine[2],
        keyval_all[:, :both],
        mine[3, :v_block],
        mixer_grad,
        mine[6],
        mine[4],
        mine[5],
        up_grad.astype(F32),
        ubias[0],
        down_grad,
        mine[7],
    )


def body(
    tokens,
    lengths,
    cotangent,
    norm_gain,
    norm_shift,
    query_weight,
    query_bias,
    keyval_weight,
    value_bias,
    mixer_weight,
    mixer_bias,
    ffnorm_gain,
    ffnorm_shift,
    up_weight,
    up_bias,
    down_weight,
    down_bias,
):
    y, c, z, x = [lax.axis_index(name) for name in ("y", "c", "z", "x")]
    length = lax.axis_size("z")
    place = y * 2 + c
    slots, seg, width = tokens.shape
    rows = slots * seg
    head_dim = value_bias.shape[0] * 4
    hidden = up_weight.shape[1]
    hidden_block = hidden // (8 * length)
    hidden_mine = hidden // 8
    with_length = 2 * length * seg > MIN_LEN
    scal = jnp.concatenate([jnp.stack([z, x]).astype(jnp.int32), lengths])

    quarter = width // 4
    v_part = value_bias.shape[0]
    lane = jnp.arange(quarter, dtype=jnp.int32) - place * v_part
    v_wide = jnp.tile(value_bias, quarter // v_part)
    v_place = jnp.where((lane >= 0) & (lane < v_part), v_wide, jnp.zeros_like(v_wide))
    small = jnp.concatenate(
        [
            v.astype(F32)[None]
            for v in (
                norm_gain,
                norm_shift,
                query_bias,
                mixer_bias,
                ffnorm_gain,
                ffnorm_shift,
                down_bias,
                v_place,
            )
        ],
        axis=0,
    )

    down_mine = pick(down_weight.reshape(length, 2, hidden_block, width), x, 1).reshape(
        hidden_mine, width
    )
    up_bias_mine = pick(up_bias.reshape(length, 2, hidden_block), x, 1).reshape(1, hidden_mine)
    aligned = hidden_block % 128 == 0
    up_given = up_weight
    if not aligned:
        up_given = pick(up_weight.reshape(quarter, 4, length, 2, hidden_block), x, 3)
        up_given = up_given.reshape(quarter, 4, hidden_mine).transpose(1, 0, 2)

    token_pos = (z * 2 + x) * seg + jnp.arange(seg, dtype=jnp.int32)
    valid = (token_pos[None, :] < lengths[:, None]).astype(F32).reshape(rows, 1)
    d_down = cotangent.reshape(rows, width)
    if with_length:
        d_down = (d_down.astype(F32) * valid).astype(BF)
    d_out = d_down.astype(F32)

    flat = tokens.reshape(rows, width)
    (
        second,
        residual,
        first,
        queries,
        kv_all,
        mixed,
        lse,
        vectors,
        full_query,
        full_mixer,
        full_keyval,
        up_mine,
        down_all,
    ) = front(
        lengths,
        flat,
        small,
        keyval_weight,
        query_weight,
        mixer_weight,
        up_given,
        d_down,
        slots,
        length,
        with_length,
        aligned,
        hidden_mine,
    )
    if aligned and length == 4:
        return finish_fast(
            (
                tokens,
                lengths,
                d_down,
                up_weight,
                down_weight,
                up_bias_mine.astype(F32),
                (y, c, z, x),
                slots,
                length,
                with_length,
            ),
            (second, residual, first, queries, kv_all, mixed, lse, vectors),
            (full_query, full_mixer, full_keyval, up_mine, down_all.reshape(8 * rows, width)),
        )
    inputs = flat.astype(F32)
    gain, ffgain, d_bias = vectors[0:1], vectors[4:5], vectors[6:7]
    unit1, rstd1 = norm_stats(inputs)
    unit2, rstd2 = norm_stats(residual)
    q_t, mixed_t = queries.T, mixed.T

    d_second, out_parts, down_part, up_part, ubias_part = ffn(
        second,
        down_all.reshape(8 * rows, width),
        up_mine,
        up_bias_mine.astype(F32),
        down_mine,
        length,
    )
    output = residual + scatter_plane([out_parts[i] for i in range(4)]) + d_bias
    layer_out = output.astype(BF).reshape(tokens.shape)
    down_grad = scatter_line(down_part.reshape(length, hidden_block, width), z, length)
    ubias_grad = scatter_line(ubias_part.reshape(length, hidden_block), z, length)
    out_rows = width // (8 * length)
    up_sum = scatter_line(up_part, z, length).astype(BF)
    up_rows = lax.all_to_all(
        up_sum.reshape(8, out_rows, hidden_mine), ("y", "c", "x"), 0, 0, tiled=True
    )
    up_grad = (
        up_rows.reshape(4, 2, out_rows, length, hidden_block)
        .transpose(2, 0, 3, 1, 4)
        .reshape(out_rows, hidden)
        .astype(F32)
    )

    d_residual = d_out + norm_backward(d_second, unit2, rstd2, ffgain)
    d_mix = d_residual.astype(BF)
    d_mixed_t = dot(full_mixer, d_mix, ((1,), (1,))).astype(BF)
    where = (y, c, z, x)
    sizes = (length, width)
    mixer_all = scatter_all(
        mixed,
        d_mix,
        (
            jnp.sum(d_mix.astype(F32), axis=0),
            jnp.sum(d_second * unit2, axis=0),
            jnp.sum(d_second, axis=0),
            jnp.sum(d_out, axis=0),
        ),
        where,
        sizes,
    )

    dq_t, dkv = attn_backward(scal, q_t, kv_all, mixed_t, d_mixed_t, lse, 4, with_length)
    dkv = dkv.reshape(slots, length, 2, seg, 2 * head_dim)
    running = None
    for step in range(length - 1, -1, -1):
        term = dkv[:, step]
        term = pick(term, x, 1) + swap(pick(term, 1 - x, 1).astype(BF), "x").astype(F32)
        if running is not None:
            term = term + lax.ppermute(
                running.astype(BF), "z", [(i, i - 1) for i in range(1, length)]
            ).astype(F32)
        running = term
    d_keyvals = running.reshape(rows, 2 * head_dim).astype(BF)
    d_first = dot(dq_t, full_query, ((0,), (1,))) + dot(d_keyvals, full_keyval, ((1,), (1,)))
    tokens_grad = (d_residual + norm_backward(d_first, unit1, rstd1, gain)).astype(BF)
    d_queries = dq_t.T
    devices = 8 * length
    vbias = jnp.sum(d_keyvals[:, head_dim:].astype(F32), axis=0)
    vbias = jnp.pad(
        vbias.reshape(devices, head_dim // devices),
        ((0, 0), (0, out_rows - head_dim // devices)),
    ).reshape(width)
    query_all = scatter_all(
        first,
        jnp.concatenate([d_queries, d_keyvals], axis=1),
        (
            jnp.sum(d_first * unit1, axis=0),
            jnp.sum(d_first, axis=0),
            jnp.sum(d_queries.astype(F32), axis=0),
            vbias,
        ),
        where,
        sizes,
    )
    kv_end = width + 2 * head_dim
    return (
        layer_out,
        tokens_grad.reshape(tokens.shape),
        query_all[:, kv_end],
        query_all[:, kv_end + 1],
        query_all[:, :width],
        query_all[:, kv_end + 2],
        query_all[:, width:kv_end],
        query_all[: head_dim // devices, kv_end + 3],
        mixer_all[:, :width],
        mixer_all[:, width],
        mixer_all[:, width + 1],
        mixer_all[:, width + 2],
        up_grad,
        ubias_grad,
        down_grad,
        mixer_all[:, width + 3],
    )


def solution(mesh):
    ctx = mesh.shape["ctx"]
    fine = Mesh(mesh.devices.reshape(2, 2, ctx // 2, 2), ("y", "c", "z", "x"))
    fsdp, both, every = ("y", "c"), ("z", "x"), ("y", "c", "z", "x")
    return jax.shard_map(
        body,
        mesh=fine,
        in_specs=(
            P(fsdp, both, None),
            P(fsdp),
            P(fsdp, both, None),
            P(fsdp),
            P(fsdp),
            P(fsdp, None),
            P(fsdp),
            P(fsdp, None),
            P(fsdp),
            P(fsdp, None),
            P(fsdp),
            P(fsdp),
            P(fsdp),
            P(fsdp, None),
            P(fsdp),
            P(fsdp, None),
            P(fsdp),
        ),
        out_specs=(
            P(fsdp, both, None),
            P(fsdp, both, None),
            P(every),
            P(every),
            P(every, None),
            P(every),
            P(every, None),
            P(every),
            P(every, None),
            P(every),
            P(every),
            P(every),
            P(every, None),
            P(every),
            P(every, None),
            P(every),
        ),
        check_vma=False,
    )
```

```python
import functools

import jax
import jax.numpy as jnp
from jax import lax
from jax.experimental import pallas as pl
from jax.experimental.pallas import tpu as pltpu
from jax.sharding import Mesh, PartitionSpec as P

EPSILON = 1e-05
NEG_LARGE = -1e30
MIN_LEN = 1024
BF = jnp.bfloat16
F32 = jnp.float32
GELU_K = 0.7978845608028654
GELU_C = 0.044715


def dot(left_side, right_side, dims=((1,), (0,))):
    return lax.dot_general(left_side, right_side, (dims, ((), ())), preferred_element_type=F32)


def swap(values, axis):
    return lax.ppermute(values, axis, [(0, 1), (1, 0)])


def pick(values, index, axis):
    return lax.dynamic_index_in_dim(values, index, axis, keepdims=False)


def stack_heads(block, head_dim):
    heads = block.shape[0] // head_dim
    return jnp.concatenate([block[h * head_dim : (h + 1) * head_dim] for h in range(heads)], axis=1)


def unstack_heads(stacked, seg):
    heads = stacked.shape[1] // seg
    return jnp.concatenate([stacked[:, h * seg : (h + 1) * seg] for h in range(heads)], axis=0)


def masked_scores(scal_ref, queries, keys, step, seg, heads, with_length, first_block):
    scores = dot(keys, queries) * (keys.shape[1] ** (-0.5))
    pair = keys.shape[0]
    if not (with_length or first_block):
        return scores
    key_pos = lax.broadcasted_iota(jnp.int32, (pair, seg), 0)
    allowed = None
    if first_block:
        query_pos = lax.broadcasted_iota(jnp.int32, (pair, seg), 1) + scal_ref[1] * seg
        allowed = key_pos <= query_pos
    if with_length:
        length = scal_ref[2 + pl.program_id(0)]
        inside = key_pos + (scal_ref[0] - step) * pair < length
        allowed = inside if allowed is None else allowed & inside
    bias = jnp.where(allowed, 0.0, NEG_LARGE).astype(F32)
    return scores + jnp.concatenate([bias] * heads, axis=1)


def attn_fwd_kernel(scal_ref, q_ref, kv_ref, out_ref, lse_ref, *, with_length):
    head_dim = kv_ref.shape[-1] // 2
    seg = q_ref.shape[1]
    heads = q_ref.shape[0] // head_dim
    queries = stack_heads(q_ref[...], head_dim)

    def block(step, state, first_block):
        top, total, accum = state
        keys = kv_ref[0, step, :, :head_dim]
        values = kv_ref[0, step, :, head_dim:]
        scores = masked_scores(scal_ref, queries, keys, step, seg, heads, with_length, first_block)
        new_top = jnp.maximum(top, jnp.max(scores, axis=0, keepdims=True))
        terms = jnp.exp(scores - new_top)
        fade = jnp.exp(top - new_top)
        total = total * fade + jnp.sum(terms, axis=0, keepdims=True)
        accum = accum * fade + dot(values, terms.astype(BF), ((0,), (0,)))
        return new_top, total, accum

    lanes = heads * seg
    state = (
        jnp.full((1, lanes), NEG_LARGE, F32),
        jnp.zeros((1, lanes), F32),
        jnp.zeros((head_dim, lanes), F32),
    )
    state = block(0, state, True)
    top, total, accum = lax.fori_loop(1, scal_ref[0] + 1, lambda t, s: block(t, s, False), state)
    out_ref[...] = unstack_heads(accum / total, seg).astype(BF)
    lse_ref[0, 0] = top + jnp.log(total)


def attn_bwd_kernel(scal_ref, q_ref, kv_ref, out_ref, dout_ref, lse_ref, dq_ref, dkv_ref, *, with_length):
    head_dim = kv_ref.shape[-1] // 2
    seg = q_ref.shape[1]
    heads = q_ref.shape[0] // head_dim
    scale = head_dim ** (-0.5)
    queries = stack_heads(q_ref[...], head_dim)
    d_mixed = stack_heads(dout_ref[...], head_dim)
    mixed = stack_heads(out_ref[...], head_dim)
    delta = jnp.sum(mixed.astype(F32) * d_mixed.astype(F32), axis=0, keepdims=True)
    lse = lse_ref[0, 0]

    @pl.when(pl.program_id(1) == 0)
    def clear():
        dkv_ref[...] = jnp.zeros_like(dkv_ref)

    def block(step, accum, first_block):
        keys = kv_ref[0, step, :, :head_dim]
        values = kv_ref[0, step, :, head_dim:]
        scores = masked_scores(scal_ref, queries, keys, step, seg, heads, with_length, first_block)
        probs = jnp.exp(scores - lse)
        d_probs = dot(values, d_mixed)
        d_scores = (probs * (d_probs - delta)).astype(BF)
        dkv_ref[0, step, :, :head_dim] += dot(d_scores, queries, ((1,), (1,))) * scale
        dkv_ref[0, step, :, head_dim:] += dot(probs.astype(BF), d_mixed, ((1,), (1,)))
        return accum + dot(keys, d_scores, ((0,), (0,)))

    accum = block(0, jnp.zeros((head_dim, heads * seg), F32), True)
    accum = lax.fori_loop(1, scal_ref[0] + 1, lambda t, s: block(t, s, False), accum)
    dq_ref[...] = (unstack_heads(accum, seg) * scale).astype(BF)


def attn_specs(slots, steps, pair, seg, rows, groups, head_dim):
    lanes = rows // groups // head_dim * seg
    scal = pl.BlockSpec(memory_space=pltpu.SMEM)
    feat = pl.BlockSpec((rows // groups, seg), lambda s, g: (g, s))
    kv = pl.BlockSpec((1, steps, pair, 2 * head_dim), lambda s, g: (s, 0, 0, 0))
    lse = pl.BlockSpec((1, 1, 1, lanes), lambda s, g: (s, g, 0, 0))
    return scal, feat, kv, lse, lanes


def attn_forward(scal, q_t, kv, groups, with_length):
    slots, steps, pair, width = kv.shape
    rows, cols = q_t.shape
    seg = cols // slots
    scal_s, feat, kv_s, lse_s, lanes = attn_specs(slots, steps, pair, seg, rows, groups, width // 2)
    return pl.pallas_call(
        functools.partial(attn_fwd_kernel, with_length=with_length),
        grid=(slots, groups),
        in_specs=[scal_s, feat, kv_s],
        out_specs=[feat, lse_s],
        out_shape=[
            jax.ShapeDtypeStruct((rows, cols), BF),
            jax.ShapeDtypeStruct((slots, groups, 1, lanes), F32),
        ],
        compiler_params=pltpu.CompilerParams(vmem_limit_bytes=40 << 20),
        cost_estimate=pl.CostEstimate(
            flops=4 * rows * cols * steps * pair, bytes_accessed=6 << 20, transcendentals=0
        ),
    )(scal, q_t, kv)


def attn_backward(scal, q_t, kv, out_t, dout_t, lse, groups, with_length):
    slots, steps, pair, width = kv.shape
    rows, cols = q_t.shape
    seg = cols // slots
    scal_s, feat, kv_s, lse_s, lanes = attn_specs(slots, steps, pair, seg, rows, groups, width // 2)
    return pl.pallas_call(
        functools.partial(attn_bwd_kernel, with_length=with_length),
        grid=(slots, groups),
        in_specs=[scal_s, feat, kv_s, feat, feat, lse_s],
        out_specs=[feat, kv_s],
        out_shape=[
            jax.ShapeDtypeStruct((rows, cols), BF),
            jax.ShapeDtypeStruct(kv.shape, F32),
        ],
        compiler_params=pltpu.CompilerParams(vmem_limit_bytes=48 << 20),
        cost_estimate=pl.CostEstimate(
            flops=10 * rows * cols * steps * pair, bytes_accessed=9 << 20, transcendentals=0
        ),
    )(scal, q_t, kv, out_t, dout_t, lse)


def norm_stats(values):
    center = values - jnp.mean(values, axis=-1, keepdims=True)
    spread = jnp.mean(center * center, axis=-1, keepdims=True)
    rstd = lax.rsqrt(spread + EPSILON)
    return center * rstd, rstd


def norm_backward(d_values, unit, rstd, gain):
    scaled = d_values * gain
    return rstd * (
        scaled
        - jnp.mean(scaled, axis=-1, keepdims=True)
        - unit * jnp.mean(scaled * unit, axis=-1, keepdims=True)
    )


def gather_rows(shard, x, place):
    rows = shard.shape[0]
    half = rows // 2
    mine = lax.dynamic_slice_in_dim(shard, x * half, half, 0)
    direct = swap(mine, "y")
    other = swap(direct, "x")
    sib = swap(shard, "c")
    sib_direct = swap(direct, "c")
    sib_other = swap(other, "c")
    full = jnp.zeros((4 * rows,) + shard.shape[1:], shard.dtype)
    far = place ^ 2
    pieces = (
        (shard, place * rows),
        (sib, (place ^ 1) * rows),
        (direct, far * rows + x * half),
        (other, far * rows + (1 - x) * half),
        (sib_direct, (far ^ 1) * rows + x * half),
        (sib_other, (far ^ 1) * rows + (1 - x) * half),
    )
    for piece, start in pieces:
        full = lax.dynamic_update_slice_in_dim(full, piece, start, 0)
    return full


def gather_plane(block):
    half = block.shape[0] // 2
    from_x = swap(block, "x")
    from_y = swap(block, "y")
    diag = jnp.concatenate([swap(from_y[:half], "x"), swap(from_x[half:], "y")], axis=0)
    return [
        jnp.concatenate([part, swap(part, "c")], axis=0) for part in (block, from_x, from_y, diag)
    ]


def scatter_plane(parts):
    rows = parts[0].shape[0] // 2
    half = rows // 2
    own, to_x, to_y, diag = [
        part[:rows].astype(F32) + swap(part[rows:].astype(BF), "c").astype(F32) for part in parts
    ]
    via_x = swap(diag[:half].astype(BF), "x").astype(F32)
    via_y = swap(diag[half:].astype(BF), "y").astype(F32)
    to_y = jnp.concatenate([to_y[:half] + via_x, to_y[half:]], axis=0)
    to_x = jnp.concatenate([to_x[:half], to_x[half:] + via_y], axis=0)
    return own + swap(to_x.astype(BF), "x").astype(F32) + swap(to_y.astype(BF), "y").astype(F32)


def scatter_line(parts, z, length):
    def block(index):
        return pick(parts, jnp.clip(index, 0, length - 1), 0).astype(F32)

    from_left = from_right = None
    for step in range(1, length):
        up = block(length - step + z)
        down = block(z - length + step)
        if from_left is not None:
            up, down = up + from_left, down + from_right
        from_left = lax.ppermute(up.astype(BF), "z", [(i, i + 1) for i in range(step)]).astype(F32)
        from_right = lax.ppermute(
            down.astype(BF), "z", [(i, i - 1) for i in range(length - step, length)]
        ).astype(F32)
    return block(z) + from_left + from_right


def scatter_all(left_side, right_side, vectors, place_yczx, sizes):
    y, c, z, x = place_yczx
    length, width = sizes
    tokens = left_side.shape[0]
    block = width // (8 * length)
    left_parts = left_side.reshape(tokens, 2, 2, width // 4)
    left_mine = pick(left_parts, c, 2).reshape(tokens, width // 2)
    left_sib = swap(pick(left_parts, 1 - c, 2), "c").reshape(tokens, width // 2)
    right_sib = swap(right_side, "c")
    partial = dot(
        jnp.concatenate([left_mine, left_sib], axis=0),
        jnp.concatenate([right_side, right_sib], axis=0),
        ((0,), (0,)),
    )
    extra = jnp.pad(jnp.stack(vectors, axis=1), ((0, 0), (0, 128 - len(vectors))))
    extra = extra.reshape(2, 2, width // 4, 128)
    extra = pick(extra, c, 1) + swap(pick(extra, 1 - c, 1).astype(BF), "c").astype(F32)
    partial = jnp.concatenate([partial, extra.reshape(width // 2, 128)], axis=1)
    cols = partial.shape[1]
    partial = partial.reshape(2, length, 2, block, cols)
    cut = (cols // 256) * 128
    side_a, side_b = partial[..., :cut], partial[..., cut:]
    side_a = pick(side_a, y, 0) + swap(pick(side_a, 1 - y, 0).astype(BF), "y").astype(F32)
    side_b = pick(side_b, x, 2) + swap(pick(side_b, 1 - x, 2).astype(BF), "x").astype(F32)
    side_a = pick(side_a, x, 1) + swap(pick(side_a, 1 - x, 1).astype(BF), "x").astype(F32)
    side_b = pick(side_b, y, 0) + swap(pick(side_b, 1 - y, 0).astype(BF), "y").astype(F32)
    return scatter_line(jnp.concatenate([side_a, side_b], axis=-1), z, length)


MESH = pl.DeviceIdType.MESH


def remote(src, dst, send_sems, recv_sems, index, device):
    return pltpu.make_async_remote_copy(
        src_ref=src,
        dst_ref=dst,
        send_sem=send_sems.at[index],
        recv_sem=recv_sems.at[index],
        device_id=device,
        device_id_type=MESH,
    )


def greet(devices):
    barrier = pltpu.get_barrier_semaphore()
    for device in devices:
        pl.semaphore_signal(barrier, inc=1, device_id=device, device_id_type=MESH)
    pl.semaphore_wait(barrier, len(devices))


def tiles(count, size):
    def over(fn):
        @pl.loop(0, count)
        def step(index):
            fn(pl.ds(pl.multiple_of(index * size, size), size), index)

    return over


def gelu_pair(upper):
    inner = jnp.tanh(upper * (GELU_K + (GELU_K * GELU_C) * (upper * upper)))
    half = 0.5 + 0.5 * inner
    slope = half + (0.5 * upper) * (1.0 - inner * inner) * (
        GELU_K + (3.0 * GELU_K * GELU_C) * (upper * upper)
    )
    return upper * half, slope


def ffn_kernel(
    second_ref,
    down_all_ref,
    up_ref,
    ubias_ref,
    down_ref,
    dsecond_ref,
    out_parts_ref,
    down_part_ref,
    up_part_ref,
    ubias_part_ref,
    tokens_v,
    cots_v,
    up_v,
    down_v,
    active_v,
    dupper_v,
    sib_out,
    sib_in,
    chip_out,
    chip_in,
    acc_v,
    stage_v,
    load_sem,
    stage_sem,
    gs_send,
    gs_recv,
    rs_send,
    rs_recv,
    *,
    length,
):
    rows, width = second_ref.shape
    hidden = up_ref.shape[1]
    half = rows // 2
    chunk = 2 * rows
    y, c, x = [lax.axis_index(name) for name in ("y", "c", "x")]
    sib, to_x, to_y = {"c": 1 - c}, {"x": 1 - x}, {"y": 1 - y}
    diag = {"x": 1 - x, "y": 1 - y}
    chips = (None, to_x, to_y, diag)

    loads = [
        pltpu.make_async_copy(second_ref, tokens_v.at[0, pl.ds(0, rows)], load_sem.at[0]),
        pltpu.make_async_copy(down_ref, down_v, load_sem.at[1]),
        pltpu.make_async_copy(down_all_ref, cots_v, load_sem.at[2]),
        pltpu.make_async_copy(up_ref, up_v, load_sem.at[3]),
    ]
    for load in loads:
        load.start()
    greet((sib, to_x, to_y, diag))
    loads[0].wait()

    same, other = pl.ds(0, rows), pl.ds(rows, rows)
    top, bottom = pl.ds(0, half), pl.ds(half, half)

    def gather(index, chip, span_src, chip_dst, span_dst, device):
        return remote(
            tokens_v.at[chip, span_src], tokens_v.at[chip_dst, span_dst], gs_send, gs_recv, index, device
        )

    send_x = gather(0, 0, same, 1, same, to_x)
    send_y = gather(1, 0, same, 2, same, to_y)
    share = [gather(2 + k, k, same, k, other, sib) for k in range(4)]
    diag_x = gather(6, 2, top, 3, top, to_x)
    diag_y = gather(7, 1, bottom, 3, bottom, to_y)
    send_x.start()
    send_y.start()
    share[0].start()

    loads[1].wait()
    loads[2].wait()

    @tiles(4 * chunk // 512, 512)
    def grad_active(span, index):
        @tiles(hidden // 512, 512)
        def columns(cols, _):
            dupper_v[span, cols] = dot(cots_v[span, :], down_v[cols, :], ((1,), (1,))).astype(BF)

    loads[3].wait()

    def chip_work(k):
        @tiles(hidden // 256, 256)
        def columns(cols, _):
            block = pl.ds(k * chunk, chunk)
            upper = dot(tokens_v[k], up_v[:, cols]) + ubias_ref[:, cols]
            active, slope = gelu_pair(upper)
            active_v[block, cols] = active.astype(BF)
            d_upper = (dupper_v[block, cols].astype(F32) * slope).astype(BF)
            dupper_v[block, cols] = d_upper
            part = jnp.sum(d_upper.astype(F32), axis=0, keepdims=True)
            if k == 0:
                ubias_part_ref[:, cols] = part
            else:
                ubias_part_ref[:, cols] += part

        @tiles(width // 512, 512)
        def to_sibling(cols, _):
            sib_out[k, :, cols] = dot(
                dupper_v[pl.ds(k * chunk + rows, rows), :], up_v[cols, :], ((1,), (1,))
            ).astype(BF)

        pair = remote(sib_out.at[k], sib_in.at[k], rs_send, rs_recv, k, sib)
        pair.start()

        @tiles(width // 512, 512)
        def keep(cols, _):
            acc_v[:, cols] = dot(dupper_v[pl.ds(k * chunk, rows), :], up_v[cols, :], ((1,), (1,)))

        pair.wait_recv()
        if k == 0:
            dsecond_ref[...] = acc_v[...] + sib_in[0].astype(F32)
            return [pair]
        chip_out[k - 1] = (acc_v[...] + sib_in[k].astype(F32)).astype(BF)
        far = remote(chip_out.at[k - 1], chip_in.at[k - 1], rs_send, rs_recv, 3 + k, chips[k])
        far.start()
        return [pair, far]

    share[0].wait_recv()
    sent = chip_work(0)
    send_x.wait_recv()
    share[1].start()
    diag_y.start()
    send_y.wait_recv()
    share[2].start()
    diag_x.start()
    share[1].wait_recv()
    sent += chip_work(1)
    share[2].wait_recv()
    sent += chip_work(2)
    diag_x.wait_recv()
    diag_y.wait_recv()
    share[3].start()
    share[3].wait_recv()
    sent += chip_work(3)

    def staged(slot, value, target):
        stage_v[slot] = value.astype(BF)
        copy = pltpu.make_async_copy(stage_v.at[slot], target, stage_sem.at[slot])
        copy.start()
        return copy

    @pl.loop(0, 4)
    def outputs(k):
        block = pl.ds(pl.multiple_of(k * chunk, chunk), chunk)
        copies = []
        for j in range(width // 512):
            cols = pl.ds(j * 512, 512)
            copies.append(
                staged(j, dot(active_v[block, :], down_v[:, cols]), out_parts_ref.at[k, :, cols])
            )
        for copy in copies:
            copy.wait()

    @pl.loop(0, hidden // 512)
    def downs(r):
        block = pl.ds(pl.multiple_of(r * 512, 512), 512)
        copies = []
        for j in range(width // 512):
            cols = pl.ds(j * 512, 512)
            copies.append(
                staged(
                    j,
                    dot(active_v[:, block], cots_v[:, cols], ((0,), (0,))),
                    down_part_ref.at[block, cols],
                )
            )
        for copy in copies:
            copy.wait()

    quarter = width // 4
    piece = quarter // length

    @pl.loop(0, hidden // 512)
    def ups(r):
        cols = pl.ds(pl.multiple_of(r * 512, 512), 512)
        copies = []
        for f in range(4):
            value = None
            for k in range(4):
                term = dot(
                    tokens_v[k, :, f * quarter : (f + 1) * quarter],
                    dupper_v[k * chunk : (k + 1) * chunk, cols],
                    ((0,), (0,)),
                )
                value = term if value is None else value + term
            stage_v[f] = value.astype(BF)
            for level in range(length):
                copy = pltpu.make_async_copy(
                    stage_v.at[f, pl.ds(level * piece, piece)],
                    up_part_ref.at[level, f, :, cols],
                    stage_sem.at[4 + f * length + level],
                )
                copy.start()
                copies.append(copy)
        for copy in copies:
            copy.wait()

    for k in range(3):
        remote(chip_out.at[k], chip_in.at[k], rs_send, rs_recv, 4 + k, chips[k + 1]).wait_recv()
    dsecond_ref[...] += (
        chip_in[0].astype(F32) + chip_in[1].astype(F32) + chip_in[2].astype(F32)
    )
    for copy in [send_x, send_y, diag_x, diag_y] + share + sent:
        copy.wait_send()


def ffn(second, down_all, up_mine, ubias, down_mine, length):
    rows, width = second.shape
    hidden = up_mine.shape[1]
    hbm = pl.BlockSpec(memory_space=pltpu.HBM)
    vmem = pl.BlockSpec(memory_space=pltpu.VMEM)
    sems = pltpu.SemaphoreType.DMA
    return pl.pallas_call(
        functools.partial(ffn_kernel, length=length),
        in_specs=[hbm, hbm, hbm, vmem, hbm],
        out_specs=[vmem, hbm, hbm, hbm, vmem],
        out_shape=[
            jax.ShapeDtypeStruct((rows, width), F32),
            jax.ShapeDtypeStruct((4, 2 * rows, width), BF),
            jax.ShapeDtypeStruct((hidden, width), BF),
            jax.ShapeDtypeStruct((length, 4, width // 4 // length, hidden), BF),
            jax.ShapeDtypeStruct((1, hidden), F32),
        ],
        scratch_shapes=[
            pltpu.VMEM((4, 2 * rows, width), BF),
            pltpu.VMEM((8 * rows, width), BF),
            pltpu.VMEM((width, hidden), BF),
            pltpu.VMEM((hidden, width), BF),
            pltpu.VMEM((8 * rows, hidden), BF),
            pltpu.VMEM((8 * rows, hidden), BF),
            pltpu.VMEM((4, rows, width), BF),
            pltpu.VMEM((4, rows, width), BF),
            pltpu.VMEM((3, rows, width), BF),
            pltpu.VMEM((3, rows, width), BF),
            pltpu.VMEM((rows, width), F32),
            pltpu.VMEM((4, 512, 512), BF),
            sems((4,)),
            sems((4 + 4 * length,)),
            sems((8,)),
            sems((8,)),
            sems((7,)),
            sems((7,)),
        ],
        compiler_params=pltpu.CompilerParams(
            collective_id=1, has_side_effects=True, vmem_limit_bytes=60 << 20
        ),
        cost_estimate=pl.CostEstimate(
            flops=12 * 8 * rows * width * hidden, bytes_accessed=40 << 20, transcendentals=0
        ),
    )(second, down_all, up_mine, ubias, down_mine)


ROW_TILE = 32


def for_rows(total, fn):
    @pl.loop(0, total // ROW_TILE)
    def step(index):
        fn(pl.ds(pl.multiple_of(index * ROW_TILE, ROW_TILE), ROW_TILE))


def norm_rows(values):
    center = values - jnp.mean(values, axis=-1, keepdims=True)
    spread = jnp.mean(center * center, axis=-1, keepdims=True)
    rstd = lax.rsqrt(spread + EPSILON)
    return center * rstd, rstd


class Gathered:
    def __init__(self, shard_ref, full_ref, sems, base, where):
        self.y, self.c, self.x = where
        self.shard, self.full, self.sems, self.base = shard_ref, full_ref, sems, base
        self.rows = shard_ref.shape[0]
        self.half = self.rows // 2
        self.step = self.half // 4
        self.place = self.y * 2 + self.c

    def copy(self, src, dst, index, device):
        send_sems, recv_sems = self.sems
        return remote(src, dst, send_sems, recv_sems, self.base + index, device)

    def span(self, place, side, i):
        start = place * self.rows + side * self.half + i * self.step
        return self.full.at[pl.ds(pl.multiple_of(start, self.step), self.step)]

    def over_y(self, i):
        start = pl.multiple_of(self.x * self.half + i * self.step, self.step)
        return self.copy(
            self.shard.at[pl.ds(start, self.step)], self.span(self.place, self.x, i), i, {"y": 1 - self.y}
        )

    def over_x(self, i):
        ref = self.span(self.place ^ 2, self.x, i)
        return self.copy(ref, ref, 4 + i, {"x": 1 - self.x})

    def over_c(self, i, side):
        ref = self.span(self.place ^ 2, self.x if side == 0 else 1 - self.x, i)
        return self.copy(ref, ref, 8 + 4 * side + i, {"c": 1 - self.c})

    def own_c(self):
        start = pl.multiple_of(self.place * self.rows, self.rows)
        return self.copy(self.shard, self.full.at[pl.ds(start, self.rows)], 16, {"c": 1 - self.c})

    def settle(self):
        self.own_c().wait_recv()
        for i in range(4):
            self.over_c(i, 0).wait_recv()
            self.over_c(i, 1).wait_recv()

    def own(self, sem):
        start = pl.multiple_of(self.place * self.rows, self.rows)
        return pltpu.make_async_copy(self.shard, self.full.at[pl.ds(start, self.rows)], sem)


class Arrivals:
    def __init__(self, order, begin):
        self.order, self.begin = order, begin
        self.next = 0
        self.behind = None

    def event(self):
        if self.next == len(self.order):
            return
        weight, i = self.order[self.next]
        self.next += 1
        weight.over_y(i).wait_recv()
        self.begin(weight.over_x(i))
        self.begin(weight.over_c(i, 0))
        self.late()
        self.behind = (weight, i)

    def late(self):
        if self.behind is not None:
            weight, i = self.behind
            weight.over_x(i).wait_recv()
            self.begin(weight.over_c(i, 1))
        self.behind = None


def front_kernel(
    lengths_ref,
    tokens_v,
    *refs,
    length,
    slots,
    with_length,
    aligned,
):
    smalls, refs = refs[:8], refs[8:]
    (
    kvw_ref,
    qw_ref,
    mw_ref,
    up_ref,
    cot_ref,
    second_ref,
    residual_ref,
    first_v,
    q_v,
    kv_v,
    mixed_v,
    lse_ref,
    vec_v,
    wq_out,
    wm_out,
    wkv_v,
    up_out,
    cots_out,
    wq_v,
    wm_v,
    smalls_v,
    local_sem,
    w_send,
    w_recv,
    s_send,
    s_recv,
    k_send,
    k_recv,
    u_send,
    u_recv,
    uz_send,
    uz_recv,
    c_send,
    c_recv,
    smalls_ref,
    ) = refs
    rows, width = tokens_v.shape
    seg = rows // slots
    head_dim = kvw_ref.shape[1] // 2
    heads = width // head_dim
    group = 4
    quarter = width // 4
    y, c, z, x = [lax.axis_index(name) for name in ("y", "c", "z", "x")]
    place = y * 2 + c
    sib, to_x, to_y = {"c": 1 - c}, {"x": 1 - x}, {"y": 1 - y}
    cross, diag = {"y": 1 - y, "c": 1 - c}, {"x": 1 - x, "y": 1 - y}

    weights = [
        Gathered(ref, full, (w_send, w_recv), 17 * n, (y, c, x))
        for n, (ref, full) in enumerate(((qw_ref, wq_v), (mw_ref, wm_v)))
    ]
    query_w, mixer_w = weights
    locals_ = [query_w.own(local_sem.at[0]), mixer_w.own(local_sem.at[1])]
    kv_rows = pl.ds(pl.multiple_of(place * quarter, quarter), quarter)
    locals_.append(pltpu.make_async_copy(kvw_ref, wkv_v.at[kv_rows], local_sem.at[2]))
    for row, vector in enumerate(smalls):
        smalls_ref[row : row + 1, :] = vector[...].astype(F32).reshape(1, -1)
    locals_.append(pltpu.make_async_copy(smalls_ref, smalls_v.at[place], local_sem.at[3]))
    for copy in locals_:
        copy.start()

    barrier = pltpu.get_barrier_semaphore()
    for device in (sib, to_x, to_y, cross, diag):
        pl.semaphore_signal(barrier, inc=1, device_id=device, device_id_type=MESH)
    for other in range(length):
        @pl.when(other != z)
        def hello():
            pl.semaphore_signal(barrier, inc=1, device_id={"z": other}, device_id_type=MESH)
    pl.semaphore_wait(barrier, 5 + length - 1)

    sent = []

    def begin(copy):
        copy.start()
        sent.append(copy)
        return copy

    small_copies = [
        begin(remote(smalls_ref, smalls_v.at[place], s_send, s_recv, n, device))
        for n, device in enumerate((sib, to_y, cross))
    ]
    kv_near = begin(remote(kvw_ref, wkv_v.at[kv_rows], s_send, s_recv, 3, sib))
    kv_far = begin(remote(kvw_ref, wkv_v.at[kv_rows], s_send, s_recv, 4, to_y))
    part = quarter // length
    hidden = up_out.shape[1]
    block = hidden // length

    def up_copies(index, flip, span, device):
        target = place ^ flip
        dst_rows = pl.ds(pl.multiple_of(place * quarter + span[0], span[1]), span[1])
        copies = []
        for b in range(length if aligned else 1):
            if aligned:
                start = target * (hidden * 2) + (2 * b + x) * block
                src = up_ref.at[pl.ds(span[0], span[1]), pl.ds(pl.multiple_of(start, block), block)]
                dst = up_out.at[dst_rows, pl.ds(b * block, block)]
            else:
                src = up_ref.at[target, pl.ds(span[0], span[1])]
                dst = up_out.at[dst_rows]
            n = index * length + b
            if device is None:
                copies.append(pltpu.make_async_copy(src, dst, u_send.at[n]))
            else:
                copies.append(remote(src, dst, u_send, u_recv, n, device))
        return copies

    up_local = [] if aligned else up_copies(0, 0, (0, quarter), None)
    up_near = up_copies(1, 1, (0, quarter), sib)
    z_part = (pl.multiple_of(z * part, part), part)
    up_far = up_copies(2, 2, z_part, to_y) + up_copies(3, 3, z_part, cross)

    def up_share(k, source, target):
        start = (place ^ (2 + k)) * quarter + source * part
        ref = up_out.at[pl.ds(pl.multiple_of(start, part), part)]
        return pltpu.make_async_remote_copy(
            src_ref=ref,
            dst_ref=ref,
            send_sem=uz_send.at[k, target],
            recv_sem=uz_recv.at[k, source],
            device_id={"z": target},
            device_id_type=MESH,
        )

    same, other_half = pl.ds(0, rows), pl.ds(rows, rows)
    for copy in up_far:
        begin(copy)
    for i in range(4):
        begin(query_w.over_y(i))
    for i in range(4):
        begin(mixer_w.over_y(i))
    cot_y = begin(remote(cot_ref, cots_out.at[2, same], c_send, c_recv, 1, to_y))
    cot_x = begin(remote(cot_ref, cots_out.at[1, same], c_send, c_recv, 0, to_x))
    stream = Arrivals([(query_w, i) for i in range(4)] + [(mixer_w, i) for i in range(4)], begin)
    begin(query_w.own_c())

    for copy in small_copies:
        copy.wait_recv()
    locals_[3].wait()
    vec_v[...] = jnp.concatenate([smalls_v[f] for f in range(4)], axis=1)

    def first_norm(span):
        unit, _ = norm_rows(tokens_v[span, :].astype(F32))
        first_v[span, :] = (unit * vec_v[0:1, :] + vec_v[1:2, :]).astype(BF)

    for_rows(rows, first_norm)

    kv_far.wait_recv()
    far_rows = wkv_v.at[pl.ds(pl.multiple_of((place ^ 2) * quarter, quarter), quarter)]
    kv_pass = begin(remote(far_rows, far_rows, s_send, s_recv, 5, sib))
    kv_near.wait_recv()
    locals_[2].wait()
    kv_pass.wait_recv()
    v_bias = (
        vec_v[7:8, 0:head_dim]
        + vec_v[7:8, quarter : quarter + head_dim]
        + vec_v[7:8, 2 * quarter : 2 * quarter + head_dim]
        + vec_v[7:8, 3 * quarter : 3 * quarter + head_dim]
    )
    keyvals = dot(first_v[...], wkv_v[...]) + jnp.concatenate([jnp.zeros_like(v_bias), v_bias], axis=1)
    mine = pl.ds(pl.multiple_of(x * seg, seg), seg)
    for s in range(slots):
        kv_v[s, 0, mine, :] = keyvals[s * seg : (s + 1) * seg].astype(BF)

    def kv_up(t):
        return remote(kv_v.at[:, t - 1, mine], kv_v.at[:, t, mine], k_send, k_recv, t, {"z": z + 1})

    def kv_side(t):
        ref = kv_v.at[:, t, mine]
        return remote(ref, ref, k_send, k_recv, length + t, to_x)

    def kv_step(t):
        if t:
            @pl.when(z >= t)
            def arrive():
                kv_up(t).wait_recv()

        @pl.when(z >= t)
        def side():
            kv_side(t).start()

        if t + 1 < length:
            @pl.when((z >= t) & (z < length - 1))
            def onward():
                kv_up(t + 1).start()

    for t in range(length):
        kv_step(t)
    for copy in up_far:
        copy.wait_recv()
    for target in range(length):
        @pl.when(target != z)
        def share():
            for k in range(2):
                up_share(k, z, target).start()

    while stream.next < 4:
        stream.event()

    top, bottom = pl.ds(0, rows // 2), pl.ds(rows // 2, rows // 2)
    if not aligned:
        cot_local = pltpu.make_async_copy(cot_ref, cots_out.at[0, same], local_sem.at[4])
        cot_local.start()
    cot_share = [
        remote(cot_ref if k == 0 else cots_out.at[k, same], cots_out.at[k, other_half], c_send, c_recv, 2 + k, sib)
        for k in range(3 if aligned else 4)
    ]

    for copy in up_local:
        copy.start()
    for copy in up_near:
        begin(copy)
    begin(mixer_w.own_c())
    begin(cot_share[0])
    stream.late()
    locals_[0].wait()
    query_w.settle()

    @tiles(width // 512, 512)
    def project(cols, _):
        q_v[:, cols] = (dot(first_v[...], wq_v[:, cols]) + vec_v[2:3, cols]).astype(BF)

    wq_copy = pltpu.make_async_copy(wq_v, wq_out, local_sem.at[5])
    wq_copy.start()
    for t in range(length):
        @pl.when(z >= t)
        def arrived():
            kv_side(t).wait_recv()
            kv_side(t).wait_send()

        if t:
            @pl.when((z >= t - 1) & (z < length - 1))
            def gone():
                kv_up(t).wait_send()

    scale = head_dim ** (-0.5)

    def attend(s, g):
        lanes = pl.ds(pl.multiple_of(g * group * head_dim, group * head_dim), group * head_dim)
        wide = q_v[pl.ds(s * seg, seg), lanes]
        queries = jnp.concatenate(
            [wide[:, h * head_dim : (h + 1) * head_dim] for h in range(group)], axis=0
        )

        def step(t, state, diagonal):
            top_, total, accum = state
            keys = kv_v[s, t, :, :head_dim]
            values = kv_v[s, t, :, head_dim:]
            scores = dot(keys, queries, ((1,), (1,))) * scale
            if diagonal or with_length:
                key_pos = lax.broadcasted_iota(jnp.int32, (2 * seg, seg), 0)
                allowed = None
                if diagonal:
                    query_pos = lax.broadcasted_iota(jnp.int32, (2 * seg, seg), 1) + x * seg
                    allowed = key_pos <= query_pos
                if with_length:
                    inside = key_pos + (z - t) * (2 * seg) < lengths_ref[s]
                    allowed = inside if allowed is None else allowed & inside
                bias = jnp.where(allowed, 0.0, NEG_LARGE).astype(F32)
                scores = scores + jnp.concatenate([bias] * group, axis=1)
            new_top = jnp.maximum(top_, jnp.max(scores, axis=0, keepdims=True))
            terms = jnp.exp(scores - new_top)
            fade = jnp.exp(top_ - new_top)
            total = total * fade + jnp.sum(terms, axis=0, keepdims=True)
            accum = accum * fade + dot(values, terms.astype(BF), ((0,), (0,)))
            return new_top, total, accum

        span = group * seg
        state = (
            jnp.full((1, span), NEG_LARGE, F32),
            jnp.zeros((1, span), F32),
            jnp.zeros((head_dim, span), F32),
        )
        state = step(0, state, True)
        top_, total, accum = lax.fori_loop(1, z + 1, lambda t, st: step(t, st, False), state)
        out = accum / total
        mixed_v[pl.ds(s * seg, seg), lanes] = jnp.concatenate(
            [out[:, h * seg : (h + 1) * seg].T for h in range(group)], axis=1
        ).astype(BF)
        lse_ref[s, g] = top_ + jnp.log(total)

    for s in range(slots):
        for g in range(heads // group):
            attend(s, g)
            stream.event()

    stream.late()
    locals_[1].wait()
    mixer_w.settle()
    wm_copy = pltpu.make_async_copy(wm_v, wm_out, local_sem.at[6])
    wm_copy.start()

    @tiles(width // 512, 512)
    def mix(cols, _):
        residual_ref[:, cols] = (
            tokens_v[:, cols].astype(F32) + dot(mixed_v[...], wm_v[:, cols]) + vec_v[3:4, cols]
        )

    def second_norm(span):
        unit, _ = norm_rows(residual_ref[span, :])
        second_ref[span, :] = (unit * vec_v[4:5, :] + vec_v[5:6, :]).astype(BF)

    for_rows(rows, second_norm)

    cot_x.wait_recv()
    cot_y.wait_recv()
    begin(cot_share[1])
    begin(cot_share[2])
    if not aligned:
        cot_dx = begin(remote(cots_out.at[2, top], cots_out.at[3, top], c_send, c_recv, 6, to_x))
        cot_dy = begin(remote(cots_out.at[1, bottom], cots_out.at[3, bottom], c_send, c_recv, 7, to_y))
        cot_dx.wait_recv()
        cot_dy.wait_recv()
        begin(cot_share[3])
    for copy in cot_share + up_near:
        copy.wait_recv()
    for copy in up_local:
        copy.wait()
    for target in range(length):
        @pl.when(target != z)
        def shared():
            for k in range(2):
                up_share(k, z, target).wait_send()
                up_share(k, target, z).wait_recv()
    for copy in sent:
        copy.wait_send()
    for copy in (wq_copy, wm_copy) + (() if aligned else (cot_local,)):
        copy.wait()


def front(lengths, tokens, smalls, kvw, qw, mw, up, cot, slots, length, with_length, aligned, hidden):
    rows, width = tokens.shape
    seg = rows // slots
    both = kvw.shape[1]
    groups = width // (both // 2) // 4
    hbm = pl.BlockSpec(memory_space=pltpu.HBM)
    vmem = pl.BlockSpec(memory_space=pltpu.VMEM)
    sems = pltpu.SemaphoreType.DMA
    return pl.pallas_call(
        functools.partial(
            front_kernel, length=length, slots=slots, with_length=with_length, aligned=aligned
        ),
        in_specs=[pl.BlockSpec(memory_space=pltpu.SMEM), vmem] + [vmem] * 8 + [hbm] * 5,
        out_specs=[vmem] * 8 + [hbm, hbm, vmem, hbm, hbm],
        out_shape=[
            jax.ShapeDtypeStruct((rows, width), BF),
            jax.ShapeDtypeStruct((rows, width), F32),
            jax.ShapeDtypeStruct((rows, width), BF),
            jax.ShapeDtypeStruct((rows, width), BF),
            jax.ShapeDtypeStruct((slots, length, 2 * seg, both), BF),
            jax.ShapeDtypeStruct((rows, width), BF),
            jax.ShapeDtypeStruct((slots, groups, 1, 4 * seg), F32),
            jax.ShapeDtypeStruct((8, width), F32),
            jax.ShapeDtypeStruct((width, width), BF),
            jax.ShapeDtypeStruct((width, width), BF),
            jax.ShapeDtypeStruct((width, both), BF),
            jax.ShapeDtypeStruct((width, hidden), BF),
            jax.ShapeDtypeStruct((4, 2 * rows, width), BF),
        ],
        scratch_shapes=[
            pltpu.VMEM((width, width), BF),
            pltpu.VMEM((width, width), BF),
            pltpu.VMEM((4, 8, width // 4), F32),
            sems((7,)),
            sems((34,)),
            sems((34,)),
            sems((6,)),
            sems((6,)),
            sems((2 * length,)),
            sems((2 * length,)),
            sems((4 * length,)),
            sems((4 * length,)),
            sems((2, length)),
            sems((2, length)),
            sems((8,)),
            sems((8,)),
            pltpu.VMEM((8, width // 4), F32),
        ],
        compiler_params=pltpu.CompilerParams(
            collective_id=2, has_side_effects=True, vmem_limit_bytes=60 << 20
        ),
        cost_estimate=pl.CostEstimate(
            flops=6 * rows * width * width, bytes_accessed=40 << 20, transcendentals=0
        ),
    )(lengths, tokens, *smalls, kvw, qw, mw, up, cot)


def feed_kernel(
    second_ref,
    cot_ref,
    down_all_ref,
    up_ref,
    upw_ref,
    ubias_ref,
    residual_ref,
    vec_ref,
    down_ref,
    dres_ref,
    red_ref,
    down_part_ref,
    up_part_ref,
    ubias_part_ref,
    vsum_ref,
    first_ref,
    tokens_v,
    cots_v,
    up_v,
    down_v,
    active_v,
    dupper_v,
    sib_out,
    sib_in,
    chip_out,
    chip_in,
    acc_v,
    stage_v,
    credit,
    load_sem,
    stage_sem,
    gs_send,
    gs_recv,
    rs_send,
    rs_recv,
    *,
    length,
):
    rows, width = second_ref.shape
    hidden = up_ref.shape[1]
    half = rows // 2
    chunk = 2 * rows
    y, c, z, x = [lax.axis_index(name) for name in ("y", "c", "z", "x")]
    sib, to_x, to_y = {"c": 1 - c}, {"x": 1 - x}, {"y": 1 - y}
    diag = {"x": 1 - x, "y": 1 - y}
    chips = (None, to_x, to_y, diag)

    loads = [
        pltpu.make_async_copy(second_ref, tokens_v.at[pl.ds(0, rows)], load_sem.at[0]),
        pltpu.make_async_copy(cot_ref, cots_v.at[pl.ds(0, rows)], load_sem.at[1]),
        pltpu.make_async_copy(
            down_all_ref.at[pl.ds(rows, 5 * rows)], cots_v.at[pl.ds(rows, 5 * rows)], load_sem.at[2]
        ),
    ]
    block = hidden // length
    quarter = width // 4
    place = y * 2 + c
    ups_in = []
    for flip in range(1, 4):
        span = pl.ds(pl.multiple_of((place ^ flip) * quarter, quarter), quarter)
        ups_in.append(pltpu.make_async_copy(up_ref.at[span], up_v.at[span], load_sem.at[3 + flip]))
    own_rows = pl.ds(pl.multiple_of(place * quarter, quarter), quarter)
    for b in range(length):
        start = place * (2 * hidden) + (2 * b + x) * block
        ups_in.append(
            pltpu.make_async_copy(
                upw_ref.at[:, pl.ds(pl.multiple_of(start, block), block)],
                up_v.at[own_rows, pl.ds(b * block, block)],
                load_sem.at[7 + length + b],
            )
        )
    downs_in = [
        pltpu.make_async_copy(
            down_ref.at[pl.ds(pl.multiple_of((2 * b + x) * block, block), block)],
            down_v.at[pl.ds(b * block, block)],
            load_sem.at[7 + b],
        )
        for b in range(length)
    ]
    for load in loads + downs_in + ups_in:
        load.start()
    barrier = pltpu.get_barrier_semaphore()
    for device in (sib, to_x, to_y, diag):
        pl.semaphore_signal(barrier, inc=1, device_id=device, device_id_type=MESH)
    for step in (-1, 1):
        @pl.when((z + step >= 0) & (z + step < length))
        def hello():
            pl.semaphore_signal(barrier, inc=1, device_id={"z": z + step}, device_id_type=MESH)
    inner = (z > 0).astype(jnp.int32) + (z < length - 1).astype(jnp.int32)
    pl.semaphore_wait(barrier, 4 + inner)
    loads[0].wait()

    same, other = (0, rows), (rows, rows)
    top, bottom = (0, half), (half, half)

    def gather(index, chip, span_src, chip_dst, span_dst, device):
        src = tokens_v.at[pl.ds(chip * chunk + span_src[0], span_src[1])]
        dst = tokens_v.at[pl.ds(chip_dst * chunk + span_dst[0], span_dst[1])]
        return remote(src, dst, gs_send, gs_recv, index, device)

    send_x = gather(0, 0, same, 1, same, to_x)
    send_y = gather(1, 0, same, 2, same, to_y)
    share = [gather(2 + k, k, same, k, other, sib) for k in range(4)]
    diag_x = gather(6, 2, top, 3, top, to_x)
    diag_y = gather(7, 1, bottom, 3, bottom, to_y)
    send_x.start()
    send_y.start()
    share[0].start()

    loads[1].wait()
    loads[2].wait()
    for load in downs_in:
        load.wait()

    def cot_part(chip, start, size):
        return cots_v.at[pl.ds(chip * chunk + start, size)]

    cot_dx = remote(cot_part(2, 0, half), cot_part(3, 0, half), gs_send, gs_recv, 8, to_x)
    cot_dy = remote(cot_part(1, half, half), cot_part(3, half, half), gs_send, gs_recv, 9, to_y)
    cot_dc = remote(cot_part(3, 0, rows), cot_part(3, rows, rows), gs_send, gs_recv, 10, sib)

    def grad_active(span, index):
        dupper_v[span, :] = dot(cots_v[span, :], down_v[...], ((1,), (1,))).astype(BF)

    @pl.loop(0, 3)
    def near_grads(k):
        grad_active(pl.ds(pl.multiple_of(k * chunk, chunk), chunk), k)

    for load in ups_in:
        load.wait()

    def chip_work(k):
        block = pl.ds(k * chunk, chunk)

        @tiles(hidden // 512, 512)
        def columns(cols, _):
            if k < 3:
                upper = dot(tokens_v[block, :], up_v[:, cols]) + ubias_ref[:, cols]
                active, slope = gelu_pair(upper)
                active_v[block, cols] = active.astype(BF)
                d_upper = (dupper_v[block, cols].astype(F32) * slope).astype(BF)
            else:
                d_active = dot(cots_v[block, :], down_v[cols, :], ((1,), (1,)))
                d_upper = (d_active * dupper_v[block, cols].astype(F32)).astype(BF)
            dupper_v[block, cols] = d_upper
            part = jnp.sum(d_upper.astype(F32), axis=0, keepdims=True)
            if k == 0:
                ubias_part_ref[:, cols] = part
            else:
                ubias_part_ref[:, cols] += part

        theirs, mine = pl.ds(k * chunk + rows, rows), pl.ds(k * chunk, rows)

        @tiles(width // 1024, 1024)
        def to_sibling(cols, _):
            sib_out[k, :, cols] = dot(dupper_v[theirs, :], up_v[cols, :], ((1,), (1,))).astype(BF)

        pair = remote(sib_out.at[k], sib_in.at[k], rs_send, rs_recv, k, sib)
        pair.start()

        @tiles(width // 1024, 1024)
        def keep(cols, _):
            dres_ref[:, cols] = dot(dupper_v[mine, :], up_v[cols, :], ((1,), (1,)))

        pair.wait_recv()

        def total(span):
            value = dres_ref[span, :] + sib_in[k, span, :].astype(F32)
            if k == 0:
                acc_v[span, :] = value
            else:
                chip_out[k - 1, span, :] = value.astype(BF)

        for_rows(rows, total)
        if k == 0:
            return [pair]
        far = remote(chip_out.at[k - 1], chip_in.at[k - 1], rs_send, rs_recv, 3 + k, chips[k])
        far.start()
        return [pair, far]

    share[0].wait_recv()
    sent = chip_work(0)
    send_x.wait_recv()
    share[1].start()
    diag_y.start()
    send_y.wait_recv()
    share[2].start()
    diag_x.start()
    cot_dx.start()
    cot_dy.start()
    share[1].wait_recv()
    sent += chip_work(1)
    share[2].wait_recv()
    sent += chip_work(2)
    diag_x.wait_recv()
    diag_y.wait_recv()
    share[3].start()
    share[3].wait_recv()

    @tiles(hidden // 512, 512)
    def last_slopes(cols, _):
        block = pl.ds(3 * chunk, chunk)
        upper = dot(tokens_v[block, :], up_v[:, cols]) + ubias_ref[:, cols]
        active, slope = gelu_pair(upper)
        active_v[block, cols] = active.astype(BF)
        dupper_v[block, cols] = slope.astype(BF)

    cot_dx.wait_recv()
    cot_dy.wait_recv()
    cot_dc.start()
    cot_dc.wait_recv()

    @pl.loop(0, 2)
    def downs(n):
        block = pl.ds(pl.multiple_of(n * 512, 512), 512)
        copies = []
        for m in range(2):
            cols = pl.ds(m * (width // 2), width // 2)
            stage_v[m] = dot(active_v[:, block], cots_v[:, cols], ((0,), (0,))).astype(BF)
            copy = pltpu.make_async_copy(
                stage_v.at[m], down_part_ref.at[block, cols], stage_sem.at[m * length]
            )
            copy.start()
            copies.append(copy)
        for copy in copies:
            copy.wait()

    line_block = hidden // length
    ends = []
    for n in range(2):
        for way, device in ((0, {"z": z + 1}), (1, {"z": z - 1})):
            b = length - 1 if way == 0 else 0
            part = down_part_ref.at[pl.ds(b * line_block, line_block)] if n else up_part_ref.at[b]
            ends.append(remote(part, first_ref.at[n, way], rs_send, rs_recv, 11 + 2 * n + way, device))

    def send_ends(n):
        for way, edge in ((0, 0), (1, length - 1)):
            @pl.when(z == edge)
            def send_end():
                ends[2 * n + way].start()

    send_ends(1)
    sent += chip_work(3)

    pl.semaphore_signal(credit, inc=1, device_id=sib, device_id_type=MESH)
    pl.semaphore_wait(credit, 1)

    piece = quarter // length

    @pl.loop(0, 2)
    def ups(lane_half):
        lanes = pl.ds(pl.multiple_of(lane_half * hidden, hidden), hidden)
        copies = []
        for n in range(2):
            cols = pl.ds(pl.multiple_of((lane_half * 2 + n) * quarter, quarter), quarter)
            stage_v[n] = dot(tokens_v[:, cols], dupper_v[...], ((0,), (0,))).astype(BF)
            for level in range(length):
                copy = pltpu.make_async_copy(
                    stage_v.at[n, pl.ds(level * piece, piece)],
                    up_part_ref.at[level, pl.ds(n * piece, piece), lanes],
                    stage_sem.at[n * length + level],
                )
                copy.start()
                copies.append(copy)
        for copy in copies:
            copy.wait()

    send_ends(0)

    for k in range(4):
        sent[0 if k == 0 else 2 * k - 1].wait_send()

    def out_pair(k):
        return remote(sib_out.at[k], sib_in.at[k], rs_send, rs_recv, 7 + k, sib)

    @pl.loop(0, 4)
    def outs_away(k):
        theirs = pl.ds(pl.multiple_of(k * chunk + rows, rows), rows)

        @tiles(width // 1024, 1024)
        def columns(cols, _):
            sib_out[k, :, cols] = dot(active_v[theirs, :], down_v[:, cols]).astype(BF)

        out_pair(k).start()

    @pl.loop(0, 4)
    def outs_here(k):
        mine = pl.ds(pl.multiple_of(k * chunk, rows), rows)

        @tiles(width // 1024, 1024)
        def columns(cols, _):
            dres_ref[:, cols] = dot(active_v[mine, :], down_v[:, cols])

        out_pair(k).wait_recv()

        def total(span):
            sib_in[k, span, :] = (dres_ref[span, :] + sib_in[k, span, :].astype(F32)).astype(BF)

        for_rows(rows, total)

    red_copy = pltpu.make_async_copy(sib_in, red_ref, load_sem.at[3])
    red_copy.start()

    for k in range(3):
        remote(chip_out.at[k], chip_in.at[k], rs_send, rs_recv, 4 + k, chips[k + 1]).wait_recv()
    vsum_ref[...] = jnp.zeros(vsum_ref.shape, F32)

    def norm_back(span):
        d_second = acc_v[span, :]
        for k in range(3):
            d_second = d_second + chip_in[k, span, :].astype(F32)
        unit, rstd = norm_rows(residual_ref[span, :])
        d_out = cots_v[span, :].astype(F32)
        d_residual = d_out + norm_backward(d_second, unit, rstd, vec_ref[4:5, :])
        dres_ref[span, :] = d_residual
        vsum_ref[0:1, :] += jnp.sum(d_second * unit, axis=0, keepdims=True)
        vsum_ref[1:2, :] += jnp.sum(d_second, axis=0, keepdims=True)
        vsum_ref[2:3, :] += jnp.sum(d_residual.astype(BF).astype(F32), axis=0, keepdims=True)
        vsum_ref[3:4, :] += jnp.sum(d_out, axis=0, keepdims=True)

    for_rows(rows, norm_back)
    red_copy.wait()
    for n in range(2):
        for way, edge in ((0, 0), (1, length - 1)):
            @pl.when(z == edge)
            def end_sent():
                ends[2 * n + way].wait_send()

            @pl.when(z == (1 if way == 0 else length - 2))
            def end_here():
                ends[2 * n + way].wait_recv()

    for k in range(4):
        out_pair(k).wait_send()
    for copy in [send_x, send_y, diag_x, diag_y, cot_dx, cot_dy, cot_dc] + share + sent[2::2]:
        copy.wait_send()


def feed(second, d_down, down_all, up_mine, up_weight, ubias, residual, vectors, down_weight, length):
    rows, width = second.shape
    hidden = up_mine.shape[1]
    hbm = pl.BlockSpec(memory_space=pltpu.HBM)
    vmem = pl.BlockSpec(memory_space=pltpu.VMEM)
    sems = pltpu.SemaphoreType.DMA
    return pl.pallas_call(
        functools.partial(feed_kernel, length=length),
        in_specs=[hbm, hbm, hbm, hbm, hbm, vmem, vmem, vmem, hbm],
        out_specs=[vmem, hbm, hbm, hbm, vmem, vmem, hbm],
        out_shape=[
            jax.ShapeDtypeStruct((rows, width), F32),
            jax.ShapeDtypeStruct((4, rows, width), BF),
            jax.ShapeDtypeStruct((hidden, width), BF),
            jax.ShapeDtypeStruct((length, hidden // length, width), BF),
            jax.ShapeDtypeStruct((1, hidden), F32),
            jax.ShapeDtypeStruct((8, width), F32),
            jax.ShapeDtypeStruct((2, 2, hidden // length, width), BF),
        ],
        scratch_shapes=[
            pltpu.VMEM((8 * rows, width), BF),
            pltpu.VMEM((8 * rows, width), BF),
            pltpu.VMEM((width, hidden), BF),
            pltpu.VMEM((hidden, width), BF),
            pltpu.VMEM((8 * rows, hidden), BF),
            pltpu.VMEM((8 * rows, hidden), BF),
            pltpu.VMEM((4, rows, width), BF),
            pltpu.VMEM((4, rows, width), BF),
            pltpu.VMEM((3, rows, width), BF),
            pltpu.VMEM((3, rows, width), BF),
            pltpu.VMEM((rows, width), F32),
            pltpu.VMEM((2, 512, 1024), BF),
            pltpu.SemaphoreType.REGULAR,
            sems((7 + 2 * length,)),
            sems((2 * length,)),
            sems((11,)),
            sems((11,)),
            sems((15,)),
            sems((15,)),
        ],
        compiler_params=pltpu.CompilerParams(
            collective_id=4, has_side_effects=True, vmem_limit_bytes=62 << 20
        ),
        cost_estimate=pl.CostEstimate(
            flops=12 * 8 * rows * width * hidden, bytes_accessed=40 << 20, transcendentals=0
        ),
    )(second, d_down, down_all, up_mine, up_weight, ubias, residual, vectors, down_weight)


class Links:
    def __init__(self, send_sems, recv_sems, count):
        self.send_sems, self.recv_sems, self.count = send_sems, recv_sems, count
        self.used = 0

    def copy(self, src, dst, device):
        index = self.used
        self.used += 1
        assert index < self.count
        return self.again(src, dst, device, index)

    def again(self, src, dst, device, index):
        return remote(src, dst, self.send_sems, self.recv_sems, index, device)


class LineSum:
    def __init__(self, links, z, length, parts, landing, source=None, given=None):
        self.z, self.length, self.parts, self.landing = z, length, parts, landing
        self.source = parts if source is None else source
        self.given = given
        self.copies, self.indices = {}, {}
        self.links = links

    def position(self, way):
        return self.z if way == 0 else self.length - 1 - self.z

    def block(self, way, t):
        index = self.length - t + self.position(way)
        index = index if way == 0 else self.length - 1 - index
        return jnp.clip(index, 0, self.length - 1)

    def clear(self):
        last = self.length - 1
        for way in range(2):
            @pl.when(self.position(way) == 0)
            def zero():
                ref = self.landing(way, last)
                ref[...] = jnp.zeros(ref.shape, ref.dtype)

    def direct(self, t, ways=(0, 1)):
        for way in ways:
            device = {"z": self.z + (1 if way == 0 else -1)}
            index = self.links.used
            copy = self.links.copy(
                self.source.at[self.block(way, t)], self.landing(way, t), device
            )
            self.copies[way, t] = copy
            self.indices[way, t] = index

            @pl.when(self.position(way) == 0)
            def first():
                copy.start()

    def onward(self, t):
        for way in range(2):
            pos = self.position(way)
            device = {"z": self.z + (1 if way == 0 else -1)}
            ref = self.landing(way, t - 1)
            passed = self.links.again(ref, self.landing(way, t), device, self.indices[way, t])

            @pl.when((pos >= 1) & (pos <= t - 1))
            def add():
                if t == 2 and self.given is not None:
                    self.given[way].wait()
                else:
                    self.copies[way, t - 1].wait_recv()
                add_rows(ref, self.parts.at[self.block(way, t)])
                passed.start()

    def step(self, t):
        self.direct(t)
        if t > 1:
            self.onward(t)

    def finish(self, own, out):
        last = self.length - 1
        for way in range(2):
            @pl.when(self.position(way) >= 1)
            def arrive():
                self.copies[way, last].wait_recv()

        right, left = self.landing(0, last), self.landing(1, last)
        rows = out.shape[0]
        tile = min(rows, ROW_TILE)

        @pl.loop(0, rows // tile)
        def add(index):
            span = pl.ds(pl.multiple_of(index * tile, tile), tile)
            out[span, :] = (
                own[span, :].astype(F32) + right[span, :].astype(F32) + left[span, :].astype(F32)
            ).astype(out.dtype)

    def settle(self, t):
        for way in range(2):
            @pl.when((self.position(way) <= t - 1) & (self.position(way) < self.length - 1))
            def sent():
                self.copies[way, t].wait_send()

    def drain(self):
        for t in range(1 if self.given is None else 2, self.length):
            self.settle(t)


def add_rows(ref, term):
    rows = ref.shape[0]
    tile = min(rows, ROW_TILE)

    @pl.loop(0, rows // tile)
    def add(index):
        span = pl.ds(pl.multiple_of(index * tile, tile), tile)
        ref[span, :] = (ref[span, :].astype(F32) + term[span, :].astype(F32)).astype(ref.dtype)


class GradSum:
    def __init__(self, links, where, length, width, cols, left, right, bufs):
        self.y, self.c, self.z, self.x = where
        self.length, self.width, self.half = length, width, cols // 2
        self.left, self.right = left, right
        self.cols = cols
        (
            self.left_own,
            self.left_out,
            self.left_in,
            self.right_in,
            self.send1,
            self.recv1,
            self.send2,
            self.recv2,
            self.hold,
            self.zpart,
            self.zland,
        ) = bufs
        self.links = links
        self.sent = []
        self.left_copy = self.sum_copy = None

    def begin(self, copy):
        copy.start()
        self.sent.append(copy)
        return copy

    def share(self):
        quarter = self.width // 4
        block = quarter // (2 * self.length)
        for core, target in ((1 - self.c, self.left_out), (self.c, self.left_own)):
            for y_part in range(2):
                lanes = pl.ds(pl.multiple_of((y_part * 2 + core) * quarter, quarter), quarter)
                turned = self.left[:, lanes].T
                for x_part in range(2):
                    for level in range(self.length):
                        start = (level * 2 + x_part) * block
                        target[y_part * 2 + x_part, level * block : (level + 1) * block, :] = turned[
                            start : start + block
                        ]
        sib = {"c": 1 - self.c}
        self.left_copy = self.begin(self.links.copy(self.left_out, self.left_in, sib))
        self.share_right()

    def share_right(self):
        sib = {"c": 1 - self.c}
        self.right_copy = self.begin(self.links.copy(self.right, self.right_in, sib))

    def share_sums(self, sums, own, out, landing):
        self.sum_own, self.sum_in = own, landing
        quarter = self.width // 4
        block = quarter // (2 * self.length)
        for core, target in ((1 - self.c, out), (self.c, own)):
            for y_part in range(2):
                lanes = pl.ds(pl.multiple_of((y_part * 2 + core) * quarter, quarter), quarter)
                filler = jnp.zeros((own.shape[2] - sums.shape[0], quarter), F32)
                turned = jnp.concatenate([sums[:, lanes], filler], axis=0).T.astype(BF)
                for x_part in range(2):
                    for level in range(self.length):
                        start = (level * 2 + x_part) * block
                        target[y_part * 2 + x_part, level * block : (level + 1) * block, :] = turned[
                            start : start + block
                        ]
        self.sum_copy = self.begin(self.links.copy(out, landing, {"c": 1 - self.c}))

    def term(self, y_part, x_part, cols):
        g = y_part * 2 + x_part
        if cols.start >= self.right.shape[1]:
            total = self.sum_own[g].astype(F32) + self.sum_in[g].astype(F32)
            return jnp.concatenate([total, jnp.zeros((total.shape[0], cols.size - total.shape[1]), F32)], axis=1)
        return dot(self.left_own[g], self.right[:, cols]) + dot(self.left_in[g], self.right_in[:, cols])

    def columns(self, side, fn):
        count = self.half // 128
        size = 128 * max(n for n in range(1, 5) if count % n == 0)
        for j in range(self.half // size):
            fn(pl.ds(side * self.half + j * size, size), pl.ds(j * size, size))

    def first(self):
        if self.left_copy is not None:
            self.left_copy.wait_recv()
        self.right_copy.wait_recv()
        if self.sum_copy is not None:
            self.sum_copy.wait_recv()
        for n in range(2):

            def over_y(cols, local):
                self.send1[0, n, :, local] = self.term(1 - self.y, n, cols).astype(BF)

            def over_x(cols, local):
                self.send1[1, n, :, local] = self.term(n, 1 - self.x, cols).astype(BF)

            self.columns(0, over_y)
            self.columns(1, over_x)
        self.copies1 = [
            self.begin(
                self.links.copy(self.send1.at[side], self.recv1.at[side], device)
            )
            for side, device in ((0, {"y": 1 - self.y}), (1, {"x": 1 - self.x}))
        ]

    def second(self):
        for copy in self.copies1:
            copy.wait_recv()

        def a_out(cols, local):
            term = self.term(self.y, 1 - self.x, cols) + self.recv1[0, 1 - self.x, :, local].astype(F32)
            self.send2[0, :, local] = term.astype(BF)

        def b_out(cols, local):
            term = self.term(1 - self.y, self.x, cols) + self.recv1[1, 1 - self.y, :, local].astype(F32)
            self.send2[1, :, local] = term.astype(BF)

        def a_keep(cols, local):
            self.hold[:, cols] = self.term(self.y, self.x, cols) + self.recv1[0, self.x, :, local].astype(F32)

        def b_keep(cols, local):
            self.hold[:, cols] = self.term(self.y, self.x, cols) + self.recv1[1, self.y, :, local].astype(F32)

        self.columns(0, a_out)
        self.columns(1, b_out)
        self.copies2 = [
            self.begin(
                self.links.copy(self.send2.at[side], self.recv2.at[side], device)
            )
            for side, device in ((0, {"x": 1 - self.x}), (1, {"y": 1 - self.y}))
        ]
        self.columns(0, a_keep)
        self.columns(1, b_keep)

    def third(self, out):
        for copy in self.copies2:
            copy.wait_recv()
        block = self.hold.shape[0] // self.length
        for side in range(2):

            def add(cols, local):
                total = self.hold[:, cols] + self.recv2[side, :, local].astype(F32)
                self.hold[:, cols] = total
                for level in range(self.length):
                    self.zpart[level, :, cols] = total[level * block : (level + 1) * block].astype(BF)

            self.columns(side, add)
        rows = pl.ds(pl.multiple_of(self.z * block, block), block)
        out[...] = self.hold[rows, :]
        self.line = LineSum(
            self.links,
            self.z,
            self.length,
            self.zpart,
            lambda way, t: self.zland.at[way, t - 1],
        )

    def finish(self, out):
        self.line.finish(out, out)

    def drain(self):
        for copy in self.sent:
            copy.wait_send()
        self.line.drain()


def back_kernel(
    lengths_ref,
    dres_ref,
    q_ref,
    kv_ref,
    mixed_ref,
    lse_ref,
    vec_ref,
    wkv_ref,
    vsum_ref,
    ubias_ref,
    tokens_ref,
    first_ref,
    wq_ref,
    wm_ref,
    red_ref,
    down_part,
    up_part,
    first_ref_z,
    tgrad_ref,
    query_ref,
    keyval_ref,
    mixer_ref,
    up_ref,
    ubias_out,
    far_ref,
    down_last,
    w_v,
    dmix_v,
    dmixed_v,
    right_v,
    dfirst_v,
    dkv_v,
    keep_v,
    xsend_v,
    xrecv_v,
    csend_v,
    crecv_v,
    line_v,
    land_v,
    last_v,
    upsend_v,
    uprecv_v,
    sums_v,
    s_own,
    s_out,
    s_in,
    ub_part,
    ub_land,
    left_own,
    left_out,
    left_in,
    right_in,
    send1,
    recv1,
    send2,
    recv2,
    hold,
    zpart,
    zland,
    zpart_q,
    zland_q,
    pair_v,
    k_right,
    k_send1,
    k_recv1,
    k_send2,
    k_recv2,
    k_hold,
    k_zpart,
    k_zland,
    load_sem,
    credit,
    send_sems,
    recv_sems,
    *,
    length,
    slots,
    with_length,
    count,
):
    rows, width = dres_ref.shape
    seg = rows // slots
    both = wkv_ref.shape[1]
    head_dim = both // 2
    heads = width // head_dim
    group = 4
    y, c, z, x = [lax.axis_index(name) for name in ("y", "c", "z", "x")]
    place = y * 2 + c
    sib, to_x, to_y, diag = {"c": 1 - c}, {"x": 1 - x}, {"y": 1 - y}, {"x": 1 - x, "y": 1 - y}
    links = Links(send_sems, recv_sems, count)
    scale = head_dim ** (-0.5)

    def load(src, dst, n):
        copy = pltpu.make_async_copy(src, dst, load_sem.at[n])
        copy.start()
        return copy

    load_up = load(up_part, line_v.at[0], 0)
    load_down = load(down_part, line_v.at[1], 1)
    strip = w_v.shape[1]

    class Strips:
        def __init__(self, ref):
            self.ref, self.loads = ref, {}

        def start(self, j):
            if (j + 1) * strip <= width:
                self.loads[j] = load(self.ref.at[pl.ds(j * strip, strip)], w_v.at[j % 2], 2 + j % 2)

        def over(self, fn):
            for j in range(width // strip):
                self.loads[j].wait()
                fn(pl.ds(j * strip, strip), w_v.at[j % 2])
                self.start(j + 2)

    mixer_strips, query_strips = Strips(wm_ref), Strips(wq_ref)
    mixer_strips.start(0)
    mixer_strips.start(1)

    def landing(n, final):
        return lambda way, t: land_v.at[n, way, t - 1] if t < length - 1 else final.at[way]

    given = [
        [
            pltpu.make_async_copy(first_ref_z.at[n, way], land_v.at[n, way, 0], load_sem.at[4 + 2 * n + way])
            for way in range(2)
        ]
        for n in range(2)
    ]
    for way, inner in ((0, 1), (1, length - 2)):
        @pl.when(z == inner)
        def load_first():
            given[0][way].start()
            given[1][way].start()

    up_line = LineSum(links, z, length, line_v.at[0], landing(0, last_v), up_part, given[0])
    down_line = LineSum(links, z, length, line_v.at[1], landing(1, down_last), down_part, given[1])
    lanes = ubias_ref.shape[1] // length
    for level in range(length):
        ub_part[level] = jnp.broadcast_to(ubias_ref[:, level * lanes : (level + 1) * lanes], ub_part.shape[1:])
    ubias_line = LineSum(links, z, length, ub_part, lambda way, t: ub_land.at[way, t - 1])
    bufs = (left_own, left_out, left_in, right_in, send1, recv1, send2, recv2, hold)
    where = (y, c, z, x)
    mixer = GradSum(links, where, length, width, width, mixed_ref, dmix_v, bufs + (zpart, zland))
    query = GradSum(links, where, length, width, width, dmix_v, right_v, bufs + (zpart_q, zland_q))
    keyval = GradSum(
        links,
        where,
        length,
        width,
        2 * both,
        dmix_v,
        pair_v,
        (left_own, left_out, left_in)
        + (k_right, k_send1, k_recv1, k_send2, k_recv2, k_hold, k_zpart, k_zland),
    )
    up_line.clear()
    for way, edge in ((0, 0), (1, length - 1)):
        @pl.when(z == edge)
        def clear_edge():
            zland[way, length - 2] = jnp.zeros(zland.shape[2:], BF)
            zland_q[way, length - 2] = jnp.zeros(zland_q.shape[2:], BF)
            k_zland[way, length - 2] = jnp.zeros(k_zland.shape[2:], BF)
            ub_land[way, length - 2] = jnp.zeros(ub_land.shape[2:], F32)

    @pl.when(z == length - 1)
    def clear_hops():
        crecv_v[...] = jnp.zeros(crecv_v.shape, BF)

    barrier = pltpu.get_barrier_semaphore()
    plane = []
    for flip in range(1, 8):
        device = {"y": y ^ (flip // 4), "c": c ^ (flip // 2 % 2), "x": x ^ (flip % 2)}
        plane.append(device)
    for device in plane:
        pl.semaphore_signal(barrier, inc=1, device_id=device, device_id_type=MESH)
    for other in range(length):
        @pl.when(other != z)
        def hello():
            pl.semaphore_signal(barrier, inc=1, device_id={"z": other}, device_id_type=MESH)
    pl.semaphore_wait(barrier, 7 + length - 1)

    sent = []

    def begin(copy):
        copy.start()
        sent.append(copy)
        return copy

    far = [
        links.copy(red_ref.at[k + 1], far_ref.at[k], device)
        for k, device in enumerate((to_x, to_y, diag))
    ]
    ubias_line.direct(1)
    ubias_line.direct(2)
    ubias_line.direct(3)
    up_line.direct(2)
    down_line.direct(2)

    def to_bf(span):
        dmix_v[span, :] = dres_ref[span, :].astype(BF)

    for_rows(rows, to_bf)
    mixer.share()
    ubias_line.onward(2)
    load_up.wait()
    up_line.onward(2)
    load_down.wait()
    down_line.onward(2)

    def mix_back(cols, strip_v):
        dmixed_v[:, cols] = dot(dmix_v[...], strip_v[...], ((1,), (1,))).astype(BF)

    mixer_strips.over(mix_back)
    query_strips.start(0)
    query_strips.start(1)
    mixer.first()

    def attend(s, g):
        lanes = pl.ds(pl.multiple_of(g * group * head_dim, group * head_dim), group * head_dim)
        span = pl.ds(s * seg, seg)

        def stack(wide):
            return jnp.concatenate(
                [wide[:, h * head_dim : (h + 1) * head_dim] for h in range(group)], axis=0
            )

        queries = stack(q_ref[span, lanes])
        d_mixed = stack(dmixed_v[span, lanes])
        inner = mixed_ref[span, lanes].astype(F32) * dmixed_v[span, lanes].astype(F32)
        delta = jnp.concatenate(
            [
                jnp.sum(inner[:, h * head_dim : (h + 1) * head_dim].T, axis=0, keepdims=True)
                for h in range(group)
            ],
            axis=1,
        )
        lse = lse_ref[s, g]

        def step(t, accum, diagonal):
            keys = kv_ref[s, t, :, :head_dim]
            values = kv_ref[s, t, :, head_dim:]
            scores = dot(keys, queries, ((1,), (1,))) * scale
            if diagonal or with_length:
                key_pos = lax.broadcasted_iota(jnp.int32, (2 * seg, seg), 0)
                allowed = None
                if diagonal:
                    query_pos = lax.broadcasted_iota(jnp.int32, (2 * seg, seg), 1) + x * seg
                    allowed = key_pos <= query_pos
                if with_length:
                    inside = key_pos + (z - t) * (2 * seg) < lengths_ref[s]
                    allowed = inside if allowed is None else allowed & inside
                bias = jnp.where(allowed, 0.0, NEG_LARGE).astype(F32)
                scores = scores + jnp.concatenate([bias] * group, axis=1)
            probs = jnp.exp(scores - lse)
            d_probs = dot(values, d_mixed, ((1,), (1,)))
            d_scores = (probs * (d_probs - delta)).astype(BF)
            dkv_v[t, :, :head_dim] += dot(d_scores, queries) * scale
            dkv_v[t, :, head_dim:] += dot(probs.astype(BF), d_mixed)
            return accum + dot(keys, d_scores, ((0,), (0,)))

        accum = step(0, jnp.zeros((head_dim, group * seg), F32), True)
        accum = lax.fori_loop(1, z + 1, lambda t, a: step(t, a, False), accum)
        right_v[span, lanes] = (
            jnp.concatenate([accum[:, h * seg : (h + 1) * seg].T for h in range(group)], axis=1) * scale
        ).astype(BF)

    x_copies = []
    for s in range(slots):
        for t in range(length):
            dkv_v[t] = jnp.zeros(dkv_v.shape[1:], F32)

        @pl.loop(0, heads // group)
        def over_groups(g):
            attend(s, g)

        for t in range(length):
            keep_v[s, t] = dkv_v[t, pl.ds(pl.multiple_of(x * seg, seg), seg), :].astype(BF)
            xsend_v[s, t] = dkv_v[t, pl.ds(pl.multiple_of((1 - x) * seg, seg), seg), :].astype(BF)
        x_copies.append(begin(links.copy(xsend_v.at[s], xrecv_v.at[s], to_x)))
    load_tokens = load(tokens_ref, dmixed_v, 8)
    mixer.second()

    neighbours = ((0, sib), (1, to_y), (2, to_x))
    for n, device in neighbours:
        pl.semaphore_signal(credit.at[n], inc=1, device_id=device, device_id_type=MESH)
    for copy in mixer.sent[:4]:
        copy.wait_send()
    load_first = load(first_ref, dmix_v, 9)
    for n, _ in neighbours:
        pl.semaphore_wait(credit.at[n], 1)
    load_first.wait()
    query.share()
    query.first()
    mixer.third(mixer_ref)
    for n, device in neighbours[1:]:
        pl.semaphore_signal(credit.at[2 + n], inc=1, device_id=device, device_id_type=MESH)

    for copy in x_copies:
        copy.wait_recv()
    hops = [links.copy(csend_v.at[t - 1], crecv_v.at[t - 1], {"z": z - 1}) for t in range(1, length)]
    for t in range(length - 1, -1, -1):
        @pl.when(t <= z)
        def hop():
            if t + 1 < length:
                @pl.when(z < length - 1)
                def arrive():
                    hops[t].wait_recv()

            total = keep_v[:, t].astype(F32) + xrecv_v[:, t].astype(F32)
            if t + 1 < length:
                total = total + crecv_v[t].astype(F32)
            if t:
                csend_v[t - 1] = total.astype(BF)
                hops[t - 1].start()
            else:
                for s in range(slots):
                    pair_v[s * seg : (s + 1) * seg, :] = total[s].astype(BF)

    keyval.share_right()
    up_line.direct(3)
    down_line.direct(3)
    for t in range(1, length):
        mixer.line.direct(t)
    up_line.onward(3)
    ubias_line.onward(3)

    def first_back(cols, strip_v):
        dfirst_v[:, cols] = dot(right_v[...], strip_v[...], ((1,), (1,))) + dot(
            pair_v[...], wkv_ref[cols, :], ((1,), (1,))
        )

    query_strips.over(first_back)
    load_tokens.wait()

    sums_v[...] = jnp.zeros(sums_v.shape, F32)

    def first_norm_back(span):
        unit, rstd = norm_rows(dmixed_v[span, :].astype(F32))
        d_first = dfirst_v[span, :]
        dmixed_v[span, :] = (
            dres_ref[span, :] + norm_backward(d_first, unit, rstd, vec_ref[0:1, :])
        ).astype(BF)
        sums_v[0:1, :] += jnp.sum(d_first * unit, axis=0, keepdims=True)
        sums_v[1:2, :] += jnp.sum(d_first, axis=0, keepdims=True)
        sums_v[2:3, :] += jnp.sum(right_v[span, :].astype(F32), axis=0, keepdims=True)

    for_rows(rows, first_norm_back)
    tgrad_copy = load(dmixed_v, tgrad_ref, 0)
    sums_v[4:8, :] = vsum_ref[0:4, :]

    devices = 8 * length
    entries, span = head_dim // devices, width // devices
    v_sum = jnp.sum(pair_v[:, head_dim:].astype(F32), axis=0, keepdims=True)
    v_rows = jnp.broadcast_to(v_sum, (8, head_dim)).astype(BF)
    for j in range(width // 256):
        entry = lax.broadcasted_iota(jnp.int32, (head_dim, 256), 0)
        target = lax.broadcasted_iota(jnp.int32, (head_dim, 256), 1) + j * 256
        spread = (target // span == entry // entries) & (target % span == entry % entries)
        sums_v[3:4, j * 256 : (j + 1) * 256] = dot(v_rows, jnp.where(spread, 1.0, 0.0).astype(BF))[0:1]
    keyval.share_sums(sums_v, s_own, s_out, s_in)

    for copy in mixer.sent[4:]:
        copy.wait_send()
    for n, _ in neighbours[1:]:
        pl.semaphore_wait(credit.at[2 + n], 1)
    query.second()
    keyval.first()
    down_line.onward(3)
    query.third(query_ref)
    for t in range(1, length):
        query.line.direct(t)
    keyval.second()

    tgrad_copy.wait()
    upsum_v = dmixed_v
    up_line.finish(line_v.at[0, z], upsum_v)
    hidden = upsum_v.shape[1] // 2
    piece = upsum_v.shape[0] // 2
    block = piece // 2
    for f in range(4):
        for x_part in range(2):
            start = (f % 2) * piece + x_part * block
            lanes = slice((f // 2) * hidden, (f // 2 + 1) * hidden)
            upsend_v[f * 2 + x_part] = upsum_v[start : start + block, lanes]
    mine = place * 2 + x
    up_copies = []
    for flip, device in zip(range(1, 8), plane):
        up_copies.append(begin(links.copy(upsend_v.at[mine ^ flip], uprecv_v.at[flip], device)))
    for copy in far:
        begin(copy)
    keyval.third(keyval_ref)
    for t in range(1, length):
        keyval.line.direct(t)
    for t in range(2, length):
        mixer.line.onward(t)
        query.line.onward(t)
        keyval.line.onward(t)
    out_block = hidden // length

    def place_up(flip, ref):
        source = mine ^ flip
        base = (source // 2) * (2 * hidden) + (source % 2) * out_block
        for level in range(length):
            lanes = pl.ds(pl.multiple_of(base + level * 2 * out_block, out_block), out_block)
            up_ref[:, lanes] = ref[:, level * out_block : (level + 1) * out_block].astype(up_ref.dtype)

    place_up(0, upsend_v.at[mine])
    for flip, copy in zip(range(1, 8), up_copies):
        copy.wait_recv()
        place_up(flip, uprecv_v.at[flip])
    mixer.finish(mixer_ref)
    for copy in far:
        copy.wait_recv()
    query.finish(query_ref)
    keyval.finish(keyval_ref)
    ubias_line.finish(ub_part.at[z], ubias_out)
    for way in range(2):
        @pl.when(down_line.position(way) >= 1)
        def down_landed():
            down_line.copies[way, length - 1].wait_recv()
    for copy in sent:
        copy.wait_send()
    mixer.line.drain()
    ubias_line.drain()
    query.drain()
    keyval.drain()
    up_line.drain()
    down_line.drain()
    for t in range(1, length):
        @pl.when(t <= z)
        def hopped():
            hops[t - 1].wait_send()


def back(lengths, vmem_args, hbm_args, slots, length, with_length):
    d_residual, kv, wkv = vmem_args[0], vmem_args[2], vmem_args[6]
    rows, width = d_residual.shape
    seg = rows // slots
    both = wkv.shape[1]
    cols = width
    hidden = width // 2
    block = width // (8 * length)
    count = 96 + 16 * length
    hbm = pl.BlockSpec(memory_space=pltpu.HBM)
    vmem = pl.BlockSpec(memory_space=pltpu.VMEM)
    sems = pltpu.SemaphoreType.DMA

    def half(*dims):
        return pltpu.VMEM(dims, BF)

    return pl.pallas_call(
        functools.partial(
            back_kernel, length=length, slots=slots, with_length=with_length, count=count
        ),
        in_specs=[pl.BlockSpec(memory_space=pltpu.SMEM)]
        + [vmem] * len(vmem_args)
        + [hbm] * len(hbm_args),
        out_specs=[hbm] + [vmem] * 5 + [hbm, hbm],
        out_shape=[
            jax.ShapeDtypeStruct((rows, width), BF),
            jax.ShapeDtypeStruct((block, cols), F32),
            jax.ShapeDtypeStruct((block, 2 * both), F32),
            jax.ShapeDtypeStruct((block, width), F32),
            jax.ShapeDtypeStruct((block, 8 * hidden), BF),
            jax.ShapeDtypeStruct((8, hidden // length), F32),
            jax.ShapeDtypeStruct((3, rows, width), BF),
            jax.ShapeDtypeStruct((2, hidden // length, width), BF),
        ],
        scratch_shapes=[
            half(2, width // 4, width),
            half(rows, width),
            half(rows, width),
            half(rows, cols),
            pltpu.VMEM((rows, width), F32),
            pltpu.VMEM((length, 2 * seg, both), F32),
            half(slots, length, seg, both),
            half(slots, length, seg, both),
            half(slots, length, seg, both),
            half(length - 1, slots, seg, both),
            half(length - 1, slots, seg, both),
            half(2, length, hidden // length, width),
            half(2, 2, length - 2, hidden // length, width),
            half(2, hidden // length, width),
            half(8, block, hidden),
            half(8, block, hidden),
            pltpu.VMEM((8, width), F32),
            half(4, width // 8, 128),
            half(4, width // 8, 128),
            half(4, width // 8, 128),
            pltpu.VMEM((length, 8, hidden // length), F32),
            pltpu.VMEM((2, length - 1, 8, hidden // length), F32),
            half(4, width // 8, rows),
            half(4, width // 8, rows),
            half(4, width // 8, rows),
            half(rows, cols),
            half(2, 2, width // 8, cols // 2),
            half(2, 2, width // 8, cols // 2),
            half(2, width // 8, cols // 2),
            half(2, width // 8, cols // 2),
            pltpu.VMEM((width // 8, cols), F32),
            half(length, block, width),
            half(2, length - 1, block, width),
            half(length, block, cols),
            half(2, length - 1, block, cols),
            half(rows, both),
            half(rows, both),
            half(2, 2, width // 8, both),
            half(2, 2, width // 8, both),
            half(2, width // 8, both),
            half(2, width // 8, both),
            pltpu.VMEM((width // 8, 2 * both), F32),
            half(length, block, 2 * both),
            half(2, length - 1, block, 2 * both),
            sems((10,)),
            pltpu.SemaphoreType.REGULAR((5,)),
            sems((count,)),
            sems((count,)),
        ],
        compiler_params=pltpu.CompilerParams(
            collective_id=3, has_side_effects=True, vmem_limit_bytes=125 << 19
        ),
        cost_estimate=pl.CostEstimate(
            flops=12 * rows * width * width, bytes_accessed=40 << 20, transcendentals=0
        ),
    )(lengths, *vmem_args, *hbm_args)


def finish_fast(given, kept, weights):
    tokens, lengths, d_down, up_weight, down_weight, up_bias, where, slots, length, with_length = given
    second, residual, first, queries, kv_all, mixed, lse, vectors = kept
    full_query, full_mixer, full_keyval, up_mine, down_all = weights
    y, c, z, x = where
    rows, width = second.shape
    flat = tokens.reshape(rows, width)
    d_residual, reduced, down_part, up_part, ubias_part, vsum, ends = feed(
        second, d_down, down_all, up_mine, up_weight, up_bias, residual, vectors, down_weight, length
    )
    tokens_grad, query_grad, keyval_all, mixer_grad, up_grad, ubias, far, down_last = back(
        lengths,
        (d_residual, queries, kv_all, mixed, lse, vectors, full_keyval, vsum, ubias_part),
        (flat, first, full_query, full_mixer, reduced, down_part.reshape(length, -1, width), up_part, ends),
        slots,
        length,
        with_length,
    )
    down_grad = pick(down_part.reshape(length, -1, width), z, 0).astype(F32)
    down_grad = down_grad + jnp.where(z > 0, down_last[0].astype(F32), 0.0)
    down_grad = down_grad + jnp.where(z < length - 1, down_last[1].astype(F32), 0.0)
    output = residual + vectors[6:7]
    for term in (reduced[0], far[0], far[1], far[2]):
        output = output + term.astype(F32)
    layer_out = output.astype(BF).reshape(tokens.shape)
    both = full_keyval.shape[1]
    v_block = both // 2 // (8 * length)
    mine = keyval_all[:, both : both + 8].T
    return (
        layer_out,
        tokens_grad.reshape(tokens.shape),
        mine[0],
        mine[1],
        query_grad,
        mine[2],
        keyval_all[:, :both],
        mine[3, :v_block],
        mixer_grad,
        mine[6],
        mine[4],
        mine[5],
        up_grad.astype(F32),
        ubias[0],
        down_grad,
        mine[7],
    )


def body(
    tokens,
    lengths,
    cotangent,
    norm_gain,
    norm_shift,
    query_weight,
    query_bias,
    keyval_weight,
    value_bias,
    mixer_weight,
    mixer_bias,
    ffnorm_gain,
    ffnorm_shift,
    up_weight,
    up_bias,
    down_weight,
    down_bias,
):
    y, c, z, x = [lax.axis_index(name) for name in ("y", "c", "z", "x")]
    length = lax.axis_size("z")
    place = y * 2 + c
    slots, seg, width = tokens.shape
    rows = slots * seg
    head_dim = value_bias.shape[0] * 4
    hidden = up_weight.shape[1]
    hidden_block = hidden // (8 * length)
    hidden_mine = hidden // 8
    with_length = 2 * length * seg > MIN_LEN
    scal = jnp.concatenate([jnp.stack([z, x]).astype(jnp.int32), lengths])

    quarter = width // 4
    v_part = value_bias.shape[0]
    lane = jnp.arange(quarter, dtype=jnp.int32) - place * v_part
    v_wide = jnp.tile(value_bias, quarter // v_part)
    v_place = jnp.where((lane >= 0) & (lane < v_part), v_wide, jnp.zeros_like(v_wide))
    small = [
        v
        for v in (
            norm_gain,
            norm_shift,
            query_bias,
            mixer_bias,
            ffnorm_gain,
            ffnorm_shift,
            down_bias,
            v_place,
        )
    ]

    down_mine = pick(down_weight.reshape(length, 2, hidden_block, width), x, 1).reshape(
        hidden_mine, width
    )
    up_bias_mine = pick(up_bias.reshape(length, 2, hidden_block), x, 1).reshape(1, hidden_mine)
    aligned = hidden_block % 128 == 0
    up_given = up_weight
    if not aligned:
        up_given = pick(up_weight.reshape(quarter, 4, length, 2, hidden_block), x, 3)
        up_given = up_given.reshape(quarter, 4, hidden_mine).transpose(1, 0, 2)

    token_pos = (z * 2 + x) * seg + jnp.arange(seg, dtype=jnp.int32)
    valid = (token_pos[None, :] < lengths[:, None]).astype(F32).reshape(rows, 1)
    d_down = cotangent.reshape(rows, width)
    if with_length:
        d_down = (d_down.astype(F32) * valid).astype(BF)
    d_out = d_down.astype(F32)

    flat = tokens.reshape(rows, width)
    (
        second,
        residual,
        first,
        queries,
        kv_all,
        mixed,
        lse,
        vectors,
        full_query,
        full_mixer,
        full_keyval,
        up_mine,
        down_all,
    ) = front(
        lengths,
        flat,
        small,
        keyval_weight,
        query_weight,
        mixer_weight,
        up_given,
        d_down,
        slots,
        length,
        with_length,
        aligned,
        hidden_mine,
    )
    if aligned and length == 4:
        return finish_fast(
            (
                tokens,
                lengths,
                d_down,
                up_weight,
                down_weight,
                up_bias_mine.astype(F32),
                (y, c, z, x),
                slots,
                length,
                with_length,
            ),
            (second, residual, first, queries, kv_all, mixed, lse, vectors),
            (full_query, full_mixer, full_keyval, up_mine, down_all.reshape(8 * rows, width)),
        )
    inputs = flat.astype(F32)
    gain, ffgain, d_bias = vectors[0:1], vectors[4:5], vectors[6:7]
    unit1, rstd1 = norm_stats(inputs)
    unit2, rstd2 = norm_stats(residual)
    q_t, mixed_t = queries.T, mixed.T

    d_second, out_parts, down_part, up_part, ubias_part = ffn(
        second,
        down_all.reshape(8 * rows, width),
        up_mine,
        up_bias_mine.astype(F32),
        down_mine,
        length,
    )
    output = residual + scatter_plane([out_parts[i] for i in range(4)]) + d_bias
    layer_out = output.astype(BF).reshape(tokens.shape)
    down_grad = scatter_line(down_part.reshape(length, hidden_block, width), z, length)
    ubias_grad = scatter_line(ubias_part.reshape(length, hidden_block), z, length)
    out_rows = width // (8 * length)
    up_sum = scatter_line(up_part, z, length).astype(BF)
    up_rows = lax.all_to_all(
        up_sum.reshape(8, out_rows, hidden_mine), ("y", "c", "x"), 0, 0, tiled=True
    )
    up_grad = (
        up_rows.reshape(4, 2, out_rows, length, hidden_block)
        .transpose(2, 0, 3, 1, 4)
        .reshape(out_rows, hidden)
        .astype(F32)
    )

    d_residual = d_out + norm_backward(d_second, unit2, rstd2, ffgain)
    d_mix = d_residual.astype(BF)
    d_mixed_t = dot(full_mixer, d_mix, ((1,), (1,))).astype(BF)
    where = (y, c, z, x)
    sizes = (length, width)
    mixer_all = scatter_all(
        mixed,
        d_mix,
        (
            jnp.sum(d_mix.astype(F32), axis=0),
            jnp.sum(d_second * unit2, axis=0),
            jnp.sum(d_second, axis=0),
            jnp.sum(d_out, axis=0),
        ),
        where,
        sizes,
    )

    dq_t, dkv = attn_backward(scal, q_t, kv_all, mixed_t, d_mixed_t, lse, 4, with_length)
    dkv = dkv.reshape(slots, length, 2, seg, 2 * head_dim)
    running = None
    for step in range(length - 1, -1, -1):
        term = dkv[:, step]
        term = pick(term, x, 1) + swap(pick(term, 1 - x, 1).astype(BF), "x").astype(F32)
        if running is not None:
            term = term + lax.ppermute(
                running.astype(BF), "z", [(i, i - 1) for i in range(1, length)]
            ).astype(F32)
        running = term
    d_keyvals = running.reshape(rows, 2 * head_dim).astype(BF)
    d_first = dot(dq_t, full_query, ((0,), (1,))) + dot(d_keyvals, full_keyval, ((1,), (1,)))
    tokens_grad = (d_residual + norm_backward(d_first, unit1, rstd1, gain)).astype(BF)
    d_queries = dq_t.T
    devices = 8 * length
    vbias = jnp.sum(d_keyvals[:, head_dim:].astype(F32), axis=0)
    vbias = jnp.pad(
        vbias.reshape(devices, head_dim // devices),
        ((0, 0), (0, out_rows - head_dim // devices)),
    ).reshape(width)
    query_all = scatter_all(
        first,
        jnp.concatenate([d_queries, d_keyvals], axis=1),
        (
            jnp.sum(d_first * unit1, axis=0),
            jnp.sum(d_first, axis=0),
            jnp.sum(d_queries.astype(F32), axis=0),
            vbias,
        ),
        where,
        sizes,
    )
    kv_end = width + 2 * head_dim
    return (
        layer_out,
        tokens_grad.reshape(tokens.shape),
        query_all[:, kv_end],
        query_all[:, kv_end + 1],
        query_all[:, :width],
        query_all[:, kv_end + 2],
        query_all[:, width:kv_end],
        query_all[: head_dim // devices, kv_end + 3],
        mixer_all[:, :width],
        mixer_all[:, width],
        mixer_all[:, width + 1],
        mixer_all[:, width + 2],
        up_grad,
        ubias_grad,
        down_grad,
        mixer_all[:, width + 3],
    )


def solution(mesh):
    ctx = mesh.shape["ctx"]
    fine = Mesh(mesh.devices.reshape(2, 2, ctx // 2, 2), ("y", "c", "z", "x"))
    fsdp, both, every = ("y", "c"), ("z", "x"), ("y", "c", "z", "x")
    return jax.shard_map(
        body,
        mesh=fine,
        in_specs=(
            P(fsdp, both, None),
            P(fsdp),
            P(fsdp, both, None),
            P(fsdp),
            P(fsdp),
            P(fsdp, None),
            P(fsdp),
            P(fsdp, None),
            P(fsdp),
            P(fsdp, None),
            P(fsdp),
            P(fsdp),
            P(fsdp),
            P(fsdp, None),
            P(fsdp),
            P(fsdp, None),
            P(fsdp),
        ),
        out_specs=(
            P(fsdp, both, None),
            P(fsdp, both, None),
            P(every),
            P(every),
            P(every, None),
            P(every),
            P(every, None),
            P(every),
            P(every, None),
            P(every),
            P(every),
            P(every),
            P(every, None),
            P(every),
            P(every, None),
            P(every),
        ),
        check_vma=False,
    )
```
